32 devices in a mesh: section: 2 (over z_hi), dp: 8 (over y, x, core), shard: 2 (over z_lo).
Axes of the slice: x: 2, y: 2, z: 4 (z_hi: 2, z_lo: 2; z = z_hi * 2 + z_lo), core: 2. Of those that a mesh axis runs over, the one named last changes fastest.
Arguments:
- tokens: bfloat16 [2, 2048, 1536], P(None, 'dp'), may hold values from -6 to 6
- lengths: int32 [2, 8, 4], P(None, 'dp'), may hold values from 1 to 128, 256 in all within a row
- routes: int32 [2, 2, 2048, 4], P('section', None, 'dp'), may hold values from 0 to 7, all different within a row; in each aligned block of 256 rows (0 to 255, 256 to 511, ..., all dimensions but the last counted through in order) at most 256 rows name the same one
- gates: float32 [2, 2, 2048, 4], P('section', None, 'dp'), may hold values from 0.15 to 0.4
- attn_gain: float32 [2, 1536], P('section'), may hold values from 0.5 to 1.5
- q_weight: bfloat16 [2, 1536, 1536], P('section', None, 'shard'), may hold values from -0.15625 to 0.15625
- key_projection: bfloat16 [2, 1536, 256], P('section', None, 'shard'), may hold values from -0.15625 to 0.15625
- value_projection: bfloat16 [2, 1536, 256], P('section', None, 'shard'), may hold values from -0.15625 to 0.15625
- o_weight: bfloat16 [2, 1536, 1536], P('section', None, 'shard'), may hold values from -0.3125 to 0.3125
- mlp_gain: float32 [2, 1536], P('section'), may hold values from 0.5 to 1.5
- expert_gate: bfloat16 [2, 8, 1536, 768], P('section', 'dp', None, 'shard'), may hold values from -0.15625 to 0.15625
- expert_up: bfloat16 [2, 8, 1536, 768], P('section', 'dp', None, 'shard'), may hold values from -0.15625 to 0.15625
- expert_down: bfloat16 [2, 8, 768, 1536], P('section', 'dp', 'shard'), may hold values from -0.4375 to 0.4375
- cotangent: bfloat16 [2, 2048, 1536], P(None, 'dp'), may hold values from -6 to 6
Outputs:
- section_out: bfloat16 [2, 2, 2048, 1536], P('section', None, 'dp', 'shard')
- input_grad: float32 [2, 2, 2048, 1536], P('section', None, 'dp', 'shard')
- attn_gain_grad: float32 [2, 1536], P('section', 'dp')
- q_weight_grad: float32 [2, 1536, 1536], P('section', 'dp', 'shard')
- k_weight_grad: float32 [2, 1536, 256], P('section', 'dp', 'shard')
- v_weight_grad: float32 [2, 1536, 256], P('section', 'dp', 'shard')
- o_weight_grad: float32 [2, 1536, 1536], P('section', 'dp', 'shard')
- mlp_gain_grad: float32 [2, 1536], P('section', 'dp')
- expert_gate_grad: float32 [2, 8, 1536, 768], P('section', 'dp', None, 'shard')
- expert_up_grad: float32 [2, 8, 1536, 768], P('section', 'dp', None, 'shard')
- expert_down_grad: float32 [2, 8, 768, 1536], P('section', 'dp', 'shard')
The draws below stay inside these ranges and needn't reach their ends.
Inputs may be any that keep to these rules, and one draw needn't show every extreme that they name: `routes`: in each aligned block of 256 rows (one section, micro-batch and index of dp), no expert is named by more than 256 rows, a bound that some block reaches. The 4 lengths of a block sum to 256; the longest is exactly 128.
All inputs are finite; a program needn't handle non-finite values.
Results may differ from the reference program's by a relative error of at most 0.03.
Values may be sent and summed in bfloat16 or wider, within the bound.
No kernel may reach another device: no remote copies, remote signals or barrier semaphores. Data moves between devices by JAX's collectives and lax.ppermute only.
A program may use at most 256 MiB of HBM per device.

```python
import math
import jax
import jax.numpy as jnp
import numpy as np
from jax import lax

MODEL_WIDTH = 1536
QUERY_HEADS = 12
KEY_VALUE_HEADS = 2
HEAD_SIZE = 128
FFE = 768
K = 4
MB = 2
SEQS = 4
MICRO_TOKENS = 256
EXPERTS = 8
TOKENS = 2048
LMOST = 128
CAP = 256
N_DP = 8
N_SHARD = 2


def steps_of(stream_key, dims, cuts, low, high):
    gain, own = 1.0, jax.random.fold_in(stream_key, 6)
    for dim, parts in cuts:
        draws = jnp.exp(jax.random.uniform(jax.random.fold_in(own, dim), (parts,), jnp.float32, low / len(cuts), high / len(cuts)))
        gain = gain * jnp.repeat(draws, dims[dim] // parts).reshape([-1 if axis == dim else 1 for axis in range(len(dims))])
    return gain


def length_profile(number_of, total, reach, skew):
    portions = [(1 << 20) // math.isqrt(rank ** skew) + 1 for rank in range(2, number_of + 1)]
    spare, counts = total - reach - (number_of - 1), [1] * (number_of - 1)
    while spare > 0:
        free = [i for i in range(number_of - 1) if counts[i] < reach]
        pool, budget = sum([portions[i] for i in free]), spare
        for i in free:
            extra = min(reach - counts[i], max(1, budget * portions[i] // pool), spare)
            counts[i] = counts[i] + extra
            spare = spare - extra
    return np.array([reach] + counts)


def uneven(own_key, number_of, total, limit, slope):
    if number_of == 2:
        one = jax.random.randint(own_key, (), max(1, total - limit), min(limit, total - 1) + 1)
        return jnp.stack([one, total - one])
    tallies = jnp.asarray(length_profile(number_of, total, limit, slope), jnp.int32)
    twos = (number_of - 1) // 2
    donor, receiver = tallies[1:1 + 2 * twos:2], tallies[2:2 + 2 * twos:2]
    room = jnp.minimum(donor - 1, limit - receiver)
    moved = jax.random.randint(jax.random.fold_in(own_key, 1), (twos,), 0, 1 << 20) % (room + 1)
    tallies = tallies.at[1:1 + 2 * twos:2].set(donor - moved).at[2:2 + 2 * twos:2].set(receiver + moved)
    return tallies[jax.random.permutation(jax.random.fold_in(own_key, 2), number_of)]


def deal_out(stream_key, own, number, rows, amount, top, most, slope):
    ranking = jax.random.permutation(stream_key, amount)
    heavy_load, usual = shares(amount, rows * top, most, slope, True), shares(amount, rows * top, most, slope, False)
    places = jnp.arange(amount)

    def named(tallies, offset_by):
        used = int((tallies > 0).sum())
        fixed = max(1, used // 4)
        shifted = fixed + (places - fixed + offset_by * (used - fixed)) % max(1, amount - fixed)
        return jnp.zeros((amount,), jnp.int32).at[ranking[jnp.where(places < fixed, places, shifted)]].set(jnp.asarray(tallies, jnp.int32))

    tallies = jnp.where(number % 4 == 0, named(heavy_load, number // 4), named(usual, number - number // 4 - 1))
    mixed = jax.random.permutation(jax.random.fold_in(own, 3), amount)
    source_of, sink = mixed[0:amount // 2 * 2:2], mixed[1:amount // 2 * 2:2]
    slack = jnp.minimum(tallies[source_of] - 1, most - tallies[sink]) // 2
    slack = jnp.where((source_of == ranking[0]) | (sink == ranking[0]) | (tallies[sink] == 0), 0, jnp.maximum(slack, 0))
    shifted = jax.random.randint(jax.random.fold_in(own, 4), (amount // 2,), 0, 1 << 20) % (slack + 1)
    tallies = tallies.at[source_of].add(-shifted).at[sink].add(shifted)
    items = jnp.searchsorted(jnp.cumsum(tallies), jnp.arange(rows * top), side="right").astype(jnp.int32)
    grid = items.reshape(top, rows).T
    grid = grid[jax.random.permutation(jax.random.fold_in(own, 1), rows)]
    offset_by = jax.random.randint(jax.random.fold_in(own, 2), (rows, 1), 0, top)
    return jnp.take_along_axis(grid, (jnp.arange(top)[None, :] + offset_by) % top, axis=1)


def shares(amount, total, limit, slope, full):
    portions = [(1 << 20) // math.isqrt(grade ** slope) + 1 for grade in range(1, amount + 1)]
    largest = limit if full else min(limit, max(-(-total // amount), total * portions[0] // sum(portions)))
    least = 1 if total - largest >= amount - 1 else 0
    holding, spare = [largest] + [least] * (amount - 1), total - largest - least * (amount - 1)
    while spare > 0:
        movable = [i for i in range(1, amount) if holding[i] < largest] or [i for i in range(1, amount) if holding[i] < limit]
        pool, budget = sum([portions[i] for i in movable]), spare
        for i in movable:
            addition = min(limit - holding[i], max(1, budget * portions[i] // pool), spare)
            holding[i] = holding[i] + addition
            spare = spare - addition
    return np.array(holding)


def bell_draw(stream_key, dims, scale, bound, shards=(), kind=jnp.bfloat16):
    loudness = steps_of(stream_key, dims, shards, -0.22, 0.18) if shards else 1.0
    entries = jax.random.normal(stream_key, dims, jnp.float32) * scale * loudness
    return jnp.minimum(jnp.maximum(entries, -bound), bound).astype(kind)


def setup_inputs(seed: int = 0) -> dict:
    streams_of = jax.random.split(jax.random.key(seed), 15)
    tokens = bell_draw(streams_of[0], (MB, TOKENS, MODEL_WIDTH), 1.0, 6.0, ((1, 8),))
    lengths = jax.vmap(lambda own: uneven(own, SEQS, MICRO_TOKENS, LMOST, 2))(jax.random.split(streams_of[1], MB * N_DP)).reshape((MB, N_DP, SEQS)).astype(jnp.int32)
    routes_keys = jax.random.split(jax.random.fold_in(streams_of[2], 1), 2 * MB * TOKENS // MICRO_TOKENS)
    routes_turns = jax.random.permutation(jax.random.fold_in(streams_of[2], 3), 2 * MB * TOKENS // MICRO_TOKENS)
    routes = jax.vmap(lambda own, number: deal_out(jax.random.fold_in(streams_of[2], 2), own, number, MICRO_TOKENS, EXPERTS, K, CAP, 1))(routes_keys, routes_turns).reshape((2, MB, TOKENS, K))
    gates = jnp.clip(jnp.exp(math.log(0.4) - 0.98082923 * jax.random.uniform(streams_of[3], (2, MB, TOKENS, K), jnp.float32) ** steps_of(streams_of[3], (2, MB, TOKENS, K), ((0, 2), (2, 8)), -0.2, 0.2)), 0.15, 0.4)
    attn_gain = jnp.clip(1.0 + 0.1 * jax.random.normal(streams_of[4], (2, MODEL_WIDTH), jnp.float32), 0.5, 1.5)
    q_weight = bell_draw(streams_of[5], (2, MODEL_WIDTH, QUERY_HEADS * HEAD_SIZE), MODEL_WIDTH ** -0.5, 0.15625, ((0, 2), (2, 2)))
    key_projection = bell_draw(streams_of[6], (2, MODEL_WIDTH, KEY_VALUE_HEADS * HEAD_SIZE), MODEL_WIDTH ** -0.5, 0.15625, ((0, 2), (2, 2)))
    value_projection = bell_draw(streams_of[7], (2, MODEL_WIDTH, KEY_VALUE_HEADS * HEAD_SIZE), MODEL_WIDTH ** -0.5, 0.15625, ((0, 2), (2, 2)))
    o_weight = bell_draw(streams_of[8], (2, MODEL_WIDTH, QUERY_HEADS * HEAD_SIZE), (QUERY_HEADS * HEAD_SIZE // 4) ** -0.5, 0.3125, ((0, 2), (2, 2)))
    mlp_gain = jnp.clip(1.0 + 0.1 * jax.random.normal(streams_of[9], (2, MODEL_WIDTH), jnp.float32), 0.5, 1.5)
    expert_gate = bell_draw(streams_of[10], (2, EXPERTS, MODEL_WIDTH, FFE), MODEL_WIDTH ** -0.5, 0.15625, ((0, 2), (1, 8), (3, 2)))
    expert_up = bell_draw(streams_of[11], (2, EXPERTS, MODEL_WIDTH, FFE), MODEL_WIDTH ** -0.5, 0.15625, ((0, 2), (1, 8), (3, 2)))
    expert_down = bell_draw(streams_of[12], (2, EXPERTS, FFE, MODEL_WIDTH), (FFE // 4) ** -0.5, 0.4375, ((0, 2), (1, 8), (2, 2)))
    cotangent = bell_draw(streams_of[13], (MB, TOKENS, MODEL_WIDTH), 1.0, 6.0, ((1, 8),))
    return {"tokens": tokens, "lengths": lengths, "routes": routes, "gates": gates, "attn_gain": attn_gain, "q_weight": q_weight, "key_projection": key_projection, "value_projection": value_projection, "o_weight": o_weight, "mlp_gain": mlp_gain, "expert_gate": expert_gate, "expert_up": expert_up, "expert_down": expert_down, "cotangent": cotangent}


epsilon = 1e-06
masked_value = -1e+30

@jax.custom_vjp
def lower_precision(v):
    return lax.optimization_barrier(v.astype(jnp.bfloat16)).astype(jnp.float32)

@jax.custom_vjp
def lower_precision_back(v):
    return v

def low_keep(v):
    return (lower_precision(v), None)

def low_pass(kept, grad):
    return (grad,)

def back_keep(v):
    return (v, None)

def back_low(kept, grad):
    return (lower_precision(grad),)
lower_precision.defvjp(low_keep, low_pass)
lower_precision_back.defvjp(back_keep, back_low)

def product_full_precision(left_mat, right_mat):
    return jnp.dot(left_mat, right_mat, precision=lax.Precision.HIGHEST)

def norm_rows(values, gain_vec):
    factor = lax.rsqrt(lax.optimization_barrier(jnp.mean(values * values, axis=-1, keepdims=True)) + epsilon)
    return values * factor * gain_vec

def segment_mask(lens_row):
    seq_ends = jnp.cumsum(lens_row)
    position = jnp.arange(MICRO_TOKENS, dtype=jnp.int32)
    segment = lax.optimization_barrier(jnp.sum((position[:, None] >= seq_ends[None, :]).astype(jnp.int32), axis=1))
    return (segment[:, None] == segment[None, :]) & (position[None, :] <= position[:, None])

def attend_block(normalized_input, lens_row, query_matrix, key_matrix, value_matrix, w_out):
    query_group_size = QUERY_HEADS // KEY_VALUE_HEADS
    heads_of_query = lower_precision_back(lower_precision(product_full_precision(normalized_input, query_matrix))).reshape(MICRO_TOKENS, KEY_VALUE_HEADS, query_group_size, HEAD_SIZE)
    heads_of_key = lower_precision_back(lower_precision(product_full_precision(normalized_input, key_matrix))).reshape(MICRO_TOKENS, KEY_VALUE_HEADS, HEAD_SIZE)
    heads_of_value = lower_precision_back(lower_precision(product_full_precision(normalized_input, value_matrix))).reshape(MICRO_TOKENS, KEY_VALUE_HEADS, HEAD_SIZE)
    raw_scores = lower_precision_back(jnp.einsum('qngd,knd->ngqk', heads_of_query, heads_of_key, precision=lax.Precision.HIGHEST))
    scores = jnp.where(segment_mask(lens_row)[None, None], raw_scores * HEAD_SIZE ** (-0.5), masked_value)
    row_max = lax.optimization_barrier(jnp.max(scores, axis=-1, keepdims=True))
    exp_scores = jnp.exp(scores - row_max)
    attn_probs = exp_scores / lax.optimization_barrier(jnp.sum(exp_scores, axis=-1, keepdims=True))
    head_out = lower_precision_back(lower_precision(jnp.einsum('ngqk,knd->qngd', lower_precision(attn_probs), heads_of_value, precision=lax.Precision.HIGHEST)))
    return product_full_precision(head_out.reshape(MICRO_TOKENS, QUERY_HEADS * HEAD_SIZE), w_out.T)

def layer(inputs, lens_mb, route_rows, gate_vals, attn_gain, query_matrix, key_matrix, value_matrix, w_out, mlp_gain, w_gate, w_up, w_down):
    normalized_input = lower_precision(norm_rows(inputs, attn_gain))
    blocks = normalized_input.reshape(N_DP, MICRO_TOKENS, MODEL_WIDTH)

    def one_block(pair_block):
        return jax.checkpoint(attend_block)(pair_block[0], pair_block[1], query_matrix, key_matrix, value_matrix, w_out)
    attention = lax.map(one_block, (blocks, lens_mb)).reshape(TOKENS, MODEL_WIDTH)
    hidden = inputs + lower_precision_back(attention)
    normed_two = lower_precision(norm_rows(hidden, mlp_gain))
    hidden_half = FFE // N_SHARD

    def expert_term(running, stacked):
        gate_mat, up_mat, down_mat, number = stacked
        weight = lax.optimization_barrier(jnp.sum(jnp.where(route_rows == number, gate_vals, 0.0), axis=1))
        for portion in range(N_SHARD):
            columns = slice(portion * hidden_half, (portion + 1) * hidden_half)
            rows_in = lower_precision_back(normed_two)
            gate_out = lower_precision_back(product_full_precision(rows_in, gate_mat[:, columns]))
            up_out = lower_precision_back(product_full_precision(rows_in, up_mat[:, columns]))
            activated = lower_precision(jax.nn.silu(gate_out) * up_out)
            partial_value = lower_precision_back(lower_precision(product_full_precision(activated, down_mat[columns, :])))
            running = running + weight[:, None] * partial_value
        return (running, None)
    numbers = jnp.arange(EXPERTS, dtype=jnp.int32)
    mixture, unused = lax.scan(jax.checkpoint(expert_term), jnp.zeros((TOKENS, MODEL_WIDTH), jnp.float32), (w_gate, w_up, w_down, numbers))
    return hidden + mixture

def reference(tokens, lengths, routes, gates, attn_gain, q_weight, key_projection, value_projection, o_weight, mlp_gain, expert_gate, expert_up, expert_down, cotangent):

    def forward(inputs, shift_in, gain_one, query_matrix, key_matrix, value_matrix, w_out, gain_two, w_gate, w_up, w_down):
        firsts = []
        seconds = []
        for micro_index in range(MB):
            first_out = layer(inputs[micro_index], lengths[micro_index], routes[0, micro_index], gates[0, micro_index], gain_one[0], query_matrix[0], key_matrix[0], value_matrix[0], w_out[0], gain_two[0], w_gate[0], w_up[0], w_down[0])
            passed = lower_precision_back(lower_precision(first_out))
            second = layer(passed + shift_in[micro_index], lengths[micro_index], routes[1, micro_index], gates[1, micro_index], gain_one[1], query_matrix[1], key_matrix[1], value_matrix[1], w_out[1], gain_two[1], w_gate[1], w_up[1], w_down[1])
            firsts.append(passed)
            seconds.append(second)
        return (jnp.stack(seconds), jnp.stack(firsts))
    primals = (tokens.astype(jnp.float32), jnp.zeros((MB, TOKENS, MODEL_WIDTH), jnp.float32), attn_gain.astype(jnp.float32), q_weight.astype(jnp.float32), key_projection.astype(jnp.float32), value_projection.astype(jnp.float32), o_weight.astype(jnp.float32), mlp_gain.astype(jnp.float32), expert_gate.astype(jnp.float32), expert_up.astype(jnp.float32), expert_down.astype(jnp.float32))
    seconds, pullback, firsts = jax.vjp(forward, *primals, has_aux=True)
    grads = pullback(cotangent.astype(jnp.float32))
    section_out = jnp.stack([firsts, seconds]).astype(jnp.bfloat16)
    input_grad = jnp.stack([grads[0], grads[1]])
    return (section_out, input_grad, grads[2], grads[3], grads[4], grads[5], grads[6], grads[7], grads[8], grads[9], grads[10])
```

```python
import jax
import jax.numpy as jnp
import numpy as np
from jax import lax
from jax.sharding import PartitionSpec as P

HEAD_SIZE = 128
epsilon = 1e-06
masked_value = -1e30
bf16 = jnp.bfloat16
f32 = jnp.float32


def wide(a):
    return a.astype(f32)


def dot_nn(a, b):
    return lax.dot_general(a, b, (((1,), (0,)), ((), ())), preferred_element_type=f32)


def dot_nt(a, b):
    return lax.dot_general(a, b, (((1,), (1,)), ((), ())), preferred_element_type=f32)


def dot_tn(a, b):
    return lax.dot_general(a, b, (((0,), (0,)), ((), ())), preferred_element_type=f32)


class Cube:
    def __init__(self):
        peers = lax.axis_size("dp")
        bits = [1 << i for i in range(peers.bit_length() - 1)]
        rest = bits[1:]
        self.core = ("dp", bits[0])
        self.x = ("dp", rest[0])
        self.y = ("dp", rest[len(rest) // 2])
        self.z = ("shard", 1)
        self.extra = [("dp", b) for b in rest if b not in (self.x[1], self.y[1])]
        inner = [0]
        for _, bit in self.extra:
            inner = inner + [m | bit for m in inner]
        self.inner = np.array(inner)
        x, y = self.x[1], self.y[1]
        self.near = [(0, 0), (x, 0), (y, 0), (0, 1)]
        self.far = [(x | y, 0), (y, 1), (x, 1), (x | y, 1)]

    def mate(self, group):
        return [(m | self.core[1], s) for m, s in group]


def swap(value, direction):
    axis, bit = direction
    return lax.ppermute(value, axis, [(i, i ^ bit) for i in range(lax.axis_size(axis))])


def thirds(rows):
    step = -(-rows // 48) * 16
    return [(0, step), (step, 2 * step), (2 * step, rows)]


def gather_rows(cube, own):
    for direction in cube.extra:
        own = jnp.concatenate([own, swap(own, direction)], axis=0)
    rx, ry, rz = swap(own, cube.x), swap(own, cube.y), swap(own, cube.z)
    own_mate = swap(own, cube.core)
    rxy, ryz, rzx = swap(rx, cube.y), swap(ry, cube.z), swap(rz, cube.x)
    near_mate = swap(jnp.concatenate([rx, ry, rz], axis=0), cube.core)
    cuts = thirds(own.shape[0])
    last = [
        swap(block[lo:hi], direction)
        for block, direction, (lo, hi) in zip((rxy, ryz, rzx), (cube.z, cube.x, cube.y), cuts)
    ]
    far_mate = swap(jnp.concatenate([rxy, ryz, rzx], axis=0), cube.core)
    rxyz = jnp.concatenate(last, axis=0)
    last_mate = swap(rxyz, cube.core)
    near = [own, rx, ry, rz, own_mate, near_mate]
    far = [rxy, ryz, rzx, rxyz, far_mate, last_mate]
    return near, far


def low_sum(*terms):
    return sum(wide(t) for t in terms).astype(bf16)


def reduce_rows(cube, near, near_mate, far, far_mate):
    rows = near.shape[0] // 4
    far_in = swap(far_mate, cube.core)
    near_in = swap(near_mate, cube.core)
    far_sum = low_sum(far, far_in)
    cuts = thirds(rows)
    sent = far_sum[3 * rows :]
    directions = (cube.z, cube.x, cube.y)
    arrived = [swap(sent[lo:hi], d) for d, (lo, hi) in zip(directions, cuts)]
    middle = []
    for i, (lo, hi) in enumerate(cuts):
        block = far_sum[i * rows : (i + 1) * rows]
        middle.append(
            low_sum(block, jnp.pad(arrived[i], ((lo, rows - hi), (0, 0))))
        )
    back = [swap(middle[0], cube.y), swap(middle[1], cube.z), swap(middle[2], cube.x)]
    outer = [
        low_sum(near[i * rows : (i + 1) * rows], near_in[i * rows : (i + 1) * rows], back[i - 1])
        for i in (1, 2, 3)
    ]
    ends = [swap(t, d) for t, d in zip(outer, (cube.x, cube.y, cube.z))]
    total = wide(near[:rows]) + wide(near_in[:rows]) + wide(ends[0]) + wide(ends[1]) + wide(ends[2])
    for direction in reversed(cube.extra):
        half = total.shape[0] // 2
        total = total[:half] + wide(swap(total[half:].astype(bf16), direction))
    return total


def norm_factor(values):
    return lax.rsqrt(jnp.mean(values * values, axis=1, keepdims=True) + epsilon)


def norm_back(values, factor, gain, grad):
    gain_grad = jnp.sum(grad * values * factor, axis=0, keepdims=True)
    scaled = grad * gain
    inner = jnp.mean(scaled * values, axis=1, keepdims=True)
    return factor * (scaled - values * factor * factor * inner), gain_grad


def stack_heads(rows):
    return jnp.concatenate(
        [rows[:, i : i + HEAD_SIZE] for i in range(0, rows.shape[1], HEAD_SIZE)], axis=0
    )


def spread_heads(stacked, rows):
    return jnp.concatenate(
        [stacked[i : i + rows] for i in range(0, stacked.shape[0], rows)], axis=1
    )


def head_probs(query, key, allowed):
    scores = jnp.where(allowed > 0.0, dot_nt(query, key) * HEAD_SIZE ** (-0.5), masked_value)
    exp_scores = jnp.exp(scores - jnp.max(scores, axis=1, keepdims=True))
    return exp_scores / jnp.sum(exp_scores, axis=1, keepdims=True)


def attention_forward(inputs, allowed, attn_gain, mlp_gain, qkv_w, out_w):
    rows = inputs.shape[0]
    normed = (inputs * norm_factor(inputs) * attn_gain).astype(bf16)
    hidden = inputs
    projected, heads = [], []
    for w, w_out in zip(qkv_w, out_w):
        qkv = dot_nn(normed, w).astype(bf16)
        width = qkv.shape[1] - 2 * HEAD_SIZE
        query = stack_heads(qkv[:, :width])
        key, value = qkv[:, width : width + HEAD_SIZE], qkv[:, width + HEAD_SIZE :]
        tiled = jnp.concatenate([allowed] * (width // HEAD_SIZE), axis=0)
        probs = head_probs(query, key, tiled).astype(bf16)
        head_out = spread_heads(dot_nn(probs, value).astype(bf16), rows)
        hidden = hidden + dot_nt(head_out, w_out)
        projected.append(qkv)
        heads.append(head_out)
    normed_two = (hidden * norm_factor(hidden) * mlp_gain).astype(bf16)
    return hidden, normed_two, projected, heads


def attention_backward(grad, grad_two, inputs, hidden, allowed, attn_gain, mlp_gain, projected, qkv_w, out_w):
    rows = inputs.shape[0]
    normed = (inputs * norm_factor(inputs) * attn_gain).astype(bf16)
    back, mlp_gain_grad = norm_back(hidden, norm_factor(hidden), mlp_gain, grad_two)
    grad_hidden = grad + back
    grad_low = grad_hidden.astype(bf16)
    grad_normed = 0.0
    grads = []
    for qkv, w, w_out in zip(projected, qkv_w, out_w):
        width = qkv.shape[1] - 2 * HEAD_SIZE
        grad_heads = stack_heads(dot_nn(grad_low, w_out).astype(bf16))
        query = stack_heads(qkv[:, :width])
        key, value = qkv[:, width : width + HEAD_SIZE], qkv[:, width + HEAD_SIZE :]
        tiled = jnp.concatenate([allowed] * (width // HEAD_SIZE), axis=0)
        probs = head_probs(query, key, tiled)
        grad_probs = dot_nt(grad_heads, value)
        inner = jnp.sum(probs * grad_probs, axis=1, keepdims=True)
        grad_scores = (probs * (grad_probs - inner) * HEAD_SIZE ** (-0.5)).astype(bf16)
        grad_query = spread_heads(dot_nn(grad_scores, key).astype(bf16), rows)
        grad_key = dot_tn(grad_scores, query).astype(bf16)
        grad_value = dot_tn(probs.astype(bf16), grad_heads).astype(bf16)
        grad_qkv = jnp.concatenate([grad_query, grad_key, grad_value], axis=1)
        grad_normed = grad_normed + dot_nt(grad_qkv, w)
        grads.append(grad_qkv)
    back, attn_gain_grad = norm_back(inputs, norm_factor(inputs), attn_gain, grad_normed)
    return grad_hidden + back, grad_low, normed, grads, attn_gain_grad, mlp_gain_grad


def expert_forward(pieces, gate_col, w_gate, w_up, w_down):
    rows = jnp.concatenate(pieces, axis=0)
    gate_out = dot_nn(rows, w_gate)
    up_out = dot_nn(rows, w_up)
    act = (gate_out / (1.0 + jnp.exp(-gate_out)) * up_out).astype(bf16)
    part = dot_nn(act, w_down)
    part = (part if gate_col is None else gate_col * part).astype(bf16)
    return part, (rows, gate_out.astype(bf16), up_out.astype(bf16))


def expert_backward(pieces, gate_col, saved, w_gate, w_up, w_down):
    rows, gate_low, up_low = saved
    gate_out, up_out = wide(gate_low), wide(up_low)
    grad_rows = jnp.concatenate(pieces, axis=0)
    if gate_col is not None:
        grad_rows = (gate_col * wide(grad_rows)).astype(bf16)
    grad_act = dot_nt(grad_rows, w_down)
    sig = 1.0 / (1.0 + jnp.exp(-gate_out))
    silu = gate_out * sig
    grad_gate = (grad_act * up_out * sig * (1.0 + gate_out * (1.0 - sig))).astype(bf16)
    grad_up = (grad_act * silu).astype(bf16)
    act = (silu * up_out).astype(bf16)
    grad_in = (dot_nt(grad_gate, w_gate) + dot_nt(grad_up, w_up)).astype(bf16)
    weights = (dot_tn(rows, grad_gate), dot_tn(rows, grad_up), dot_tn(act, grad_rows))
    return grad_in, weights


def halves(array):
    half = array.shape[0] // 2
    return array[:half], array[half:]


class Blocks:
    def __init__(self, cube, routes, gates, weights):
        self.cube, self.weights = cube, weights
        me, shard = lax.axis_index("dp"), lax.axis_index("shard")
        rows = routes.shape[1] // lax.axis_size("shard")
        numbers = jnp.arange(lax.axis_size("dp"), dtype=jnp.int32)
        table = jnp.sum(
            jnp.where(routes[:, :rows, :, None] == numbers, gates[:, :rows, :, None], 0.0), axis=2
        )
        everyone = lax.all_gather(table, ("dp", "shard"), axis=0)
        column = lax.dynamic_index_in_dim(everyone, me, 3, keepdims=False)

        def ordered(group):
            order = [(me ^ (m ^ cube.inner)) * lax.axis_size("shard") + (shard ^ s) for m, s in group]
            weighed = jnp.take(column, jnp.concatenate(order), axis=0)
            return [weighed[:, m].reshape(-1, 1) for m in range(routes.shape[0])]

        near = ordered(cube.near + cube.mate(cube.near))
        far = ordered(cube.far + cube.mate(cube.far))
        self.tables = list(zip(near, far))

    def forward(self, own, table):
        results, saved = [], []
        for pieces, column in zip(gather_rows(self.cube, own), table):
            part, kept = expert_forward(pieces, column, *self.weights)
            results += halves(part)
            saved.append(kept)
        return reduce_rows(self.cube, *results), saved

    def backward(self, grad, table, saved):
        results, weights = [], []
        for pieces, column, kept in zip(gather_rows(self.cube, grad), table, saved):
            grad_in, weight_grads = expert_backward(pieces, column, kept, *self.weights)
            results += halves(grad_in)
            weights.append(weight_grads)
        return reduce_rows(self.cube, *results), jax.tree.map(jnp.add, *weights)


class Buckets:
    def __init__(self, cube, routes, gates, weights, capacity):
        self.cube, self.weights, self.capacity = cube, weights, capacity
        micros, self.rows, self.top = routes.shape
        self.experts = lax.axis_size("dp")
        self.tables = []
        for m in range(micros):
            flat = routes[m].reshape(-1)
            onehot = (flat[:, None] == jnp.arange(self.experts, dtype=jnp.int32)).astype(jnp.int32)
            earlier = jnp.cumsum(onehot, axis=0) - onehot
            target = flat * capacity + jnp.sum(earlier * onehot, axis=1)
            source = jnp.full((self.experts * capacity,), flat.shape[0], jnp.int32)
            source = source.at[target].set(jnp.arange(flat.shape[0], dtype=jnp.int32))
            self.tables.append((target, source, gates[m]))

    def exchange(self, rows):
        shape = (self.experts, self.capacity, rows.shape[1])
        moved = lax.all_to_all(rows.reshape(shape), "dp", split_axis=0, concat_axis=0, tiled=True)
        return moved.reshape(rows.shape)

    def whole(self, own):
        return jnp.concatenate([own, swap(own, self.cube.z)], axis=0)

    def folded(self, total):
        own, other = halves(total.astype(bf16))
        return wide(own) + wide(swap(other, self.cube.z))

    def forward(self, own, table):
        target, source, gates = table
        padded = jnp.pad(self.whole(own), ((0, 1), (0, 0)))
        arrived = self.exchange(jnp.take(padded, source // self.top, axis=0))
        part, saved = expert_forward([arrived], None, *self.weights)
        picked = jnp.take(self.exchange(part), target, axis=0).reshape(self.rows, self.top, -1)
        return self.folded(jnp.sum(gates[:, :, None] * picked, axis=1)), saved

    def backward(self, grad, table, saved):
        target, source, gates = table
        scaled = (gates[:, :, None] * wide(self.whole(grad))[:, None, :]).astype(bf16)
        padded = jnp.pad(scaled.reshape(self.rows * self.top, -1), ((0, 1), (0, 0)))
        arrived = self.exchange(jnp.take(padded, source, axis=0))
        grad_in, weights = expert_backward([arrived], None, saved, *self.weights)
        picked = jnp.take(self.exchange(grad_in), target, axis=0).reshape(self.rows, self.top, -1)
        return self.folded(jnp.sum(picked, axis=1, dtype=f32)), weights


def local(
    tokens, lengths, routes, gates, attn_gain, q_weight, key_projection, value_projection,
    o_weight, mlp_gain, expert_gate, expert_up, expert_down, cotangent,
):
    cube = Cube()
    section = lax.axis_index("section")
    shard = lax.axis_index("shard")
    me = lax.axis_index("dp")
    peers, shards = lax.axis_size("dp"), lax.axis_size("shard")
    micros, block_rows, model = tokens.shape
    rows = block_rows // shards
    first = section == 0

    starts, masks = [], []
    for m in range(micros):
        lens = lengths[m, 0]
        ends = jnp.cumsum(lens)
        longest = jnp.argmax(lens)
        start = ends[longest] - lens[longest]
        starts.append(start)
        position = (jnp.arange(rows, dtype=jnp.int32) + start + rows * shard) % block_rows
        segment = jnp.sum((position[:, None] >= ends[None, :]).astype(jnp.int32), axis=1)
        allowed = (segment[:, None] == segment[None, :]) & (position[None, :] <= position[:, None])
        masks.append(allowed.astype(f32))

    def turned(array, m, count=rows):
        doubled = jnp.concatenate([array, array], axis=0)
        return lax.dynamic_slice_in_dim(doubled, (starts[m] + rows * shard) % block_rows, count, 0)

    def pick(array, slot):
        here, there = array[min(slot, micros - 1)], array[max(slot - 1, 0)]
        return jax.tree.map(lambda a, b: jnp.where(first, a, b), here, there)

    zero_rows = jnp.zeros((rows, model), bf16)
    token_rows = [jnp.where(first, turned(tokens[m], m), zero_rows) for m in range(micros)]
    cot_rows = [jnp.where(first, zero_rows, turned(cotangent[m], m)) for m in range(micros)]

    qkv_own = jnp.concatenate([q_weight[0], key_projection[0], value_projection[0]], axis=1)
    out_own = o_weight[0]

    def other_half(weight):
        share = model // peers
        piece = lax.dynamic_slice_in_dim(weight, me * share, share, 0)
        return lax.all_gather(swap(piece, cube.z), "dp", axis=0, tiled=True)

    qkv_w = (qkv_own, other_half(qkv_own))
    out_w = (out_own, other_half(out_own))
    w_gate, w_up, w_down = expert_gate[0, 0], expert_up[0, 0], expert_down[0, 0]
    gain_one, gain_two = attn_gain[0][None], mlp_gain[0][None]

    routed = jnp.stack([turned(routes[0, m], m, block_rows) for m in range(micros)])
    weighed = jnp.stack([turned(gates[0, m], m, block_rows) for m in range(micros)])
    capacity = 2 * block_rows * routes.shape[3] // peers
    if capacity < block_rows:
        mixture = Buckets(cube, routed, weighed, (w_gate, w_up, w_down), capacity)
    else:
        mixture = Blocks(cube, routed, weighed, (w_gate, w_up, w_down))

    states, outs = [], []
    arriving = zero_rows
    for slot in range(micros + 1):
        fresh = token_rows[slot] if slot < micros else zero_rows
        inputs = wide(fresh + arriving)
        allowed = pick(masks, slot)
        hidden, normed_two, projected, heads = attention_forward(
            inputs, allowed, gain_one, gain_two, qkv_w, out_w
        )
        table = pick(mixture.tables, slot)
        total, saved = mixture.forward(normed_two, table)
        result = (hidden + total).astype(bf16)
        if slot < micros:
            arriving = lax.ppermute(result, "section", [(0, 1)])
        outs.append(result)
        states.append((inputs, hidden, allowed, projected, heads, table, saved))

    expert_sums = None
    coming = zero_rows
    attn_factors, gain_sums, input_grads = [], [], []
    for turn in range(micros + 1):
        inputs, hidden, allowed, projected, heads, table, saved = states[micros - turn]
        grad = coming + (cot_rows[micros - 1 - turn] if turn < micros else zero_rows)
        grad_two, weight_grads = mixture.backward(grad, table, saved)
        expert_sums = (
            weight_grads if expert_sums is None else jax.tree.map(jnp.add, expert_sums, weight_grads)
        )
        grad_input, grad_low, normed, grads, attn_g, mlp_g = attention_backward(
            wide(grad), grad_two, inputs, hidden, allowed, gain_one, gain_two, projected, qkv_w, out_w
        )
        if turn < micros:
            coming = lax.ppermute(grad_input.astype(bf16), "section", [(1, 0)])
        attn_factors.append((normed, grad_low, grads, heads))
        gain_sums.append(jnp.concatenate([attn_g, mlp_g], axis=0))
        input_grads.append(grad_input)

    normed_t = jnp.concatenate([f[0] for f in attn_factors], axis=0).T
    grad_t = jnp.concatenate([f[1] for f in attn_factors], axis=0).T
    full = []
    for g in range(shards):
        grad_qkv = jnp.concatenate([f[2][g] for f in attn_factors], axis=0)
        head_rows = jnp.concatenate([f[3][g] for f in attn_factors], axis=0)
        both = jnp.concatenate([dot_nn(normed_t, grad_qkv), dot_nn(grad_t, head_rows)], axis=1)
        full.append(both.astype(bf16).reshape(peers, model // peers, -1))

    def weight_group(group):
        blocks = []
        for m, s in group:
            block = jnp.take(full[s], me ^ (m ^ cube.inner), axis=0)
            blocks.append(block.reshape(-1, block.shape[2]))
        return jnp.concatenate(blocks, axis=0)

    total = reduce_rows(
        cube,
        weight_group(cube.near),
        weight_group(cube.mate(cube.near)),
        weight_group(cube.far),
        weight_group(cube.mate(cube.far)),
    )
    width = q_weight.shape[2]
    grad_q = total[:, :width]
    grad_k = total[:, width : width + HEAD_SIZE]
    grad_v = total[:, width + HEAD_SIZE : width + 2 * HEAD_SIZE]
    grad_o = total[:, width + 2 * HEAD_SIZE :]
    gain_total = lax.psum(sum(gain_sums), ("dp", "shard"))
    share = model // peers
    gain_total = lax.dynamic_slice_in_dim(gain_total, me * share, share, 1)

    def placed(own, m):
        half = model // shards
        kept = lax.dynamic_slice_in_dim(own, shard * half, half, 1)
        given = lax.dynamic_slice_in_dim(own, (1 - shard) * half, half, 1)
        got = swap(given, cube.z)
        low = jnp.where(shard == 0, kept, got)
        high = jnp.where(shard == 0, got, kept)
        return lax.dynamic_slice_in_dim(
            jnp.concatenate([low, high, low, high], axis=0), (block_rows - starts[m]) % block_rows, block_rows, 0
        )

    section_out = jnp.stack(
        [placed(jnp.where(first, outs[m], outs[m + 1]), m) for m in range(micros)]
    )
    input_grad = jnp.stack(
        [
            placed(jnp.where(first, input_grads[micros - m], input_grads[micros - m - 1]), m)
            for m in range(micros)
        ]
    )
    gate_total, up_total, down_total = expert_sums
    return (
        section_out[None],
        input_grad[None],
        gain_total[0][None],
        grad_q[None],
        grad_k[None],
        grad_v[None],
        grad_o[None],
        gain_total[1][None],
        gate_total[None, None],
        up_total[None, None],
        down_total[None, None],
    )


def solution(mesh):
    in_specs = (
        P(None, "dp", None),
        P(None, "dp", None),
        P("section", None, "dp", None),
        P("section", None, "dp", None),
        P("section", None),
        P("section", None, "shard"),
        P("section", None, "shard"),
        P("section", None, "shard"),
        P("section", None, "shard"),
        P("section", None),
        P("section", "dp", None, "shard"),
        P("section", "dp", None, "shard"),
        P("section", "dp", "shard", None),
        P(None, "dp", None),
    )
    out_specs = (
        P("section", None, "dp", "shard"),
        P("section", None, "dp", "shard"),
        P("section", "dp"),
        P("section", "dp", "shard"),
        P("section", "dp", "shard"),
        P("section", "dp", "shard"),
        P("section", "dp", "shard"),
        P("section", "dp"),
        P("section", "dp", None, "shard"),
        P("section", "dp", None, "shard"),
        P("section", "dp", "shard", None),
    )
    return jax.shard_map(local, mesh=mesh, in_specs=in_specs, out_specs=out_specs, check_vma=False)
```

```python
import jax
import jax.numpy as jnp
import numpy as np
from jax import lax
from jax.sharding import PartitionSpec as P

HEAD_SIZE = 128
epsilon = 1e-06
masked_value = -1e30
bf16 = jnp.bfloat16
f32 = jnp.float32


def wide(a):
    return a.astype(f32)


def dot_nn(a, b):
    return lax.dot_general(a, b, (((1,), (0,)), ((), ())), preferred_element_type=f32)


def dot_nt(a, b):
    return lax.dot_general(a, b, (((1,), (1,)), ((), ())), preferred_element_type=f32)


def dot_tn(a, b):
    return lax.dot_general(a, b, (((0,), (0,)), ((), ())), preferred_element_type=f32)


class Cube:
    def __init__(self):
        peers = lax.axis_size("dp")
        bits = [1 << i for i in range(peers.bit_length() - 1)]
        rest = bits[1:]
        self.core = ("dp", bits[0])
        self.x = ("dp", rest[0])
        self.y = ("dp", rest[len(rest) // 2])
        self.z = ("shard", 1)
        self.extra = [("dp", b) for b in rest if b not in (self.x[1], self.y[1])]
        inner = [0]
        for _, bit in self.extra:
            inner = inner + [m | bit for m in inner]
        self.inner = np.array(inner)
        x, y = self.x[1], self.y[1]
        near = [(0, 0), (x, 0), (y, 0), (0, 1)]
        middle = [(x | y, 0), (y, 1), (x, 1)]
        last = [(x | y, 1)]
        self.stages = [
            (group, [(m | self.core[1], s) for m, s in group]) for group in (near, middle, last)
        ]


def swap(value, direction):
    axis, bit = direction
    return lax.ppermute(value, axis, [(i, i ^ bit) for i in range(lax.axis_size(axis))])


def thirds(rows):
    step = -(-rows // 48) * 16
    return [(0, step), (step, 2 * step), (2 * step, rows)]


def gather_rows(cube, own, work):
    for direction in cube.extra:
        own = jnp.concatenate([own, swap(own, direction)], axis=0)
    near = [swap(own, d) for d in (cube.x, cube.y, cube.z)]
    own_mate = swap(own, cube.core)
    middle = [swap(block, d) for block, d in zip(near, (cube.y, cube.z, cube.x))]
    near_mate = swap(jnp.concatenate(near, axis=0), cube.core)
    done = [work(0, [own, *near, own_mate, near_mate])]
    middle, done = lax.optimization_barrier((middle, done))
    cuts = thirds(own.shape[0])
    last = [
        swap(block[lo:hi], d) for block, d, (lo, hi) in zip(middle, (cube.z, cube.x, cube.y), cuts)
    ]
    middle_mate = swap(jnp.concatenate(middle, axis=0), cube.core)
    done.append(work(1, [*middle, middle_mate]))
    last = jnp.concatenate(last, axis=0)
    done.append(work(2, [last, swap(last, cube.core)]))
    return done


def low_sum(*terms):
    return sum(wide(t) for t in terms).astype(bf16)


def reduce_rows(cube, stages):
    (near, near_mate), (middle, middle_mate), (last, last_mate) = stages
    rows = last.shape[0]
    last_in, middle_in, near_in = [swap(t, cube.core) for t in (last_mate, middle_mate, near_mate)]

    def block(i, *groups):
        return [g[i * rows : (i + 1) * rows] for g in groups]

    cuts = thirds(rows)
    sent = low_sum(last, last_in)
    arrived = [swap(sent[lo:hi], d) for d, (lo, hi) in zip((cube.z, cube.x, cube.y), cuts)]
    sent = [
        low_sum(*block(i, middle, middle_in), jnp.pad(arrived[i], ((lo, rows - hi), (0, 0))))
        for i, (lo, hi) in enumerate(cuts)
    ]
    arrived = [swap(t, d) for t, d in zip(sent, (cube.y, cube.z, cube.x))]
    sent = [low_sum(*block(i + 1, near, near_in), arrived[i]) for i in range(3)]
    arrived = [swap(t, d) for t, d in zip(sent, (cube.x, cube.y, cube.z))]
    total = sum(wide(t) for t in block(0, near, near_in) + arrived)
    for direction in reversed(cube.extra):
        half = total.shape[0] // 2
        total = total[:half] + wide(swap(total[half:].astype(bf16), direction))
    return total


def norm_factor(values):
    return lax.rsqrt(jnp.mean(values * values, axis=1, keepdims=True) + epsilon)


def norm_back(values, factor, gain, grad):
    gain_grad = jnp.sum(grad * values * factor, axis=0, keepdims=True)
    scaled = grad * gain
    inner = jnp.mean(scaled * values, axis=1, keepdims=True)
    return factor * (scaled - values * factor * factor * inner), gain_grad


def stack_heads(rows):
    return jnp.concatenate(
        [rows[:, i : i + HEAD_SIZE] for i in range(0, rows.shape[1], HEAD_SIZE)], axis=0
    )


def spread_heads(stacked, rows):
    return jnp.concatenate(
        [stacked[i : i + rows] for i in range(0, stacked.shape[0], rows)], axis=1
    )


def head_probs(query, key, allowed):
    scores = jnp.where(allowed > 0.0, dot_nt(query, key) * HEAD_SIZE ** (-0.5), masked_value)
    exp_scores = jnp.exp(scores - jnp.max(scores, axis=1, keepdims=True))
    return exp_scores / jnp.sum(exp_scores, axis=1, keepdims=True)


def normed_rows(values, gain):
    return (values * norm_factor(values) * gain).astype(bf16)


def head_group(normed, allowed, w, w_out):
    qkv = dot_nn(normed, w).astype(bf16)
    width = qkv.shape[1] - 2 * HEAD_SIZE
    query = stack_heads(qkv[:, :width])
    key, value = qkv[:, width : width + HEAD_SIZE], qkv[:, width + HEAD_SIZE :]
    tiled = jnp.concatenate([allowed] * (width // HEAD_SIZE), axis=0)
    probs = head_probs(query, key, tiled).astype(bf16)
    head_out = spread_heads(dot_nn(probs, value).astype(bf16), normed.shape[0])
    return dot_nt(head_out, w_out), qkv, head_out


def attention_backward(grad, grad_two, inputs, hidden, allowed, attn_gain, mlp_gain, projected, qkv_w, out_w):
    rows = inputs.shape[0]
    normed = (inputs * norm_factor(inputs) * attn_gain).astype(bf16)
    back, mlp_gain_grad = norm_back(hidden, norm_factor(hidden), mlp_gain, grad_two)
    grad_hidden = grad + back
    grad_low = grad_hidden.astype(bf16)
    grad_normed = 0.0
    grads = []
    for qkv, w, w_out in zip(projected, qkv_w, out_w):
        width = qkv.shape[1] - 2 * HEAD_SIZE
        grad_heads = stack_heads(dot_nn(grad_low, w_out).astype(bf16))
        query = stack_heads(qkv[:, :width])
        key, value = qkv[:, width : width + HEAD_SIZE], qkv[:, width + HEAD_SIZE :]
        tiled = jnp.concatenate([allowed] * (width // HEAD_SIZE), axis=0)
        probs = head_probs(query, key, tiled)
        grad_probs = dot_nt(grad_heads, value)
        inner = jnp.sum(probs * grad_probs, axis=1, keepdims=True)
        grad_scores = (probs * (grad_probs - inner) * HEAD_SIZE ** (-0.5)).astype(bf16)
        grad_query = spread_heads(dot_nn(grad_scores, key).astype(bf16), rows)
        grad_key = dot_tn(grad_scores, query).astype(bf16)
        grad_value = dot_tn(probs.astype(bf16), grad_heads).astype(bf16)
        grad_qkv = jnp.concatenate([grad_query, grad_key, grad_value], axis=1)
        grad_normed = grad_normed + dot_nt(grad_qkv, w)
        grads.append(grad_qkv)
    back, attn_gain_grad = norm_back(inputs, norm_factor(inputs), attn_gain, grad_normed)
    return grad_hidden + back, grad_low, normed, grads, attn_gain_grad, mlp_gain_grad


def expert_forward(pieces, gate_col, w_gate, w_up, w_down):
    rows = jnp.concatenate(pieces, axis=0)
    gate_out = dot_nn(rows, w_gate)
    up_out = dot_nn(rows, w_up)
    act = (gate_out / (1.0 + jnp.exp(-gate_out)) * up_out).astype(bf16)
    part = dot_nn(act, w_down)
    part = (part if gate_col is None else gate_col * part).astype(bf16)
    return part, (rows, gate_out.astype(bf16), up_out.astype(bf16))


def expert_backward(pieces, gate_col, saved, w_gate, w_up, w_down):
    rows, gate_low, up_low = saved
    gate_out, up_out = wide(gate_low), wide(up_low)
    grad_rows = jnp.concatenate(pieces, axis=0)
    if gate_col is not None:
        grad_rows = (gate_col * wide(grad_rows)).astype(bf16)
    grad_act = dot_nt(grad_rows, w_down)
    sig = 1.0 / (1.0 + jnp.exp(-gate_out))
    silu = gate_out * sig
    grad_gate = (grad_act * up_out * sig * (1.0 + gate_out * (1.0 - sig))).astype(bf16)
    grad_up = (grad_act * silu).astype(bf16)
    act = (silu * up_out).astype(bf16)
    grad_in = (dot_nt(grad_gate, w_gate) + dot_nt(grad_up, w_up)).astype(bf16)
    weights = (dot_tn(rows, grad_gate), dot_tn(rows, grad_up), dot_tn(act, grad_rows))
    return grad_in, weights


def halves(array):
    half = array.shape[0] // 2
    return array[:half], array[half:]


class Blocks:
    def __init__(self, cube, routes, gates, weights):
        self.cube, self.weights = cube, weights
        micros = routes.shape[0]
        peers = lax.axis_size("dp")
        rows = routes.shape[1] // lax.axis_size("shard")
        numbers = jnp.arange(peers, dtype=jnp.int32)[:, None, None]
        table = jnp.concatenate(
            [
                jnp.sum(jnp.where(routes[m, :rows].T == numbers, gates[m, :rows].T, 0.0), axis=1)
                for m in range(micros)
            ],
            axis=0,
        )
        places = [(0, 0)]
        for axis, bit in [*cube.extra, cube.core, cube.x, cube.y, cube.z]:
            table = jnp.concatenate([table, swap(table, (axis, bit))], axis=1)
            places += [(m | bit, s) if axis == "dp" else (m, s | bit) for m, s in places]
        mine = [
            lax.dynamic_index_in_dim(table, m * peers + lax.axis_index("dp"), 0, keepdims=False)
            for m in range(micros)
        ]

        def ordered(values, groups):
            order = [places.index((m ^ int(i), s)) for group in groups for m, s in group for i in cube.inner]
            return jnp.concatenate([values[p * rows : (p + 1) * rows] for p in order]).reshape(-1, 1)

        self.tables = [[ordered(values, groups) for groups in cube.stages] for values in mine]

    def forward(self, own, table):
        saved = []

        def work(stage, pieces):
            part, kept = expert_forward(pieces, table[stage], *self.weights)
            saved.append(kept)
            return halves(part)

        return reduce_rows(self.cube, gather_rows(self.cube, own, work)), saved

    def backward(self, grad, table, saved):
        weights = []

        def work(stage, pieces):
            grad_in, weight_grads = expert_backward(pieces, table[stage], saved[stage], *self.weights)
            weights.append(weight_grads)
            return halves(grad_in)

        total = reduce_rows(self.cube, gather_rows(self.cube, grad, work))
        return total, jax.tree.map(lambda *t: sum(t), *weights)


class Buckets:
    def __init__(self, cube, routes, gates, weights, capacity):
        self.cube, self.weights, self.capacity = cube, weights, capacity
        micros, self.rows, self.top = routes.shape
        self.experts = lax.axis_size("dp")
        self.tables = []
        for m in range(micros):
            flat = routes[m].reshape(-1)
            onehot = (flat[:, None] == jnp.arange(self.experts, dtype=jnp.int32)).astype(jnp.int32)
            earlier = jnp.cumsum(onehot, axis=0) - onehot
            target = flat * capacity + jnp.sum(earlier * onehot, axis=1)
            source = jnp.full((self.experts * capacity,), flat.shape[0], jnp.int32)
            source = source.at[target].set(jnp.arange(flat.shape[0], dtype=jnp.int32))
            self.tables.append((target, source, gates[m]))

    def exchange(self, rows):
        shape = (self.experts, self.capacity, rows.shape[1])
        moved = lax.all_to_all(rows.reshape(shape), "dp", split_axis=0, concat_axis=0, tiled=True)
        return moved.reshape(rows.shape)

    def whole(self, own):
        return jnp.concatenate([own, swap(own, self.cube.z)], axis=0)

    def folded(self, total):
        own, other = halves(total.astype(bf16))
        return wide(own) + wide(swap(other, self.cube.z))

    def forward(self, own, table):
        target, source, gates = table
        padded = jnp.pad(self.whole(own), ((0, 1), (0, 0)))
        arrived = self.exchange(jnp.take(padded, source // self.top, axis=0))
        part, saved = expert_forward([arrived], None, *self.weights)
        picked = jnp.take(self.exchange(part), target, axis=0).reshape(self.rows, self.top, -1)
        return self.folded(jnp.sum(gates[:, :, None] * picked, axis=1)), saved

    def backward(self, grad, table, saved):
        target, source, gates = table
        scaled = (gates[:, :, None] * wide(self.whole(grad))[:, None, :]).astype(bf16)
        padded = jnp.pad(scaled.reshape(self.rows * self.top, -1), ((0, 1), (0, 0)))
        arrived = self.exchange(jnp.take(padded, source, axis=0))
        grad_in, weights = expert_backward([arrived], None, saved, *self.weights)
        picked = jnp.take(self.exchange(grad_in), target, axis=0).reshape(self.rows, self.top, -1)
        return self.folded(jnp.sum(picked, axis=1, dtype=f32)), weights


def local(
    tokens, lengths, routes, gates, attn_gain, q_weight, key_projection, value_projection,
    o_weight, mlp_gain, expert_gate, expert_up, expert_down, cotangent,
):
    cube = Cube()
    section = lax.axis_index("section")
    shard = lax.axis_index("shard")
    me = lax.axis_index("dp")
    peers, shards = lax.axis_size("dp"), lax.axis_size("shard")
    micros, block_rows, model = tokens.shape
    rows = block_rows // shards
    first = section == 0

    starts, masks = [], []
    for m in range(micros):
        lens = lengths[m, 0]
        ends = jnp.cumsum(lens)
        longest = jnp.argmax(lens)
        start = ends[longest] - lens[longest]
        starts.append(start)
        both = []
        for side in (shard, 1 - shard):
            position = (jnp.arange(rows, dtype=jnp.int32) + start + rows * side) % block_rows
            segment = jnp.sum((position[:, None] >= ends[None, :]).astype(jnp.int32), axis=1)
            allowed = (segment[:, None] == segment[None, :]) & (position[None, :] <= position[:, None])
            both.append(allowed.astype(f32))
        masks.append(both)

    def turned(array, m, count=rows):
        doubled = jnp.concatenate([array, array], axis=0)
        return lax.dynamic_slice_in_dim(doubled, (starts[m] + rows * shard) % block_rows, count, 0)

    def pick(array, slot):
        here, there = array[min(slot, micros - 1)], array[max(slot - 1, 0)]
        return jax.tree.map(lambda a, b: jnp.where(first, a, b), here, there)

    zero_rows = jnp.zeros((rows, model), bf16)
    token_rows = [
        jnp.where(first, turned(tokens[m], m, block_rows), jnp.zeros_like(tokens[m])) for m in range(micros)
    ]
    cot_rows = [jnp.where(first, zero_rows, turned(cotangent[m], m)) for m in range(micros)]

    qkv_own = jnp.concatenate([q_weight[0], key_projection[0], value_projection[0]], axis=1)
    out_own = o_weight[0]

    def other_half(weight):
        share = model // peers
        piece = lax.dynamic_slice_in_dim(weight, me * share, share, 0)
        return lax.all_gather(swap(piece, cube.z), "dp", axis=0, tiled=True)

    qkv_w = (qkv_own, other_half(qkv_own))
    out_w = (out_own, other_half(out_own))
    w_gate, w_up, w_down = expert_gate[0, 0], expert_up[0, 0], expert_down[0, 0]
    gain_one, gain_two = attn_gain[0][None], mlp_gain[0][None]

    routed = jnp.stack([turned(routes[0, m], m, block_rows) for m in range(micros)])
    weighed = jnp.stack([turned(gates[0, m], m, block_rows) for m in range(micros)])
    capacity = 2 * block_rows * routes.shape[3] // peers
    if capacity < block_rows:
        mixture = Buckets(cube, routed, weighed, (w_gate, w_up, w_down), capacity)
    else:
        mixture = Blocks(cube, routed, weighed, (w_gate, w_up, w_down))

    states, outs = [], []
    arriving = zero_rows
    for slot in range(micros + 1):
        allowed = pick(masks, slot)[0]
        if slot == 0:
            inputs, others = wide(token_rows[0][:rows]), wide(token_rows[0][rows:])
            hidden, qkv, heads = head_group(normed_rows(inputs, gain_one), allowed, qkv_own, out_own)
            sent = head_group(normed_rows(others, gain_one), pick(masks, 0)[1], qkv_own, out_own)
            arrived = [swap(t.astype(bf16), cube.z) for t in sent]
            hidden = inputs + hidden + wide(arrived[0])
            groups = [(qkv, heads), tuple(arrived[1:])]
        else:
            fresh = token_rows[slot][:rows] if slot < micros else zero_rows
            inputs = wide(fresh + arriving)
            normed = normed_rows(inputs, gain_one)
            parts = [head_group(normed, allowed, w, w_out) for w, w_out in zip(qkv_w, out_w)]
            hidden = inputs + sum(p[0] for p in parts)
            groups = [p[1:] for p in parts]
        table = pick(mixture.tables, slot)
        total, saved = mixture.forward(normed_rows(hidden, gain_two), table)
        result = (hidden + total).astype(bf16)
        if slot < micros:
            arriving = lax.ppermute(result, "section", [(0, 1)])
        outs.append(result)
        states.append((inputs, hidden, allowed, groups, table, saved))

    expert_sums = None
    coming = zero_rows
    attn_factors, gain_sums, input_grads = [], [], []
    for turn in range(micros + 1):
        sources = [turn - 1, turn + 1]
        sources = [i if 0 <= i <= micros else None for i in sources]
        if sources[0] is None or sources[1] is None:
            state = states[sources[1] if sources[0] is None else sources[0]]
        else:
            state = jax.tree.map(
                lambda a, b: jnp.where(first, a, b), states[sources[0]], states[sources[1]]
            )
        inputs, hidden, allowed, groups, table, saved = state
        grad = coming + (cot_rows[turn] if turn < micros else zero_rows)
        grad_two, weight_grads = mixture.backward(grad, table, saved)
        expert_sums = (
            weight_grads if expert_sums is None else jax.tree.map(jnp.add, expert_sums, weight_grads)
        )
        grad_input, grad_low, normed, grads, attn_g, mlp_g = attention_backward(
            wide(grad), grad_two, inputs, hidden, allowed, gain_one, gain_two,
            [g[0] for g in groups], qkv_w, out_w,
        )
        if turn < micros:
            coming = lax.ppermute(grad_input.astype(bf16), "section", [(1, 0)])
        attn_factors.append((normed, grad_low, grads, [g[1] for g in groups]))
        gain_sums.append(jnp.concatenate([attn_g, mlp_g], axis=0))
        input_grads.append(grad_input)

    normed_t = jnp.concatenate([f[0] for f in attn_factors], axis=0).T
    grad_t = jnp.concatenate([f[1] for f in attn_factors], axis=0).T
    share = model // peers

    def owned(left, rights):
        full = [dot_nn(left, right).astype(bf16).reshape(peers, share, -1) for right in rights]

        def blocks(group):
            taken = [jnp.take(full[s], me ^ (m ^ cube.inner), axis=0) for m, s in group]
            return jnp.concatenate(taken, axis=0).reshape(-1, rights[0].shape[1])

        return reduce_rows(cube, [tuple(blocks(group) for group in pair) for pair in cube.stages])

    grad_o = owned(
        grad_t, [jnp.concatenate([f[3][g] for f in attn_factors], axis=0) for g in range(shards)]
    )
    total = owned(
        normed_t, [jnp.concatenate([f[2][g] for f in attn_factors], axis=0) for g in range(shards)]
    )
    width = q_weight.shape[2]
    grad_q = total[:, :width]
    grad_k = total[:, width : width + HEAD_SIZE]
    grad_v = total[:, width + HEAD_SIZE :]
    gain_total = sum(gain_sums)
    for direction in [*cube.extra, cube.core, cube.x, cube.y, cube.z]:
        gain_total = gain_total + swap(gain_total, direction)
    gain_total = lax.dynamic_slice_in_dim(gain_total, me * share, share, 1)

    def placed(own, m):
        half = model // shards
        kept = lax.dynamic_slice_in_dim(own, shard * half, half, 1)
        given = lax.dynamic_slice_in_dim(own, (1 - shard) * half, half, 1)
        got = swap(given, cube.z)
        low = jnp.where(shard == 0, kept, got)
        high = jnp.where(shard == 0, got, kept)
        return lax.dynamic_slice_in_dim(
            jnp.concatenate([low, high, low, high], axis=0), (block_rows - starts[m]) % block_rows, block_rows, 0
        )

    section_out = jnp.stack(
        [placed(jnp.where(first, outs[m], outs[m + 1]), m) for m in range(micros)]
    )
    input_grad = jnp.stack(
        [
            placed(jnp.where(first, input_grads[m + 1], input_grads[m]), m)
            for m in range(micros)
        ]
    )
    gate_total, up_total, down_total = expert_sums
    return (
        section_out[None],
        input_grad[None],
        gain_total[0][None],
        grad_q[None],
        grad_k[None],
        grad_v[None],
        grad_o[None],
        gain_total[1][None],
        gate_total[None, None],
        up_total[None, None],
        down_total[None, None],
    )


def solution(mesh):
    in_specs = (
        P(None, "dp", None),
        P(None, "dp", None),
        P("section", None, "dp", None),
        P("section", None, "dp", None),
        P("section", None),
        P("section", None, "shard"),
        P("section", None, "shard"),
        P("section", None, "shard"),
        P("section", None, "shard"),
        P("section", None),
        P("section", "dp", None, "shard"),
        P("section", "dp", None, "shard"),
        P("section", "dp", "shard", None),
        P(None, "dp", None),
    )
    out_specs = (
        P("section", None, "dp", "shard"),
        P("section", None, "dp", "shard"),
        P("section", "dp"),
        P("section", "dp", "shard"),
        P("section", "dp", "shard"),
        P("section", "dp", "shard"),
        P("section", "dp", "shard"),
        P("section", "dp"),
        P("section", "dp", None, "shard"),
        P("section", "dp", None, "shard"),
        P("section", "dp", "shard", None),
    )
    return jax.shard_map(local, mesh=mesh, in_specs=in_specs, out_specs=out_specs, check_vma=False)
```

```python
import functools

import jax
import jax.numpy as jnp
import numpy as np
from jax import lax
from jax.experimental import pallas as pl
from jax.experimental.pallas import tpu as pltpu
from jax.sharding import PartitionSpec as P

HEAD_SIZE = 128
epsilon = 1e-06
masked_value = -1e30
bf16 = jnp.bfloat16
f32 = jnp.float32


def wide(a):
    return a.astype(f32)


def dot_nn(a, b):
    return lax.dot_general(a, b, (((1,), (0,)), ((), ())), preferred_element_type=f32)


def dot_nt(a, b):
    return lax.dot_general(a, b, (((1,), (1,)), ((), ())), preferred_element_type=f32)


def dot_tn(a, b):
    return lax.dot_general(a, b, (((0,), (0,)), ((), ())), preferred_element_type=f32)


class Cube:
    def __init__(self):
        peers = lax.axis_size("dp")
        bits = [1 << i for i in range(peers.bit_length() - 1)]
        rest = bits[1:]
        self.core = ("dp", bits[0])
        self.x = ("dp", rest[0])
        self.y = ("dp", rest[len(rest) // 2])
        self.z = ("shard", 1)
        self.extra = [("dp", b) for b in rest if b not in (self.x[1], self.y[1])]
        inner = [0]
        for _, bit in self.extra:
            inner = inner + [m | bit for m in inner]
        self.inner = np.array(inner)
        x, y = self.x[1], self.y[1]
        near = [(0, 0), (x, 0), (y, 0), (0, 1)]
        middle = [(x | y, 0), (y, 1), (x, 1)]
        last = [(x | y, 1)]
        self.stages = [
            (group, [(m | self.core[1], s) for m, s in group]) for group in (near, middle, last)
        ]


def swap(value, direction):
    axis, bit = direction
    return lax.ppermute(value, axis, [(i, i ^ bit) for i in range(lax.axis_size(axis))])


def thirds(rows):
    step = -(-rows // 48) * 16
    return [(0, step), (step, 2 * step), (2 * step, rows)]


def gather_rows(cube, own, work):
    for direction in cube.extra:
        own = jnp.concatenate([own, swap(own, direction)], axis=0)
    near = [swap(own, d) for d in (cube.x, cube.y, cube.z)]
    own_mate = swap(own, cube.core)
    middle = [swap(block, d) for block, d in zip(near, (cube.y, cube.z, cube.x))]
    near_mate = [swap(block, cube.core) for block in near]
    done = [work(0, [own, *near, own_mate, *near_mate])]
    middle, done = lax.optimization_barrier((middle, done))
    cuts = thirds(own.shape[0])
    last = [
        swap(block[lo:hi], d) for block, d, (lo, hi) in zip(middle, (cube.z, cube.x, cube.y), cuts)
    ]
    middle_mate = [swap(block, cube.core) for block in middle]
    done.append(work(1, [*middle, *middle_mate]))
    last_mate = [swap(block, cube.core) for block in last]
    done.append(work(2, [*last, *last_mate]))
    return done


def low_sum(*terms):
    return sum(wide(t) for t in terms).astype(bf16)


def reduce_rows(cube, stages):
    (near, near_mate), (middle, middle_mate), (last, last_mate) = stages
    rows = last.shape[0]
    last_in, middle_in, near_in = [swap(t, cube.core) for t in (last_mate, middle_mate, near_mate)]

    def block(i, *groups):
        return [g[i * rows : (i + 1) * rows] for g in groups]

    cuts = thirds(rows)
    sent = low_sum(last, last_in)
    arrived = [swap(sent[lo:hi], d) for d, (lo, hi) in zip((cube.z, cube.x, cube.y), cuts)]
    sent = [
        low_sum(*block(i, middle, middle_in), jnp.pad(arrived[i], ((lo, rows - hi), (0, 0))))
        for i, (lo, hi) in enumerate(cuts)
    ]
    arrived = [swap(t, d) for t, d in zip(sent, (cube.y, cube.z, cube.x))]
    sent = [low_sum(*block(i + 1, near, near_in), arrived[i]) for i in range(3)]
    arrived = [swap(t, d) for t, d in zip(sent, (cube.x, cube.y, cube.z))]
    total = sum(wide(t) for t in block(0, near, near_in) + arrived)
    for direction in reversed(cube.extra):
        half = total.shape[0] // 2
        total = total[:half] + wide(swap(total[half:].astype(bf16), direction))
    return total


def norm_factor(values):
    return lax.rsqrt(jnp.mean(values * values, axis=1, keepdims=True) + epsilon)


def norm_back(values, factor, gain, grad):
    gain_grad = jnp.sum(grad * values * factor, axis=0, keepdims=True)
    scaled = grad * gain
    inner = jnp.mean(scaled * values, axis=1, keepdims=True)
    return factor * (scaled - values * factor * factor * inner), gain_grad


def stack_heads(rows):
    return jnp.concatenate(
        [rows[:, i : i + HEAD_SIZE] for i in range(0, rows.shape[1], HEAD_SIZE)], axis=0
    )


def spread_heads(stacked, rows):
    return jnp.concatenate(
        [stacked[i : i + rows] for i in range(0, stacked.shape[0], rows)], axis=1
    )


def head_probs(query, key, allowed):
    scores = jnp.where(allowed > 0.0, dot_nt(query, key) * HEAD_SIZE ** (-0.5), masked_value)
    exp_scores = jnp.exp(scores - jnp.max(scores, axis=1, keepdims=True))
    return exp_scores / jnp.sum(exp_scores, axis=1, keepdims=True)


def normed_rows(values, gain):
    return (values * norm_factor(values) * gain).astype(bf16)


def head_group(normed, allowed, w, w_out):
    qkv = dot_nn(normed, w).astype(bf16)
    width = qkv.shape[1] - 2 * HEAD_SIZE
    query = stack_heads(qkv[:, :width])
    key, value = qkv[:, width : width + HEAD_SIZE], qkv[:, width + HEAD_SIZE :]
    tiled = jnp.concatenate([allowed] * (width // HEAD_SIZE), axis=0)
    probs = head_probs(query, key, tiled).astype(bf16)
    head_out = spread_heads(dot_nn(probs, value).astype(bf16), normed.shape[0])
    return dot_nt(head_out, w_out), qkv, head_out


VMEM = pl.BlockSpec(memory_space=pltpu.VMEM)
SMEM = pl.BlockSpec(memory_space=pltpu.SMEM)
MIB = 1 << 20


def like(shape, dtype):
    return jax.ShapeDtypeStruct(shape, dtype)


def on_device(body, outs, args, flops, mib, scalars=()):
    moved = sum(a.size * a.dtype.itemsize for a in [*args, *outs])
    return pl.pallas_call(
        body,
        out_shape=outs,
        in_specs=[SMEM] * len(scalars) + [VMEM] * len(args),
        out_specs=[VMEM] * len(outs),
        compiler_params=pltpu.CompilerParams(vmem_limit_bytes=mib * MIB),
        cost_estimate=pl.CostEstimate(flops=flops, bytes_accessed=moved, transcendentals=0),
    )(*scalars, *args)


def half_heads_body(inputs, others, mask, other_mask, gain, w, w_out, *outs):
    for rows, allowed, (part, qkv, heads) in (
        (inputs, mask, outs[:3]),
        (others, other_mask, outs[3:]),
    ):
        normed = normed_rows(wide(rows[...]), gain[...])
        value, qkv[...], heads[...] = head_group(normed, allowed[...], w[...], w_out[...])
        part[...] = value.astype(part.dtype)


def half_heads(inputs, others, mask, other_mask, gain, w, w_out):
    rows, model = inputs.shape
    shapes = [
        like((rows, model), f32), like((rows, w.shape[1]), bf16), like((rows, w_out.shape[1]), bf16),
        like((rows, model), bf16), like((rows, w.shape[1]), bf16), like((rows, w_out.shape[1]), bf16),
    ]
    args = [inputs, others, mask, other_mask, gain, w, w_out]
    return on_device(half_heads_body, shapes, args, 4 * rows * (w.size + w_out.size), 32)


def joined_body(inputs, own, other, gain, extra, hidden, payload):
    total = wide(inputs[...]) + own[...] + wide(other[...])
    hidden[...] = total
    model = total.shape[1]
    payload[:, :model] = normed_rows(total, gain[...])
    payload[:, model:] = extra[...]


def joined(inputs, own, other, gain, extra):
    rows, model = inputs.shape
    shapes = [like((rows, model), f32), like((rows, model + extra.shape[1]), bf16)]
    return on_device(joined_body, shapes, [inputs, own, other, gain, extra], 10 * rows * model, 16)


def attention_body(fresh, arriving, mask, gain, gain_two, extra, w0, w1, o0, o1, *outs):
    inputs, hidden, payload, qkv0, qkv1, heads0, heads1 = outs
    rows = fresh[...] + arriving[...]
    inputs[...] = rows
    total = wide(rows)
    normed = normed_rows(total, gain[...])
    for w, w_out, qkv, heads in ((w0, o0, qkv0, heads0), (w1, o1, qkv1, heads1)):
        value, qkv[...], heads[...] = head_group(normed, mask[...], w[...], w_out[...])
        total = total + value
    hidden[...] = total
    model = total.shape[1]
    payload[:, :model] = normed_rows(total, gain_two[...])
    payload[:, model:] = extra[...]


def attention_forward(fresh, arriving, mask, gain, gain_two, extra, qkv_w, out_w):
    rows, model = fresh.shape
    w, w_out = qkv_w[0], out_w[0]
    shapes = [
        like((rows, model), bf16), like((rows, model), f32), like((rows, model + extra.shape[1]), bf16),
        like((rows, w.shape[1]), bf16), like((rows, w.shape[1]), bf16),
        like((rows, w_out.shape[1]), bf16), like((rows, w_out.shape[1]), bf16),
    ]
    args = [fresh, arriving, mask, gain, gain_two, extra, *qkv_w, *out_w]
    outs = on_device(attention_body, shapes, args, 4 * rows * (w.size + w_out.size), 40)
    inputs, hidden, payload, qkv0, qkv1, heads0, heads1 = outs
    return inputs, hidden, payload, [(qkv0, heads0), (qkv1, heads1)]


def attention_back_body(grad, grad_two, inputs, hidden, mask, gain, gain_two, q0, q1, w0, w1, o0, o1, *outs):
    grad_input, grad_input_low, grad_low, normed, g0, g1, gain_grad, gain_two_grad = outs
    rows = inputs.shape[0]
    values = wide(inputs[...])
    normed[...] = normed_rows(values, gain[...])
    total = hidden[...]
    back, gain_two_grad[...] = norm_back(total, norm_factor(total), gain_two[...], grad_two[...])
    grad_hidden = wide(grad[...]) + back
    low = grad_hidden.astype(bf16)
    grad_low[...] = low
    grad_normed = jnp.zeros_like(grad_hidden)
    for qkv_ref, w, w_out, grad_qkv in ((q0, w0, o0, g0), (q1, w1, o1, g1)):
        qkv = qkv_ref[...]
        width = qkv.shape[1] - 2 * HEAD_SIZE
        grad_heads = stack_heads(dot_nn(low, w_out[...]).astype(bf16))
        query = stack_heads(qkv[:, :width])
        key, value = qkv[:, width : width + HEAD_SIZE], qkv[:, width + HEAD_SIZE :]
        tiled = jnp.concatenate([mask[...]] * (width // HEAD_SIZE), axis=0)
        probs = head_probs(query, key, tiled)
        grad_probs = dot_nt(grad_heads, value)
        inner = jnp.sum(probs * grad_probs, axis=1, keepdims=True)
        grad_scores = (probs * (grad_probs - inner) * HEAD_SIZE ** (-0.5)).astype(bf16)
        grad_qkv[:, :width] = spread_heads(dot_nn(grad_scores, key).astype(bf16), rows)
        grad_qkv[:, width : width + HEAD_SIZE] = dot_tn(grad_scores, query).astype(bf16)
        grad_qkv[:, width + HEAD_SIZE :] = dot_tn(probs.astype(bf16), grad_heads).astype(bf16)
        grad_normed = grad_normed + dot_nt(grad_qkv[...], w[...])
    back, gain_grad[...] = norm_back(values, norm_factor(values), gain[...], grad_normed)
    result = grad_hidden + back
    grad_input[...] = result
    grad_input_low[...] = result.astype(bf16)


def attention_backward(grad, grad_two, inputs, hidden, mask, gain, gain_two, projected, qkv_w, out_w):
    rows, model = inputs.shape
    w, w_out = qkv_w[0], out_w[0]
    shapes = [
        like((rows, model), f32), like((rows, model), bf16), like((rows, model), bf16),
        like((rows, model), bf16), like((rows, w.shape[1]), bf16), like((rows, w.shape[1]), bf16),
        like((1, model), f32), like((1, model), f32),
    ]
    args = [grad, grad_two, inputs, hidden, mask, gain, gain_two, *projected, *qkv_w, *out_w]
    return on_device(attention_back_body, shapes, args, 4 * rows * (w.size + w_out.size), 40)


def place(pieces, *targets):
    at = 0
    for piece in pieces:
        rows, first = piece.shape[0], 0
        for target in targets:
            target[at : at + rows, :] = piece[:, first : first + target.shape[1]]
            first += target.shape[1]
        at += rows


def own_gate(extra, me, peers):
    lane = lax.broadcasted_iota(jnp.int32, extra.shape, 1)
    return jnp.sum(jnp.where((lane == me) | (lane == me + peers), wide(extra), 0.0), axis=1, keepdims=True)


def chunked(rows, step):
    count = max(c for c in (128, 192, 256, 384) if rows % c == 0)
    if rows == count:
        step(0, count)
    else:
        pl.loop(0, rows // count)(lambda i: step(pl.multiple_of(i * count, count), count))


def expert_stage_body(peers, pieces, me_ref, *refs):
    ins, (rows, extra, gate_out, up_out, *parts) = refs[:pieces], refs[pieces + 3 :]
    w_gate, w_up, w_down = refs[pieces : pieces + 3]
    me = me_ref[0]
    place(ins, rows, extra)
    half = rows.shape[0] // 2
    for i, part in enumerate(parts):

        def step(first, count, i=i, part=part):
            here = pl.ds(first + i * half, count)
            values = rows[here, :]
            gate = dot_nn(values, w_gate[...])
            up = dot_nn(values, w_up[...])
            gate_out[here, :] = gate.astype(bf16)
            up_out[here, :] = up.astype(bf16)
            act = (gate / (1.0 + jnp.exp(-gate)) * up).astype(bf16)
            scale = own_gate(extra[here, :], me, peers)
            part[pl.ds(first, count), :] = (scale * dot_nn(act, w_down[...])).astype(bf16)

        chunked(half, step)


def expert_stage(pieces, me, peers, w_gate, w_up, w_down):
    count = sum(p.shape[0] for p in pieces)
    model, units = w_gate.shape
    shapes = [
        like((count, model), bf16), like((count, pieces[0].shape[1] - model), bf16),
        like((count, units), bf16), like((count, units), bf16),
        like((count // 2, model), bf16), like((count // 2, model), bf16),
    ]
    body = functools.partial(expert_stage_body, peers, len(pieces))
    outs = on_device(body, shapes, [*pieces, w_gate, w_up, w_down], 6 * count * w_gate.size, 40, (me,))
    return outs[4:], outs[:4]


def expert_back_body(peers, pieces, me_ref, *refs):
    ins = refs[:pieces]
    extra, gate_in, up_in, w_gate, w_up, w_down, grad_rows, grad_gate, grad_up, act, *parts = refs[pieces:]
    me = me_ref[0]
    place(ins, grad_rows)
    half = grad_rows.shape[0] // 2
    for i, part in enumerate(parts):

        def step(first, count, i=i, part=part):
            here = pl.ds(first + i * half, count)
            scale = own_gate(extra[here, :], me, peers)
            scaled = (scale * wide(grad_rows[here, :])).astype(bf16)
            grad_rows[here, :] = scaled
            grad_act = dot_nt(scaled, w_down[...])
            gate, up = wide(gate_in[here, :]), wide(up_in[here, :])
            sig = 1.0 / (1.0 + jnp.exp(-gate))
            silu = gate * sig
            low_gate = (grad_act * up * sig * (1.0 + gate * (1.0 - sig))).astype(bf16)
            low_up = (grad_act * silu).astype(bf16)
            grad_gate[here, :] = low_gate
            grad_up[here, :] = low_up
            act[here, :] = (silu * up).astype(bf16)
            grad_in = dot_nt(low_gate, w_gate[...]) + dot_nt(low_up, w_up[...])
            part[pl.ds(first, count), :] = grad_in.astype(bf16)

        chunked(half, step)


def expert_back_stage(pieces, me, peers, saved, w_gate, w_up, w_down):
    rows, extra, gate_out, up_out = saved
    count = rows.shape[0]
    model, units = w_gate.shape
    shapes = [
        like((count, model), bf16), like((count, units), bf16), like((count, units), bf16),
        like((count, units), bf16), like((count // 2, model), bf16), like((count // 2, model), bf16),
    ]
    body = functools.partial(expert_back_body, peers, len(pieces))
    args = [*pieces, extra, gate_out, up_out, w_gate, w_up, w_down]
    outs = on_device(body, shapes, args, 6 * count * w_gate.size, 40, (me,))
    return outs[4:], outs[:4]


def expert_forward(pieces, gate_col, w_gate, w_up, w_down):
    rows = jnp.concatenate(pieces, axis=0)
    gate_out = dot_nn(rows, w_gate)
    up_out = dot_nn(rows, w_up)
    act = (gate_out / (1.0 + jnp.exp(-gate_out)) * up_out).astype(bf16)
    part = dot_nn(act, w_down)
    part = (part if gate_col is None else gate_col * part).astype(bf16)
    return part, (rows, gate_out.astype(bf16), up_out.astype(bf16))


def expert_backward(pieces, gate_col, saved, w_gate, w_up, w_down):
    rows, gate_low, up_low = saved
    gate_out, up_out = wide(gate_low), wide(up_low)
    grad_rows = jnp.concatenate(pieces, axis=0)
    if gate_col is not None:
        grad_rows = (gate_col * wide(grad_rows)).astype(bf16)
    grad_act = dot_nt(grad_rows, w_down)
    sig = 1.0 / (1.0 + jnp.exp(-gate_out))
    silu = gate_out * sig
    grad_gate = (grad_act * up_out * sig * (1.0 + gate_out * (1.0 - sig))).astype(bf16)
    grad_up = (grad_act * silu).astype(bf16)
    act = (silu * up_out).astype(bf16)
    grad_in = (dot_nt(grad_gate, w_gate) + dot_nt(grad_up, w_up)).astype(bf16)
    weights = (dot_tn(rows, grad_gate), dot_tn(rows, grad_up), dot_tn(act, grad_rows))
    return grad_in, weights


def halves(array):
    half = array.shape[0] // 2
    return array[:half], array[half:]


class Blocks:
    def __init__(self, cube, routes, gates, weights):
        self.cube, self.weights = cube, weights
        self.peers = lax.axis_size("dp")
        self.me = lax.axis_index("dp").astype(jnp.int32).reshape(1)
        rows = routes.shape[1] // lax.axis_size("shard")
        numbers = jnp.arange(self.peers, dtype=jnp.int32)
        table = jnp.sum(
            jnp.where(routes[:, :rows, :, None] == numbers, gates[:, :rows, :, None], 0.0), axis=2
        )
        high = lax.reduce_precision(table, 8, 7)
        both = jnp.concatenate([high, table - high], axis=2).astype(bf16)
        self.extras = jnp.pad(both, ((0, 0), (0, 0), (0, 128 - both.shape[2])))
        self.tables = [()] * routes.shape[0]

    def forward(self, payload, table):
        saved = []

        def work(stage, pieces):
            parts, kept = expert_stage(pieces, self.me, self.peers, *self.weights)
            saved.append(kept)
            return parts

        return reduce_rows(self.cube, gather_rows(self.cube, payload, work)), saved

    def backward(self, grad, table, saved):
        weights = []

        def work(stage, pieces):
            parts, kept = expert_back_stage(pieces, self.me, self.peers, saved[stage], *self.weights)
            grad_rows, grad_gate, grad_up, act = kept
            rows = saved[stage][0]
            weights.append((dot_tn(rows, grad_gate), dot_tn(rows, grad_up), dot_tn(act, grad_rows)))
            return parts

        total = reduce_rows(self.cube, gather_rows(self.cube, grad, work))
        return total, jax.tree.map(lambda *t: sum(t), *weights)


class Buckets:
    def __init__(self, cube, routes, gates, weights, capacity):
        self.cube, self.weights, self.capacity = cube, weights, capacity
        micros, self.rows, self.top = routes.shape
        self.experts = lax.axis_size("dp")
        self.extras = jnp.zeros((micros, self.rows // lax.axis_size("shard"), 128), bf16)
        self.tables = []
        for m in range(micros):
            flat = routes[m].reshape(-1)
            onehot = (flat[:, None] == jnp.arange(self.experts, dtype=jnp.int32)).astype(jnp.int32)
            earlier = jnp.cumsum(onehot, axis=0) - onehot
            target = flat * capacity + jnp.sum(earlier * onehot, axis=1)
            source = jnp.full((self.experts * capacity,), flat.shape[0], jnp.int32)
            source = source.at[target].set(jnp.arange(flat.shape[0], dtype=jnp.int32))
            self.tables.append((target, source, gates[m]))

    def exchange(self, rows):
        shape = (self.experts, self.capacity, rows.shape[1])
        moved = lax.all_to_all(rows.reshape(shape), "dp", split_axis=0, concat_axis=0, tiled=True)
        return moved.reshape(rows.shape)

    def whole(self, own):
        return jnp.concatenate([own, swap(own, self.cube.z)], axis=0)

    def folded(self, total):
        own, other = halves(total.astype(bf16))
        return wide(own) + wide(swap(other, self.cube.z))

    def forward(self, own, table):
        target, source, gates = table
        own = own[:, : own.shape[1] - self.extras.shape[2]]
        padded = jnp.pad(self.whole(own), ((0, 1), (0, 0)))
        arrived = self.exchange(jnp.take(padded, source // self.top, axis=0))
        part, saved = expert_forward([arrived], None, *self.weights)
        picked = jnp.take(self.exchange(part), target, axis=0).reshape(self.rows, self.top, -1)
        return self.folded(jnp.sum(gates[:, :, None] * picked, axis=1)), saved

    def backward(self, grad, table, saved):
        target, source, gates = table
        scaled = (gates[:, :, None] * wide(self.whole(grad))[:, None, :]).astype(bf16)
        padded = jnp.pad(scaled.reshape(self.rows * self.top, -1), ((0, 1), (0, 0)))
        arrived = self.exchange(jnp.take(padded, source, axis=0))
        grad_in, weights = expert_backward([arrived], None, saved, *self.weights)
        picked = jnp.take(self.exchange(grad_in), target, axis=0).reshape(self.rows, self.top, -1)
        return self.folded(jnp.sum(picked, axis=1, dtype=f32)), weights


def local(
    tokens, lengths, routes, gates, attn_gain, q_weight, key_projection, value_projection,
    o_weight, mlp_gain, expert_gate, expert_up, expert_down, cotangent,
):
    cube = Cube()
    section = lax.axis_index("section")
    shard = lax.axis_index("shard")
    me = lax.axis_index("dp")
    peers, shards = lax.axis_size("dp"), lax.axis_size("shard")
    micros, block_rows, model = tokens.shape
    rows = block_rows // shards
    first = section == 0

    starts, masks = [], []
    for m in range(micros):
        lens = lengths[m, 0]
        ends = jnp.cumsum(lens)
        longest = jnp.argmax(lens)
        start = ends[longest] - lens[longest]
        starts.append(start)
        both = []
        for side in (shard, 1 - shard):
            position = (jnp.arange(rows, dtype=jnp.int32) + start + rows * side) % block_rows
            segment = jnp.sum((position[:, None] >= ends[None, :]).astype(jnp.int32), axis=1)
            allowed = (segment[:, None] == segment[None, :]) & (position[None, :] <= position[:, None])
            both.append(allowed.astype(f32))
        masks.append(both)

    def turned(array, m, count=rows):
        doubled = jnp.concatenate([array, array], axis=0)
        return lax.dynamic_slice_in_dim(doubled, (starts[m] + rows * shard) % block_rows, count, 0)

    def pick(array, slot):
        here, there = array[min(slot, micros - 1)], array[max(slot - 1, 0)]
        return jax.tree.map(lambda a, b: jnp.where(first, a, b), here, there)

    zero_rows = jnp.zeros((rows, model), bf16)
    token_rows = [
        jnp.where(first, turned(tokens[m], m, block_rows), jnp.zeros_like(tokens[m])) for m in range(micros)
    ]
    cot_rows = [jnp.where(first, zero_rows, turned(cotangent[m], m)) for m in range(micros)]

    qkv_own = jnp.concatenate([q_weight[0], key_projection[0], value_projection[0]], axis=1)
    out_own = o_weight[0]

    def other_half(weight):
        share = model // peers
        piece = lax.dynamic_slice_in_dim(weight, me * share, share, 0)
        return lax.all_gather(swap(piece, cube.z), "dp", axis=0, tiled=True)

    qkv_w = (qkv_own, other_half(qkv_own))
    out_w = (out_own, other_half(out_own))
    w_gate, w_up, w_down = expert_gate[0, 0], expert_up[0, 0], expert_down[0, 0]
    gain_one, gain_two = attn_gain[0][None], mlp_gain[0][None]

    routed = jnp.stack([turned(routes[0, m], m, block_rows) for m in range(micros)])
    weighed = jnp.stack([turned(gates[0, m], m, block_rows) for m in range(micros)])
    capacity = 2 * block_rows * routes.shape[3] // peers
    if capacity < block_rows:
        mixture = Buckets(cube, routed, weighed, (w_gate, w_up, w_down), capacity)
    else:
        mixture = Blocks(cube, routed, weighed, (w_gate, w_up, w_down))

    states, outs = [], []
    arriving = zero_rows
    for slot in range(micros + 1):
        allowed = pick(masks, slot)[0]
        extra = pick(mixture.extras, slot)
        if slot == 0:
            inputs, others = token_rows[0][:rows], token_rows[0][rows:]
            own, qkv, heads, *sent = half_heads(
                inputs, others, allowed, pick(masks, 0)[1], gain_one, qkv_own, out_own
            )
            arrived = [swap(t, cube.z) for t in sent]
            hidden, payload = joined(inputs, own, arrived[0], gain_two, extra)
            groups = [(qkv, heads), tuple(arrived[1:])]
        else:
            fresh = token_rows[slot][:rows] if slot < micros else zero_rows
            inputs, hidden, payload, groups = attention_forward(
                fresh, arriving, allowed, gain_one, gain_two, extra, qkv_w, out_w
            )
        table = pick(mixture.tables, slot)
        total, saved = mixture.forward(payload, table)
        result = (hidden + total).astype(bf16)
        if slot < micros:
            arriving = lax.ppermute(result, "section", [(0, 1)])
        outs.append(result)
        states.append((inputs, hidden, allowed, groups, table, saved))

    expert_sums = None
    coming = zero_rows
    attn_factors, gain_sums, input_grads = [], [], []
    for turn in range(micros + 1):
        sources = [turn - 1, turn + 1]
        sources = [i if 0 <= i <= micros else None for i in sources]
        if sources[0] is None or sources[1] is None:
            state = states[sources[1] if sources[0] is None else sources[0]]
        else:
            state = jax.tree.map(
                lambda a, b: jnp.where(first, a, b), states[sources[0]], states[sources[1]]
            )
        inputs, hidden, allowed, groups, table, saved = state
        grad = coming + (cot_rows[turn] if turn < micros else zero_rows)
        grad_two, weight_grads = mixture.backward(grad, table, saved)
        expert_sums = (
            weight_grads if expert_sums is None else jax.tree.map(jnp.add, expert_sums, weight_grads)
        )
        grad_input, sent, grad_low, normed, *grads, attn_g, mlp_g = attention_backward(
            grad, grad_two, inputs, hidden, allowed, gain_one, gain_two, [g[0] for g in groups], qkv_w, out_w
        )
        if turn < micros:
            coming = lax.ppermute(sent, "section", [(1, 0)])
        attn_factors.append((normed, grad_low, grads, [g[1] for g in groups]))
        gain_sums.append(jnp.concatenate([attn_g, mlp_g], axis=0))
        input_grads.append(grad_input)

    normed_t = jnp.concatenate([f[0] for f in attn_factors], axis=0).T
    grad_t = jnp.concatenate([f[1] for f in attn_factors], axis=0).T
    share = model // peers

    def owned(left, rights):
        full = [dot_nn(left, right).astype(bf16).reshape(peers, share, -1) for right in rights]

        def blocks(group):
            taken = [jnp.take(full[s], me ^ (m ^ cube.inner), axis=0) for m, s in group]
            return jnp.concatenate(taken, axis=0).reshape(-1, rights[0].shape[1])

        return reduce_rows(cube, [tuple(blocks(group) for group in pair) for pair in cube.stages])

    grad_o = owned(
        grad_t, [jnp.concatenate([f[3][g] for f in attn_factors], axis=0) for g in range(shards)]
    )
    total = owned(
        normed_t, [jnp.concatenate([f[2][g] for f in attn_factors], axis=0) for g in range(shards)]
    )
    width = q_weight.shape[2]
    grad_q = total[:, :width]
    grad_k = total[:, width : width + HEAD_SIZE]
    grad_v = total[:, width + HEAD_SIZE :]
    gain_total = sum(gain_sums)
    for direction in [*cube.extra, cube.core, cube.x, cube.y, cube.z]:
        gain_total = gain_total + swap(gain_total, direction)
    gain_total = lax.dynamic_slice_in_dim(gain_total, me * share, share, 1)

    def placed(own, m):
        half = model // shards
        kept = lax.dynamic_slice_in_dim(own, shard * half, half, 1)
        given = lax.dynamic_slice_in_dim(own, (1 - shard) * half, half, 1)
        got = swap(given, cube.z)
        low = jnp.where(shard == 0, kept, got)
        high = jnp.where(shard == 0, got, kept)
        return lax.dynamic_slice_in_dim(
            jnp.concatenate([low, high, low, high], axis=0), (block_rows - starts[m]) % block_rows, block_rows, 0
        )

    section_out = jnp.stack(
        [placed(jnp.where(first, outs[m], outs[m + 1]), m) for m in range(micros)]
    )
    input_grad = jnp.stack(
        [
            placed(jnp.where(first, input_grads[m + 1], input_grads[m]), m)
            for m in range(micros)
        ]
    )
    gate_total, up_total, down_total = expert_sums
    return (
        section_out[None],
        input_grad[None],
        gain_total[0][None],
        grad_q[None],
        grad_k[None],
        grad_v[None],
        grad_o[None],
        gain_total[1][None],
        gate_total[None, None],
        up_total[None, None],
        down_total[None, None],
    )


def solution(mesh):
    in_specs = (
        P(None, "dp", None),
        P(None, "dp", None),
        P("section", None, "dp", None),
        P("section", None, "dp", None),
        P("section", None),
        P("section", None, "shard"),
        P("section", None, "shard"),
        P("section", None, "shard"),
        P("section", None, "shard"),
        P("section", None),
        P("section", "dp", None, "shard"),
        P("section", "dp", None, "shard"),
        P("section", "dp", "shard", None),
        P(None, "dp", None),
    )
    out_specs = (
        P("section", None, "dp", "shard"),
        P("section", None, "dp", "shard"),
        P("section", "dp"),
        P("section", "dp", "shard"),
        P("section", "dp", "shard"),
        P("section", "dp", "shard"),
        P("section", "dp", "shard"),
        P("section", "dp"),
        P("section", "dp", None, "shard"),
        P("section", "dp", None, "shard"),
        P("section", "dp", "shard", None),
    )
    return jax.shard_map(local, mesh=mesh, in_specs=in_specs, out_specs=out_specs, check_vma=False)
```

```python
import functools

import jax
import jax.numpy as jnp
import numpy as np
from jax import lax
from jax.experimental import pallas as pl
from jax.experimental.pallas import tpu as pltpu
from jax.sharding import PartitionSpec as P

HEAD_SIZE = 128
epsilon = 1e-06
masked_value = -1e30
bf16 = jnp.bfloat16
f32 = jnp.float32


def wide(a):
    return a.astype(f32)


def dot_nn(a, b):
    return lax.dot_general(a, b, (((1,), (0,)), ((), ())), preferred_element_type=f32)


def dot_nt(a, b):
    return lax.dot_general(a, b, (((1,), (1,)), ((), ())), preferred_element_type=f32)


def dot_tn(a, b):
    return lax.dot_general(a, b, (((0,), (0,)), ((), ())), preferred_element_type=f32)


class Cube:
    def __init__(self):
        peers = lax.axis_size("dp")
        bits = [1 << i for i in range(peers.bit_length() - 1)]
        rest = bits[1:]
        self.core = ("dp", bits[0])
        self.x = ("dp", rest[0])
        self.y = ("dp", rest[len(rest) // 2])
        self.z = ("shard", 1)
        self.extra = [("dp", b) for b in rest if b not in (self.x[1], self.y[1])]
        inner = [0]
        for _, bit in self.extra:
            inner = inner + [m | bit for m in inner]
        self.inner = np.array(inner)
        x, y = self.x[1], self.y[1]
        stages = [[(0, 0)], [(x, 0), (y, 0), (0, 1)], [(x | y, 0), (y, 1), (x, 1)], [(x | y, 1)]]
        self.stages = [(g, [(m | self.core[1], s) for m, s in g]) for g in stages]


def swap(value, direction):
    axis, bit = direction
    return lax.ppermute(value, axis, [(i, i ^ bit) for i in range(lax.axis_size(axis))])


def thirds(rows):
    step = -(-rows // 48) * 16
    return [(0, step), (step, 2 * step), (2 * step, rows)]


together = lax.optimization_barrier


def ready(thunks, step):
    return thunks[step]() if step < len(thunks) else ()


def gather_rows(cube, own, work, side=()):
    core = cube.core
    near = [swap(own, d) for d in (cube.x, cube.y, cube.z)]
    mine0, other0 = work(0, [own, swap(own, core)])
    near, mine0, other0, _ = together((near, mine0, other0, ready(side, 0)))

    middle = [swap(block, d) for block, d in zip(near, (cube.y, cube.z, cube.x))]
    in0 = swap(other0, core)
    mine1, other1 = work(1, [*near, *[swap(block, core) for block in near]])
    middle, in0, mine1, other1, _ = together((middle, in0, mine1, other1, ready(side, 1)))

    cuts = thirds(own.shape[0])
    last = [
        swap(block[lo:hi], d) for block, d, (lo, hi) in zip(middle, (cube.z, cube.x, cube.y), cuts)
    ]
    in1 = swap(other1, core)
    mine2, other2 = work(2, [*middle, *[swap(block, core) for block in middle]])
    last, in1, mine2, other2, _ = together((last, in1, mine2, other2, ready(side, 2)))

    in2 = swap(other2, core)
    mine3, other3 = work(3, [*last, *[swap(block, core) for block in last]])
    return [(mine0, in0), (mine1, in1), (mine2, in2), (mine3, swap(other3, core))]


def low_sum(*terms):
    return sum(wide(t) for t in terms).astype(bf16)


def reduce_rows(cube, pairs, side=()):
    own, near, middle, last = pairs
    rows = last[0].shape[0]

    def block(i, pair):
        return [g[i * rows : (i + 1) * rows] for g in pair]

    cuts = thirds(rows)
    sent = low_sum(*last)
    arrived = [swap(sent[lo:hi], d) for d, (lo, hi) in zip((cube.z, cube.x, cube.y), cuts)]
    arrived, middle, _ = together((arrived, middle, ready(side, 0)))
    sent = [
        low_sum(*block(i, middle), jnp.pad(arrived[i], ((lo, rows - hi), (0, 0))))
        for i, (lo, hi) in enumerate(cuts)
    ]
    arrived = [swap(t, d) for t, d in zip(sent, (cube.y, cube.z, cube.x))]
    arrived, near, _ = together((arrived, near, ready(side, 1)))
    sent = [low_sum(*block(i, near), arrived[i]) for i in range(3)]
    arrived = [swap(t, d) for t, d in zip(sent, (cube.x, cube.y, cube.z))]
    arrived, own, _ = together((arrived, own, ready(side, 2)))
    total = sum(wide(t) for t in [*own, *arrived])
    for direction in reversed(cube.extra):
        half = total.shape[0] // 2
        total = total[:half] + wide(swap(total[half:].astype(bf16), direction))
    return total


def norm_factor(values):
    return lax.rsqrt(jnp.mean(values * values, axis=1, keepdims=True) + epsilon)


def norm_back(values, factor, gain, grad):
    gain_grad = jnp.sum(grad * values * factor, axis=0, keepdims=True)
    scaled = grad * gain
    inner = jnp.mean(scaled * values, axis=1, keepdims=True)
    return factor * (scaled - values * factor * factor * inner), gain_grad


def stack_heads(rows):
    return jnp.concatenate(
        [rows[:, i : i + HEAD_SIZE] for i in range(0, rows.shape[1], HEAD_SIZE)], axis=0
    )


def spread_heads(stacked, rows):
    return jnp.concatenate(
        [stacked[i : i + rows] for i in range(0, stacked.shape[0], rows)], axis=1
    )


def head_probs(query, key, allowed):
    scores = jnp.where(allowed > 0.0, dot_nt(query, key) * HEAD_SIZE ** (-0.5), masked_value)
    exp_scores = jnp.exp(scores - jnp.max(scores, axis=1, keepdims=True))
    return exp_scores / jnp.sum(exp_scores, axis=1, keepdims=True)


def normed_rows(values, gain):
    return (values * norm_factor(values) * gain).astype(bf16)


def group_probs(qkv, allowed):
    width = qkv.shape[1] - 2 * HEAD_SIZE
    query = stack_heads(qkv[:, :width])
    key, value = qkv[:, width : width + HEAD_SIZE], qkv[:, width + HEAD_SIZE :]
    tiled = jnp.concatenate([allowed] * (width // HEAD_SIZE), axis=0)
    return query, key, value, head_probs(query, key, tiled)


def head_group(normed, allowed, weights, qkv, heads):
    w_query, w_key, w_value, w_out = weights
    width = w_query.shape[1]
    qkv[:, :width] = dot_nn(normed, w_query).astype(bf16)
    qkv[:, width : width + HEAD_SIZE] = dot_nn(normed, w_key).astype(bf16)
    qkv[:, width + HEAD_SIZE :] = dot_nn(normed, w_value).astype(bf16)
    _, _, value, probs = group_probs(qkv[...], allowed)
    heads[...] = spread_heads(dot_nn(probs.astype(bf16), value).astype(bf16), normed.shape[0])
    return dot_nt(heads[...], w_out)


VMEM = pl.BlockSpec(memory_space=pltpu.VMEM)
SMEM = pl.BlockSpec(memory_space=pltpu.SMEM)
MIB = 1 << 20


def like(shape, dtype):
    return jax.ShapeDtypeStruct(shape, dtype)


def on_device(body, outs, args, flops, mib, scalars=()):
    moved = sum(a.size * a.dtype.itemsize for a in [*args, *outs])
    return pl.pallas_call(
        body,
        out_shape=outs,
        in_specs=[SMEM] * len(scalars) + [VMEM] * len(args),
        out_specs=[VMEM] * len(outs),
        compiler_params=pltpu.CompilerParams(vmem_limit_bytes=mib * MIB),
        cost_estimate=pl.CostEstimate(flops=flops, bytes_accessed=moved, transcendentals=0),
    )(*scalars, *args)


def geometry(lens, first, count, side, rows, block):
    ends, total, best, start = [], 0, lens[first], 0
    for i in range(count):
        length = lens[first + i]
        if i:
            start = jnp.where(length > best, total, start)
            best = jnp.maximum(best, length)
        total = total + length
        ends.append(total)
    return ends, lax.rem(start + rows * side, block)


def positions(shape, axis, begin, block):
    place = lax.broadcasted_iota(jnp.int32, shape, axis) + begin
    return jnp.where(place >= block, place - block, place)


def selection(begin, rows, block):
    wanted = positions((rows, block), 0, begin, block)
    return (wanted == lax.broadcasted_iota(jnp.int32, (rows, block), 1)).astype(f32)


def sequence_mask(ends, begin, rows, block):
    row, col = [positions((rows, rows), axis, begin, block) for axis in (0, 1)]
    inside = sum(jnp.abs((row >= e).astype(jnp.int32) - (col >= e).astype(jnp.int32)) for e in ends)
    return ((inside == 0) & (col <= row)).astype(f32)


def gate_columns(pick, routes, gates, peers):
    lane = lax.broadcasted_iota(jnp.int32, (routes.shape[0], 128), 1)
    table = jnp.zeros(lane.shape, f32)
    for k in range(routes.shape[1]):
        gate = gates[:, k : k + 1]
        high = wide(gate.astype(bf16))
        table += jnp.where(lane == routes[:, k : k + 1], high, 0.0)
        table += jnp.where(lane == routes[:, k : k + 1] + peers, gate - high, 0.0)
    return dot_nn(pick, table.astype(bf16)).astype(bf16)


def opening_body(peers, seqs, lens, ids, tokens, routes, gates, gain, wq, wk, wv, wo, *outs):
    inputs, part, qkv, heads, sent, qkv_other, heads_other, mask, extra = outs
    block = tokens.shape[0]
    rows = block // 2
    here = jnp.where(ids[1] == 0, 1.0, 0.0)
    weights = [w[...] for w in (wq, wk, wv, wo)]
    for side, to_qkv, to_heads in ((ids[0], qkv, heads), (1 - ids[0], qkv_other, heads_other)):
        ends, begin = geometry(lens, 0, seqs, side, rows, block)
        pick = selection(begin, rows, block)
        values = dot_nn((pick * here).astype(bf16), tokens[...])
        allowed = sequence_mask(ends, begin, rows, block)
        value = head_group(normed_rows(values, gain[...]), allowed, weights, to_qkv, to_heads)
        if to_qkv is qkv:
            inputs[...] = values.astype(bf16)
            part[...] = values + value
            mask[...] = allowed
            extra[...] = gate_columns(pick.astype(bf16), routes[...], gates[...], peers)
        else:
            sent[...] = value.astype(bf16)


def opening(lens, ids, peers, tokens, routes, gates, gain, weights):
    block, model = tokens.shape
    rows = block // 2
    width, out = sum(w.shape[1] for w in weights[:3]), weights[3].shape[1]
    shapes = [
        like((rows, model), bf16), like((rows, model), f32), like((rows, width), bf16), like((rows, out), bf16),
        like((rows, model), bf16), like((rows, width), bf16), like((rows, out), bf16),
        like((rows, rows), f32), like((rows, 128), bf16),
    ]
    args = [tokens, routes, gates, gain, *weights]
    body = functools.partial(opening_body, peers, lens.shape[0] // 2)
    outs = on_device(body, shapes, args, 4 * rows * model * (width + out), 40, (lens, ids))
    return outs[:5], outs[7], outs[8]


def settle_cot_body(seqs, lens, ids, block_rows, own, other):
    block = block_rows.shape[0]
    here = jnp.where(ids[1] == 0, 0.0, 1.0)
    for side, out in ((ids[0], own), (1 - ids[0], other)):
        _, begin = geometry(lens, 0, seqs, side, out.shape[0], block)
        pick = selection(begin, out.shape[0], block) * here
        out[...] = dot_nn(pick.astype(bf16), block_rows[...]).astype(bf16)


def settle_cot(lens, ids, block_rows):
    block, model = block_rows.shape
    shapes = [like((block // 2, model), bf16)] * 2
    body = functools.partial(settle_cot_body, lens.shape[0] // 2)
    return on_device(body, shapes, [block_rows], 2 * block * block * model, 16, (lens, ids))


def settle_body(peers, seqs, lens, ids, tokens, grad, routes, gates, fresh, cot, mask, extra):
    block = tokens.shape[0]
    rows = block // 2
    first = jnp.where(ids[1] == 0, 1.0, 0.0)
    ends, begin = geometry(lens, seqs, seqs, ids[0], rows, block)
    pick = selection(begin, rows, block)
    fresh[...] = dot_nn((pick * first).astype(bf16), tokens[...]).astype(bf16)
    cot[...] = dot_nn((pick * (1.0 - first)).astype(bf16), grad[...]).astype(bf16)
    mask[...] = sequence_mask(ends, begin, rows, block)
    extra[...] = gate_columns(pick.astype(bf16), routes[...], gates[...], peers)


def settle(lens, ids, peers, tokens, grad, routes, gates):
    block, model = tokens.shape
    rows = block // 2
    shapes = [like((rows, model), bf16)] * 2 + [like((rows, rows), f32), like((rows, 128), bf16)]
    body = functools.partial(settle_body, peers, lens.shape[0] // 2)
    args = [tokens, grad, routes, gates]
    return on_device(body, shapes, args, 2 * block * block * model, 16, (lens, ids))


def joined_body(part, other, gain, extra, hidden, payload):
    total = part[...] + wide(other[...])
    hidden[...] = total
    model = total.shape[1]
    payload[:, :model] = normed_rows(total, gain[...])
    payload[:, model:] = extra[...]


def joined(part, other, gain, extra):
    rows, model = part.shape
    shapes = [like((rows, model), f32), like((rows, model + extra.shape[1]), bf16)]
    return on_device(joined_body, shapes, [part, other, gain, extra], 10 * rows * model, 16)


def split_packed(packed, weights):
    at, parts = 0, []
    for w in weights:
        parts.append(packed[:, at : at + w.shape[1]])
        at += w.shape[1]
    return parts


def other_heads_body(inputs, mask, gain, wq, wk, wv, wo, packed, qkv, heads):
    normed = normed_rows(wide(inputs[...]), gain[...])
    head_group(normed, mask[...], split_packed(packed, (wq, wk, wv, wo)), qkv, heads)


def other_heads(inputs, mask, gain, weights, packed):
    rows = inputs.shape[0]
    width, out = sum(w.shape[1] for w in weights[:3]), weights[3].shape[1]
    shapes = [like((rows, width), bf16), like((rows, out), bf16)]
    args = [inputs, mask, gain, *weights, packed]
    return on_device(other_heads_body, shapes, args, 2 * rows * packed.size, 40)


def attention_body(fresh, arriving, mask, gain, gain_two, extra, wq, wk, wv, wo, packed, *outs):
    inputs, hidden, payload, qkv0, qkv1, heads0, heads1 = outs
    rows = fresh[...] + arriving[...]
    inputs[...] = rows
    total = wide(rows)
    normed = normed_rows(total, gain[...])
    own = [w[...] for w in (wq, wk, wv, wo)]
    total = total + head_group(normed, mask[...], own, qkv0, heads0)
    total = total + head_group(normed, mask[...], split_packed(packed, own), qkv1, heads1)
    hidden[...] = total
    model = total.shape[1]
    payload[:, :model] = normed_rows(total, gain_two[...])
    payload[:, model:] = extra[...]


def attention_forward(fresh, arriving, mask, gain, gain_two, extra, weights, packed):
    rows, model = fresh.shape
    width, out = sum(w.shape[1] for w in weights[:3]), weights[3].shape[1]
    shapes = [
        like((rows, model), bf16), like((rows, model), f32), like((rows, model + extra.shape[1]), bf16),
        like((rows, width), bf16), like((rows, width), bf16), like((rows, out), bf16), like((rows, out), bf16),
    ]
    args = [fresh, arriving, mask, gain, gain_two, extra, *weights, packed]
    outs = on_device(attention_body, shapes, args, 4 * rows * packed.size, 40)
    inputs, hidden, payload, qkv0, qkv1, heads0, heads1 = outs
    return inputs, hidden, payload, [(qkv0, heads0), (qkv1, heads1)]


def attention_back_body(grad, grad_two, inputs, hidden, mask, gain, gain_two, q0, q1, wq, wk, wv, wo, packed, *outs):
    grad_input, grad_input_low, grad_low, normed, g0, g1, gain_grad, gain_two_grad = outs
    rows = inputs.shape[0]
    values = wide(inputs[...])
    normed[...] = normed_rows(values, gain[...])
    total = hidden[...]
    back, gain_two_grad[...] = norm_back(total, norm_factor(total), gain_two[...], grad_two[...])
    grad_hidden = wide(grad[...]) + back
    low = grad_hidden.astype(bf16)
    grad_low[...] = low
    grad_normed = jnp.zeros_like(grad_hidden)
    own = [w[...] for w in (wq, wk, wv, wo)]
    for qkv, weights, grad_qkv in ((q0, own, g0), (q1, split_packed(packed, own), g1)):
        query, key, value, probs = group_probs(qkv[...], mask[...])
        grad_heads = stack_heads(dot_nn(low, weights[3]).astype(bf16))
        grad_probs = dot_nt(grad_heads, value)
        inner = jnp.sum(probs * grad_probs, axis=1, keepdims=True)
        grad_scores = (probs * (grad_probs - inner) * HEAD_SIZE ** (-0.5)).astype(bf16)
        grads = [
            spread_heads(dot_nn(grad_scores, key).astype(bf16), rows),
            dot_tn(grad_scores, query).astype(bf16),
            dot_tn(probs.astype(bf16), grad_heads).astype(bf16),
        ]
        at = 0
        for part, w in zip(grads, weights):
            grad_qkv[:, at : at + part.shape[1]] = part
            at += part.shape[1]
            grad_normed = grad_normed + dot_nt(part, w)
    back, gain_grad[...] = norm_back(values, norm_factor(values), gain[...], grad_normed)
    result = grad_hidden + back
    grad_input[...] = result
    grad_input_low[...] = result.astype(bf16)


def attention_backward(grad, grad_two, inputs, hidden, mask, gain, gain_two, projected, weights, packed):
    rows, model = inputs.shape
    width = projected[0].shape[1]
    shapes = [
        like((rows, model), f32), like((rows, model), bf16), like((rows, model), bf16),
        like((rows, model), bf16), like((rows, width), bf16), like((rows, width), bf16),
        like((1, model), f32), like((1, model), f32),
    ]
    args = [grad, grad_two, inputs, hidden, mask, gain, gain_two, *projected, *weights, packed]
    return on_device(attention_back_body, shapes, args, 8 * rows * packed.size, 44)


def place(pieces, *targets):
    at = 0
    for piece in pieces:
        rows, first = piece.shape[0], 0
        for target in targets:
            target[at : at + rows, :] = piece[:, first : first + target.shape[1]]
            first += target.shape[1]
        at += rows


def own_gate(extra, me, peers):
    lane = lax.broadcasted_iota(jnp.int32, extra.shape, 1)
    return jnp.sum(jnp.where((lane == me) | (lane == me + peers), wide(extra), 0.0), axis=1, keepdims=True)


def chunked(rows, step):
    count = max(c for c in (128, 192, 256, 384) if rows % c == 0)
    if rows == count:
        step(0, count)
    else:
        pl.loop(0, rows // count)(lambda i: step(pl.multiple_of(i * count, count), count))


def expert_stage_body(peers, pieces, me_ref, *refs):
    ins, (rows, extra, gate_out, up_out, *parts) = refs[:pieces], refs[pieces + 3 :]
    w_gate, w_up, w_down = refs[pieces : pieces + 3]
    me = me_ref[0]
    place(ins, rows, extra)
    half = rows.shape[0] // 2
    for i, part in enumerate(parts):

        def step(first, count, i=i, part=part):
            here = pl.ds(first + i * half, count)
            values = rows[here, :]
            gate = dot_nn(values, w_gate[...])
            up = dot_nn(values, w_up[...])
            gate_out[here, :] = gate.astype(bf16)
            up_out[here, :] = up.astype(bf16)
            act = (gate / (1.0 + jnp.exp(-gate)) * up).astype(bf16)
            scale = own_gate(extra[here, :], me, peers)
            part[pl.ds(first, count), :] = (scale * dot_nn(act, w_down[...])).astype(bf16)

        chunked(half, step)


def expert_stage(pieces, me, peers, w_gate, w_up, w_down):
    count = sum(p.shape[0] for p in pieces)
    model, units = w_gate.shape
    shapes = [
        like((count, model), bf16), like((count, pieces[0].shape[1] - model), bf16),
        like((count, units), bf16), like((count, units), bf16),
        like((count // 2, model), bf16), like((count // 2, model), bf16),
    ]
    body = functools.partial(expert_stage_body, peers, len(pieces))
    outs = on_device(body, shapes, [*pieces, w_gate, w_up, w_down], 6 * count * w_gate.size, 40, (me,))
    return outs[4:], outs[:4]


def expert_back_body(peers, pieces, me_ref, *refs):
    ins = refs[:pieces]
    extra, gate_in, up_in, w_gate, w_up, w_down, grad_rows, grad_gate, grad_up, act, *parts = refs[pieces:]
    me = me_ref[0]
    place(ins, grad_rows)
    half = grad_rows.shape[0] // 2
    for i, part in enumerate(parts):

        def step(first, count, i=i, part=part):
            here = pl.ds(first + i * half, count)
            scale = own_gate(extra[here, :], me, peers)
            scaled = (scale * wide(grad_rows[here, :])).astype(bf16)
            grad_rows[here, :] = scaled
            grad_act = dot_nt(scaled, w_down[...])
            gate, up = wide(gate_in[here, :]), wide(up_in[here, :])
            sig = 1.0 / (1.0 + jnp.exp(-gate))
            silu = gate * sig
            low_gate = (grad_act * up * sig * (1.0 + gate * (1.0 - sig))).astype(bf16)
            low_up = (grad_act * silu).astype(bf16)
            grad_gate[here, :] = low_gate
            grad_up[here, :] = low_up
            act[here, :] = (silu * up).astype(bf16)
            grad_in = dot_nt(low_gate, w_gate[...]) + dot_nt(low_up, w_up[...])
            part[pl.ds(first, count), :] = grad_in.astype(bf16)

        chunked(half, step)


def expert_back_stage(pieces, me, peers, saved, w_gate, w_up, w_down):
    rows, extra, gate_out, up_out = saved
    count = rows.shape[0]
    model, units = w_gate.shape
    shapes = [
        like((count, model), bf16), like((count, units), bf16), like((count, units), bf16),
        like((count, units), bf16), like((count // 2, model), bf16), like((count // 2, model), bf16),
    ]
    body = functools.partial(expert_back_body, peers, len(pieces))
    args = [*pieces, extra, gate_out, up_out, w_gate, w_up, w_down]
    outs = on_device(body, shapes, args, 6 * count * w_gate.size, 40, (me,))
    return outs[4:], outs[:4]


def expert_weights_body(stages, *refs):
    ins, (gate_sum, up_sum, down_sum) = refs[:-3], refs[-3:]
    total = [ref[...] for ref in ins[5 * stages :]] or [0.0] * 3
    for i in range(stages):
        rows, grad_rows, grad_gate, grad_up, act = [r[...] for r in ins[5 * i : 5 * i + 5]]
        total[0] = total[0] + dot_tn(rows, grad_gate)
        total[1] = total[1] + dot_tn(rows, grad_up)
        total[2] = total[2] + dot_tn(act, grad_rows)
    gate_sum[...], up_sum[...], down_sum[...] = total


def expert_weights(kept, sums):
    model, units = kept[0][0].shape[1], kept[0][2].shape[1]
    step = units
    args, specs = [], []
    for stage in kept:
        args += stage
        count = stage[0].shape[0]
        wide_spec = pl.BlockSpec((count, step), lambda j: (0, j))
        narrow = pl.BlockSpec((count, units), lambda j: (0, 0))
        specs += [wide_spec, wide_spec, narrow, narrow, narrow]
    tall = pl.BlockSpec((step, units), lambda j: (j, 0))
    flat = pl.BlockSpec((units, step), lambda j: (0, j))
    rows = sum(stage[0].shape[0] for stage in kept)
    first = len(args)
    if sums is not None:
        args += sums
        specs += [tall, tall, flat]
    shapes = [like((model, units), f32), like((model, units), f32), like((units, model), f32)]
    return pl.pallas_call(
        functools.partial(expert_weights_body, len(kept)),
        grid=(model // step,),
        out_shape=shapes,
        in_specs=specs,
        out_specs=[tall, tall, flat],
        input_output_aliases={} if sums is None else {first + i: i for i in range(3)},
        compiler_params=pltpu.CompilerParams(vmem_limit_bytes=40 * MIB),
        cost_estimate=pl.CostEstimate(
            flops=6 * rows * model * units, bytes_accessed=4 * rows * model + 24 * model * units, transcendentals=0
        ),
    )(*args)


def expert_forward(rows, w_gate, w_up, w_down):
    gate_out = dot_nn(rows, w_gate)
    up_out = dot_nn(rows, w_up)
    act = (gate_out / (1.0 + jnp.exp(-gate_out)) * up_out).astype(bf16)
    part = dot_nn(act, w_down).astype(bf16)
    return part, (rows, gate_out.astype(bf16), up_out.astype(bf16))


def expert_backward(grad_rows, saved, w_gate, w_up, w_down):
    rows, gate_low, up_low = saved
    gate_out, up_out = wide(gate_low), wide(up_low)
    grad_act = dot_nt(grad_rows, w_down)
    sig = 1.0 / (1.0 + jnp.exp(-gate_out))
    silu = gate_out * sig
    grad_gate = (grad_act * up_out * sig * (1.0 + gate_out * (1.0 - sig))).astype(bf16)
    grad_up = (grad_act * silu).astype(bf16)
    act = (silu * up_out).astype(bf16)
    grad_in = (dot_nt(grad_gate, w_gate) + dot_nt(grad_up, w_up)).astype(bf16)
    return grad_in, (dot_tn(rows, grad_gate), dot_tn(rows, grad_up), dot_tn(act, grad_rows))


def halves(array):
    half = array.shape[0] // 2
    return array[:half], array[half:]


class Blocks:
    def __init__(self, cube, weights):
        self.cube, self.weights = cube, weights
        self.peers = lax.axis_size("dp")
        self.me = lax.axis_index("dp").astype(jnp.int32).reshape(1)

    def forward(self, payload, micro, side=()):
        saved = []

        def work(stage, pieces):
            parts, kept = expert_stage(pieces, self.me, self.peers, *self.weights)
            saved.append(kept)
            return parts

        return gather_rows(self.cube, payload, work, side), saved

    def back_stage(self, stage, pieces, saved):
        parts, kept = expert_back_stage(pieces, self.me, self.peers, saved[stage], *self.weights)
        return parts, [saved[stage][0], *kept]

    def backward(self, grad, micro, saved, side=()):
        keeps = []

        def work(stage, pieces):
            parts, kept = self.back_stage(stage, pieces, saved)
            keeps.append(kept)
            return parts

        return gather_rows(self.cube, grad, work, side), keeps

    def early_gather(self, own, other):
        cube = self.cube

        def start():
            return [[swap(t, d) for t in (own, other)] for d in (cube.x, cube.y)]

        def finish(near):
            (x0, x1), (y0, y1) = near
            stages = [[own], [x0, y0, other], [swap(x0, cube.y), y1, x1], [swap(y1, cube.x)]]
            return [[*stage, *[swap(t, cube.core) for t in stage]] for stage in stages]

        return start, finish

    def late_backward(self, pieces, saved):
        results, keeps = [None] * 4, [None] * 4

        def run(*stages):
            for stage in stages:
                (mine, other), keeps[stage] = self.back_stage(stage, pieces[stage], saved)
                results[stage] = (mine, swap(other, self.cube.core))
            return [results[stage] for stage in stages]

        return [lambda: run(3), lambda: run(2), lambda: run(1, 0)], results, keeps

    def total(self, results, side=()):
        return reduce_rows(self.cube, results, side)

    def weight_sums(self, keeps, sums):
        return expert_weights(keeps, sums)


class Buckets:
    def __init__(self, cube, weights, routes, gates, capacity):
        self.cube, self.weights, self.capacity = cube, weights, capacity
        micros, self.rows, self.top = routes.shape
        self.experts = lax.axis_size("dp")
        self.tables = []
        for m in range(micros):
            flat = routes[m].reshape(-1)
            onehot = (flat[:, None] == jnp.arange(self.experts, dtype=jnp.int32)).astype(jnp.int32)
            earlier = jnp.cumsum(onehot, axis=0) - onehot
            target = flat * capacity + jnp.sum(earlier * onehot, axis=1)
            source = jnp.full((self.experts * capacity,), flat.shape[0], jnp.int32)
            source = source.at[target].set(jnp.arange(flat.shape[0], dtype=jnp.int32))
            self.tables.append((target, source, gates[m]))

    def table(self, micro):
        return jax.tree.map(lambda a, b: jnp.where(micro == 0, a, b), self.tables[0], self.tables[1])

    def exchange(self, rows):
        shape = (self.experts, self.capacity, rows.shape[1])
        moved = lax.all_to_all(rows.reshape(shape), "dp", split_axis=0, concat_axis=0, tiled=True)
        return moved.reshape(rows.shape)

    def whole(self, own):
        return jnp.concatenate([own, swap(own, self.cube.z)], axis=0)

    def forward(self, payload, micro, side=()):
        target, source, gates = self.table(micro)
        own = payload[:, : self.weights[0].shape[0]]
        padded = jnp.pad(self.whole(own), ((0, 1), (0, 0)))
        arrived = self.exchange(jnp.take(padded, source // self.top, axis=0))
        part, saved = expert_forward(arrived, *self.weights)
        picked = jnp.take(self.exchange(part), target, axis=0).reshape(self.rows, self.top, -1)
        for thunk in side:
            thunk()
        return jnp.sum(gates[:, :, None] * picked, axis=1), saved

    def backward(self, grad, micro, saved, side=()):
        target, source, gates = self.table(micro)
        scaled = (gates[:, :, None] * wide(self.whole(grad))[:, None, :]).astype(bf16)
        padded = jnp.pad(scaled.reshape(self.rows * self.top, -1), ((0, 1), (0, 0)))
        arrived = self.exchange(jnp.take(padded, source, axis=0))
        grad_in, weights = expert_backward(arrived, saved, *self.weights)
        picked = jnp.take(self.exchange(grad_in), target, axis=0).reshape(self.rows, self.top, -1)
        for thunk in side:
            thunk()
        return jnp.sum(picked, axis=1, dtype=f32), weights

    def total(self, results, side=()):
        own, other = halves(results.astype(bf16))
        for thunk in side:
            thunk()
        return wide(own) + wide(swap(other, self.cube.z))

    def weight_sums(self, weights, sums):
        return weights if sums is None else jax.tree.map(jnp.add, sums, weights)


def local(
    tokens, lengths, routes, gates, attn_gain, q_weight, key_projection, value_projection,
    o_weight, mlp_gain, expert_gate, expert_up, expert_down, cotangent,
):
    cube = Cube()
    section = lax.axis_index("section")
    shard = lax.axis_index("shard")
    me = lax.axis_index("dp")
    peers, shards = lax.axis_size("dp"), lax.axis_size("shard")
    _, block_rows, model = tokens.shape
    rows = block_rows // shards
    share = model // peers
    first = section == 0
    lens = lengths.reshape(-1)
    ids = jnp.stack([shard, section]).astype(jnp.int32)
    gain_one, gain_two = attn_gain[0][None], mlp_gain[0][None]
    weights = [q_weight[0], key_projection[0], value_projection[0], o_weight[0]]
    expert_w = (expert_gate[0, 0], expert_up[0, 0], expert_down[0, 0])
    capacity = 2 * block_rows * routes.shape[3] // peers
    whole_blocks = capacity >= block_rows

    def chosen(here, there):
        return jax.tree.map(lambda a, b: jnp.where(first, a, b), here, there)

    def begins(lens):
        lens = lens.reshape(2, -1)
        ends, longest = jnp.cumsum(lens, axis=1), jnp.argmax(lens, axis=1)
        return [ends[m, longest[m]] - lens[m, longest[m]] for m in range(2)]

    def turned(array, begin):
        doubled = jnp.concatenate([array, array], axis=0)
        return lax.dynamic_slice_in_dim(doubled, (begin + rows * shard) % block_rows, block_rows, 0)

    if whole_blocks:
        mixture = Blocks(cube, expert_w)
    else:
        early = begins(lens)
        mixture = Buckets(
            cube,
            expert_w,
            jnp.stack([turned(routes[0, m], early[m]) for m in range(2)]),
            jnp.stack([turned(gates[0, m], early[m]) for m in range(2)]),
            capacity,
        )

    slices = jnp.concatenate([lax.dynamic_slice_in_dim(w, me * share, share, 0) for w in weights], axis=1)
    slices = swap(slices, cube.z)
    packed = lax.all_gather(slices, "dp", axis=0, tiled=True)

    cot_own, cot_other = settle_cot(lens, ids, cotangent[0])
    (inputs, part, qkv, heads, sent), mask0, extra0 = opening(
        lens, ids, peers, tokens[0], routes[0, 0], gates[0, 0], gain_one, weights
    )
    if whole_blocks:
        start_cot, finish_cot = mixture.early_gather(cot_own, cot_other)
        near_cot = start_cot()
    fresh1, cot1, mask1, extra1 = settle(lens, ids, peers, tokens[1], cotangent[1], routes[0, 1], gates[0, 1])
    arrived, fresh1, cot1, mask1, extra1 = together((swap(sent, cube.z), fresh1, cot1, mask1, extra1))
    hidden, payload = joined(part, arrived, gain_two, extra0)
    results, saved = mixture.forward(payload, 0)
    total = mixture.total(results)
    result0 = (hidden + total).astype(bf16)
    arriving = lax.ppermute(result0, "section", [(0, 1)])
    if whole_blocks:
        near_cot, result0 = together((near_cot, result0))
        pieces_cot = finish_cot(near_cot)
    state0 = [inputs, hidden, mask0, None, saved]

    mask_mid, extra_mid = chosen((mask1, extra1), (mask0, extra0))
    inputs1, hidden1, payload, groups1 = attention_forward(
        fresh1, arriving, mask_mid, gain_one, gain_two, extra_mid, weights, packed
    )

    def first_groups():
        groups = other_heads(inputs, mask0, gain_one, weights, packed)
        state0[3] = [(qkv, heads), tuple(groups)]
        return groups

    micro_mid = 1 - section
    results, saved1 = mixture.forward(payload, micro_mid, [first_groups])

    grad0 = cot_own
    if whole_blocks:
        thunks, back_results, keeps0 = mixture.late_backward(pieces_cot, saved1)
        total = mixture.total(results, thunks)
    else:
        back_results, keeps0 = mixture.backward(grad0, micro_mid, saved1)
        total = mixture.total(results)
    result1 = (hidden1 + total).astype(bf16)
    arriving = lax.ppermute(result1, "section", [(0, 1)])

    slot2 = []

    def last_attention():
        zero = jnp.zeros((rows, model), bf16)
        slot2.extend(
            attention_forward(zero, arriving, mask1, gain_one, gain_two, extra1, weights, packed)
        )
        return slot2

    grad_two = mixture.total(back_results, [lambda: (), lambda: (), last_attention])
    inputs2, hidden2, payload, groups2 = slot2

    def attention_turn(grad, grad_two, state):
        inputs, hidden, mask, groups, _ = state
        outs = attention_backward(
            grad, grad_two, inputs, hidden, mask, gain_one, gain_two, [g[0] for g in groups], weights, packed
        )
        grad_input, low, grad_low, normed, g0, g1, attn_g, mlp_g = outs
        factors = (normed, grad_low, (g0, g1), [g[1] for g in groups])
        return grad_input, low, factors, jnp.concatenate([attn_g, mlp_g], axis=0)

    turn0 = []
    state1 = [inputs1, hidden1, mask_mid, groups1, saved1]

    def first_turn():
        turn0.extend(attention_turn(grad0, grad_two, state1))
        return turn0

    results2, saved2 = mixture.forward(payload, 1, [first_turn])
    coming = lax.ppermute(turn0[1], "section", [(1, 0)])
    state2 = [inputs2, hidden2, mask1, groups2, saved2]

    sums = []

    def weights_of(keeps):
        def thunk():
            sums.append(mixture.weight_sums(keeps, sums[-1] if sums else None))
            return sums[-1]

        return thunk

    grad1 = coming + cot1
    state_mid = chosen(state0, state2)
    micro_back = section
    back_results, keeps1 = mixture.backward(grad1, micro_back, state_mid[4])
    grad_two = mixture.total(back_results, [lambda: (), weights_of(keeps0)])
    turn1 = attention_turn(grad1, grad_two, state_mid)
    coming = lax.ppermute(turn1[1], "section", [(1, 0)])

    grad2 = coming
    total = mixture.total(results2, [lambda: (), weights_of(keeps1)])
    result2 = (hidden2 + total).astype(bf16)

    back_results, keeps2 = mixture.backward(grad2, 1 - section, saved1)
    grad_two = mixture.total(back_results)
    turn2 = attention_turn(grad2, grad_two, state1)

    turns = (turn0, turn1, turn2)
    factors = [t[2] for t in turns]
    starts = begins(together((lens, turn1[0]))[0])

    def owned(left, rights, side):
        full = [dot_tn(left, right).astype(bf16).reshape(peers, share, -1) for right in rights]

        def blocks(group):
            taken = [jnp.take(full[s], me ^ (m ^ cube.inner), axis=0) for m, s in group]
            return jnp.concatenate(taken, axis=0).reshape(-1, rights[0].shape[1])

        pairs = [(blocks(g), swap(blocks(mate), cube.core)) for g, mate in cube.stages]
        return reduce_rows(cube, pairs, side)

    def placed(own, m):
        half = model // shards
        kept = lax.dynamic_slice_in_dim(own, shard * half, half, 1)
        given = lax.dynamic_slice_in_dim(own, (1 - shard) * half, half, 1)
        got = swap(given, cube.z)
        low = jnp.where(shard == 0, kept, got)
        high = jnp.where(shard == 0, got, kept)
        return lax.dynamic_slice_in_dim(
            jnp.concatenate([low, high, low, high], axis=0), (block_rows - starts[m]) % block_rows, block_rows, 0
        )

    gain_total = [sum(t[3] for t in turns)]

    def gain_step(*directions):
        def thunk():
            for direction in directions:
                gain_total.append(gain_total[-1] + swap(gain_total[-1], direction))
            return gain_total[-1]

        return thunk

    placings = []

    def last_placing():
        placings.append(placed(chosen(turn2[0], turn1[0]), 1))
        return placings

    grad_o = owned(
        jnp.concatenate([f[1] for f in factors], axis=0),
        [jnp.concatenate([f[3][g] for f in factors], axis=0) for g in range(shards)],
        [gain_step(*cube.extra, cube.core), gain_step(cube.x), weights_of(keeps2)],
    )
    grad_qkv = owned(
        jnp.concatenate([f[0] for f in factors], axis=0),
        [jnp.concatenate([f[2][g] for f in factors], axis=0) for g in range(shards)],
        [gain_step(cube.y), gain_step(cube.z), last_placing],
    )
    width = q_weight.shape[2]
    grad_q = grad_qkv[:, :width]
    grad_k = grad_qkv[:, width : width + HEAD_SIZE]
    grad_v = grad_qkv[:, width + HEAD_SIZE :]
    gain_sums = lax.dynamic_slice_in_dim(gain_total[-1], me * share, share, 1)
    section_out = jnp.stack([placed(chosen(result0, result1), 0), placed(chosen(result1, result2), 1)])
    input_grad = jnp.stack([placed(chosen(turn1[0], turn0[0]), 0), placings[0]])
    gate_total, up_total, down_total = sums[-1]
    return (
        section_out[None],
        input_grad[None],
        gain_sums[0][None],
        grad_q[None],
        grad_k[None],
        grad_v[None],
        grad_o[None],
        gain_sums[1][None],
        gate_total[None, None],
        up_total[None, None],
        down_total[None, None],
    )


def solution(mesh):
    in_specs = (
        P(None, "dp", None),
        P(None, "dp", None),
        P("section", None, "dp", None),
        P("section", None, "dp", None),
        P("section", None),
        P("section", None, "shard"),
        P("section", None, "shard"),
        P("section", None, "shard"),
        P("section", None, "shard"),
        P("section", None),
        P("section", "dp", None, "shard"),
        P("section", "dp", None, "shard"),
        P("section", "dp", "shard", None),
        P(None, "dp", None),
    )
    out_specs = (
        P("section", None, "dp", "shard"),
        P("section", None, "dp", "shard"),
        P("section", "dp"),
        P("section", "dp", "shard"),
        P("section", "dp", "shard"),
        P("section", "dp", "shard"),
        P("section", "dp", "shard"),
        P("section", "dp"),
        P("section", "dp", None, "shard"),
        P("section", "dp", None, "shard"),
        P("section", "dp", "shard", None),
    )
    return jax.shard_map(local, mesh=mesh, in_specs=in_specs, out_specs=out_specs, check_vma=False)
```

```python
import functools

import jax
import jax.numpy as jnp
import numpy as np
from jax import lax
from jax.experimental import pallas as pl
from jax.experimental.pallas import tpu as pltpu
from jax.sharding import PartitionSpec as P

HEAD_SIZE = 128
epsilon = 1e-06
masked_value = -1e30
bf16 = jnp.bfloat16
f32 = jnp.float32


def wide(a):
    return a.astype(f32)


def dot_nn(a, b):
    return lax.dot_general(a, b, (((1,), (0,)), ((), ())), preferred_element_type=f32)


def dot_nt(a, b):
    return lax.dot_general(a, b, (((1,), (1,)), ((), ())), preferred_element_type=f32)


def dot_tn(a, b):
    return lax.dot_general(a, b, (((0,), (0,)), ((), ())), preferred_element_type=f32)


class Cube:
    def __init__(self):
        peers = lax.axis_size("dp")
        bits = [1 << i for i in range(peers.bit_length() - 1)]
        rest = bits[1:]
        self.core = ("dp", bits[0])
        self.x = ("dp", rest[0])
        self.y = ("dp", rest[len(rest) // 2])
        self.z = ("shard", 1)
        self.extra = [("dp", b) for b in rest if b not in (self.x[1], self.y[1])]
        inner = [0]
        for _, bit in self.extra:
            inner = inner + [m | bit for m in inner]
        self.inner = np.array(inner)
        x, y = self.x[1], self.y[1]
        stages = [[(0, 0)], [(x, 0), (y, 0), (0, 1)], [(x | y, 0), (y, 1), (x, 1)], [(x | y, 1)]]
        self.stages = [(g, [(m | self.core[1], s) for m, s in g]) for g in stages]


def swap(value, direction):
    axis, bit = direction
    return lax.ppermute(value, axis, [(i, i ^ bit) for i in range(lax.axis_size(axis))])


def thirds(rows):
    step = -(-rows // 48) * 16
    return [(0, step), (step, 2 * step), (2 * step, rows)]


together = lax.optimization_barrier


def after(payload, thunks, step):
    if step >= len(thunks) or thunks[step] is None:
        return payload, lambda: ()
    inputs, work = thunks[step]
    payload, inputs = together((payload, inputs()))
    return payload, lambda: work(*inputs)


def gather_rows(cube, own, work, side=()):
    core = cube.core
    own, beside = after(own, side, 0)
    near = [swap(own, d) for d in (cube.x, cube.y, cube.z)]
    mine0, other0 = work(0, [own, swap(own, core)])
    near, mine0, other0, _ = together((near, mine0, other0, beside()))

    near, beside = after(near, side, 1)
    middle = [swap(block, d) for block, d in zip(near, (cube.y, cube.z, cube.x))]
    in0 = swap(other0, core)
    mine1, other1 = work(1, [*near, *[swap(block, core) for block in near]])
    middle, in0, mine1, other1, _ = together((middle, in0, mine1, other1, beside()))

    middle, beside = after(middle, side, 2)
    cuts = thirds(own.shape[0])
    last = [
        swap(block[lo:hi], d) for block, d, (lo, hi) in zip(middle, (cube.z, cube.x, cube.y), cuts)
    ]
    in1 = swap(other1, core)
    mine2, other2 = work(2, [*middle, *[swap(block, core) for block in middle]])
    last, in1, mine2, other2, _ = together((last, in1, mine2, other2, beside()))

    in2 = swap(other2, core)
    mine3, other3 = work(3, [*last, *[swap(block, core) for block in last]])
    return [(mine0, in0), (mine1, in1), (mine2, in2), (mine3, swap(other3, core))]


def low_sum(*terms):
    return sum(wide(t) for t in terms).astype(bf16)


def reduce_rows(cube, pairs, side=()):
    own, near, middle, last = pairs
    rows = last[0].shape[0]

    def block(i, pair):
        return [g[i * rows : (i + 1) * rows] for g in pair]

    cuts = thirds(rows)
    sent, beside = after(low_sum(*last), side, 0)
    arrived = [swap(sent[lo:hi], d) for d, (lo, hi) in zip((cube.z, cube.x, cube.y), cuts)]
    arrived, middle, _ = together((arrived, middle, beside()))
    sent = [
        low_sum(*block(i, middle), jnp.pad(arrived[i], ((lo, rows - hi), (0, 0))))
        for i, (lo, hi) in enumerate(cuts)
    ]
    sent, beside = after(sent, side, 1)
    arrived = [swap(t, d) for t, d in zip(sent, (cube.y, cube.z, cube.x))]
    arrived, near, _ = together((arrived, near, beside()))
    sent = [low_sum(*block(i, near), arrived[i]) for i in range(3)]
    sent, beside = after(sent, side, 2)
    arrived = [swap(t, d) for t, d in zip(sent, (cube.x, cube.y, cube.z))]
    arrived, own, _ = together((arrived, own, beside()))
    total = sum(wide(t) for t in [*own, *arrived])
    for direction in reversed(cube.extra):
        half = total.shape[0] // 2
        total = total[:half] + wide(swap(total[half:].astype(bf16), direction))
    return total


def norm_factor(values):
    return lax.rsqrt(jnp.mean(values * values, axis=1, keepdims=True) + epsilon)


def norm_back(values, factor, gain, grad):
    gain_grad = jnp.sum(grad * values * factor, axis=0, keepdims=True)
    scaled = grad * gain
    inner = jnp.mean(scaled * values, axis=1, keepdims=True)
    return factor * (scaled - values * factor * factor * inner), gain_grad


def stack_heads(rows):
    return jnp.concatenate(
        [rows[:, i : i + HEAD_SIZE] for i in range(0, rows.shape[1], HEAD_SIZE)], axis=0
    )


def spread_heads(stacked, rows):
    return jnp.concatenate(
        [stacked[i : i + rows] for i in range(0, stacked.shape[0], rows)], axis=1
    )


def head_probs(query, key, allowed):
    scores = jnp.where(allowed > 0.0, dot_nt(query, key) * HEAD_SIZE ** (-0.5), masked_value)
    exp_scores = jnp.exp(scores - jnp.max(scores, axis=1, keepdims=True))
    return exp_scores / jnp.sum(exp_scores, axis=1, keepdims=True)


def normed_rows(values, gain):
    return (values * norm_factor(values) * gain).astype(bf16)


def group_probs(qkv, allowed):
    width = qkv.shape[1] - 2 * HEAD_SIZE
    query = stack_heads(qkv[:, :width])
    key, value = qkv[:, width : width + HEAD_SIZE], qkv[:, width + HEAD_SIZE :]
    tiled = jnp.concatenate([allowed] * (width // HEAD_SIZE), axis=0)
    return query, key, value, head_probs(query, key, tiled)


def head_group(normed, allowed, weights, qkv, heads):
    w_query, w_key, w_value, w_out = weights
    width = w_query.shape[1]
    qkv[:, :width] = dot_nn(normed, w_query).astype(bf16)
    qkv[:, width : width + HEAD_SIZE] = dot_nn(normed, w_key).astype(bf16)
    qkv[:, width + HEAD_SIZE :] = dot_nn(normed, w_value).astype(bf16)
    _, _, value, probs = group_probs(qkv[...], allowed)
    heads[...] = spread_heads(dot_nn(probs.astype(bf16), value).astype(bf16), normed.shape[0])
    return dot_nt(heads[...], w_out)


VMEM = pl.BlockSpec(memory_space=pltpu.VMEM)
SMEM = pl.BlockSpec(memory_space=pltpu.SMEM)
KERNEL_VMEM = 62 << 20


def like(shape, dtype):
    return jax.ShapeDtypeStruct(shape, dtype)


def on_device(body, outs, args, flops, scalars=()):
    moved = sum(a.size * a.dtype.itemsize for a in [*args, *outs])
    return pl.pallas_call(
        body,
        out_shape=outs,
        in_specs=[SMEM] * len(scalars) + [VMEM] * len(args),
        out_specs=[VMEM] * len(outs),
        compiler_params=pltpu.CompilerParams(vmem_limit_bytes=KERNEL_VMEM),
        cost_estimate=pl.CostEstimate(flops=flops, bytes_accessed=moved, transcendentals=0),
    )(*scalars, *args)


def geometry(lens, micro, side, rows, block):
    ends, total, best, start = [], 0, lens[micro, 0, 0], 0
    for i in range(lens.shape[2]):
        length = lens[micro, 0, i]
        if i:
            start = jnp.where(length > best, total, start)
            best = jnp.maximum(best, length)
        total = total + length
        ends.append(total)
    return ends, lax.rem(start + rows * side, block)


def positions(shape, axis, begin, block):
    place = lax.broadcasted_iota(jnp.int32, shape, axis) + begin
    return jnp.where(place >= block, place - block, place)


def selection(begin, rows, block):
    wanted = positions((rows, block), 0, begin, block)
    return (wanted == lax.broadcasted_iota(jnp.int32, (rows, block), 1)).astype(f32)


def sequence_mask(ends, begin, rows, block):
    row, col = [positions((rows, rows), axis, begin, block) for axis in (0, 1)]
    inside = sum(jnp.abs((row >= e).astype(jnp.int32) - (col >= e).astype(jnp.int32)) for e in ends)
    return ((inside == 0) & (col <= row)).astype(f32)


def gate_columns(pick, routes, gates):
    peers = lax.axis_size("dp")
    expert = lax.broadcasted_iota(jnp.int32, (128, routes.shape[1]), 0)
    table = jnp.zeros(expert.shape, f32)
    for k in range(routes.shape[0]):
        gate, route = gates[k : k + 1, :], routes[k : k + 1, :]
        high = wide(gate.astype(bf16))
        table += jnp.where(expert == route, high, 0.0) + jnp.where(expert == route + peers, gate - high, 0.0)
    return dot_nt(pick, table.astype(bf16)).astype(bf16)


def opening_body(lens, tokens, grad, routes, gates, gain, wq, wk, wv, wo, *outs):
    inputs, part, qkv, heads, sent, qkv_other, heads_other, mask, extra, cot, cot_other = outs
    block = tokens.shape[0]
    rows = block // 2
    shard = lax.axis_index("shard")
    first = jnp.where(lax.axis_index("section") == 0, 1.0, 0.0)
    weights = [w[...] for w in (wq, wk, wv, wo)]
    for own in (False, True):
        to_qkv, to_heads = (qkv, heads) if own else (qkv_other, heads_other)
        ends, begin = geometry(lens, 0, shard if own else 1 - shard, rows, block)
        pick = selection(begin, rows, block)
        values = dot_nn((pick * first).astype(bf16), tokens[...])
        allowed = sequence_mask(ends, begin, rows, block)
        value = head_group(normed_rows(values, gain[...]), allowed, weights, to_qkv, to_heads)
        cot_rows = dot_nn((pick * (1.0 - first)).astype(bf16), grad[...]).astype(bf16)
        if own:
            inputs[...] = values.astype(bf16)
            part[...] = values + value
            mask[...] = allowed
            extra[...] = gate_columns(pick.astype(bf16), routes[...], gates[...])
            cot[...] = cot_rows
        else:
            sent[...] = value.astype(bf16)
            cot_other[...] = cot_rows


def opening(lens, tokens, grad, routes, gates, gain, weights):
    block, model = tokens.shape
    rows = block // 2
    width, out = sum(w.shape[1] for w in weights[:3]), weights[3].shape[1]
    shapes = [
        like((rows, model), bf16), like((rows, model), f32), like((rows, width), bf16), like((rows, out), bf16),
        like((rows, model), bf16), like((rows, width), bf16), like((rows, out), bf16),
        like((rows, rows), f32), like((rows, 128), bf16), like((rows, model), bf16), like((rows, model), bf16),
    ]
    args = [tokens, grad, routes, gates, gain, *weights]
    outs = on_device(opening_body, shapes, args, 4 * rows * model * (width + out), (lens,))
    return outs[:5], outs[7:]


def settle_body(lens, tokens, grad, routes, gates, fresh, cot, mask, extra):
    block = tokens.shape[0]
    rows = block // 2
    first = jnp.where(lax.axis_index("section") == 0, 1.0, 0.0)
    ends, begin = geometry(lens, 1, lax.axis_index("shard"), rows, block)
    pick = selection(begin, rows, block)
    fresh[...] = dot_nn((pick * first).astype(bf16), tokens[...]).astype(bf16)
    cot[...] = dot_nn((pick * (1.0 - first)).astype(bf16), grad[...]).astype(bf16)
    mask[...] = sequence_mask(ends, begin, rows, block)
    extra[...] = gate_columns(pick.astype(bf16), routes[...], gates[...])


def settle(lens, tokens, grad, routes, gates):
    block, model = tokens.shape
    rows = block // 2
    shapes = [like((rows, model), bf16)] * 2 + [like((rows, rows), f32), like((rows, 128), bf16)]
    args = [tokens, grad, routes, gates]
    return on_device(settle_body, shapes, args, 2 * block * block * model, (lens,))


def joined_body(part, other, gain, extra, hidden, payload):
    total = part[...] + wide(other[...])
    hidden[...] = total
    model = total.shape[1]
    payload[:, :model] = normed_rows(total, gain[...])
    payload[:, model:] = extra[...]


def joined(part, other, gain, extra):
    rows, model = part.shape
    shapes = [like((rows, model), f32), like((rows, model + extra.shape[1]), bf16)]
    return on_device(joined_body, shapes, [part, other, gain, extra], 10 * rows * model)


def split_packed(packed, weights):
    at, parts = 0, []
    for w in weights:
        parts.append(packed[:, at : at + w.shape[1]])
        at += w.shape[1]
    return parts


def other_heads_body(inputs, mask, gain, wq, wk, wv, wo, packed, qkv, heads):
    normed = normed_rows(wide(inputs[...]), gain[...])
    head_group(normed, mask[...], split_packed(packed, (wq, wk, wv, wo)), qkv, heads)


def other_heads(inputs, mask, gain, weights, packed):
    rows = inputs.shape[0]
    width, out = sum(w.shape[1] for w in weights[:3]), weights[3].shape[1]
    shapes = [like((rows, width), bf16), like((rows, out), bf16)]
    args = [inputs, mask, gain, *weights, packed]
    return on_device(other_heads_body, shapes, args, 2 * rows * packed.size)


def attention_body(fresh, arriving, mask, gain, gain_two, extra, wq, wk, wv, wo, packed, *outs):
    inputs, hidden, payload, qkv0, qkv1, heads0, heads1 = outs
    rows = fresh[...] + arriving[...]
    inputs[...] = rows
    total = wide(rows)
    normed = normed_rows(total, gain[...])
    own = [w[...] for w in (wq, wk, wv, wo)]
    total = total + head_group(normed, mask[...], own, qkv0, heads0)
    total = total + head_group(normed, mask[...], split_packed(packed, own), qkv1, heads1)
    hidden[...] = total
    model = total.shape[1]
    payload[:, :model] = normed_rows(total, gain_two[...])
    payload[:, model:] = extra[...]


def attention_forward(fresh, arriving, mask, gain, gain_two, extra, weights, packed):
    rows, model = fresh.shape
    width, out = sum(w.shape[1] for w in weights[:3]), weights[3].shape[1]
    shapes = [
        like((rows, model), bf16), like((rows, model), f32), like((rows, model + extra.shape[1]), bf16),
        like((rows, width), bf16), like((rows, width), bf16), like((rows, out), bf16), like((rows, out), bf16),
    ]
    args = [fresh, arriving, mask, gain, gain_two, extra, *weights, packed]
    outs = on_device(attention_body, shapes, args, 4 * rows * packed.size)
    inputs, hidden, payload, qkv0, qkv1, heads0, heads1 = outs
    return inputs, hidden, payload, [(qkv0, heads0), (qkv1, heads1)]


def attention_back_body(grad, grad_two, inputs, hidden, mask, gain, gain_two, q0, q1, wq, wk, wv, wo, packed, *outs):
    grad_input, grad_input_low, grad_low, normed, g0, g1, gain_grad, gain_two_grad = outs
    rows = inputs.shape[0]
    values = wide(inputs[...])
    normed[...] = normed_rows(values, gain[...])
    total = hidden[...]
    back, gain_two_grad[...] = norm_back(total, norm_factor(total), gain_two[...], grad_two[...])
    grad_hidden = wide(grad[...]) + back
    low = grad_hidden.astype(bf16)
    grad_low[...] = low
    grad_normed = jnp.zeros_like(grad_hidden)
    own = [w[...] for w in (wq, wk, wv, wo)]
    for qkv, weights, grad_qkv in ((q0, own, g0), (q1, split_packed(packed, own), g1)):
        query, key, value, probs = group_probs(qkv[...], mask[...])
        grad_heads = stack_heads(dot_nn(low, weights[3]).astype(bf16))
        grad_probs = dot_nt(grad_heads, value)
        inner = jnp.sum(probs * grad_probs, axis=1, keepdims=True)
        grad_scores = (probs * (grad_probs - inner) * HEAD_SIZE ** (-0.5)).astype(bf16)
        grads = [
            spread_heads(dot_nn(grad_scores, key).astype(bf16), rows),
            dot_tn(grad_scores, query).astype(bf16),
            dot_tn(probs.astype(bf16), grad_heads).astype(bf16),
        ]
        at = 0
        for part, w in zip(grads, weights):
            grad_qkv[:, at : at + part.shape[1]] = part
            at += part.shape[1]
            grad_normed = grad_normed + dot_nt(part, w)
    back, gain_grad[...] = norm_back(values, norm_factor(values), gain[...], grad_normed)
    result = grad_hidden + back
    grad_input[...] = result
    grad_input_low[...] = result.astype(bf16)


def attention_backward(grad, grad_two, inputs, hidden, mask, gain, gain_two, projected, weights, packed):
    rows, model = inputs.shape
    width = projected[0].shape[1]
    shapes = [
        like((rows, model), f32), like((rows, model), bf16), like((rows, model), bf16),
        like((rows, model), bf16), like((rows, width), bf16), like((rows, width), bf16),
        like((1, model), f32), like((1, model), f32),
    ]
    args = [grad, grad_two, inputs, hidden, mask, gain, gain_two, *projected, *weights, packed]
    return on_device(attention_back_body, shapes, args, 8 * rows * packed.size)


def place(pieces, *targets):
    at = 0
    for piece in pieces:
        rows, first = piece.shape[0], 0
        for target in targets:
            target[at : at + rows, :] = piece[:, first : first + target.shape[1]]
            first += target.shape[1]
        at += rows


def own_gate(extra):
    me, peers = lax.axis_index("dp"), lax.axis_size("dp")
    lane = lax.broadcasted_iota(jnp.int32, extra.shape, 1)
    return jnp.sum(jnp.where((lane == me) | (lane == me + peers), wide(extra), 0.0), axis=1, keepdims=True)


def chunked(rows, step):
    count = max(c for c in (128, 192, 256, 384) if rows % c == 0)
    if rows == count:
        step(0, count)
    else:
        pl.loop(0, rows // count)(lambda i: step(pl.multiple_of(i * count, count), count))


def expert_stage_body(pieces, *refs):
    ins, (rows, extra, gate_out, up_out, *parts) = refs[:pieces], refs[pieces + 3 :]
    w_gate, w_up, w_down = refs[pieces : pieces + 3]
    place(ins, rows, extra)
    half = rows.shape[0] // 2
    for i, part in enumerate(parts):

        def step(first, count, i=i, part=part):
            here = pl.ds(first + i * half, count)
            values = rows[here, :]
            gate = dot_nn(values, w_gate[...])
            up = dot_nn(values, w_up[...])
            gate_out[here, :] = gate.astype(bf16)
            up_out[here, :] = up.astype(bf16)
            act = (gate / (1.0 + jnp.exp(-gate)) * up).astype(bf16)
            scale = own_gate(extra[here, :])
            part[pl.ds(first, count), :] = (scale * dot_nn(act, w_down[...])).astype(bf16)

        chunked(half, step)


def expert_stage(pieces, w_gate, w_up, w_down):
    count = sum(p.shape[0] for p in pieces)
    model, units = w_gate.shape
    shapes = [
        like((count, model), bf16), like((count, pieces[0].shape[1] - model), bf16),
        like((count, units), bf16), like((count, units), bf16),
        like((count // 2, model), bf16), like((count // 2, model), bf16),
    ]
    body = functools.partial(expert_stage_body, len(pieces))
    outs = on_device(body, shapes, [*pieces, w_gate, w_up, w_down], 6 * count * w_gate.size)
    return outs[4:], outs[:4]


def expert_back_body(pieces, *refs):
    ins = refs[:pieces]
    extra, gate_in, up_in, w_gate, w_up, w_down, grad_rows, grad_gate, grad_up, act, *parts = refs[pieces:]
    place(ins, grad_rows)
    half = grad_rows.shape[0] // 2
    for i, part in enumerate(parts):

        def step(first, count, i=i, part=part):
            here = pl.ds(first + i * half, count)
            scale = own_gate(extra[here, :])
            scaled = (scale * wide(grad_rows[here, :])).astype(bf16)
            grad_rows[here, :] = scaled
            grad_act = dot_nt(scaled, w_down[...])
            gate, up = wide(gate_in[here, :]), wide(up_in[here, :])
            sig = 1.0 / (1.0 + jnp.exp(-gate))
            silu = gate * sig
            low_gate = (grad_act * up * sig * (1.0 + gate * (1.0 - sig))).astype(bf16)
            low_up = (grad_act * silu).astype(bf16)
            grad_gate[here, :] = low_gate
            grad_up[here, :] = low_up
            act[here, :] = (silu * up).astype(bf16)
            grad_in = dot_nt(low_gate, w_gate[...]) + dot_nt(low_up, w_up[...])
            part[pl.ds(first, count), :] = grad_in.astype(bf16)

        chunked(half, step)


def expert_back_stage(pieces, saved, w_gate, w_up, w_down):
    rows, extra, gate_out, up_out = saved
    count = rows.shape[0]
    model, units = w_gate.shape
    shapes = [
        like((count, model), bf16), like((count, units), bf16), like((count, units), bf16),
        like((count, units), bf16), like((count // 2, model), bf16), like((count // 2, model), bf16),
    ]
    body = functools.partial(expert_back_body, len(pieces))
    args = [*pieces, extra, gate_out, up_out, w_gate, w_up, w_down]
    outs = on_device(body, shapes, args, 6 * count * w_gate.size)
    return outs[4:], outs[:4]


def product_sums_body(stages, products, *refs):
    ins, outs = refs[: -len(products)], refs[-len(products) :]
    fields = 1 + max(max(p) for p in products)
    totals = [ref[...] for ref in ins[fields * stages :]] or [0.0] * len(products)
    for i in range(stages):
        stage = [r[...] for r in ins[fields * i : fields * (i + 1)]]
        totals = [t + dot_tn(stage[a], stage[b]) for t, (a, b) in zip(totals, products)]
    for out, total in zip(outs, totals):
        out[...] = total


def product_sums(stages, products, swept, sums):
    width = stages[0][swept].shape[1]
    step = min(t.shape[1] for t in stages[0])
    rows = sum(stage[0].shape[0] for stage in stages)
    args, specs = [], []
    for stage in stages:
        args += stage
        for i, t in enumerate(stage):
            if i == swept:
                specs.append(pl.BlockSpec((t.shape[0], step), lambda j: (0, j)))
            else:
                specs.append(pl.BlockSpec(t.shape, lambda j: (0, 0)))
    shapes, outs = [], []
    for left, right in products:
        other = stages[0][right if left == swept else left].shape[1]
        if left == swept:
            shapes.append(like((width, other), f32))
            outs.append(pl.BlockSpec((step, other), lambda j: (j, 0)))
        else:
            shapes.append(like((other, width), f32))
            outs.append(pl.BlockSpec((other, step), lambda j: (0, j)))
    first = len(args)
    if sums is not None:
        args += sums
        specs += outs
    return pl.pallas_call(
        functools.partial(product_sums_body, len(stages), products),
        grid=(width // step,),
        out_shape=shapes,
        in_specs=specs,
        out_specs=outs,
        input_output_aliases={} if sums is None else {first + i: i for i in range(len(shapes))},
        compiler_params=pltpu.CompilerParams(vmem_limit_bytes=KERNEL_VMEM),
        cost_estimate=pl.CostEstimate(
            flops=2 * rows * sum(t.size for t in shapes),
            bytes_accessed=sum(a.size * a.dtype.itemsize for a in args),
            transcendentals=0,
        ),
    )(*args)


def expert_forward(rows, w_gate, w_up, w_down):
    gate_out = dot_nn(rows, w_gate)
    up_out = dot_nn(rows, w_up)
    act = (gate_out / (1.0 + jnp.exp(-gate_out)) * up_out).astype(bf16)
    part = dot_nn(act, w_down).astype(bf16)
    return part, (rows, gate_out.astype(bf16), up_out.astype(bf16))


def expert_backward(grad_rows, saved, w_gate, w_up, w_down):
    rows, gate_low, up_low = saved
    gate_out, up_out = wide(gate_low), wide(up_low)
    grad_act = dot_nt(grad_rows, w_down)
    sig = 1.0 / (1.0 + jnp.exp(-gate_out))
    silu = gate_out * sig
    grad_gate = (grad_act * up_out * sig * (1.0 + gate_out * (1.0 - sig))).astype(bf16)
    grad_up = (grad_act * silu).astype(bf16)
    act = (silu * up_out).astype(bf16)
    grad_in = (dot_nt(grad_gate, w_gate) + dot_nt(grad_up, w_up)).astype(bf16)
    return grad_in, (dot_tn(rows, grad_gate), dot_tn(rows, grad_up), dot_tn(act, grad_rows))


def halves(array):
    half = array.shape[0] // 2
    return array[:half], array[half:]


class Blocks:
    def __init__(self, cube, weights):
        self.cube, self.weights = cube, weights

    def forward(self, payload, micro, side=()):
        saved = []

        def work(stage, pieces):
            parts, kept = expert_stage(pieces, *self.weights)
            saved.append(kept)
            return parts

        return gather_rows(self.cube, payload, work, side), saved

    def back_stage(self, stage, pieces, saved):
        parts, kept = expert_back_stage(pieces, saved[stage], *self.weights)
        return parts, [saved[stage][0], *kept]

    def backward(self, grad, micro, saved, side=()):
        keeps = []

        def work(stage, pieces):
            parts, kept = self.back_stage(stage, pieces, saved)
            keeps.append(kept)
            return parts

        return gather_rows(self.cube, grad, work, side), keeps

    def late_backward(self, pieces, saved):
        results, keeps = [None] * 4, [None] * 4

        def run(*stages):
            def work(*gathered):
                for stage, rows in zip(stages, gathered):
                    (mine, other), keeps[stage] = self.back_stage(stage, rows, saved)
                    results[stage] = (mine, swap(other, self.cube.core))
                return [results[stage] for stage in stages]

            return lambda: [pieces[stage] for stage in stages], work

        return [run(3), run(2), run(1, 0)], results, keeps

    def total(self, results, side=()):
        return reduce_rows(self.cube, results, side)

    def weight_sums(self, keeps, sums):
        def hidden(*stages):
            sums[0] = product_sums(stages, ((0, 1), (0, 2)), 0, sums[0])
            return sums[0]

        def back(*stages):
            sums[1] = product_sums(stages, ((0, 1),), 1, sums[1])
            return sums[1]

        return [
            (lambda: [[rows, gate, up] for rows, _, gate, up, _ in keeps], hidden),
            (lambda: [[act, grad] for _, grad, _, _, act in keeps], back),
        ]


def run_all(side):
    for thunk in side:
        if thunk is not None:
            thunk[1](*thunk[0]())


class Buckets:
    def __init__(self, cube, weights, routes, gates, capacity):
        self.cube, self.weights, self.capacity = cube, weights, capacity
        micros, self.rows, self.top = routes.shape
        self.experts = lax.axis_size("dp")
        self.tables = []
        for m in range(micros):
            flat = routes[m].reshape(-1)
            onehot = (flat[:, None] == jnp.arange(self.experts, dtype=jnp.int32)).astype(jnp.int32)
            earlier = jnp.cumsum(onehot, axis=0) - onehot
            target = flat * capacity + jnp.sum(earlier * onehot, axis=1)
            source = jnp.full((self.experts * capacity,), flat.shape[0], jnp.int32)
            source = source.at[target].set(jnp.arange(flat.shape[0], dtype=jnp.int32))
            self.tables.append((target, source, gates[m]))

    def table(self, micro):
        return jax.tree.map(lambda a, b: jnp.where(micro == 0, a, b), self.tables[0], self.tables[1])

    def exchange(self, rows):
        shape = (self.experts, self.capacity, rows.shape[1])
        moved = lax.all_to_all(rows.reshape(shape), "dp", split_axis=0, concat_axis=0, tiled=True)
        return moved.reshape(rows.shape)

    def whole(self, own):
        return jnp.concatenate([own, swap(own, self.cube.z)], axis=0)

    def forward(self, payload, micro, side=()):
        target, source, gates = self.table(micro)
        own = payload[:, : self.weights[0].shape[0]]
        padded = jnp.pad(self.whole(own), ((0, 1), (0, 0)))
        arrived = self.exchange(jnp.take(padded, source // self.top, axis=0))
        part, saved = expert_forward(arrived, *self.weights)
        picked = jnp.take(self.exchange(part), target, axis=0).reshape(self.rows, self.top, -1)
        run_all(side)
        return jnp.sum(gates[:, :, None] * picked, axis=1), saved

    def backward(self, grad, micro, saved, side=()):
        target, source, gates = self.table(micro)
        scaled = (gates[:, :, None] * wide(self.whole(grad))[:, None, :]).astype(bf16)
        padded = jnp.pad(scaled.reshape(self.rows * self.top, -1), ((0, 1), (0, 0)))
        arrived = self.exchange(jnp.take(padded, source, axis=0))
        grad_in, weights = expert_backward(arrived, saved, *self.weights)
        picked = jnp.take(self.exchange(grad_in), target, axis=0).reshape(self.rows, self.top, -1)
        run_all(side)
        return jnp.sum(picked, axis=1, dtype=f32), weights

    def total(self, results, side=()):
        own, other = halves(results.astype(bf16))
        run_all(side)
        return wide(own) + wide(swap(other, self.cube.z))

    def weight_sums(self, weights, sums):
        def add(*weights):
            for i, part in enumerate((list(weights[:2]), list(weights[2:]))):
                sums[i] = part if sums[i] is None else [a + b for a, b in zip(sums[i], part)]

        return [None, (lambda: weights, add)]


def local(
    tokens, lengths, routes, gates, attn_gain, q_weight, key_projection, value_projection,
    o_weight, mlp_gain, expert_gate, expert_up, expert_down, cotangent,
):
    cube = Cube()
    section = lax.axis_index("section")
    shard = lax.axis_index("shard")
    me = lax.axis_index("dp")
    peers, shards = lax.axis_size("dp"), lax.axis_size("shard")
    _, block_rows, model = tokens.shape
    rows = block_rows // shards
    share = model // peers
    first = section == 0
    gain_one, gain_two = attn_gain[0][None], mlp_gain[0][None]
    weights = [q_weight[0], key_projection[0], value_projection[0], o_weight[0]]
    expert_w = (expert_gate[0, 0], expert_up[0, 0], expert_down[0, 0])
    capacity = 2 * block_rows * routes.shape[3] // peers
    whole_blocks = capacity >= block_rows

    def chosen(here, there):
        return jax.tree.map(lambda a, b: jnp.where(first, a, b), here, there)

    def begins(lens):
        lens = lens[:, 0]
        ends, longest = jnp.cumsum(lens, axis=1), jnp.argmax(lens, axis=1)
        return [ends[m, longest[m]] - lens[m, longest[m]] for m in range(2)]

    def turned(array, begin):
        doubled = jnp.concatenate([array, array], axis=0)
        return lax.dynamic_slice_in_dim(doubled, (begin + rows * shard) % block_rows, block_rows, 0)

    if whole_blocks:
        mixture = Blocks(cube, expert_w)
    else:
        early = begins(lengths)
        mixture = Buckets(
            cube,
            expert_w,
            jnp.stack([turned(routes[0, m], early[m]) for m in range(2)]),
            jnp.stack([turned(gates[0, m], early[m]) for m in range(2)]),
            capacity,
        )

    slices = jnp.concatenate([lax.dynamic_slice_in_dim(w, me * share, share, 0) for w in weights], axis=1)
    slices = swap(slices, cube.z)

    route_cols = [routes[0, m].T for m in range(2)]
    gate_cols = [gates[0, m].T for m in range(2)]
    (inputs, part, qkv, heads, sent, *_), (mask0, extra0, cot_own, cot_other) = opening(
        lengths, tokens[0], cotangent[0], route_cols[0], gate_cols[0], gain_one, weights
    )
    settled = [tokens[1], cotangent[1], route_cols[1], gate_cols[1]]
    sent, settled = together((sent, settled))
    moved = [swap(sent, cube.z)]
    if whole_blocks:
        moved += [swap(cot_own, cube.x), swap(cot_own, cube.y)]
    (arrived, *near_cot), slices, settled = together((moved, slices, settle(lengths, *settled)))
    fresh1, cot1, mask1, extra1 = settled
    packed = lax.all_gather(slices, "dp", axis=0, tiled=True)
    hidden, payload = joined(part, arrived, gain_two, extra0)
    results, saved = mixture.forward(payload, 0)
    total = mixture.total(results)
    result0 = (hidden + total).astype(bf16)
    if whole_blocks:
        result0, cot_other, near_cot = together((result0, cot_other, near_cot))
    arriving = lax.ppermute(result0, "section", [(0, 1)])
    state0 = [inputs, hidden, mask0, None, saved]

    mask_mid, extra_mid = chosen((mask1, extra1), (mask0, extra0))
    if whole_blocks:
        x0, y0 = near_cot
        y1 = swap(cot_other, cube.y)
        pieces_cot = [[cot_own], [x0, y0, cot_other], [swap(x0, cube.y), y1, swap(cot_other, cube.x)], [swap(y1, cube.x)]]
        pieces_cot = [[*stage, *[swap(t, cube.core) for t in stage]] for stage in pieces_cot]
    inputs1, hidden1, payload, groups1 = attention_forward(
        fresh1, arriving, mask_mid, gain_one, gain_two, extra_mid, weights, packed
    )
    if whole_blocks:
        payload, pieces_cot = together((payload, pieces_cot))

    def first_groups(*args):
        groups = other_heads(*args)
        state0[3] = [(qkv, heads), tuple(groups)]
        return groups

    micro_mid = 1 - section
    results, saved1 = mixture.forward(
        payload, micro_mid, [(lambda: [inputs, mask0, gain_one, weights, packed], first_groups)]
    )

    grad0 = cot_own
    if whole_blocks:
        thunks, back_results, keeps0 = mixture.late_backward(pieces_cot, saved1)
        total = mixture.total(results, thunks)
    else:
        back_results, keeps0 = mixture.backward(grad0, micro_mid, saved1)
        total = mixture.total(results)
    result1 = (hidden1 + total).astype(bf16)
    arriving = lax.ppermute(result1, "section", [(0, 1)])

    slot2 = []

    def last_attention(arriving):
        zero = jnp.zeros((rows, model), bf16)
        slot2.extend(
            attention_forward(zero, arriving, mask1, gain_one, gain_two, extra1, weights, packed)
        )
        return slot2

    grad_two = mixture.total(back_results, [None, None, (lambda: [arriving], last_attention)])
    inputs2, hidden2, payload, groups2 = slot2

    def attention_turn(grad, grad_two, state):
        inputs, hidden, mask, groups, _ = state
        outs = attention_backward(
            grad, grad_two, inputs, hidden, mask, gain_one, gain_two, [g[0] for g in groups], weights, packed
        )
        grad_input, low, grad_low, normed, g0, g1, attn_g, mlp_g = outs
        factors = (normed, grad_low, (g0, g1), [g[1] for g in groups])
        return grad_input, low, factors, jnp.concatenate([attn_g, mlp_g], axis=0)

    turn0 = []
    state1 = [inputs1, hidden1, mask_mid, groups1, saved1]

    def first_turn(grad_two):
        turn0.extend(attention_turn(grad0, grad_two, state1))
        return turn0

    results2, saved2 = mixture.forward(payload, 1, [(lambda: [grad_two], first_turn)])
    coming = lax.ppermute(turn0[1], "section", [(1, 0)])
    state2 = [inputs2, hidden2, mask1, groups2, saved2]

    sums = [None, None]
    coming, results2, saved2 = together((coming, results2, saved2))
    state2[4] = saved2
    grad1 = coming + cot1
    state_mid = chosen(state0, state2)
    back_results, keeps1 = mixture.backward(grad1, section, state_mid[4])
    grad_two = mixture.total(back_results, [None, *mixture.weight_sums(keeps0, sums)])
    grad_two, results2 = together((grad_two, results2))
    turn1 = attention_turn(grad1, grad_two, state_mid)
    coming = lax.ppermute(turn1[1], "section", [(1, 0)])

    total = mixture.total(results2)
    result2 = (hidden2 + total).astype(bf16)

    grad2, result2 = together((coming, result2))
    back_results, keeps2 = mixture.backward(grad2, 1 - section, saved1)
    grad_two = mixture.total(back_results, [None, *mixture.weight_sums(keeps1, sums)])
    turn2 = attention_turn(grad2, grad_two, state1)

    turns = (turn0, turn1, turn2)
    factors = [t[2] for t in turns]
    starts = begins(together((lengths, turn1[0]))[0])

    def owned(left, rights, side):
        full = [dot_tn(left, right).astype(bf16).reshape(peers, share, -1) for right in rights]

        def blocks(group):
            taken = [jnp.take(full[s], me ^ (m ^ cube.inner), axis=0) for m, s in group]
            return jnp.concatenate(taken, axis=0).reshape(-1, rights[0].shape[1])

        pairs = [(blocks(g), swap(blocks(mate), cube.core)) for g, mate in cube.stages]
        return reduce_rows(cube, pairs, side)

    def placed(own, m):
        half = model // shards
        kept = lax.dynamic_slice_in_dim(own, shard * half, half, 1)
        given = lax.dynamic_slice_in_dim(own, (1 - shard) * half, half, 1)
        got = swap(given, cube.z)
        low = jnp.where(shard == 0, kept, got)
        high = jnp.where(shard == 0, got, kept)
        return lax.dynamic_slice_in_dim(
            jnp.concatenate([low, high, low, high], axis=0), (block_rows - starts[m]) % block_rows, block_rows, 0
        )

    gain_total = [sum(t[3] for t in turns)]

    def gain_step(*directions):
        def step(total):
            for direction in directions:
                total = total + swap(total, direction)
            gain_total.append(total)
            return total

        return lambda: gain_total[-1:], step

    placings = []

    def last_placing(own):
        placings.append(placed(own, 1))
        return placings

    grad_o = owned(
        jnp.concatenate([f[1] for f in factors], axis=0),
        [jnp.concatenate([f[3][g] for f in factors], axis=0) for g in range(shards)],
        [gain_step(*cube.extra, cube.core), *mixture.weight_sums(keeps2, sums)],
    )
    grad_qkv = owned(
        jnp.concatenate([f[0] for f in factors], axis=0),
        [jnp.concatenate([f[2][g] for f in factors], axis=0) for g in range(shards)],
        [gain_step(cube.x), gain_step(cube.y, cube.z), (lambda: [chosen(turn2[0], turn1[0])], last_placing)],
    )
    width = q_weight.shape[2]
    grad_q = grad_qkv[:, :width]
    grad_k = grad_qkv[:, width : width + HEAD_SIZE]
    grad_v = grad_qkv[:, width + HEAD_SIZE :]
    gain_sums = lax.dynamic_slice_in_dim(gain_total[-1], me * share, share, 1)
    section_out = jnp.stack([placed(chosen(result0, result1), 0), placed(chosen(result1, result2), 1)])
    input_grad = jnp.stack([placed(chosen(turn1[0], turn0[0]), 0), placings[0]])
    (gate_total, up_total), (down_total,) = sums
    return (
        section_out[None],
        input_grad[None],
        gain_sums[0][None],
        grad_q[None],
        grad_k[None],
        grad_v[None],
        grad_o[None],
        gain_sums[1][None],
        gate_total[None, None],
        up_total[None, None],
        down_total[None, None],
    )


def solution(mesh):
    in_specs = (
        P(None, "dp", None),
        P(None, "dp", None),
        P("section", None, "dp", None),
        P("section", None, "dp", None),
        P("section", None),
        P("section", None, "shard"),
        P("section", None, "shard"),
        P("section", None, "shard"),
        P("section", None, "shard"),
        P("section", None),
        P("section", "dp", None, "shard"),
        P("section", "dp", None, "shard"),
        P("section", "dp", "shard", None),
        P(None, "dp", None),
    )
    out_specs = (
        P("section", None, "dp", "shard"),
        P("section", None, "dp", "shard"),
        P("section", "dp"),
        P("section", "dp", "shard"),
        P("section", "dp", "shard"),
        P("section", "dp", "shard"),
        P("section", "dp", "shard"),
        P("section", "dp"),
        P("section", "dp", None, "shard"),
        P("section", "dp", None, "shard"),
        P("section", "dp", "shard", None),
    )
    return jax.shard_map(local, mesh=mesh, in_specs=in_specs, out_specs=out_specs, check_vma=False)
```

```python
import functools

import jax
import jax.numpy as jnp
import numpy as np
from jax import lax
from jax.experimental import pallas as pl
from jax.experimental.pallas import tpu as pltpu
from jax.sharding import PartitionSpec as P

HEAD_SIZE = 128
epsilon = 1e-06
masked_value = -1e30
bf16 = jnp.bfloat16
f32 = jnp.float32


def wide(a):
    return a.astype(f32)


def dot_nn(a, b):
    return lax.dot_general(a, b, (((1,), (0,)), ((), ())), preferred_element_type=f32)


def dot_nt(a, b):
    return lax.dot_general(a, b, (((1,), (1,)), ((), ())), preferred_element_type=f32)


def dot_tn(a, b):
    return lax.dot_general(a, b, (((0,), (0,)), ((), ())), preferred_element_type=f32)


class Cube:
    def __init__(self):
        peers = lax.axis_size("dp")
        bits = [1 << i for i in range(peers.bit_length() - 1)]
        rest = bits[1:]
        self.core = ("dp", bits[0])
        self.x = ("dp", rest[0])
        self.y = ("dp", rest[len(rest) // 2])
        self.z = ("shard", 1)
        self.extra = [("dp", b) for b in rest if b not in (self.x[1], self.y[1])]
        inner = [0]
        for _, bit in self.extra:
            inner = inner + [m | bit for m in inner]
        self.inner = np.array(inner)
        x, y = self.x[1], self.y[1]
        self.corner = (x | y, 1)
        stages = [[(0, 0)], [(x, 0), (y, 0), (0, 1)], [(x | y, 0), (y, 1), (x, 1)], [self.corner]]
        self.stages = [(g, [(m | self.core[1], s) for m, s in g]) for g in stages]


def swap(value, direction):
    axis, bit = direction
    return lax.ppermute(value, axis, [(i, i ^ bit) for i in range(lax.axis_size(axis))])


def across(value, cube):
    mask, flip = cube.corner
    shards = lax.axis_size("shard")
    pairs = [
        (d * shards + s, (d ^ mask) * shards + (s ^ flip))
        for d in range(lax.axis_size("dp"))
        for s in range(shards)
    ]
    return lax.ppermute(value, ("dp", "shard"), pairs)


together = lax.optimization_barrier


def both(*thunks):
    def work(*groups):
        return [thunk[1](*group) for thunk, group in zip(thunks, groups)]

    return lambda: [thunk[0]() for thunk in thunks], work


def after(payload, thunks, step):
    if step >= len(thunks) or thunks[step] is None:
        return payload, lambda: ()
    inputs, work = thunks[step]
    payload, inputs = together((payload, inputs()))
    return payload, lambda: work(*inputs)


def gather_rows(cube, own, work, side=()):
    core = cube.core
    own, beside = after(own, side, 0)
    near = [swap(own, d) for d in (cube.x, cube.y, cube.z)]
    mine0, other0 = work(0, [own, swap(own, core)])
    near, mine0, other0, _ = together((near, mine0, other0, beside()))

    near, beside = after(near, side, 1)
    middle = [swap(block, d) for block, d in zip(near, (cube.y, cube.z, cube.x))]
    in0 = swap(other0, core)
    mine1, other1 = work(1, [*near, *[swap(block, core) for block in near]])
    middle, in0, mine1, other1, _ = together((middle, in0, mine1, other1, beside()))

    middle, beside = after(middle, side, 2)
    corner = swap(middle[0], cube.z)
    mine2, other2 = work(2, [*middle, *[swap(block, core) for block in middle]])
    corner, mine2, other2, _ = together((corner, mine2, other2, beside()))
    other2, beside = after(other2, side, 3)
    in2 = swap(other2, core)
    mine3, other3 = work(3, [corner, swap(corner, core)])
    in2, mine3, other3, _ = together((in2, mine3, other3, beside()))
    return [(mine0, in0), (mine1, other1), (mine2, in2), (mine3, other3)]


def low_sum(*terms):
    return sum(wide(t) for t in terms).astype(bf16)


def reduce_start(cube, pairs, side=()):
    own, near, middle, corner = pairs
    rows = corner[0].shape[0]
    sent = [low_sum(*[g[i * rows : (i + 1) * rows] for g in middle]) for i in range(3)]
    (sent, near, corner), beside = after((sent, near, corner), side, 0)
    arrived = [swap(t, d) for t, d in zip(sent, (cube.y, cube.z, cube.x))]
    near, corner = [(mine, swap(other, cube.core)) for mine, other in (near, corner)]
    arrived, own, near, corner, _ = together((arrived, own, near, corner, beside()))
    return own, near, arrived, corner


def reduce_finish(cube, state, side=()):
    own, near, arrived, corner = state
    rows = corner[0].shape[0]
    sent = [low_sum(*corner)] + [low_sum(*[g[i * rows : (i + 1) * rows] for g in near], arrived[i]) for i in range(3)]
    sent, beside = after(sent, side, 0)
    arrived = [swap(t, d) for t, d in zip(sent[1:], (cube.x, cube.y, cube.z))] + [across(sent[0], cube)]
    arrived, own, _ = together((arrived, own, beside()))
    total = sum(wide(t) for t in [*own, *arrived])
    for direction in reversed(cube.extra):
        half = total.shape[0] // 2
        total = total[:half] + wide(swap(total[half:].astype(bf16), direction))
    return total


def norm_factor(values):
    return lax.rsqrt(jnp.mean(values * values, axis=1, keepdims=True) + epsilon)


def norm_back(values, factor, gain, grad):
    gain_grad = jnp.sum(grad * values * factor, axis=0, keepdims=True)
    scaled = grad * gain
    inner = jnp.mean(scaled * values, axis=1, keepdims=True)
    return factor * (scaled - values * factor * factor * inner), gain_grad


def stack_heads(rows):
    return jnp.concatenate(
        [rows[:, i : i + HEAD_SIZE] for i in range(0, rows.shape[1], HEAD_SIZE)], axis=0
    )


def spread_heads(stacked, rows):
    return jnp.concatenate(
        [stacked[i : i + rows] for i in range(0, stacked.shape[0], rows)], axis=1
    )


def head_probs(query, key, allowed):
    scores = jnp.where(allowed > 0.0, dot_nt(query, key) * HEAD_SIZE ** (-0.5), masked_value)
    exp_scores = jnp.exp(scores - jnp.max(scores, axis=1, keepdims=True))
    return exp_scores / jnp.sum(exp_scores, axis=1, keepdims=True)


def normed_rows(values, gain):
    return (values * norm_factor(values) * gain).astype(bf16)


def group_probs(qkv, allowed):
    width = qkv.shape[1] - 2 * HEAD_SIZE
    query = stack_heads(qkv[:, :width])
    key, value = qkv[:, width : width + HEAD_SIZE], qkv[:, width + HEAD_SIZE :]
    tiled = jnp.concatenate([allowed] * (width // HEAD_SIZE), axis=0)
    return query, key, value, head_probs(query, key, tiled)


def head_group(normed, allowed, weights, qkv, heads):
    *projections, w_out = weights
    at = 0
    for w in projections:
        part = dot_nn(normed, w()).astype(bf16)
        qkv[:, at : at + part.shape[1]] = part
        at += part.shape[1]
    _, _, value, probs = group_probs(qkv[...], allowed)
    heads[...] = spread_heads(dot_nn(probs.astype(bf16), value).astype(bf16), normed.shape[0])
    return dot_nt(heads[...], w_out())


VMEM = pl.BlockSpec(memory_space=pltpu.VMEM)
SMEM = pl.BlockSpec(memory_space=pltpu.SMEM)
ANY = pl.BlockSpec(memory_space=pl.ANY)
KERNEL_VMEM = 42 << 20


def held(shape, dtype):
    return pltpu.VMEM(shape, dtype)


def like(shape, dtype):
    return pltpu.HBM(shape, dtype)


def close(value):
    return pltpu.with_memory_space_constraint(value, pltpu.VMEM)


def distant(value):
    return pltpu.with_memory_space_constraint(value, pltpu.HBM)


def pinned(*values):
    def body(*refs):
        ins, outs, sems = refs[: len(values)], refs[len(values) : -1], refs[-1]
        copies = Copies(sems)
        for copy in [copies.start(a, b) for a, b in zip(ins, outs)]:
            copy.wait()

    return pl.pallas_call(
        body,
        out_shape=[held(v.shape, v.dtype) for v in values],
        in_specs=[ANY] * len(values),
        out_specs=[VMEM] * len(values),
        scratch_shapes=[pltpu.SemaphoreType.DMA((len(values),))],
        compiler_params=pltpu.CompilerParams(vmem_limit_bytes=1 << 20),
    )(*values)


def put_together(pieces, spans, shape):
    starts = jnp.stack([first for first, _, _ in spans]).astype(jnp.int32)

    def body(starts, *refs):
        ins, out, sems = refs[:-2], refs[-2], refs[-1]
        copies, waits = Copies(sems), []
        for i, (piece, (_, unit, column)) in enumerate(zip(ins, spans)):
            rows = pl.ds(pl.multiple_of(starts[i] * unit, unit), piece.shape[0])
            waits.append(copies.start(piece, out.at[rows, pl.ds(column, piece.shape[1])]))
        for copy in waits:
            copy.wait()

    return pl.pallas_call(
        body,
        out_shape=held(shape, pieces[0].dtype),
        in_specs=[SMEM] + [ANY] * len(pieces),
        out_specs=VMEM,
        scratch_shapes=[pltpu.SemaphoreType.DMA((len(pieces),))],
        compiler_params=pltpu.CompilerParams(vmem_limit_bytes=KERNEL_VMEM),
    )(starts, *map(distant, pieces))


class Copies:
    def __init__(self, sems):
        self.sems, self.count = sems, 0

    def start(self, source, target):
        copy = pltpu.make_async_copy(source, target, self.sems.at[self.count])
        self.count += 1
        copy.start()
        return copy

    def fetch(self, source, target):
        copy, waited = self.start(source, target), []

        def value():
            if not waited:
                copy.wait()
                waited.append(True)
            return target[...]

        return value


def on_device(body, outs, args, flops, scalars=(), kept=(), far=(), scratch=(), direct=False):
    moved = sum(a.size * a.dtype.itemsize for a in args)
    return pl.pallas_call(
        body,
        out_shape=outs,
        in_specs=[SMEM] * len(scalars) + [VMEM] * (len(args) + len(kept)) + [ANY] * len(far),
        out_specs=[SMEM if o.dtype == jnp.int32 else ANY if direct else VMEM for o in outs],
        scratch_shapes=scratch,
        compiler_params=pltpu.CompilerParams(vmem_limit_bytes=KERNEL_VMEM),
        cost_estimate=pl.CostEstimate(flops=flops // 64, bytes_accessed=moved // 64, transcendentals=0),
    )(*scalars, *map(distant, args), *map(close, kept), *far)


def holders(*arrays):
    return [pltpu.VMEM(a.shape, a.dtype) for a in arrays] + [pltpu.SemaphoreType.DMA((len(arrays) + 1,))]


def geometry(lens, micro, side, rows, block):
    ends, total, best, start = [], 0, lens[micro, 0, 0], 0
    for i in range(lens.shape[2]):
        length = lens[micro, 0, i]
        if i:
            start = jnp.where(length > best, total, start)
            best = jnp.maximum(best, length)
        total = total + length
        ends.append(total)
    return ends, lax.rem(start + rows * side, block)


def positions(shape, axis, begin, block):
    place = lax.broadcasted_iota(jnp.int32, shape, axis) + begin
    return jnp.where(place >= block, place - block, place)


def selection(begin, rows, block):
    wanted = positions((rows, block), 0, begin, block)
    return (wanted == lax.broadcasted_iota(jnp.int32, (rows, block), 1)).astype(f32)


def sequence_mask(ends, begin, rows, block):
    row, col = [positions((rows, rows), axis, begin, block) for axis in (0, 1)]
    inside = sum(jnp.abs((row >= e).astype(jnp.int32) - (col >= e).astype(jnp.int32)) for e in ends)
    return ((inside == 0) & (col <= row)).astype(f32)


def gate_columns(pick, routes, gates):
    peers = lax.axis_size("dp")
    expert = lax.broadcasted_iota(jnp.int32, (128, routes.shape[1]), 0)
    table = jnp.zeros(expert.shape, f32)
    for k in range(routes.shape[0]):
        gate, route = gates[k : k + 1, :], routes[k : k + 1, :]
        high = wide(gate.astype(bf16))
        table += jnp.where(expert == route, high, 0.0) + jnp.where(expert == route + peers, gate - high, 0.0)
    return dot_nt(pick, table.astype(bf16)).astype(bf16)


def turned_body(lens, blocks, own, other, block_rows, sems):
    copy = Copies(sems).fetch(blocks.at[0], block_rows)
    block = block_rows.shape[0]
    here = jnp.where(lax.axis_index("section") == 0, 0.0, 1.0)
    shard = lax.axis_index("shard")
    for side, out in ((shard, own), (1 - shard, other)):
        _, begin = geometry(lens, 0, side, block // 2, block)
        out[...] = dot_nn((selection(begin, block // 2, block) * here).astype(bf16), copy()).astype(bf16)


def turned_block(lens, blocks):
    _, block, model = blocks.shape
    scratch = [pltpu.VMEM((block, model), bf16), pltpu.SemaphoreType.DMA((1,))]
    shapes = [like((block // 2, model), bf16)] * 2
    return on_device(
        turned_body, shapes, [], 2 * block * block * model, (lens,), far=[distant(blocks)], scratch=scratch
    )


def opening_body(lens, gain, tokens, *refs):
    wq, wk, wv, wo, inputs, part, qkv, heads, sent, qkv_other, heads_other, mask, *scratch, sems = refs
    copies = Copies(sems)
    sources = [tokens.at[0], wq, wk, wv, wo]
    block_rows, *weights = [copies.fetch(a, b) for a, b in zip(sources, scratch)]
    block = tokens.shape[1]
    rows = block // 2
    shard = lax.axis_index("shard")
    first = jnp.where(lax.axis_index("section") == 0, 1.0, 0.0)
    for own in (False, True):
        to_qkv, to_heads = (qkv, heads) if own else (qkv_other, heads_other)
        ends, begin = geometry(lens, 0, shard if own else 1 - shard, rows, block)
        pick = selection(begin, rows, block)
        values = dot_nn((pick * first).astype(bf16), block_rows())
        allowed = sequence_mask(ends, begin, rows, block)
        value = head_group(normed_rows(values, gain[...]), allowed, weights, to_qkv, to_heads)
        if own:
            inputs[...] = values.astype(bf16)
            part[...] = values + value
            mask[...] = allowed
        else:
            sent[...] = value.astype(bf16)


def opening(lens, tokens, gain, weights):
    _, block, model = tokens.shape
    rows = block // 2
    width, out = sum(w.shape[1] for w in weights[:3]), weights[3].shape[1]
    shapes = [
        like((rows, model), bf16), like((rows, model), f32), like((rows, width), bf16), like((rows, out), bf16),
        like((rows, model), bf16), like((rows, width), bf16), like((rows, out), bf16), like((rows, rows), f32),
    ]
    scratch = [pltpu.VMEM((block, model), bf16), *holders(*weights)]
    outs = on_device(
        opening_body, shapes, [gain], 4 * rows * model * (width + out), (lens,), far=[distant(t) for t in (tokens, *weights)], scratch=scratch
    )
    return outs[:5], outs[7]


def settle_body(lens, routes0, gates0, routes1, gates1, tokens, grad, *refs):
    fresh, cot, mask, extra0, extra1, starts, token_rows, grad_rows, sems = refs
    copies = Copies(sems)
    for micro in range(2):
        _, starts[micro] = geometry(lens, micro, 0, tokens.shape[1] // 2, tokens.shape[1])
    token_rows = copies.fetch(tokens.at[1], token_rows)
    grad_rows = copies.fetch(grad.at[1], grad_rows)
    block = tokens.shape[1]
    rows = block // 2
    first = jnp.where(lax.axis_index("section") == 0, 1.0, 0.0)
    for micro, routes, gates, extra in ((0, routes0, gates0, extra0), (1, routes1, gates1, extra1)):
        ends, begin = geometry(lens, micro, lax.axis_index("shard"), rows, block)
        pick = selection(begin, rows, block)
        extra[...] = gate_columns(pick.astype(bf16), routes[...], gates[...])
    fresh[...] = dot_nn((pick * first).astype(bf16), token_rows()).astype(bf16)
    cot[...] = dot_nn((pick * (1.0 - first)).astype(bf16), grad_rows()).astype(bf16)
    mask[...] = sequence_mask(ends, begin, rows, block)


def settle(lens, tokens, grad, routes, gates):
    _, block, model = tokens.shape
    rows = block // 2
    shapes = [like((rows, model), bf16)] * 2 + [like((rows, rows), f32)] + [like((rows, 128), bf16)] * 2
    shapes.append(pltpu.SMEM((2,), jnp.int32))
    args = [routes[0], gates[0], routes[1], gates[1]]
    scratch = [pltpu.VMEM((block, model), bf16)] * 2 + [pltpu.SemaphoreType.DMA((2,))]
    return on_device(
        settle_body, shapes, args, 2 * block * block * model, (lens,), far=[distant(tokens), distant(grad)], scratch=scratch
    )


def joined_body(part, other, extra, gain, hidden, payload):
    total = part[...] + wide(other[...])
    hidden[...] = total
    model = total.shape[1]
    payload[:, :model] = normed_rows(total, gain[...])
    payload[:, model:] = extra[...]


def joined(part, other, gain, extra):
    rows, model = part.shape
    shapes = [like((rows, model), f32), like((rows, model + extra.shape[1]), bf16)]
    return on_device(joined_body, shapes, [part, other, extra, gain], 10 * rows * model)


def by_halves(refs):
    *own, packed = refs
    widths = [w.shape[1] for w in own]
    firsts = [sum(widths[:i]) for i in range(4)]
    other = [lambda f=f, w=w: packed[:, f : f + w] for f, w in zip(firsts, widths)]
    return [lambda w=w: w[...] for w in own], other


def other_heads_body(inputs, mask, gain, wq, wk, wv, wo, packed, qkv, heads):
    _, weights = by_halves((wq, wk, wv, wo, packed))
    head_group(normed_rows(wide(inputs[...]), gain[...]), mask[...], weights, qkv, heads)


def other_heads(inputs, mask, gain, weights, packed):
    rows = inputs.shape[0]
    width, out = sum(w.shape[1] for w in weights[:3]), weights[3].shape[1]
    shapes = [like((rows, width), bf16), like((rows, out), bf16)]
    return on_device(
        other_heads_body, shapes, [inputs, mask, gain], 2 * rows * packed.size, kept=[*weights, packed]
    )


def attention_body(fresh, arriving, mask, extra, gain, gain_two, *refs):
    own, other = by_halves(refs[:5])
    inputs, hidden, payload, qkv0, qkv1, heads0, heads1 = refs[5:]
    rows = fresh[...] + arriving[...]
    inputs[...] = rows
    total = wide(rows)
    normed = normed_rows(total, gain[...])
    total = total + head_group(normed, mask[...], own, qkv0, heads0)
    total = total + head_group(normed, mask[...], other, qkv1, heads1)
    hidden[...] = total
    model = total.shape[1]
    payload[:, :model] = normed_rows(total, gain_two[...])
    payload[:, model:] = extra[...]


def attention_forward(fresh, arriving, mask, gain, gain_two, extra, weights, packed):
    rows, model = fresh.shape
    width, out = sum(w.shape[1] for w in weights[:3]), weights[3].shape[1]
    shapes = [
        like((rows, model), bf16), like((rows, model), f32), like((rows, model + extra.shape[1]), bf16),
        like((rows, width), bf16), like((rows, width), bf16), like((rows, out), bf16), like((rows, out), bf16),
    ]
    args = [fresh, arriving, mask, extra, gain, gain_two]
    outs = on_device(attention_body, shapes, args, 4 * rows * packed.size, kept=[*weights, packed])
    inputs, hidden, payload, qkv0, qkv1, heads0, heads1 = outs
    return inputs, hidden, payload, [(qkv0, heads0), (qkv1, heads1)]


def attention_back_body(grad, grad_two, inputs, hidden, mask, q0, q1, gain, gain_two, *refs):
    own, other = by_halves(refs[:5])
    grad_input, grad_input_low, grad_low, normed, g0, g1, gain_grad, gain_two_grad = refs[5:]
    rows = inputs.shape[0]
    values = wide(inputs[...])
    normed[...] = normed_rows(values, gain[...])
    total = hidden[...]
    back, gain_two_grad[...] = norm_back(total, norm_factor(total), gain_two[...], grad_two[...])
    grad_hidden = wide(grad[...]) + back
    low = grad_hidden.astype(bf16)
    grad_low[...] = low
    grad_normed = jnp.zeros_like(grad_hidden)
    for qkv, weights, grad_qkv in ((q0, own, g0), (q1, other, g1)):
        query, key, value, probs = group_probs(qkv[...], mask[...])
        grad_heads = stack_heads(dot_nn(low, weights[3]()).astype(bf16))
        grad_probs = dot_nt(grad_heads, value)
        inner = jnp.sum(probs * grad_probs, axis=1, keepdims=True)
        grad_scores = (probs * (grad_probs - inner) * HEAD_SIZE ** (-0.5)).astype(bf16)
        grads = [
            spread_heads(dot_nn(grad_scores, key).astype(bf16), rows),
            dot_tn(grad_scores, query).astype(bf16),
            dot_tn(probs.astype(bf16), grad_heads).astype(bf16),
        ]
        at = 0
        for part, w in zip(grads, weights):
            grad_qkv[:, at : at + part.shape[1]] = part
            at += part.shape[1]
            grad_normed = grad_normed + dot_nt(part, w())
    back, gain_grad[...] = norm_back(values, norm_factor(values), gain[...], grad_normed)
    result = grad_hidden + back
    grad_input[...] = result
    grad_input_low[...] = result.astype(bf16)


def attention_backward(grad, grad_two, inputs, hidden, mask, gain, gain_two, projected, weights, packed):
    rows, model = inputs.shape
    width = projected[0].shape[1]
    shapes = [
        like((rows, model), f32), like((rows, model), bf16), like((rows, model), bf16),
        like((rows, model), bf16), like((rows, width), bf16), like((rows, width), bf16),
        like((1, model), f32), like((1, model), f32),
    ]
    args = [grad, grad_two, inputs, hidden, mask, *projected, gain, gain_two]
    return on_device(attention_back_body, shapes, args, 8 * rows * packed.size, kept=[*weights, packed])


def ranges(pieces):
    pairs = [p if isinstance(p, tuple) else (p, (0, p.shape[0])) for p in pieces]
    return [p for p, _ in pairs], [r for _, r in pairs]


def place(copies, pieces, spans, *targets):
    halves_of, at = ([], []), 0
    for piece, (lo, hi) in zip(pieces, spans):
        first, count = 0, hi - lo
        for target in targets:
            source = piece.at[pl.ds(lo, count), pl.ds(first, target.shape[1])]
            copy = copies.start(source, target.at[pl.ds(at, count), :])
            halves_of[2 * at // targets[0].shape[0]].append(copy)
            first += target.shape[1]
        at += count
    return halves_of


def own_gate(extra):
    me, peers = lax.axis_index("dp"), lax.axis_size("dp")
    lane = lax.broadcasted_iota(jnp.int32, extra.shape, 1)
    return jnp.sum(jnp.where((lane == me) | (lane == me + peers), wide(extra), 0.0), axis=1, keepdims=True)


def expert_stage_body(spans, *refs):
    pieces = len(spans)
    (w_gate, w_up, w_down), ins = refs[:3], refs[3 : pieces + 3]
    rows_out, extra_out, gate_out, up_out, *part_outs = refs[pieces + 3 : pieces + 9]
    rows, extra, gate_held, up_held, part, sems = refs[pieces + 9 :]
    copies, leaving = Copies(sems), []
    arriving = place(copies, ins, spans, rows, extra)
    half = rows.shape[0] // 2
    for i, part_out in enumerate(part_outs):
        here = pl.ds(i * half, half)
        for copy in arriving[i]:
            copy.wait()
        leaving.append(copies.start(rows.at[here, :], rows_out.at[here, :]))
        leaving.append(copies.start(extra.at[here, :], extra_out.at[here, :]))
        values = rows[here, :]
        gate = dot_nn(values, w_gate[...])
        up = dot_nn(values, w_up[...])
        gate_held[here, :] = gate.astype(bf16)
        up_held[here, :] = up.astype(bf16)
        leaving.append(copies.start(gate_held.at[here, :], gate_out.at[here, :]))
        leaving.append(copies.start(up_held.at[here, :], up_out.at[here, :]))
        act = (gate / (1.0 + jnp.exp(-gate)) * up).astype(bf16)
        part[here, :] = (own_gate(extra[here, :]) * dot_nn(act, w_down[...])).astype(bf16)
        leaving.append(copies.start(part.at[here, :], part_out))
    for copy in leaving:
        copy.wait()


def expert_stage(pieces, *weights):
    pieces, spans = ranges(pieces)
    count = sum(hi - lo for lo, hi in spans)
    model, units = weights[0].shape
    extra = pieces[0].shape[1] - model
    saved = [(count, model), (count, extra), (count, units), (count, units)]
    shapes = [like(t, bf16) for t in [*saved, (count // 2, model), (count // 2, model)]]
    scratch = [pltpu.VMEM(t, bf16) for t in [*saved, (count, model)]]
    scratch.append(pltpu.SemaphoreType.DMA((2 * len(pieces) + 10,)))
    body = functools.partial(expert_stage_body, spans)
    outs = on_device(
        body, shapes, [], 6 * count * weights[0].size, kept=weights, far=pieces, scratch=scratch, direct=True
    )
    return outs[4:], outs[:4]


def expert_back_body(spans, *refs):
    pieces = len(spans)
    (w_gate, w_up, w_down), ins, (extra_in, gate_in, up_in) = refs[:3], refs[3 : pieces + 3], refs[pieces + 3 : pieces + 6]
    outs = refs[pieces + 6 : pieces + 12]
    *held_back, part, extra, gate_held, up_held, sems = refs[pieces + 12 :]
    grad_rows, grad_gate, grad_up, act = held_back
    copies, leaving = Copies(sems), []
    half = grad_rows.shape[0] // 2
    arriving = [[], []]
    for i in range(2):
        here = pl.ds(i * half, half)
        for source, target in ((extra_in, extra), (gate_in, gate_held), (up_in, up_held)):
            arriving[i].append(copies.start(source.at[here, :], target.at[here, :]))
    for i, more in enumerate(place(copies, ins, spans, grad_rows)):
        arriving[i] += more
    for i, part_out in enumerate(outs[4:]):
        here = pl.ds(i * half, half)
        for copy in arriving[i]:
            copy.wait()
        scaled = (own_gate(extra[here, :]) * wide(grad_rows[here, :])).astype(bf16)
        grad_rows[here, :] = scaled
        grad_act = dot_nt(scaled, w_down[...])
        gate, up = wide(gate_held[here, :]), wide(up_held[here, :])
        sig = 1.0 / (1.0 + jnp.exp(-gate))
        silu = gate * sig
        low_gate = (grad_act * up * sig * (1.0 + gate * (1.0 - sig))).astype(bf16)
        low_up = (grad_act * silu).astype(bf16)
        grad_gate[here, :] = low_gate
        grad_up[here, :] = low_up
        act[here, :] = (silu * up).astype(bf16)
        for source, target in zip(held_back, outs):
            leaving.append(copies.start(source.at[here, :], target.at[here, :]))
        grad_in = dot_nt(low_gate, w_gate[...]) + dot_nt(low_up, w_up[...])
        part[here, :] = grad_in.astype(bf16)
        leaving.append(copies.start(part.at[here, :], part_out))
    for copy in leaving:
        copy.wait()


def expert_back_stage(pieces, saved, *weights):
    rows, extra, gate_out, up_out = saved
    pieces, spans = ranges(pieces)
    count = rows.shape[0]
    model, units = weights[0].shape
    back = [(count, model), (count, units), (count, units), (count, units)]
    shapes = [like(t, bf16) for t in [*back, (count // 2, model), (count // 2, model)]]
    scratch = [pltpu.VMEM(t, bf16) for t in [*back, (count, model), extra.shape, gate_out.shape, up_out.shape]]
    scratch.append(pltpu.SemaphoreType.DMA((len(pieces) + 16,)))
    body = functools.partial(expert_back_body, spans)
    far = [*pieces, *map(distant, (extra, gate_out, up_out))]
    outs = on_device(
        body, shapes, [], 6 * count * weights[0].size, kept=weights, far=far, scratch=scratch, direct=True
    )
    return outs[4:], outs[:4]


def product_sums_body(stages, products, *refs):
    ins, outs = refs[: -len(products)], refs[-len(products) :]
    fields = 1 + max(max(p) for p in products)
    totals = [ref[...] for ref in ins[fields * stages :]] or [0.0] * len(products)
    for i in range(stages):
        stage = [r[...] for r in ins[fields * i : fields * (i + 1)]]
        totals = [t + dot_tn(stage[a], stage[b]) for t, (a, b) in zip(totals, products)]
    for out, total in zip(outs, totals):
        out[...] = total


def product_sums(stages, products, swept, sums):
    width = stages[0][swept].shape[1]
    step = min(t.shape[1] for t in stages[0])
    rows = sum(stage[0].shape[0] for stage in stages)
    args, specs = [], []
    for stage in stages:
        args += map(distant, stage)
        for i, t in enumerate(stage):
            if i == swept:
                specs.append(pl.BlockSpec((t.shape[0], step), lambda j: (0, j)))
            else:
                specs.append(pl.BlockSpec(t.shape, lambda j: (0, 0)))
    shapes, outs = [], []
    for left, right in products:
        other = stages[0][right if left == swept else left].shape[1]
        if left == swept:
            shapes.append(like((width, other), f32))
            outs.append(pl.BlockSpec((step, other), lambda j: (j, 0)))
        else:
            shapes.append(like((other, width), f32))
            outs.append(pl.BlockSpec((other, step), lambda j: (0, j)))
    model_work = width * step // 32
    first = len(args)
    if sums is not None:
        args += map(distant, sums)
        specs += outs
    return pl.pallas_call(
        functools.partial(product_sums_body, len(stages), products),
        grid=(width // step,),
        out_shape=shapes,
        in_specs=specs,
        out_specs=outs,
        input_output_aliases={} if sums is None else {first + i: i for i in range(len(shapes))},
        compiler_params=pltpu.CompilerParams(vmem_limit_bytes=KERNEL_VMEM),
        cost_estimate=pl.CostEstimate(flops=rows * model_work, bytes_accessed=rows, transcendentals=0),
    )(*args)


def expert_forward(rows, w_gate, w_up, w_down):
    gate_out = dot_nn(rows, w_gate)
    up_out = dot_nn(rows, w_up)
    act = (gate_out / (1.0 + jnp.exp(-gate_out)) * up_out).astype(bf16)
    part = dot_nn(act, w_down).astype(bf16)
    return part, (rows, gate_out.astype(bf16), up_out.astype(bf16))


def expert_backward(grad_rows, saved, w_gate, w_up, w_down):
    rows, gate_low, up_low = saved
    gate_out, up_out = wide(gate_low), wide(up_low)
    grad_act = dot_nt(grad_rows, w_down)
    sig = 1.0 / (1.0 + jnp.exp(-gate_out))
    silu = gate_out * sig
    grad_gate = (grad_act * up_out * sig * (1.0 + gate_out * (1.0 - sig))).astype(bf16)
    grad_up = (grad_act * silu).astype(bf16)
    act = (silu * up_out).astype(bf16)
    grad_in = (dot_nt(grad_gate, w_gate) + dot_nt(grad_up, w_up)).astype(bf16)
    return grad_in, (dot_tn(rows, grad_gate), dot_tn(rows, grad_up), dot_tn(act, grad_rows))


def halves(array):
    half = array.shape[0] // 2
    return array[:half], array[half:]


def owned_body(turns, groups, blocks, with_last, gains, *refs):
    refs = list(refs)
    lefts = [refs.pop(0) for _ in range(turns)]
    rights = [[refs.pop(0) for _ in range(turns + with_last)] for _ in range(groups)]
    last = [refs.pop(0) for _ in range(4 * with_last)]
    gains = [refs.pop(0)[...] for _ in range(gains)]
    outs, products, sems = refs[: 2 * len(blocks)], refs[-2], refs[-1]
    values = [t[...] for t in lefts]
    if with_last:
        grad, grad_two, hidden, gain = last
        total = hidden[...]
        back, _ = norm_back(total, norm_factor(total), gain[...], grad_two[...])
        values.append((wide(grad[...]) + back).astype(bf16))
    left = jnp.concatenate(values, axis=0)
    for g in range(groups):
        right = jnp.concatenate([t[...] for t in rights[g]], axis=0)
        products[g, :, : right.shape[1]] = dot_tn(left, right).astype(bf16)
        if gains:
            terms, at = [], right.shape[1]
            for gain in gains:
                high = gain.astype(bf16)
                terms += [high, (gain - wide(high)).astype(bf16)]
            rows = jnp.concatenate(terms + [jnp.zeros_like(terms[0])] * (-len(terms) % 16), axis=0)
            which = lax.broadcasted_iota(jnp.int32, (rows.shape[0], 128), 0)
            column = lax.broadcasted_iota(jnp.int32, (rows.shape[0], 128), 1)
            chosen = (column == (which // 2) % 2) & (which < len(terms))
            products[g, :, at : at + 128] = dot_tn(rows, jnp.where(chosen, 1.0, 0.0).astype(bf16)).astype(bf16)
    copies, leaving = Copies(sems), []
    me = lax.axis_index("dp")
    share = products.shape[1] // lax.axis_size("dp")
    for i, group in enumerate(blocks):
        for out, places in zip(outs[2 * i : 2 * i + 2], group):
            for j, (mask, side) in enumerate(places):
                rows = pl.ds(pl.multiple_of((me ^ mask) * share, share), share)
                leaving.append(copies.start(products.at[side, rows, :], out.at[pl.ds(j * share, share), :]))
    for copy in leaving:
        copy.wait()


def owned_products(cube, lefts, rights, last=(), gains=()):
    model, width = lefts[0].shape[1], rights[0][0].shape[1] + (128 if gains else 0)
    share = model // lax.axis_size("dp")
    blocks = [
        [[(m ^ int(i), s) for m, s in side for i in cube.inner] for side in pair] for pair in cube.stages
    ]
    shapes = [like((len(places) * share, width), bf16) for pair in blocks for places in pair]
    scratch = [
        pltpu.VMEM((len(rights), model, width), bf16),
        pltpu.SemaphoreType.DMA((sum(len(places) for pair in blocks for places in pair),)),
    ]
    args = [*lefts, *[t for group in rights for t in group], *last, *gains]
    outs = pl.pallas_call(
        functools.partial(owned_body, len(lefts), len(rights), blocks, 1 if last else 0, len(gains)),
        out_shape=shapes,
        in_specs=[VMEM] * len(args),
        out_specs=[ANY] * len(shapes),
        scratch_shapes=scratch,
        compiler_params=pltpu.CompilerParams(vmem_limit_bytes=KERNEL_VMEM),
    )(*map(distant, args))
    return [(outs[2 * i], outs[2 * i + 1]) for i in range(len(blocks))]


class Blocks:
    def __init__(self, cube, weights):
        self.cube, self.weights = cube, weights

    def forward(self, payload, micro, side=()):
        saved = [None] * 4

        def work(stage, pieces):
            parts, kept = expert_stage(pieces, *self.weights)
            saved[stage] = kept
            return parts

        return gather_rows(self.cube, payload, work, side), saved

    def back_stage(self, stage, pieces, saved):
        parts, kept = expert_back_stage(pieces, saved[stage], *self.weights)
        return parts, [saved[stage][0], *kept]

    def backward(self, grad, micro, saved, side=()):
        keeps = [None] * 4

        def work(stage, pieces):
            parts, kept = self.back_stage(stage, pieces, saved)
            keeps[stage] = kept
            return parts

        return gather_rows(self.cube, grad, work, side), keeps

    def late_backward(self, pieces, saved):
        parts, keeps = [None] * 4, [None] * 4

        def run(*stages):
            def work(*gathered):
                for stage, rows in zip(stages, gathered):
                    parts[stage], keeps[stage] = self.back_stage(stage, rows, saved)
                return [parts[stage] for stage in stages]

            return lambda: [pieces[stage] for stage in stages], work

        return run, parts, keeps

    def total_start(self, results, side=()):
        return reduce_start(self.cube, results, side)

    def total_finish(self, state, side=()):
        return reduce_finish(self.cube, state, side)

    def total(self, results, side=()):
        return self.total_finish(self.total_start(results, side[:1]), side[1:])

    def weight_sums(self, keeps, sums):
        def hidden(*stages):
            sums[0] = product_sums(stages, ((0, 1), (0, 2)), 0, sums[0])
            return sums[0]

        def back(*stages):
            sums[1] = product_sums(stages, ((0, 1),), 1, sums[1])
            return sums[1]

        return [
            (lambda: [[rows, gate, up] for rows, _, gate, up, _ in keeps], hidden),
            (lambda: [[act, grad] for _, grad, _, _, act in keeps], back),
        ]


def run_all(side):
    for thunk in side:
        if thunk is not None:
            thunk[1](*thunk[0]())


class Buckets:
    def __init__(self, cube, weights, routes, gates, capacity):
        self.cube, self.weights, self.capacity = cube, weights, capacity
        micros, self.rows, self.top = routes.shape
        self.experts = lax.axis_size("dp")
        self.tables = []
        for m in range(micros):
            flat = routes[m].reshape(-1)
            onehot = (flat[:, None] == jnp.arange(self.experts, dtype=jnp.int32)).astype(jnp.int32)
            earlier = jnp.cumsum(onehot, axis=0) - onehot
            target = flat * capacity + jnp.sum(earlier * onehot, axis=1)
            source = jnp.full((self.experts * capacity,), flat.shape[0], jnp.int32)
            source = source.at[target].set(jnp.arange(flat.shape[0], dtype=jnp.int32))
            self.tables.append((target, source, gates[m]))

    def table(self, micro):
        return jax.tree.map(lambda a, b: jnp.where(micro == 0, a, b), self.tables[0], self.tables[1])

    def exchange(self, rows):
        shape = (self.experts, self.capacity, rows.shape[1])
        moved = lax.all_to_all(rows.reshape(shape), "dp", split_axis=0, concat_axis=0, tiled=True)
        return moved.reshape(rows.shape)

    def whole(self, own):
        return jnp.concatenate([own, swap(own, self.cube.z)], axis=0)

    def forward(self, payload, micro, side=()):
        target, source, gates = self.table(micro)
        own = payload[:, : self.weights[0].shape[0]]
        padded = jnp.pad(self.whole(own), ((0, 1), (0, 0)))
        arrived = self.exchange(jnp.take(padded, source // self.top, axis=0))
        part, saved = expert_forward(arrived, *self.weights)
        picked = jnp.take(self.exchange(part), target, axis=0).reshape(self.rows, self.top, -1)
        run_all(side)
        return jnp.sum(gates[:, :, None] * picked, axis=1), saved

    def backward(self, grad, micro, saved, side=()):
        target, source, gates = self.table(micro)
        scaled = (gates[:, :, None] * wide(self.whole(grad))[:, None, :]).astype(bf16)
        padded = jnp.pad(scaled.reshape(self.rows * self.top, -1), ((0, 1), (0, 0)))
        arrived = self.exchange(jnp.take(padded, source, axis=0))
        grad_in, weights = expert_backward(arrived, saved, *self.weights)
        picked = jnp.take(self.exchange(grad_in), target, axis=0).reshape(self.rows, self.top, -1)
        run_all(side)
        return jnp.sum(picked, axis=1, dtype=f32), weights

    def total_start(self, results, side=()):
        run_all(side)
        return results

    def total_finish(self, results, side=()):
        own, other = halves(results.astype(bf16))
        run_all(side)
        return wide(own) + wide(swap(other, self.cube.z))

    def total(self, results, side=()):
        return self.total_finish(results, side)

    def weight_sums(self, weights, sums):
        def add(*weights):
            for i, part in enumerate((list(weights[:2]), list(weights[2:]))):
                sums[i] = part if sums[i] is None else [a + b for a, b in zip(sums[i], part)]

        return [None, (lambda: weights, add)]


def local(
    tokens, lengths, routes, gates, attn_gain, q_weight, key_projection, value_projection,
    o_weight, mlp_gain, expert_gate, expert_up, expert_down, cotangent,
):
    cube = Cube()
    section = lax.axis_index("section")
    shard = lax.axis_index("shard")
    me = lax.axis_index("dp")
    peers, shards = lax.axis_size("dp"), lax.axis_size("shard")
    _, block_rows, model = tokens.shape
    rows = block_rows // shards
    share = model // peers
    first = section == 0
    gain_one, gain_two = attn_gain[0][None], mlp_gain[0][None]
    weights = [q_weight[0], key_projection[0], value_projection[0], o_weight[0]]
    expert_w = (expert_gate[0, 0], expert_up[0, 0], expert_down[0, 0])
    capacity = 2 * block_rows * routes.shape[3] // peers
    whole_blocks = capacity >= block_rows

    def chosen(here, there):
        return jax.tree.map(lambda a, b: jnp.where(first, a, b), here, there)

    def begins(lens):
        lens = lens[:, 0]
        ends, longest = jnp.cumsum(lens, axis=1), jnp.argmax(lens, axis=1)
        return [ends[m, longest[m]] - lens[m, longest[m]] for m in range(2)]

    def turned(array, begin):
        doubled = jnp.concatenate([array, array], axis=0)
        return lax.dynamic_slice_in_dim(doubled, (begin + rows * shard) % block_rows, block_rows, 0)

    if not whole_blocks:
        early = begins(lengths)
        mixture = Buckets(
            cube,
            expert_w,
            jnp.stack([turned(routes[0, m], early[m]) for m in range(2)]),
            jnp.stack([turned(gates[0, m], early[m]) for m in range(2)]),
            capacity,
        )

    slices = [lax.dynamic_slice_in_dim(w, me * share, share, 0) for w in weights]
    qkv_slices = swap(jnp.concatenate(slices[:3], axis=1), cube.z)
    out_slices = slices[3]
    half_share = share // 2
    mask = cube.x[1] | cube.y[1]
    far_places = [2 * (me ^ mask), 2 * (me ^ mask) + 1]
    plane_places = [2 * (me ^ m) for m in (0, cube.x[1], cube.y[1])]
    mate_bit = cube.core[1]

    def mate_places(places):
        return [p ^ (2 * mate_bit) for p in places]

    def placed(own, m):
        half = model // shards
        kept = lax.dynamic_slice_in_dim(own, shard * half, half, 1)
        given = lax.dynamic_slice_in_dim(own, (1 - shard) * half, half, 1)
        got = swap(given, cube.z)
        low = jnp.where(shard == 0, kept, got)
        high = jnp.where(shard == 0, got, kept)
        return lax.dynamic_slice_in_dim(
            jnp.concatenate([low, high, low, high], axis=0), (block_rows - starts[m]) % block_rows, block_rows, 0
        )

    route_cols = [routes[0, m].T for m in range(2)]
    gate_cols = [gates[0, m].T for m in range(2)]
    cot_own, cot_other = turned_block(lengths, cotangent)
    opened, mask0 = opening(lengths, tokens, gain_one, weights)
    settled = [tokens, cotangent, route_cols, gate_cols, expert_w]
    own_near = [swap(cot_own, d) for d in (cube.x, cube.y)] if whole_blocks else []
    opened, own_near, qkv_slices, cot_other, settled = together(
        (opened, own_near, qkv_slices, cot_other, settled)
    )
    inputs, part, qkv, heads, sent = opened
    *settled, expert_w = settled
    other_near = [swap(cot_other, d) for d in (cube.x, cube.y)] if whole_blocks else []
    arrived, other_near, settled, expert_w = together(
        (swap(sent, cube.z), other_near, settle(lengths, *settled), pinned(*expert_w))
    )
    fresh1, cot1, mask1, extra0, extra1, starts = settled
    hidden, payload = joined(part, arrived, gain_two, extra0)
    if whole_blocks:
        mixture = Blocks(cube, expert_w)
        plane = []

        def first_plane(qkv_slices, out_slices):
            near = [qkv_slices] + [swap(qkv_slices, d) for d in (cube.x, cube.y, ("dp", mask))]
            plane.extend([near, swap(out_slices, cube.z)])
            return plane

        side = [None, None, (lambda: [qkv_slices, out_slices], first_plane)]
        results, saved = mixture.forward(payload, 0, side)
        qkv_near, out_slices = plane
    else:
        results, saved = mixture.forward(payload, 0)
    first_mates = []

    def first_exchange(*near):
        first_mates.extend(swap(t, cube.core) for t in near)
        return first_mates

    total = mixture.total(results, [(lambda: qkv_near, first_exchange)] if whole_blocks else [])
    result0 = (hidden + total).astype(bf16)
    if whole_blocks:
        result0, qkv_near, out_slices = together((result0, qkv_near, out_slices))
        arriving = lax.ppermute(result0, "section", [(0, 1)])
        out_near = [out_slices] + [swap(out_slices, d) for d in (cube.x, cube.y, ("dp", mask))]
        arriving, out_near, weights = together((arriving, out_near, pinned(*weights)))
        qkv_mates, out_mates = first_mates, [swap(t, cube.core) for t in out_near]
        all_places = [*plane_places, far_places[0]]
        width = qkv_slices.shape[1]
        spans, pieces = [], []
        for group, places, column in (
            (qkv_near, all_places, 0), (qkv_mates, mate_places(all_places), 0),
            (out_near, all_places, width), (out_mates, mate_places(all_places), width),
        ):
            pieces += group
            spans += [(p, half_share, column) for p in places]
        packed = put_together(pieces, spans, (model, width + out_slices.shape[1]))
    else:
        arriving = lax.ppermute(result0, "section", [(0, 1)])
        packed = lax.all_gather(
            jnp.concatenate([qkv_slices, swap(out_slices, cube.z)], axis=1), "dp", axis=0, tiled=True
        )
    state0 = [inputs, hidden, mask0, None, saved]

    mask_mid, extra_mid = chosen((mask1, extra1), (mask0, extra0))

    inputs1, hidden1, payload, groups1 = attention_forward(
        fresh1, arriving, mask_mid, gain_one, gain_two, extra_mid, weights, packed
    )
    def first_groups(*args):
        groups = other_heads(*args)
        state0[3] = [(qkv, heads), tuple(groups)]
        return groups

    micro_mid = 1 - section
    late = []

    def cot_mates(*cots):
        late.append([swap(t, cube.core) for t in cots])
        return late[0]

    def cot_far(x0, y1):
        late.append([swap(x0, cube.y), swap(y1, cube.x)])
        return late[1]

    side = [(lambda: [inputs, mask0, gain_one, weights, packed], first_groups)]
    if whole_blocks:
        (x0, y0), (x1, y1) = own_near, other_near
        side += [(lambda: [cot_own, cot_other, x0, y0, x1, y1], cot_mates), (lambda: [x0, y1], cot_far)]
    results, saved1 = mixture.forward(payload, micro_mid, side)

    grad0 = cot_own
    if whole_blocks:
        (own_c, other_c, x0_c, y0_c, x1_c, y1_c), far = late
        far_c = [swap(t, cube.core) for t in far]
        pieces = [
            [cot_own, own_c],
            [x0, y0, cot_other, x0_c, y0_c, other_c],
            [far[0], y1, x1, far_c[0], y1_c, x1_c],
            [far[1], far_c[1]],
        ]
        run, back_results, keeps0 = mixture.late_backward(pieces, saved1)

        def exchange(*others):
            back_results[2] = (back_results[2][0], swap(others[0], cube.core))
            return back_results[2]

        total = mixture.total(results, [run(2), both((lambda: [back_results[2][1]], exchange), run(3, 1, 0))])
    else:
        back_results, keeps0 = mixture.backward(grad0, micro_mid, saved1)
        total = mixture.total(results)
    result1 = (hidden1 + total).astype(bf16)

    slot2 = []

    def last_attention(arriving):
        zero = jnp.zeros((rows, model), bf16)
        slot2.extend(
            attention_forward(zero, arriving, mask1, gain_one, gain_two, extra1, weights, packed)
        )
        return slot2

    arrived = []

    def second_handoff(result):
        arrived.append(lax.ppermute(result, "section", [(0, 1)]))
        return arrived

    result1, back_results = together((result1, back_results))
    if whole_blocks:
        back_results[0] = (back_results[0][0], swap(back_results[0][1], cube.core))
    state = mixture.total_start(back_results, [(lambda: [result1], second_handoff)])
    grad_two = mixture.total_finish(state, [(lambda: arrived, last_attention)])
    inputs2, hidden2, payload, groups2 = slot2

    def attention_turn(grad, grad_two, state):
        inputs, hidden, mask, groups, _ = state
        outs = attention_backward(
            grad, grad_two, inputs, hidden, mask, gain_one, gain_two, [g[0] for g in groups], weights, packed
        )
        grad_input, low, grad_low, normed, g0, g1, attn_g, mlp_g = outs
        factors = (normed, grad_low, (g0, g1), [g[1] for g in groups])
        return grad_input, low, factors, (attn_g, mlp_g)

    state1 = [inputs1, hidden1, mask_mid, groups1, saved1]
    turn0, returned = [], []

    def first_turn(grad_two):
        turn0.extend(attention_turn(grad0, grad_two, state1))
        return turn0

    def first_return(low):
        returned.append(lax.ppermute(low, "section", [(1, 0)]))
        return returned

    side = [(lambda: [grad_two], first_turn), None, (lambda: [turn0[1]], first_return)]
    results2, saved2 = mixture.forward(payload, 1, side)
    coming = returned[0]
    state2 = [inputs2, hidden2, mask1, groups2, saved2]

    sums = [None, None]
    coming, results2, saved2 = together((coming, results2, saved2))
    state2[4] = saved2
    grad1 = coming + cot1
    state_mid = chosen(state0, state2)
    back_results, keeps1 = mixture.backward(grad1, section, state_mid[4])
    placings = {}

    def placing(name, micro, own):
        def work(rows):
            placings[name, micro] = placed(rows, micro)
            return placings[name, micro]

        return lambda: [own()], work

    work0 = mixture.weight_sums(keeps0, sums)
    work0[0] = both(*[w for w in work0[:1] if w], placing("out", 0, lambda: chosen(result0, result1)))
    grad_two = mixture.total(back_results, work0)
    turn1 = attention_turn(grad1, grad_two, state_mid)
    low, results2 = together((turn1[1], results2))
    coming = lax.ppermute(low, "section", [(1, 0)])
    state = mixture.total_start(results2)
    grad2, state = together((coming, state))

    last_total = []

    def finish_last(*state):
        last_total.append(mixture.total_finish(state[0] if len(state) == 1 else state))
        return last_total

    side = [None, None, (lambda: [state] if not whole_blocks else list(state), finish_last)]
    side.append(placing("grad", 0, lambda: chosen(turn1[0], turn0[0])))
    back_results, keeps2 = mixture.backward(grad2, 1 - section, saved1, side)
    result2 = (hidden2 + last_total[0]).astype(bf16)
    work1 = mixture.weight_sums(keeps1, sums)
    work1[0] = both(*[w for w in work1[:1] if w], placing("out", 1, lambda: chosen(result1, result2)))
    grad_two = mixture.total(back_results, work1)

    inputs, hidden, _, groups, _ = state1
    heads_all = [[t[2][3][g] for t in (turn0, turn1)] + [groups[g][1]] for g in range(shards)]
    out_pairs = owned_products(cube, [turn0[2][1], turn1[2][1]], heads_all, (grad2, grad_two, hidden, gain_two))
    turn2 = []

    def last_turn(grad_two):
        turn2.extend(attention_turn(grad2, grad_two, state1))
        return turn2

    def exchanged(pairs):
        return [(mine, swap(other, cube.core)) if i in (0, 2) else (mine, other) for i, (mine, other) in enumerate(pairs)]

    out_state = reduce_start(cube, exchanged(out_pairs), [(lambda: [grad_two], last_turn)])
    turns = (turn0, turn1, turn2)
    factors = [t[2] for t in turns]
    qkv_pairs = []

    def qkv_products(*_):
        rights = [[f[2][g] for f in factors] for g in range(shards)]
        gains = [g for t in turns for g in t[3]]
        qkv_pairs.extend(owned_products(cube, [f[0] for f in factors], rights, gains=gains))
        return qkv_pairs

    grad_o = reduce_finish(cube, out_state, [(lambda: [], qkv_products)])
    hidden_work, down_work = mixture.weight_sums(keeps2, sums)
    qkv_pairs, grad_o = together((qkv_pairs, grad_o))
    hidden_work = both(*[w for w in [hidden_work] if w], placing("grad", 1, lambda: chosen(turn2[0], turn1[0])))
    qkv_state = reduce_start(cube, exchanged(qkv_pairs), [hidden_work])
    grad_qkv = reduce_finish(cube, qkv_state, [down_work])
    width = q_weight.shape[2]
    grad_q = grad_qkv[:, :width]
    grad_k = grad_qkv[:, width : width + HEAD_SIZE]
    grad_v = grad_qkv[:, width + HEAD_SIZE : width + 2 * HEAD_SIZE]
    gain_pair = [grad_qkv[:, width + 2 * HEAD_SIZE + i] for i in range(2)]
    section_out = jnp.stack([placings["out", 0], placings["out", 1]])
    input_grad = jnp.stack([placings["grad", 0], placings["grad", 1]])
    (gate_total, up_total), (down_total,) = sums
    return (
        section_out[None],
        input_grad[None],
        gain_pair[0][None],
        grad_q[None],
        grad_k[None],
        grad_v[None],
        grad_o[None],
        gain_pair[1][None],
        gate_total[None, None],
        up_total[None, None],
        down_total[None, None],
    )


def solution(mesh):
    in_specs = (
        P(None, "dp", None),
        P(None, "dp", None),
        P("section", None, "dp", None),
        P("section", None, "dp", None),
        P("section", None),
        P("section", None, "shard"),
        P("section", None, "shard"),
        P("section", None, "shard"),
        P("section", None, "shard"),
        P("section", None),
        P("section", "dp", None, "shard"),
        P("section", "dp", None, "shard"),
        P("section", "dp", "shard", None),
        P(None, "dp", None),
    )
    out_specs = (
        P("section", None, "dp", "shard"),
        P("section", None, "dp", "shard"),
        P("section", "dp"),
        P("section", "dp", "shard"),
        P("section", "dp", "shard"),
        P("section", "dp", "shard"),
        P("section", "dp", "shard"),
        P("section", "dp"),
        P("section", "dp", None, "shard"),
        P("section", "dp", None, "shard"),
        P("section", "dp", "shard", None),
    )
    return jax.shard_map(local, mesh=mesh, in_specs=in_specs, out_specs=out_specs, check_vma=False)
```

```python
import functools

import jax
import jax.numpy as jnp
import numpy as np
from jax import lax
from jax.experimental import pallas as pl
from jax.experimental.pallas import tpu as pltpu
from jax.sharding import PartitionSpec as P

HEAD_SIZE = 128
epsilon = 1e-06
masked_value = -1e30
bf16 = jnp.bfloat16
f32 = jnp.float32


def wide(a):
    return a.astype(f32)


def dot_nn(a, b):
    return lax.dot_general(a, b, (((1,), (0,)), ((), ())), preferred_element_type=f32)


def dot_nt(a, b):
    return lax.dot_general(a, b, (((1,), (1,)), ((), ())), preferred_element_type=f32)


def dot_tn(a, b):
    return lax.dot_general(a, b, (((0,), (0,)), ((), ())), preferred_element_type=f32)


class Cube:
    def __init__(self):
        peers = lax.axis_size("dp")
        bits = [1 << i for i in range(peers.bit_length() - 1)]
        rest = bits[1:]
        self.core = ("dp", bits[0])
        self.x = ("dp", rest[0])
        self.y = ("dp", rest[len(rest) // 2])
        self.z = ("shard", 1)
        self.extra = [("dp", b) for b in rest if b not in (self.x[1], self.y[1])]
        inner = [0]
        for _, bit in self.extra:
            inner = inner + [m | bit for m in inner]
        self.inner = np.array(inner)
        x, y = self.x[1], self.y[1]
        self.corner = (x | y, 1)
        stages = [[(0, 0)], [(x, 0), (y, 0), (0, 1)], [(x | y, 0), (y, 1), (x, 1)], [self.corner]]
        self.stages = [(g, [(m | self.core[1], s) for m, s in g]) for g in stages]


def swap(value, direction):
    axis, bit = direction
    return lax.ppermute(value, axis, [(i, i ^ bit) for i in range(lax.axis_size(axis))])


def across(value, cube):
    mask, flip = cube.corner
    shards = lax.axis_size("shard")
    pairs = [
        (d * shards + s, (d ^ mask) * shards + (s ^ flip))
        for d in range(lax.axis_size("dp"))
        for s in range(shards)
    ]
    return lax.ppermute(value, ("dp", "shard"), pairs)


together = lax.optimization_barrier


def both(*thunks):
    def work(*groups):
        return [thunk[1](*group) for thunk, group in zip(thunks, groups)]

    return lambda: [thunk[0]() for thunk in thunks], work


def after(payload, thunks, step):
    if step >= len(thunks) or thunks[step] is None:
        return payload, lambda: ()
    inputs, work = thunks[step]
    payload, inputs = together((payload, inputs()))
    return payload, lambda: work(*inputs)


def gather_rows(cube, own, work, side=()):
    own, beside = after(own, side, 0)
    near = [swap(own, d) for d in (cube.x, cube.y, cube.z)]
    first = work(0, [own])
    near, first, _ = together((near, first, beside()))

    near, beside = after(near, side, 1)
    middle = [swap(block, d) for block, d in zip(near, (cube.y, cube.z, cube.x))]
    second = work(1, near)
    middle, second, _ = together((middle, second, beside()))

    middle, beside = after(middle, side, 2)
    corner = swap(middle[0], cube.z)
    third = work(2, middle)
    corner, third, _ = together((corner, third, beside()))
    return first, second, third, (lambda: [corner], lambda *blocks: work(3, list(blocks)))


def low_sum(*terms):
    return sum(wide(t) for t in terms).astype(bf16)


def reduce_start(cube, middle, corner, rest, side=()):
    (middle, rest), beside = after((middle, rest), side, 0)
    middle, inputs = together((middle, corner[0]()))
    arrived = [swap(t, d) for t, d in zip(middle, (cube.y, cube.z, cube.x))]
    return together((arrived, corner[1](*inputs), rest, beside()))[:3]


def reduce_finish(cube, arrived, corner, near, own, side=()):
    sent = [low_sum(*corner)] + [low_sum(*terms, a) for terms, a in zip(near, arrived)]
    sent, beside = after(sent, side, 0)
    arrived = [swap(t, d) for t, d in zip(sent[1:], (cube.x, cube.y, cube.z))] + [across(sent[0], cube)]
    arrived, own, _ = together((arrived, own, beside()))
    total = sum(wide(t) for t in [*own, *arrived])
    for direction in reversed(cube.extra):
        half = total.shape[0] // 2
        total = total[:half] + wide(swap(total[half:].astype(bf16), direction))
    return total


def norm_factor(values):
    return lax.rsqrt(jnp.mean(values * values, axis=1, keepdims=True) + epsilon)


def norm_back(values, factor, gain, grad):
    gain_grad = jnp.sum(grad * values * factor, axis=0, keepdims=True)
    scaled = grad * gain
    inner = jnp.mean(scaled * values, axis=1, keepdims=True)
    return factor * (scaled - values * factor * factor * inner), gain_grad


def stack_heads(rows):
    return jnp.concatenate(
        [rows[:, i : i + HEAD_SIZE] for i in range(0, rows.shape[1], HEAD_SIZE)], axis=0
    )


def spread_heads(stacked, rows):
    return jnp.concatenate(
        [stacked[i : i + rows] for i in range(0, stacked.shape[0], rows)], axis=1
    )


def head_probs(query, key, allowed):
    scores = jnp.where(allowed > 0.0, dot_nt(query, key) * HEAD_SIZE ** (-0.5), masked_value)
    exp_scores = jnp.exp(scores - jnp.max(scores, axis=1, keepdims=True))
    return exp_scores / jnp.sum(exp_scores, axis=1, keepdims=True)


def normed_rows(values, gain):
    return (values * norm_factor(values) * gain).astype(bf16)


def group_probs(qkv, allowed):
    width = qkv.shape[1] - 2 * HEAD_SIZE
    query = stack_heads(qkv[:, :width])
    key, value = qkv[:, width : width + HEAD_SIZE], qkv[:, width + HEAD_SIZE :]
    tiled = jnp.concatenate([allowed] * (width // HEAD_SIZE), axis=0)
    return query, key, value, head_probs(query, key, tiled)


def head_group(normed, allowed, weights, qkv, heads):
    *projections, w_out = weights
    at = 0
    for w in projections:
        part = dot_nn(normed, w()).astype(bf16)
        qkv[:, at : at + part.shape[1]] = part
        at += part.shape[1]
    _, _, value, probs = group_probs(qkv[...], allowed)
    heads[...] = spread_heads(dot_nn(probs.astype(bf16), value).astype(bf16), normed.shape[0])
    return dot_nt(heads[...], w_out())


VMEM = pl.BlockSpec(memory_space=pltpu.VMEM)
SMEM = pl.BlockSpec(memory_space=pltpu.SMEM)
ANY = pl.BlockSpec(memory_space=pl.ANY)
KERNEL_VMEM = 42 << 20


def held(shape, dtype):
    return pltpu.VMEM(shape, dtype)


def like(shape, dtype):
    return pltpu.HBM(shape, dtype)


def close(value):
    return pltpu.with_memory_space_constraint(value, pltpu.VMEM)


def distant(value):
    return pltpu.with_memory_space_constraint(value, pltpu.HBM)


def pinned(groups, axes=None):
    groups = [g if isinstance(g, (list, tuple)) else (g,) for g in groups]
    axes = axes or [0] * len(groups)
    values = [v for g in groups for v in g]
    shapes = [
        tuple(n * len(g) if i == axis else n for i, n in enumerate(g[0].shape)) for g, axis in zip(groups, axes)
    ]

    def body(*refs):
        ins, outs, sems = list(refs[: len(values)]), refs[len(values) : -1], refs[-1]
        copies, waits = Copies(sems), []
        for group, axis, out in zip(groups, axes, outs):
            for i, value in enumerate(group):
                size = value.shape[axis]
                place = [slice(None)] * axis + [pl.ds(i * size, size)]
                waits.append(copies.start(ins.pop(0), out.at[tuple(place)]))
        for copy in waits:
            copy.wait()

    return pl.pallas_call(
        body,
        out_shape=[held(shape, g[0].dtype) for g, shape in zip(groups, shapes)],
        in_specs=[ANY] * len(values),
        out_specs=[VMEM] * len(groups),
        scratch_shapes=[pltpu.SemaphoreType.DMA((len(values),))],
        compiler_params=pltpu.CompilerParams(vmem_limit_bytes=1 << 20),
    )(*map(distant, values))


def put_together(pieces, spans, shape):
    starts = jnp.stack([first for first, _, _ in spans]).astype(jnp.int32)

    def body(starts, *refs):
        ins, out, sems = refs[:-2], refs[-2], refs[-1]
        copies, waits = Copies(sems), []
        for i, (piece, (_, unit, column)) in enumerate(zip(ins, spans)):
            rows = pl.ds(pl.multiple_of(starts[i] * unit, unit), piece.shape[0])
            waits.append(copies.start(piece, out.at[rows, pl.ds(column, piece.shape[1])]))
        for copy in waits:
            copy.wait()

    return pl.pallas_call(
        body,
        out_shape=held(shape, pieces[0].dtype),
        in_specs=[SMEM] + [ANY] * len(pieces),
        out_specs=VMEM,
        scratch_shapes=[pltpu.SemaphoreType.DMA((len(pieces),))],
        compiler_params=pltpu.CompilerParams(vmem_limit_bytes=KERNEL_VMEM),
    )(starts, *map(distant, pieces))


class Copies:
    def __init__(self, sems):
        self.sems, self.count = sems, 0

    def start(self, source, target):
        copy = pltpu.make_async_copy(source, target, self.sems.at[self.count])
        self.count += 1
        copy.start()
        return copy

    def fetch(self, source, target):
        copy, waited = self.start(source, target), []

        def value():
            if not waited:
                copy.wait()
                waited.append(True)
            return target[...]

        return value


def on_device(body, outs, args, flops, scalars=(), kept=(), far=(), scratch=(), direct=False):
    moved = sum(a.size * a.dtype.itemsize for a in args)
    return pl.pallas_call(
        body,
        out_shape=outs,
        in_specs=[SMEM] * len(scalars) + [VMEM] * (len(args) + len(kept)) + [ANY] * len(far),
        out_specs=[SMEM if o.dtype == jnp.int32 else ANY if direct else VMEM for o in outs],
        scratch_shapes=scratch,
        compiler_params=pltpu.CompilerParams(vmem_limit_bytes=KERNEL_VMEM),
        cost_estimate=pl.CostEstimate(flops=flops // 64, bytes_accessed=moved // 64, transcendentals=0),
    )(*scalars, *map(distant, args), *map(close, kept), *far)


def holders(*arrays):
    return [pltpu.VMEM(a.shape, a.dtype) for a in arrays] + [pltpu.SemaphoreType.DMA((len(arrays) + 1,))]


def geometry(lens, micro, side, rows, block):
    ends, total, best, start = [], 0, lens[micro, 0, 0], 0
    for i in range(lens.shape[2]):
        length = lens[micro, 0, i]
        if i:
            start = jnp.where(length > best, total, start)
            best = jnp.maximum(best, length)
        total = total + length
        ends.append(total)
    return ends, lax.rem(start + rows * side, block)


def positions(shape, axis, begin, block):
    place = lax.broadcasted_iota(jnp.int32, shape, axis) + begin
    return jnp.where(place >= block, place - block, place)


def selection(begin, rows, block):
    wanted = positions((rows, block), 0, begin, block)
    return (wanted == lax.broadcasted_iota(jnp.int32, (rows, block), 1)).astype(f32)


def sequence_mask(ends, begin, rows, block):
    row, col = [positions((rows, rows), axis, begin, block) for axis in (0, 1)]
    inside = sum(jnp.abs((row >= e).astype(jnp.int32) - (col >= e).astype(jnp.int32)) for e in ends)
    return ((inside == 0) & (col <= row)).astype(f32)


def gate_columns(pick, routes, gates):
    peers = lax.axis_size("dp")
    expert = lax.broadcasted_iota(jnp.int32, (128, routes.shape[1]), 0)
    table = jnp.zeros(expert.shape, f32)
    for k in range(routes.shape[0]):
        gate, route = gates[k : k + 1, :], routes[k : k + 1, :]
        high = wide(gate.astype(bf16))
        table += jnp.where(expert == route, high, 0.0) + jnp.where(expert == route + peers, gate - high, 0.0)
    return dot_nt(pick, table.astype(bf16)).astype(bf16)


def turned_body(lens, blocks, own, other, block_rows, sems):
    copy = Copies(sems).fetch(blocks.at[0], block_rows)
    block = block_rows.shape[0]
    here = jnp.where(lax.axis_index("section") == 0, 0.0, 1.0)
    shard = lax.axis_index("shard")
    for side, out in ((shard, own), (1 - shard, other)):
        _, begin = geometry(lens, 0, side, block // 2, block)
        out[...] = dot_nn((selection(begin, block // 2, block) * here).astype(bf16), copy()).astype(bf16)


def turned_block(lens, blocks):
    _, block, model = blocks.shape
    scratch = [pltpu.VMEM((block, model), bf16), pltpu.SemaphoreType.DMA((1,))]
    shapes = [like((block // 2, model), bf16)] * 2
    return on_device(
        turned_body, shapes, [], 2 * block * block * model, (lens,), far=[distant(blocks)], scratch=scratch
    )


def opening_body(lens, gain, tokens, *refs):
    wq, wk, wv, wo, inputs, part, qkv, heads, sent, qkv_other, heads_other, mask, *scratch, sems = refs
    copies = Copies(sems)
    sources = [tokens.at[0], wq, wk, wv, wo]
    block_rows, *weights = [copies.fetch(a, b) for a, b in zip(sources, scratch)]
    block = tokens.shape[1]
    rows = block // 2
    shard = lax.axis_index("shard")
    first = jnp.where(lax.axis_index("section") == 0, 1.0, 0.0)
    for own in (False, True):
        to_qkv, to_heads = (qkv, heads) if own else (qkv_other, heads_other)
        ends, begin = geometry(lens, 0, shard if own else 1 - shard, rows, block)
        pick = selection(begin, rows, block)
        values = dot_nn((pick * first).astype(bf16), block_rows())
        allowed = sequence_mask(ends, begin, rows, block)
        value = head_group(normed_rows(values, gain[...]), allowed, weights, to_qkv, to_heads)
        if own:
            inputs[...] = values.astype(bf16)
            part[...] = values + value
            mask[...] = allowed
        else:
            sent[...] = value.astype(bf16)


def opening(lens, tokens, gain, weights):
    _, block, model = tokens.shape
    rows = block // 2
    width, out = sum(w.shape[1] for w in weights[:3]), weights[3].shape[1]
    shapes = [
        like((rows, model), bf16), like((rows, model), f32), like((rows, width), bf16), like((rows, out), bf16),
        like((rows, model), bf16), like((rows, width), bf16), like((rows, out), bf16), like((rows, rows), f32),
    ]
    scratch = [pltpu.VMEM((block, model), bf16), *holders(*weights)]
    outs = on_device(
        opening_body, shapes, [gain], 4 * rows * model * (width + out), (lens,), far=[distant(t) for t in (tokens, *weights)], scratch=scratch
    )
    return outs[:5], outs[7]


def settle_body(lens, routes0, gates0, routes1, gates1, tokens, grad, *refs):
    fresh, cot, mask, extra0, extra1, starts, token_rows, grad_rows, sems = refs
    copies = Copies(sems)
    for micro in range(2):
        _, starts[micro] = geometry(lens, micro, 0, tokens.shape[1] // 2, tokens.shape[1])
    token_rows = copies.fetch(tokens.at[1], token_rows)
    grad_rows = copies.fetch(grad.at[1], grad_rows)
    block = tokens.shape[1]
    rows = block // 2
    first = jnp.where(lax.axis_index("section") == 0, 1.0, 0.0)
    for micro, routes, gates, extra in ((0, routes0, gates0, extra0), (1, routes1, gates1, extra1)):
        ends, begin = geometry(lens, micro, lax.axis_index("shard"), rows, block)
        pick = selection(begin, rows, block)
        extra[...] = gate_columns(pick.astype(bf16), routes[...], gates[...])
    fresh[...] = dot_nn((pick * first).astype(bf16), token_rows()).astype(bf16)
    cot[...] = dot_nn((pick * (1.0 - first)).astype(bf16), grad_rows()).astype(bf16)
    mask[...] = sequence_mask(ends, begin, rows, block)


def settle(lens, tokens, grad, routes, gates):
    _, block, model = tokens.shape
    rows = block // 2
    shapes = [like((rows, model), bf16)] * 2 + [like((rows, rows), f32)] + [like((rows, 128), bf16)] * 2
    shapes.append(pltpu.SMEM((2,), jnp.int32))
    args = [routes[0], gates[0], routes[1], gates[1]]
    scratch = [pltpu.VMEM((block, model), bf16)] * 2 + [pltpu.SemaphoreType.DMA((2,))]
    return on_device(
        settle_body, shapes, args, 2 * block * block * model, (lens,), far=[distant(tokens), distant(grad)], scratch=scratch
    )


def joined_body(part, other, extra, gain, hidden, payload):
    total = part[...] + wide(other[...])
    hidden[...] = total
    model = total.shape[1]
    payload[:, :model] = normed_rows(total, gain[...])
    payload[:, model:] = extra[...]


def joined(part, other, gain, extra):
    rows, model = part.shape
    shapes = [like((rows, model), f32), like((rows, model + extra.shape[1]), bf16)]
    return on_device(joined_body, shapes, [part, other, extra, gain], 10 * rows * model)


def by_halves(refs):
    *own, packed = refs
    widths = [w.shape[1] for w in own]
    firsts = [sum(widths[:i]) for i in range(4)]
    other = [lambda f=f, w=w: packed[:, f : f + w] for f, w in zip(firsts, widths)]
    return [lambda w=w: w[...] for w in own], other


def other_heads_body(inputs, mask, gain, wq, wk, wv, wo, packed, qkv, heads):
    _, weights = by_halves((wq, wk, wv, wo, packed))
    head_group(normed_rows(wide(inputs[...]), gain[...]), mask[...], weights, qkv, heads)


def other_heads(inputs, mask, gain, weights, packed):
    rows = inputs.shape[0]
    width, out = sum(w.shape[1] for w in weights[:3]), weights[3].shape[1]
    shapes = [like((rows, width), bf16), like((rows, out), bf16)]
    return on_device(
        other_heads_body, shapes, [inputs, mask, gain], 2 * rows * packed.size, kept=[*weights, packed]
    )


def attention_body(fresh, arriving, mask, extra, gain, gain_two, *refs):
    own, other = by_halves(refs[:5])
    inputs, hidden, payload, qkv0, qkv1, heads0, heads1 = refs[5:]
    rows = fresh[...] + arriving[...]
    inputs[...] = rows
    total = wide(rows)
    normed = normed_rows(total, gain[...])
    total = total + head_group(normed, mask[...], own, qkv0, heads0)
    total = total + head_group(normed, mask[...], other, qkv1, heads1)
    hidden[...] = total
    model = total.shape[1]
    payload[:, :model] = normed_rows(total, gain_two[...])
    payload[:, model:] = extra[...]


def attention_forward(fresh, arriving, mask, gain, gain_two, extra, weights, packed):
    rows, model = fresh.shape
    width, out = sum(w.shape[1] for w in weights[:3]), weights[3].shape[1]
    shapes = [
        like((rows, model), bf16), like((rows, model), f32), like((rows, model + extra.shape[1]), bf16),
        like((rows, width), bf16), like((rows, width), bf16), like((rows, out), bf16), like((rows, out), bf16),
    ]
    args = [fresh, arriving, mask, extra, gain, gain_two]
    outs = on_device(attention_body, shapes, args, 4 * rows * packed.size, kept=[*weights, packed])
    inputs, hidden, payload, qkv0, qkv1, heads0, heads1 = outs
    return inputs, hidden, payload, [(qkv0, heads0), (qkv1, heads1)]


def attention_back_body(grad, grad_two, inputs, hidden, mask, q0, q1, gain, gain_two, *refs):
    own, other = by_halves(refs[:5])
    grad_input, grad_input_low, grad_low, normed, g0, g1, gain_grad, gain_two_grad = refs[5:]
    rows = inputs.shape[0]
    values = wide(inputs[...])
    normed[...] = normed_rows(values, gain[...])
    total = hidden[...]
    back, gain_two_grad[...] = norm_back(total, norm_factor(total), gain_two[...], grad_two[...])
    grad_hidden = wide(grad[...]) + back
    low = grad_hidden.astype(bf16)
    grad_low[...] = low
    grad_normed = jnp.zeros_like(grad_hidden)
    for qkv, weights, grad_qkv in ((q0, own, g0), (q1, other, g1)):
        query, key, value, probs = group_probs(qkv[...], mask[...])
        grad_heads = stack_heads(dot_nn(low, weights[3]()).astype(bf16))
        grad_probs = dot_nt(grad_heads, value)
        inner = jnp.sum(probs * grad_probs, axis=1, keepdims=True)
        grad_scores = (probs * (grad_probs - inner) * HEAD_SIZE ** (-0.5)).astype(bf16)
        grads = [
            spread_heads(dot_nn(grad_scores, key).astype(bf16), rows),
            dot_tn(grad_scores, query).astype(bf16),
            dot_tn(probs.astype(bf16), grad_heads).astype(bf16),
        ]
        at = 0
        for part, w in zip(grads, weights):
            grad_qkv[:, at : at + part.shape[1]] = part
            at += part.shape[1]
            grad_normed = grad_normed + dot_nt(part, w())
    back, gain_grad[...] = norm_back(values, norm_factor(values), gain[...], grad_normed)
    result = grad_hidden + back
    grad_input[...] = result
    grad_input_low[...] = result.astype(bf16)


def attention_backward(grad, grad_two, inputs, hidden, mask, gain, gain_two, projected, weights, packed):
    rows, model = inputs.shape
    width = projected[0].shape[1]
    shapes = [
        like((rows, model), f32), like((rows, model), bf16), like((rows, model), bf16),
        like((rows, model), bf16), like((rows, width), bf16), like((rows, width), bf16),
        like((1, model), f32), like((1, model), f32),
    ]
    args = [grad, grad_two, inputs, hidden, mask, *projected, gain, gain_two]
    return on_device(attention_back_body, shapes, args, 8 * rows * packed.size, kept=[*weights, packed])


def place(copies, pieces, *targets):
    started, at = [], 0
    for piece in pieces:
        first, count = 0, piece.shape[0]
        for target in targets:
            source = piece.at[:, pl.ds(first, target.shape[1])]
            started.append(copies.start(source, target.at[pl.ds(at, count), :]))
            first += target.shape[1]
        at += count
    return started


def pair_gates(extra, width):
    me, peers = lax.axis_index("dp"), lax.axis_size("dp")
    lane = lax.broadcasted_iota(jnp.int32, extra.shape, 1)

    def gate(expert):
        return jnp.sum(jnp.where((lane == expert) | (lane == expert + peers), wide(extra), 0.0), axis=1, keepdims=True)

    column = lax.broadcasted_iota(jnp.int32, (extra.shape[0], width), 1)
    return jnp.where(column < width // 2, gate(me), gate(me ^ 1))


def expert_stage_body(count, w_gate, w_up, w_down, *refs):
    ins, (gate_out, up_out), outs = refs[:count], refs[count : count + 2], refs[count + 2 : 2 * count + 2]
    rows, extra, gate_held, up_held, part, sems = refs[2 * count + 2 :]
    copies, leaving = Copies(sems), []
    for copy in place(copies, ins, rows, extra):
        copy.wait()
    values = rows[...]
    gate = dot_nn(values, w_gate[...])
    up = dot_nn(values, w_up[...])
    gate_held[...] = gate.astype(bf16)
    leaving.append(copies.start(gate_held, gate_out))
    up_held[...] = up.astype(bf16)
    leaving.append(copies.start(up_held, up_out))
    act = gate / (1.0 + jnp.exp(-gate)) * up * pair_gates(extra[...], gate.shape[1])
    part[...] = dot_nn(act.astype(bf16), w_down[...]).astype(bf16)
    at = 0
    for out in outs:
        leaving.append(copies.start(part.at[pl.ds(at, out.shape[0]), :], out))
        at += out.shape[0]
    for copy in leaving:
        copy.wait()


def expert_stage(pieces, *weights):
    count = sum(p.shape[0] for p in pieces)
    model, units = weights[0].shape
    extra = pieces[0].shape[1] - model
    shapes = [like((count, units), bf16)] * 2 + [like((p.shape[0], model), bf16) for p in pieces]
    scratch = [pltpu.VMEM((count, n), bf16) for n in (model, extra, units, units, model)]
    scratch.append(pltpu.SemaphoreType.DMA((3 * len(pieces) + 2,)))
    body = functools.partial(expert_stage_body, len(pieces))
    outs = on_device(
        body, shapes, [], 6 * count * weights[0].size, kept=weights, far=pieces, scratch=scratch, direct=True
    )
    return outs[2:], (pieces, *outs[:2])


def expert_back_body(count, w_gate, w_up, w_down, *refs):
    ins, payloads, (gate_in, up_in) = refs[:count], refs[count : 2 * count], refs[2 * count : 2 * count + 2]
    grad_outs, outs = refs[2 * count + 2 : 2 * count + 5], refs[2 * count + 5 : 3 * count + 5]
    grads, extra, gate_held, up_held, *held_back, part, sems = refs[3 * count + 5 :]
    copies, leaving, first = Copies(sems), [], w_gate.shape[0]
    arriving = place(copies, ins, grads)
    at = 0
    for payload in payloads:
        size = payload.shape[0]
        arriving.append(
            copies.start(payload.at[:, pl.ds(first, extra.shape[1])], extra.at[pl.ds(at, size), :])
        )
        at += size
    arriving += [copies.start(gate_in, gate_held), copies.start(up_in, up_held)]
    for copy in arriving:
        copy.wait()
    scale = pair_gates(extra[...], w_gate.shape[1])
    grad_act = scale * dot_nt(grads[...], w_down[...])
    gate, up = wide(gate_held[...]), wide(up_held[...])
    sig = 1.0 / (1.0 + jnp.exp(-gate))
    silu = gate * sig
    low_gate = (grad_act * up * sig * (1.0 + gate * (1.0 - sig))).astype(bf16)
    low_up = (grad_act * silu).astype(bf16)
    for value, held_value, out in zip((low_gate, low_up, (scale * silu * up).astype(bf16)), held_back, grad_outs):
        held_value[...] = value
        leaving.append(copies.start(held_value, out))
    part[...] = (dot_nt(low_gate, w_gate[...]) + dot_nt(low_up, w_up[...])).astype(bf16)
    at = 0
    for out in outs:
        leaving.append(copies.start(part.at[pl.ds(at, out.shape[0]), :], out))
        at += out.shape[0]
    for copy in leaving:
        copy.wait()


def expert_back_stage(pieces, saved, *weights):
    payloads, gate_out, up_out = saved
    count = sum(p.shape[0] for p in pieces)
    model, units = weights[0].shape
    extra = payloads[0].shape[1] - model
    shapes = [like((count, units), bf16)] * 3 + [like((p.shape[0], model), bf16) for p in pieces]
    scratch = [pltpu.VMEM((count, n), bf16) for n in (model, extra, units, units, units, units, units, model)]
    scratch.append(pltpu.SemaphoreType.DMA((3 * len(pieces) + 5,)))
    body = functools.partial(expert_back_body, len(pieces))
    far = [*pieces, *payloads, gate_out, up_out]
    outs = on_device(
        body, shapes, [], 6 * count * weights[0].size, kept=weights, far=far, scratch=scratch, direct=True
    )
    return outs[3:], (payloads, pieces, *outs[:3])


def swept_products(swept, fixed, sums, swept_left, final):
    width = fixed[0][0].shape[1]
    step, steps = width // 2, 4
    rows = sum(t.shape[0] for t in swept)

    def body(*refs):
        refs = list(refs)
        left = jnp.concatenate([refs.pop(0)[...] for _ in swept], axis=0)
        rights = [jnp.concatenate([refs.pop(0)[...] for _ in group], axis=0) for group in fixed]
        totals = [refs.pop(0)[...] for _ in sums or ()] or [0.0] * len(fixed)
        for total, right in zip(totals, rights):
            total = total + (dot_tn(left, right) if swept_left else dot_tn(right, left))
            if final:
                parts = (total[:, :step], total[:, step:]) if swept_left else (total[:step], total[step:])
                refs.pop(0)[...] = parts[0]
                refs.pop(0)[...] = parts[1].astype(bf16)
            else:
                refs.pop(0)[...] = total

    def spec(size):
        return pl.BlockSpec((step, size), lambda j: (j, 0)) if swept_left else pl.BlockSpec((size, step), lambda j: (0, j))

    def shape(size):
        return (step * steps, size) if swept_left else (size, step * steps)

    shapes, out_specs = [], []
    for _ in fixed:
        for size, dtype in ((step, f32), (step, bf16)) if final else ((width, f32),):
            shapes.append(like(shape(size), dtype))
            out_specs.append(spec(size))
    in_specs = [pl.BlockSpec((t.shape[0], step), lambda j: (0, j)) for t in swept]
    in_specs += [pl.BlockSpec(t.shape, lambda j: (0, 0)) for group in fixed for t in group]
    in_specs += [spec(width) for _ in sums or ()]
    return pl.pallas_call(
        body,
        grid=(steps,),
        out_shape=shapes,
        in_specs=in_specs,
        out_specs=out_specs,
        compiler_params=pltpu.CompilerParams(vmem_limit_bytes=KERNEL_VMEM),
        cost_estimate=pl.CostEstimate(flops=rows * width, bytes_accessed=rows, transcendentals=0),
    )(*map(distant, [*swept, *[t for group in fixed for t in group], *(sums or ())]))


def expert_forward(rows, w_gate, w_up, w_down):
    gate_out = dot_nn(rows, w_gate)
    up_out = dot_nn(rows, w_up)
    act = (gate_out / (1.0 + jnp.exp(-gate_out)) * up_out).astype(bf16)
    part = dot_nn(act, w_down).astype(bf16)
    return part, (rows, gate_out.astype(bf16), up_out.astype(bf16))


def expert_backward(grad_rows, saved, w_gate, w_up, w_down):
    rows, gate_low, up_low = saved
    gate_out, up_out = wide(gate_low), wide(up_low)
    grad_act = dot_nt(grad_rows, w_down)
    sig = 1.0 / (1.0 + jnp.exp(-gate_out))
    silu = gate_out * sig
    grad_gate = (grad_act * up_out * sig * (1.0 + gate_out * (1.0 - sig))).astype(bf16)
    grad_up = (grad_act * silu).astype(bf16)
    act = (silu * up_out).astype(bf16)
    grad_in = (dot_nt(grad_gate, w_gate) + dot_nt(grad_up, w_up)).astype(bf16)
    return grad_in, (dot_tn(rows, grad_gate), dot_tn(rows, grad_up), dot_tn(act, grad_rows))


def halves(array):
    half = array.shape[0] // 2
    return array[:half], array[half:]


def owned_body(turns, groups, blocks, with_last, gains, *refs):
    refs = list(refs)
    lefts = [refs.pop(0) for _ in range(turns)]
    rights = [[refs.pop(0) for _ in range(turns + with_last)] for _ in range(groups)]
    last = [refs.pop(0) for _ in range(4 * with_last)]
    gains = [refs.pop(0)[...] for _ in range(gains)]
    outs, products, sems = refs[: 2 * len(blocks)], refs[-2], refs[-1]
    values = [t[...] for t in lefts]
    if with_last:
        grad, grad_two, hidden, gain = last
        total = hidden[...]
        back, _ = norm_back(total, norm_factor(total), gain[...], grad_two[...])
        values.append((wide(grad[...]) + back).astype(bf16))
    left = jnp.concatenate(values, axis=0)
    for g in range(groups):
        right = jnp.concatenate([t[...] for t in rights[g]], axis=0)
        products[g, :, : right.shape[1]] = dot_tn(left, right).astype(bf16)
        if gains:
            terms, at = [], right.shape[1]
            for gain in gains:
                high = gain.astype(bf16)
                terms += [high, (gain - wide(high)).astype(bf16)]
            rows = jnp.concatenate(terms + [jnp.zeros_like(terms[0])] * (-len(terms) % 16), axis=0)
            which = lax.broadcasted_iota(jnp.int32, (rows.shape[0], 128), 0)
            column = lax.broadcasted_iota(jnp.int32, (rows.shape[0], 128), 1)
            chosen = (column == (which // 2) % 2) & (which < len(terms))
            products[g, :, at : at + 128] = dot_tn(rows, jnp.where(chosen, 1.0, 0.0).astype(bf16)).astype(bf16)
    copies, leaving = Copies(sems), []
    me = lax.axis_index("dp")
    share = products.shape[1] // lax.axis_size("dp")
    for i, group in enumerate(blocks):
        for out, places in zip(outs[2 * i : 2 * i + 2], group):
            for j, (mask, side) in enumerate(places):
                rows = pl.ds(pl.multiple_of((me ^ mask) * share, share), share)
                leaving.append(copies.start(products.at[side, rows, :], out.at[pl.ds(j * share, share), :]))
    for copy in leaving:
        copy.wait()


def owned_products(cube, lefts, rights, last=(), gains=()):
    model, width = lefts[0].shape[1], rights[0][0].shape[1] + (128 if gains else 0)
    share = model // lax.axis_size("dp")
    blocks = [
        [[(m ^ int(i), s) for m, s in side for i in cube.inner] for side in pair] for pair in cube.stages
    ]
    shapes = [like((len(places) * share, width), bf16) for pair in blocks for places in pair]
    scratch = [
        pltpu.VMEM((len(rights), model, width), bf16),
        pltpu.SemaphoreType.DMA((sum(len(places) for pair in blocks for places in pair),)),
    ]
    args = [*lefts, *[t for group in rights for t in group], *last, *gains]
    outs = pl.pallas_call(
        functools.partial(owned_body, len(lefts), len(rights), blocks, 1 if last else 0, len(gains)),
        out_shape=shapes,
        in_specs=[VMEM] * len(args),
        out_specs=[ANY] * len(shapes),
        scratch_shapes=scratch,
        compiler_params=pltpu.CompilerParams(vmem_limit_bytes=KERNEL_VMEM),
    )(*map(distant, args))
    return [(outs[2 * i], outs[2 * i + 1]) for i in range(len(blocks))]


class Blocks:
    def __init__(self, cube, weights):
        self.cube, self.weights = cube, weights

    def forward(self, payload, micro, side=()):
        saved = [None] * 4

        def work(stage, pieces):
            parts, saved[stage] = expert_stage(pieces, *self.weights)
            return parts

        return gather_rows(self.cube, payload, work, side), saved

    def backward(self, grad, micro, saved, side=()):
        keeps = [None] * 4

        def work(stage, pieces):
            parts, keeps[stage] = expert_back_stage(pieces, saved[stage], *self.weights)
            return parts

        return gather_rows(self.cube, grad, work, side), keeps

    def late_backward(self, pieces, saved):
        parts, keeps = [None] * 4, [None] * 4

        def run(*stages):
            def work(*gathered):
                for stage, rows in zip(stages, gathered):
                    parts[stage], keeps[stage] = expert_back_stage(rows, saved[stage], *self.weights)
                return [t for stage in stages for t in parts[stage]]

            return lambda: [pieces[stage] for stage in stages], work

        return run, parts, keeps

    def total_start(self, results, side=()):
        own, near, middle, corner = results
        arrived, corner, (own, near) = reduce_start(self.cube, middle, corner, (own, near), side)
        return arrived, corner, [[t] for t in near], own

    def total_finish(self, state, side=()):
        return reduce_finish(self.cube, *state, side)

    def total(self, results, side=()):
        return self.total_finish(self.total_start(results, side[:1]), side[1:])

    def weight_sums(self, slots, sums, final=False):
        def stages():
            return [stage for keeps in slots for stage in keeps]

        def hidden(*args):
            payloads, gates, ups = args
            sums[0] = swept_products(payloads, [gates, ups], sums[0], True, final)
            return sums[0]

        def down(*args):
            grads, acts = args
            sums[1] = swept_products(grads, [acts], sums[1], False, final)
            return sums[1]

        return [
            (lambda: [[t for s in stages() for t in s[0]], [s[2] for s in stages()], [s[3] for s in stages()]], hidden),
            (lambda: [[t for s in stages() for t in s[1]], [s[4] for s in stages()]], down),
        ]


def run_all(side):
    for thunk in side:
        if thunk is not None:
            thunk[1](*thunk[0]())


class Buckets:
    def __init__(self, cube, weights, routes, gates, capacity):
        self.cube, self.weights, self.capacity = cube, weights, capacity
        micros, self.rows, self.top = routes.shape
        self.experts = lax.axis_size("dp")
        self.tables = []
        for m in range(micros):
            flat = routes[m].reshape(-1)
            onehot = (flat[:, None] == jnp.arange(self.experts, dtype=jnp.int32)).astype(jnp.int32)
            earlier = jnp.cumsum(onehot, axis=0) - onehot
            target = flat * capacity + jnp.sum(earlier * onehot, axis=1)
            source = jnp.full((self.experts * capacity,), flat.shape[0], jnp.int32)
            source = source.at[target].set(jnp.arange(flat.shape[0], dtype=jnp.int32))
            self.tables.append((target, source, gates[m]))

    def table(self, micro):
        return jax.tree.map(lambda a, b: jnp.where(micro == 0, a, b), self.tables[0], self.tables[1])

    def exchange(self, rows):
        shape = (self.experts, self.capacity, rows.shape[1])
        moved = lax.all_to_all(rows.reshape(shape), "dp", split_axis=0, concat_axis=0, tiled=True)
        return moved.reshape(rows.shape)

    def whole(self, own):
        return jnp.concatenate([own, swap(own, self.cube.z)], axis=0)

    def forward(self, payload, micro, side=()):
        target, source, gates = self.table(micro)
        own = payload[:, : self.weights[0].shape[0]]
        padded = jnp.pad(self.whole(own), ((0, 1), (0, 0)))
        arrived = self.exchange(jnp.take(padded, source // self.top, axis=0))
        part, saved = expert_forward(arrived, *self.weights)
        picked = jnp.take(self.exchange(part), target, axis=0).reshape(self.rows, self.top, -1)
        run_all(side)
        return jnp.sum(gates[:, :, None] * picked, axis=1), saved

    def backward(self, grad, micro, saved, side=()):
        target, source, gates = self.table(micro)
        scaled = (gates[:, :, None] * wide(self.whole(grad))[:, None, :]).astype(bf16)
        padded = jnp.pad(scaled.reshape(self.rows * self.top, -1), ((0, 1), (0, 0)))
        arrived = self.exchange(jnp.take(padded, source, axis=0))
        grad_in, weights = expert_backward(arrived, saved, *self.weights)
        picked = jnp.take(self.exchange(grad_in), target, axis=0).reshape(self.rows, self.top, -1)
        run_all(side)
        return jnp.sum(picked, axis=1, dtype=f32), weights

    def total_start(self, results, side=()):
        run_all(side)
        return results

    def total_finish(self, results, side=()):
        own, other = halves(results.astype(bf16))
        run_all(side)
        return wide(own) + wide(swap(other, self.cube.z))

    def total(self, results, side=()):
        return self.total_finish(results, side)

    def weight_sums(self, slots, sums, final=False):
        def add(*slots):
            for weights in slots:
                for i, part in enumerate((list(weights[:2]), list(weights[2:]))):
                    sums[i] = part if sums[i] is None else [a + b for a, b in zip(sums[i], part)]

        return [None, (lambda: slots, add)]


def local(
    tokens, lengths, routes, gates, attn_gain, q_weight, key_projection, value_projection,
    o_weight, mlp_gain, expert_gate, expert_up, expert_down, cotangent,
):
    cube = Cube()
    section = lax.axis_index("section")
    shard = lax.axis_index("shard")
    me = lax.axis_index("dp")
    peers, shards = lax.axis_size("dp"), lax.axis_size("shard")
    _, block_rows, model = tokens.shape
    rows = block_rows // shards
    share = model // peers
    first = section == 0
    gain_one, gain_two = attn_gain[0][None], mlp_gain[0][None]
    weights = [q_weight[0], key_projection[0], value_projection[0], o_weight[0]]
    expert_w = (expert_gate[0, 0], expert_up[0, 0], expert_down[0, 0])
    capacity = 2 * block_rows * routes.shape[3] // peers
    whole_blocks = capacity >= block_rows

    def chosen(here, there):
        return jax.tree.map(lambda a, b: jnp.where(first, a, b), here, there)

    def begins(lens):
        lens = lens[:, 0]
        ends, longest = jnp.cumsum(lens, axis=1), jnp.argmax(lens, axis=1)
        return [ends[m, longest[m]] - lens[m, longest[m]] for m in range(2)]

    def turned(array, begin):
        doubled = jnp.concatenate([array, array], axis=0)
        return lax.dynamic_slice_in_dim(doubled, (begin + rows * shard) % block_rows, block_rows, 0)

    if not whole_blocks:
        early = begins(lengths)
        mixture = Buckets(
            cube,
            expert_w,
            jnp.stack([turned(routes[0, m], early[m]) for m in range(2)]),
            jnp.stack([turned(gates[0, m], early[m]) for m in range(2)]),
            capacity,
        )

    slices = [lax.dynamic_slice_in_dim(w, me * share, share, 0) for w in weights]
    qkv_slices = swap(jnp.concatenate(slices[:3], axis=1), cube.z)
    out_slices = slices[3]
    half_share = share // 2
    mask = cube.x[1] | cube.y[1]
    far_places = [2 * (me ^ mask), 2 * (me ^ mask) + 1]
    plane_places = [2 * (me ^ m) for m in (0, cube.x[1], cube.y[1])]
    mate_bit = cube.core[1]

    def mate_places(places):
        return [p ^ (2 * mate_bit) for p in places]

    def placed(own, m):
        half = model // shards
        kept = lax.dynamic_slice_in_dim(own, shard * half, half, 1)
        given = lax.dynamic_slice_in_dim(own, (1 - shard) * half, half, 1)
        got = swap(given, cube.z)
        low = jnp.where(shard == 0, kept, got)
        high = jnp.where(shard == 0, got, kept)
        return lax.dynamic_slice_in_dim(
            jnp.concatenate([low, high, low, high], axis=0), (block_rows - starts[m]) % block_rows, block_rows, 0
        )

    route_cols = [routes[0, m].T for m in range(2)]
    gate_cols = [gates[0, m].T for m in range(2)]
    cot_own, cot_other = turned_block(lengths, cotangent)
    opened, mask0 = opening(lengths, tokens, gain_one, weights)
    settled = [tokens, cotangent, route_cols, gate_cols]
    own_near = [swap(cot_own, d) for d in (cube.x, cube.y)] if whole_blocks else []
    mate_w = [swap(w, cube.core) for w in expert_w] if whole_blocks else []
    opened, own_near, qkv_slices, cot_other, settled, mate_w = together(
        (opened, own_near, qkv_slices, cot_other, settled, mate_w)
    )
    inputs, part, qkv, heads, sent = opened
    other_near = [swap(cot_other, d) for d in (cube.x, cube.y)] if whole_blocks else []
    if whole_blocks:
        expert_w = pinned(list(zip(expert_w, mate_w)), (1, 1, 0))
    arrived, other_near, settled, expert_w = together(
        (swap(sent, cube.z), other_near, settle(lengths, *settled), expert_w)
    )
    fresh1, cot1, mask1, extra0, extra1, starts = settled
    hidden, payload = joined(part, arrived, gain_two, extra0)
    if whole_blocks:
        mixture = Blocks(cube, expert_w)
        plane = []

        def first_plane(qkv_slices, out_slices):
            near = [qkv_slices] + [swap(qkv_slices, d) for d in (cube.x, cube.y, ("dp", mask))]
            plane.extend([near, swap(out_slices, cube.z)])
            return plane

        side = [None, None, (lambda: [qkv_slices, out_slices], first_plane)]
        results, saved = mixture.forward(payload, 0, side)
        qkv_near, out_slices = plane
    else:
        results, saved = mixture.forward(payload, 0)
    first_mates = []

    def first_exchange(*near):
        first_mates.extend(swap(t, cube.core) for t in near)
        return first_mates

    total = mixture.total(results, [(lambda: qkv_near, first_exchange)] if whole_blocks else [])
    result0 = (hidden + total).astype(bf16)
    if whole_blocks:
        result0, qkv_near, out_slices = together((result0, qkv_near, out_slices))
        arriving = lax.ppermute(result0, "section", [(0, 1)])
        out_near = [out_slices] + [swap(out_slices, d) for d in (cube.x, cube.y, ("dp", mask))]
        arriving, out_near, weights = together((arriving, out_near, pinned(weights)))
        qkv_mates, out_mates = first_mates, [swap(t, cube.core) for t in out_near]
        all_places = [*plane_places, far_places[0]]
        width = qkv_slices.shape[1]
        spans, pieces = [], []
        for group, places, column in (
            (qkv_near, all_places, 0), (qkv_mates, mate_places(all_places), 0),
            (out_near, all_places, width), (out_mates, mate_places(all_places), width),
        ):
            pieces += group
            spans += [(p, half_share, column) for p in places]
        packed = put_together(pieces, spans, (model, width + out_slices.shape[1]))
    else:
        arriving = lax.ppermute(result0, "section", [(0, 1)])
        packed = lax.all_gather(
            jnp.concatenate([qkv_slices, swap(out_slices, cube.z)], axis=1), "dp", axis=0, tiled=True
        )
    state0 = [inputs, hidden, mask0, None, saved]

    mask_mid, extra_mid = chosen((mask1, extra1), (mask0, extra0))

    inputs1, hidden1, payload, groups1 = attention_forward(
        fresh1, arriving, mask_mid, gain_one, gain_two, extra_mid, weights, packed
    )
    def first_groups(*args):
        groups = other_heads(*args)
        state0[3] = [(qkv, heads), tuple(groups)]
        return groups

    micro_mid = 1 - section
    late = []

    def cot_far(x0, y1):
        late.extend([swap(x0, cube.y), swap(y1, cube.x)])
        return late

    side = [(lambda: [inputs, mask0, gain_one, weights, packed], first_groups)]
    if whole_blocks:
        (x0, y0), (x1, y1) = own_near, other_near
        side += [None, (lambda: [x0, y1], cot_far)]
    results, saved1 = mixture.forward(payload, micro_mid, side)

    grad0 = cot_own
    if whole_blocks:
        pieces = [[cot_own], [x0, y0, cot_other], [late[0], y1, x1], [late[1]]]
        run, back_results, keeps0 = mixture.late_backward(pieces, saved1)
        total = mixture.total(results, [run(2), run(1, 0)])
        back_results[3] = run(3)
    else:
        back_results, keeps0 = mixture.backward(grad0, micro_mid, saved1)
        total = mixture.total(results)
    result1 = (hidden1 + total).astype(bf16)

    slot2 = []

    def last_attention(arriving):
        zero = jnp.zeros((rows, model), bf16)
        slot2.extend(
            attention_forward(zero, arriving, mask1, gain_one, gain_two, extra1, weights, packed)
        )
        return slot2

    arrived = []

    def second_handoff(result):
        arrived.append(lax.ppermute(result, "section", [(0, 1)]))
        return arrived

    if whole_blocks:
        result1, back_results[:3] = together((result1, back_results[:3]))
    else:
        result1, back_results = together((result1, back_results))
    state = mixture.total_start(back_results, [(lambda: [result1], second_handoff)])
    grad_two = mixture.total_finish(state, [(lambda: arrived, last_attention)])
    inputs2, hidden2, payload, groups2 = slot2

    def attention_turn(grad, grad_two, state):
        inputs, hidden, mask, groups, _ = state
        outs = attention_backward(
            grad, grad_two, inputs, hidden, mask, gain_one, gain_two, [g[0] for g in groups], weights, packed
        )
        grad_input, low, grad_low, normed, g0, g1, attn_g, mlp_g = outs
        factors = (normed, grad_low, (g0, g1), [g[1] for g in groups])
        return grad_input, low, factors, (attn_g, mlp_g)

    state1 = [inputs1, hidden1, mask_mid, groups1, saved1]
    turn0, returned = [], []

    def first_turn(grad_two):
        turn0.extend(attention_turn(grad0, grad_two, state1))
        return turn0

    def first_return(low):
        returned.append(lax.ppermute(low, "section", [(1, 0)]))
        return returned

    side = [(lambda: [grad_two], first_turn), None, (lambda: [turn0[1]], first_return)]
    results2, saved2 = mixture.forward(payload, 1, side)
    coming = returned[0]
    state2 = [inputs2, hidden2, mask1, groups2, saved2]

    sums = [None, None]
    if whole_blocks:
        *results2, corner = results2
        coming, results2, inputs = together((coming, results2, corner[0]()))
        corner = corner[1](*inputs)
        results2 = [*results2, (lambda: [corner], lambda t: t)]
    else:
        coming, results2, saved2 = together((coming, results2, saved2))
    state2[4] = saved2
    grad1 = coming + cot1
    state_mid = chosen(state0, state2)
    back_results, keeps1 = mixture.backward(grad1, section, state_mid[4])
    placings = {}

    def placing(name, micro, own):
        def work(rows):
            placings[name, micro] = placed(rows, micro)
            return placings[name, micro]

        return lambda: [own()], work

    hidden_work, down_work = mixture.weight_sums([keeps0, keeps1], sums)
    grad_two = mixture.total(back_results, [placing("out", 0, lambda: chosen(result0, result1)), hidden_work])
    turn1 = attention_turn(grad1, grad_two, state_mid)
    if whole_blocks:
        low, results2[:3] = together((turn1[1], list(results2[:3])))
    else:
        low, results2 = together((turn1[1], results2))
    coming = lax.ppermute(low, "section", [(1, 0)])
    state = mixture.total_start(results2)
    grad2, state = together((coming, state))

    last_total = []

    def finish_last(*state):
        last_total.append(mixture.total_finish(state[0] if len(state) == 1 else state))
        return last_total

    side = [None, None, (lambda: [state] if not whole_blocks else list(state), finish_last)]
    back_results, keeps2 = mixture.backward(grad2, 1 - section, saved1, side)
    result2 = (hidden2 + last_total[0]).astype(bf16)
    placing_out = placing("out", 1, lambda: chosen(result1, result2))
    placing_grad = placing("grad", 0, lambda: chosen(turn1[0], turn0[0]))
    grad_two = mixture.total(back_results, [both(placing_out, placing_grad), down_work])

    inputs, hidden, _, groups, _ = state1
    heads_all = [[t[2][3][g] for t in (turn0, turn1)] + [groups[g][1]] for g in range(shards)]
    out_pairs = owned_products(cube, [turn0[2][1], turn1[2][1]], heads_all, (grad2, grad_two, hidden, gain_two))
    turn2 = []

    def last_turn(grad_two):
        turn2.extend(attention_turn(grad2, grad_two, state1))
        return turn2

    def exchange(*others):
        return [swap(t, cube.core) for t in others]

    def sums_start(pairs, side):
        own, near, middle, corner = pairs
        size = corner[0].shape[0]

        def blocks(*terms):
            return [[t[i * size : (i + 1) * size] for t in terms] for i in range(3)]

        middle = [low_sum(*terms) for terms in blocks(middle[0], swap(middle[1], cube.core))]
        others = (lambda: [own[1], near[1], corner[1]], exchange)
        arrived, others, mine = reduce_start(cube, middle, others, (own[0], near[0], corner[0]), side)
        return arrived, [mine[2], others[2]], blocks(mine[1], others[1]), [mine[0], others[0]]

    def run_both(*works):
        works = [w for w in works if w]
        return both(*works) if works else None

    hidden_end, down_end = mixture.weight_sums([keeps2], sums, True)
    out_state = sums_start(out_pairs, [run_both((lambda: [grad_two], last_turn), down_end)])
    turns = (turn0, turn1, turn2)
    factors = [t[2] for t in turns]
    qkv_pairs = []

    def qkv_products(*_):
        rights = [[f[2][g] for f in factors] for g in range(shards)]
        gains = [g for t in turns for g in t[3]]
        qkv_pairs.extend(owned_products(cube, [f[0] for f in factors], rights, gains=gains))
        return qkv_pairs

    grad_o = reduce_finish(cube, *out_state, [run_both((lambda: [], qkv_products), hidden_end)])
    qkv_pairs, grad_o = together((qkv_pairs, grad_o))
    last_rows = placing("grad", 1, lambda: chosen(turn2[0], turn1[0]))
    if whole_blocks:
        (gate_total, gate_other, up_total, up_other), (down_total, down_other) = sums
        arrived_sums = []

        def last_exchange(*others):
            arrived_sums.extend(exchange(*others))
            return arrived_sums

        last_rows = both(last_rows, (lambda: [gate_other, up_other, down_other], last_exchange))
    else:
        (gate_total, up_total), (down_total,) = sums
    qkv_state = sums_start(qkv_pairs, [last_rows])
    expert_sums = [gate_total, up_total, down_total]

    def last_sums(*arrived):
        expert_sums[:] = [mine + wide(other) for mine, other in zip(expert_sums, arrived)]
        return expert_sums

    grad_qkv = reduce_finish(cube, *qkv_state, [(lambda: arrived_sums, last_sums)] if whole_blocks else [])
    gate_total, up_total, down_total = expert_sums
    width = q_weight.shape[2]
    grad_q = grad_qkv[:, :width]
    grad_k = grad_qkv[:, width : width + HEAD_SIZE]
    grad_v = grad_qkv[:, width + HEAD_SIZE : width + 2 * HEAD_SIZE]
    gain_pair = [grad_qkv[:, width + 2 * HEAD_SIZE + i] for i in range(2)]
    section_out = jnp.stack([placings["out", 0], placings["out", 1]])
    input_grad = jnp.stack([placings["grad", 0], placings["grad", 1]])
    return (
        section_out[None],
        input_grad[None],
        gain_pair[0][None],
        grad_q[None],
        grad_k[None],
        grad_v[None],
        grad_o[None],
        gain_pair[1][None],
        gate_total[None, None],
        up_total[None, None],
        down_total[None, None],
    )


def solution(mesh):
    in_specs = (
        P(None, "dp", None),
        P(None, "dp", None),
        P("section", None, "dp", None),
        P("section", None, "dp", None),
        P("section", None),
        P("section", None, "shard"),
        P("section", None, "shard"),
        P("section", None, "shard"),
        P("section", None, "shard"),
        P("section", None),
        P("section", "dp", None, "shard"),
        P("section", "dp", None, "shard"),
        P("section", "dp", "shard", None),
        P(None, "dp", None),
    )
    out_specs = (
        P("section", None, "dp", "shard"),
        P("section", None, "dp", "shard"),
        P("section", "dp"),
        P("section", "dp", "shard"),
        P("section", "dp", "shard"),
        P("section", "dp", "shard"),
        P("section", "dp", "shard"),
        P("section", "dp"),
        P("section", "dp", None, "shard"),
        P("section", "dp", None, "shard"),
        P("section", "dp", "shard", None),
    )
    return jax.shard_map(local, mesh=mesh, in_specs=in_specs, out_specs=out_specs, check_vma=False)
```

```python
import functools

import jax
import jax.numpy as jnp
import numpy as np
from jax import lax
from jax.experimental import pallas as pl
from jax.experimental.pallas import tpu as pltpu
from jax.sharding import PartitionSpec as P

HEAD_SIZE = 128
epsilon = 1e-06
masked_value = -1e30
bf16 = jnp.bfloat16
f32 = jnp.float32


def wide(a):
    return a.astype(f32)


def dot_nn(a, b):
    return lax.dot_general(a, b, (((1,), (0,)), ((), ())), preferred_element_type=f32)


def dot_nt(a, b):
    return lax.dot_general(a, b, (((1,), (1,)), ((), ())), preferred_element_type=f32)


def dot_tn(a, b):
    return lax.dot_general(a, b, (((0,), (0,)), ((), ())), preferred_element_type=f32)


class Cube:
    def __init__(self):
        peers = lax.axis_size("dp")
        bits = [1 << i for i in range(peers.bit_length() - 1)]
        rest = bits[1:]
        self.core = ("dp", bits[0])
        self.x = ("dp", rest[0])
        self.y = ("dp", rest[len(rest) // 2])
        self.z = ("shard", 1)
        self.extra = [("dp", b) for b in rest if b not in (self.x[1], self.y[1])]
        inner = [0]
        for _, bit in self.extra:
            inner = inner + [m | bit for m in inner]
        self.inner = np.array(inner)
        x, y = self.x[1], self.y[1]
        self.corner = (x | y, 1)
        stages = [[(0, 0)], [(x, 0), (y, 0), (0, 1)], [(x | y, 0), (y, 1), (x, 1)], [self.corner]]
        self.stages = [(g, [(m | self.core[1], s) for m, s in g]) for g in stages]


def swap(value, direction):
    axis, bit = direction
    return lax.ppermute(value, axis, [(i, i ^ bit) for i in range(lax.axis_size(axis))])


def across(value, cube):
    mask, flip = cube.corner
    shards = lax.axis_size("shard")
    pairs = [
        (d * shards + s, (d ^ mask) * shards + (s ^ flip))
        for d in range(lax.axis_size("dp"))
        for s in range(shards)
    ]
    return lax.ppermute(value, ("dp", "shard"), pairs)


together = lax.optimization_barrier


def both(*thunks):
    def work(*groups):
        return [thunk[1](*group) for thunk, group in zip(thunks, groups)]

    return lambda: [thunk[0]() for thunk in thunks], work


def after(payload, thunks, step):
    if step >= len(thunks) or thunks[step] is None:
        return payload, lambda: ()
    inputs, work = thunks[step]
    payload, inputs = together((payload, inputs()))
    return payload, lambda: work(*inputs)


def gather_rows(cube, own, work, side=()):
    own, beside = after(own, side, 0)
    near = [swap(own, d) for d in (cube.x, cube.y, cube.z)]
    first = work(0, [own])
    near, first, _ = together((near, first, beside()))

    near, beside = after(near, side, 1)
    middle = [swap(block, d) for block, d in zip(near, (cube.y, cube.z, cube.x))]
    second = work(1, near)
    middle, second, _ = together((middle, second, beside()))

    middle, beside = after(middle, side, 2)
    corner = swap(middle[0], cube.z)
    third = work(2, middle)
    corner, third, _ = together((corner, third, beside()))
    return first, second, third, (lambda: [corner], lambda *blocks: work(3, list(blocks)))


def low_sum(*terms):
    return sum(wide(t) for t in terms).astype(bf16)


def reduce_start(cube, middle, corner, rest, side=()):
    (middle, rest), beside = after((middle, rest), side, 0)
    middle, inputs = together((middle, corner[0]()))
    arrived = [swap(t, d) for t, d in zip(middle, (cube.y, cube.z, cube.x))]
    return together((arrived, corner[1](*inputs), rest, beside()))[:3]


def reduce_finish(cube, arrived, corner, near, own, side=()):
    sent = [low_sum(*corner)] + [low_sum(*terms, a) for terms, a in zip(near, arrived)]
    sent, beside = after(sent, side, 0)
    arrived = [swap(t, d) for t, d in zip(sent[1:], (cube.x, cube.y, cube.z))] + [across(sent[0], cube)]
    arrived, own, _ = together((arrived, own, beside()))
    total = sum(wide(t) for t in [*own, *arrived])
    for direction in reversed(cube.extra):
        half = total.shape[0] // 2
        total = total[:half] + wide(swap(total[half:].astype(bf16), direction))
    return total


def norm_factor(values):
    return lax.rsqrt(jnp.mean(values * values, axis=1, keepdims=True) + epsilon)


def norm_back(values, factor, gain, grad):
    gain_grad = jnp.sum(grad * values * factor, axis=0, keepdims=True)
    scaled = grad * gain
    inner = jnp.mean(scaled * values, axis=1, keepdims=True)
    return factor * (scaled - values * factor * factor * inner), gain_grad


def stack_heads(rows):
    return jnp.concatenate(
        [rows[:, i : i + HEAD_SIZE] for i in range(0, rows.shape[1], HEAD_SIZE)], axis=0
    )


def spread_heads(stacked, rows):
    return jnp.concatenate(
        [stacked[i : i + rows] for i in range(0, stacked.shape[0], rows)], axis=1
    )


def head_probs(query, key, allowed):
    scores = jnp.where(allowed > 0.0, dot_nt(query, key) * HEAD_SIZE ** (-0.5), masked_value)
    exp_scores = jnp.exp(scores - jnp.max(scores, axis=1, keepdims=True))
    return exp_scores / jnp.sum(exp_scores, axis=1, keepdims=True)


def normed_rows(values, gain):
    return (values * norm_factor(values) * gain).astype(bf16)


def group_probs(qkv, allowed):
    width = qkv.shape[1] - 2 * HEAD_SIZE
    query = stack_heads(qkv[:, :width])
    key, value = qkv[:, width : width + HEAD_SIZE], qkv[:, width + HEAD_SIZE :]
    tiled = jnp.concatenate([allowed] * (width // HEAD_SIZE), axis=0)
    return query, key, value, head_probs(query, key, tiled)


def head_group(normed, allowed, weights, qkv, heads):
    *projections, w_out = weights
    at = 0
    for w in projections:
        part = dot_nn(normed, w()).astype(bf16)
        qkv[:, at : at + part.shape[1]] = part
        at += part.shape[1]
    _, _, value, probs = group_probs(qkv[...], allowed)
    heads[...] = spread_heads(dot_nn(probs.astype(bf16), value).astype(bf16), normed.shape[0])
    return dot_nt(heads[...], w_out())


VMEM = pl.BlockSpec(memory_space=pltpu.VMEM)
SMEM = pl.BlockSpec(memory_space=pltpu.SMEM)
ANY = pl.BlockSpec(memory_space=pl.ANY)
KERNEL_VMEM = 42 << 20
COST = 16


def held(shape, dtype):
    return pltpu.VMEM(shape, dtype)


def like(shape, dtype):
    return pltpu.HBM(shape, dtype)


def close(value):
    return pltpu.with_memory_space_constraint(value, pltpu.VMEM)


def distant(value):
    return pltpu.with_memory_space_constraint(value, pltpu.HBM)


def pinned(groups, axes=None):
    groups = [g if isinstance(g, (list, tuple)) else (g,) for g in groups]
    axes = axes or [0] * len(groups)
    values = [v for g in groups for v in g]
    shapes = [
        tuple(n * len(g) if i == axis else n for i, n in enumerate(g[0].shape)) for g, axis in zip(groups, axes)
    ]

    def body(*refs):
        ins, outs, sems = list(refs[: len(values)]), refs[len(values) : -1], refs[-1]
        copies, waits = Copies(sems), []
        for group, axis, out in zip(groups, axes, outs):
            for i, value in enumerate(group):
                size = value.shape[axis]
                place = [slice(None)] * axis + [pl.ds(i * size, size)]
                waits.append(copies.start(ins.pop(0), out.at[tuple(place)]))
        for copy in waits:
            copy.wait()

    return pl.pallas_call(
        body,
        out_shape=[held(shape, g[0].dtype) for g, shape in zip(groups, shapes)],
        in_specs=[ANY] * len(values),
        out_specs=[VMEM] * len(groups),
        scratch_shapes=[pltpu.SemaphoreType.DMA((len(values),))],
        compiler_params=pltpu.CompilerParams(vmem_limit_bytes=1 << 20),
    )(*map(distant, values))


def put_together(pieces, spans, shape):
    starts = jnp.stack([first for first, _, _ in spans]).astype(jnp.int32)

    def body(starts, *refs):
        ins, out, sems = refs[:-2], refs[-2], refs[-1]
        copies, waits = Copies(sems), []
        for i, (piece, (_, unit, column)) in enumerate(zip(ins, spans)):
            rows = pl.ds(pl.multiple_of(starts[i] * unit, unit), piece.shape[0])
            waits.append(copies.start(piece, out.at[rows, pl.ds(column, piece.shape[1])]))
        for copy in waits:
            copy.wait()

    return pl.pallas_call(
        body,
        out_shape=held(shape, pieces[0].dtype),
        in_specs=[SMEM] + [ANY] * len(pieces),
        out_specs=VMEM,
        scratch_shapes=[pltpu.SemaphoreType.DMA((len(pieces),))],
        compiler_params=pltpu.CompilerParams(vmem_limit_bytes=KERNEL_VMEM),
    )(starts, *map(distant, pieces))


class Copies:
    def __init__(self, sems):
        self.sems, self.count = sems, 0

    def start(self, source, target):
        copy = pltpu.make_async_copy(source, target, self.sems.at[self.count])
        self.count += 1
        copy.start()
        return copy

    def fetch(self, source, target):
        copy, waited = self.start(source, target), []

        def value():
            if not waited:
                copy.wait()
                waited.append(True)
            return target[...]

        return value


def on_device(body, outs, args, flops, scalars=(), kept=(), far=(), scratch=(), direct=False):
    moved = sum(a.size * a.dtype.itemsize for a in args)
    return pl.pallas_call(
        body,
        out_shape=outs,
        in_specs=[SMEM] * len(scalars) + [VMEM] * (len(args) + len(kept)) + [ANY] * len(far),
        out_specs=[SMEM if o.dtype == jnp.int32 else ANY if direct else VMEM for o in outs],
        scratch_shapes=scratch,
        compiler_params=pltpu.CompilerParams(vmem_limit_bytes=KERNEL_VMEM),
        cost_estimate=pl.CostEstimate(flops=COST * flops, bytes_accessed=moved, transcendentals=0),
    )(*scalars, *map(distant, args), *map(close, kept), *far)


def holders(*arrays):
    return [pltpu.VMEM(a.shape, a.dtype) for a in arrays] + [pltpu.SemaphoreType.DMA((len(arrays) + 1,))]


def geometry(lens, micro, side, rows, block):
    ends, total, best, start = [], 0, lens[micro, 0, 0], 0
    for i in range(lens.shape[2]):
        length = lens[micro, 0, i]
        if i:
            start = jnp.where(length > best, total, start)
            best = jnp.maximum(best, length)
        total = total + length
        ends.append(total)
    return ends, lax.rem(start + rows * side, block)


def positions(shape, axis, begin, block):
    place = lax.broadcasted_iota(jnp.int32, shape, axis) + begin
    return jnp.where(place >= block, place - block, place)


def selection(begin, rows, block):
    wanted = positions((rows, block), 0, begin, block)
    return (wanted == lax.broadcasted_iota(jnp.int32, (rows, block), 1)).astype(f32)


def sequence_mask(ends, begin, rows, block):
    row, col = [positions((rows, rows), axis, begin, block) for axis in (0, 1)]
    inside = sum(jnp.abs((row >= e).astype(jnp.int32) - (col >= e).astype(jnp.int32)) for e in ends)
    return ((inside == 0) & (col <= row)).astype(f32)


def gate_columns(pick, routes, gates):
    peers = lax.axis_size("dp")
    expert = lax.broadcasted_iota(jnp.int32, (128, routes.shape[1]), 0)
    table = jnp.zeros(expert.shape, f32)
    for k in range(routes.shape[0]):
        gate, route = gates[k : k + 1, :], routes[k : k + 1, :]
        high = wide(gate.astype(bf16))
        table += jnp.where(expert == route, high, 0.0) + jnp.where(expert == route + peers, gate - high, 0.0)
    return dot_nt(pick, table.astype(bf16)).astype(bf16)


def turned_body(lens, blocks, own, other, block_rows, sems):
    copy = Copies(sems).fetch(blocks.at[0], block_rows)
    block = block_rows.shape[0]
    here = jnp.where(lax.axis_index("section") == 0, 0.0, 1.0)
    shard = lax.axis_index("shard")
    for side, out in ((shard, own), (1 - shard, other)):
        _, begin = geometry(lens, 0, side, block // 2, block)
        out[...] = dot_nn((selection(begin, block // 2, block) * here).astype(bf16), copy()).astype(bf16)


def turned_block(lens, blocks):
    _, block, model = blocks.shape
    scratch = [pltpu.VMEM((block, model), bf16), pltpu.SemaphoreType.DMA((1,))]
    shapes = [like((block // 2, model), bf16)] * 2
    return on_device(
        turned_body, shapes, [], 2 * block * block * model, (lens,), far=[distant(blocks)], scratch=scratch
    )


def opening_body(lens, gain, tokens, *refs):
    wq, wk, wv, wo, inputs, part, qkv, heads, sent, qkv_other, heads_other, mask, *scratch, sems = refs
    copies = Copies(sems)
    sources = [tokens.at[0], wq, wk, wv, wo]
    block_rows, *weights = [copies.fetch(a, b) for a, b in zip(sources, scratch)]
    block = tokens.shape[1]
    rows = block // 2
    shard = lax.axis_index("shard")
    first = jnp.where(lax.axis_index("section") == 0, 1.0, 0.0)
    for own in (False, True):
        to_qkv, to_heads = (qkv, heads) if own else (qkv_other, heads_other)
        ends, begin = geometry(lens, 0, shard if own else 1 - shard, rows, block)
        pick = selection(begin, rows, block)
        values = dot_nn((pick * first).astype(bf16), block_rows())
        allowed = sequence_mask(ends, begin, rows, block)
        value = head_group(normed_rows(values, gain[...]), allowed, weights, to_qkv, to_heads)
        if own:
            inputs[...] = values.astype(bf16)
            part[...] = values + value
            mask[...] = allowed
        else:
            sent[...] = value.astype(bf16)


def opening(lens, tokens, gain, weights):
    _, block, model = tokens.shape
    rows = block // 2
    width, out = sum(w.shape[1] for w in weights[:3]), weights[3].shape[1]
    shapes = [
        like((rows, model), bf16), like((rows, model), f32), like((rows, width), bf16), like((rows, out), bf16),
        like((rows, model), bf16), like((rows, width), bf16), like((rows, out), bf16), like((rows, rows), f32),
    ]
    scratch = [pltpu.VMEM((block, model), bf16), *holders(*weights)]
    outs = on_device(
        opening_body, shapes, [gain], 4 * rows * model * (width + out), (lens,), far=[distant(t) for t in (tokens, *weights)], scratch=scratch
    )
    return outs[:5], outs[7]


def settle_body(lens, routes0, gates0, routes1, gates1, tokens, grad, *refs):
    fresh, cot, mask, extra0, extra1, starts, token_rows, grad_rows, sems = refs
    copies = Copies(sems)
    for micro in range(2):
        _, starts[micro] = geometry(lens, micro, 0, tokens.shape[1] // 2, tokens.shape[1])
    token_rows = copies.fetch(tokens.at[1], token_rows)
    grad_rows = copies.fetch(grad.at[1], grad_rows)
    block = tokens.shape[1]
    rows = block // 2
    first = jnp.where(lax.axis_index("section") == 0, 1.0, 0.0)
    for micro, routes, gates, extra in ((0, routes0, gates0, extra0), (1, routes1, gates1, extra1)):
        ends, begin = geometry(lens, micro, lax.axis_index("shard"), rows, block)
        pick = selection(begin, rows, block)
        extra[...] = gate_columns(pick.astype(bf16), routes[...], gates[...])
    fresh[...] = dot_nn((pick * first).astype(bf16), token_rows()).astype(bf16)
    cot[...] = dot_nn((pick * (1.0 - first)).astype(bf16), grad_rows()).astype(bf16)
    mask[...] = sequence_mask(ends, begin, rows, block)


def settle(lens, tokens, grad, routes, gates):
    _, block, model = tokens.shape
    rows = block // 2
    shapes = [like((rows, model), bf16)] * 2 + [like((rows, rows), f32)] + [like((rows, 128), bf16)] * 2
    shapes.append(pltpu.SMEM((2,), jnp.int32))
    args = [routes[0], gates[0], routes[1], gates[1]]
    scratch = [pltpu.VMEM((block, model), bf16)] * 2 + [pltpu.SemaphoreType.DMA((2,))]
    return on_device(
        settle_body, shapes, args, 2 * block * block * model, (lens,), far=[distant(tokens), distant(grad)], scratch=scratch
    )


def joined_body(part, other, extra, gain, hidden, payload):
    total = part[...] + wide(other[...])
    hidden[...] = total
    model = total.shape[1]
    payload[:, :model] = normed_rows(total, gain[...])
    payload[:, model:] = extra[...]


def joined(part, other, gain, extra):
    rows, model = part.shape
    shapes = [like((rows, model), f32), like((rows, model + extra.shape[1]), bf16)]
    return on_device(joined_body, shapes, [part, other, extra, gain], 10 * rows * model)


def by_halves(refs):
    *own, packed = refs
    widths = [w.shape[1] for w in own]
    firsts = [sum(widths[:i]) for i in range(4)]
    other = [lambda f=f, w=w: packed[:, f : f + w] for f, w in zip(firsts, widths)]
    return [lambda w=w: w[...] for w in own], other


def other_heads_body(inputs, mask, gain, wq, wk, wv, wo, packed, qkv, heads):
    _, weights = by_halves((wq, wk, wv, wo, packed))
    head_group(normed_rows(wide(inputs[...]), gain[...]), mask[...], weights, qkv, heads)


def other_heads(inputs, mask, gain, weights, packed):
    rows = inputs.shape[0]
    width, out = sum(w.shape[1] for w in weights[:3]), weights[3].shape[1]
    shapes = [like((rows, width), bf16), like((rows, out), bf16)]
    return on_device(
        other_heads_body, shapes, [inputs, mask, gain], 2 * rows * packed.size, kept=[*weights, packed]
    )


def attention_body(fresh, arriving, mask, extra, gain, gain_two, *refs):
    own, other = by_halves(refs[:5])
    inputs, hidden, payload, qkv0, qkv1, heads0, heads1 = refs[5:]
    rows = fresh[...] + arriving[...]
    inputs[...] = rows
    total = wide(rows)
    normed = normed_rows(total, gain[...])
    total = total + head_group(normed, mask[...], own, qkv0, heads0)
    total = total + head_group(normed, mask[...], other, qkv1, heads1)
    hidden[...] = total
    model = total.shape[1]
    payload[:, :model] = normed_rows(total, gain_two[...])
    payload[:, model:] = extra[...]


def attention_forward(fresh, arriving, mask, gain, gain_two, extra, weights, packed):
    rows, model = fresh.shape
    width, out = sum(w.shape[1] for w in weights[:3]), weights[3].shape[1]
    shapes = [
        like((rows, model), bf16), like((rows, model), f32), like((rows, model + extra.shape[1]), bf16),
        like((rows, width), bf16), like((rows, width), bf16), like((rows, out), bf16), like((rows, out), bf16),
    ]
    args = [fresh, arriving, mask, extra, gain, gain_two]
    outs = on_device(attention_body, shapes, args, 4 * rows * packed.size, kept=[*weights, packed])
    inputs, hidden, payload, qkv0, qkv1, heads0, heads1 = outs
    return inputs, hidden, payload, [(qkv0, heads0), (qkv1, heads1)]


def attention_back_body(grad, grad_two, inputs, hidden, mask, q0, q1, gain, gain_two, *refs):
    own, other = by_halves(refs[:5])
    grad_input, grad_input_low, grad_low, normed, g0, g1, gain_grad, gain_two_grad = refs[5:]
    rows = inputs.shape[0]
    values = wide(inputs[...])
    normed[...] = normed_rows(values, gain[...])
    total = hidden[...]
    back, gain_two_grad[...] = norm_back(total, norm_factor(total), gain_two[...], grad_two[...])
    grad_hidden = wide(grad[...]) + back
    low = grad_hidden.astype(bf16)
    grad_low[...] = low
    grad_normed = jnp.zeros_like(grad_hidden)
    for qkv, weights, grad_qkv in ((q0, own, g0), (q1, other, g1)):
        query, key, value, probs = group_probs(qkv[...], mask[...])
        grad_heads = stack_heads(dot_nn(low, weights[3]()).astype(bf16))
        grad_probs = dot_nt(grad_heads, value)
        inner = jnp.sum(probs * grad_probs, axis=1, keepdims=True)
        grad_scores = (probs * (grad_probs - inner) * HEAD_SIZE ** (-0.5)).astype(bf16)
        grads = [
            spread_heads(dot_nn(grad_scores, key).astype(bf16), rows),
            dot_tn(grad_scores, query).astype(bf16),
            dot_tn(probs.astype(bf16), grad_heads).astype(bf16),
        ]
        at = 0
        for part, w in zip(grads, weights):
            grad_qkv[:, at : at + part.shape[1]] = part
            at += part.shape[1]
            grad_normed = grad_normed + dot_nt(part, w())
    back, gain_grad[...] = norm_back(values, norm_factor(values), gain[...], grad_normed)
    result = grad_hidden + back
    grad_input[...] = result
    grad_input_low[...] = result.astype(bf16)


def attention_backward(grad, grad_two, inputs, hidden, mask, gain, gain_two, projected, weights, packed):
    rows, model = inputs.shape
    width = projected[0].shape[1]
    shapes = [
        like((rows, model), f32), like((rows, model), bf16), like((rows, model), bf16),
        like((rows, model), bf16), like((rows, width), bf16), like((rows, width), bf16),
        like((1, model), f32), like((1, model), f32),
    ]
    args = [grad, grad_two, inputs, hidden, mask, *projected, gain, gain_two]
    return on_device(attention_back_body, shapes, args, 8 * rows * packed.size, kept=[*weights, packed])


def place(copies, pieces, *targets):
    started, at = [], 0
    for piece in pieces:
        first, count = 0, piece.shape[0]
        for target in targets:
            source = piece.at[:, pl.ds(first, target.shape[1])]
            started.append(copies.start(source, target.at[pl.ds(at, count), :]))
            first += target.shape[1]
        at += count
    return started


def pair_gates(extra, width):
    me, peers = lax.axis_index("dp"), lax.axis_size("dp")
    lane = lax.broadcasted_iota(jnp.int32, extra.shape, 1)

    def gate(expert):
        return jnp.sum(jnp.where((lane == expert) | (lane == expert + peers), wide(extra), 0.0), axis=1, keepdims=True)

    column = lax.broadcasted_iota(jnp.int32, (extra.shape[0], width), 1)
    return jnp.where(column < width // 2, gate(me), gate(me ^ 1))


def expert_stage_body(count, w_gate, w_up, w_down, *refs):
    ins, (gate_out, up_out), outs = refs[:count], refs[count : count + 2], refs[count + 2 : 2 * count + 2]
    rows, extra, gate_held, up_held, part, sems = refs[2 * count + 2 :]
    copies, leaving = Copies(sems), []
    for copy in place(copies, ins, rows, extra):
        copy.wait()
    values = rows[...]
    gate = dot_nn(values, w_gate[...])
    up = dot_nn(values, w_up[...])
    gate_held[...] = gate.astype(bf16)
    leaving.append(copies.start(gate_held, gate_out))
    up_held[...] = up.astype(bf16)
    leaving.append(copies.start(up_held, up_out))
    act = gate / (1.0 + jnp.exp(-gate)) * up * pair_gates(extra[...], gate.shape[1])
    part[...] = dot_nn(act.astype(bf16), w_down[...]).astype(bf16)
    at = 0
    for out in outs:
        leaving.append(copies.start(part.at[pl.ds(at, out.shape[0]), :], out))
        at += out.shape[0]
    for copy in leaving:
        copy.wait()


def expert_stage(pieces, *weights):
    count = sum(p.shape[0] for p in pieces)
    model, units = weights[0].shape
    extra = pieces[0].shape[1] - model
    shapes = [like((count, units), bf16)] * 2 + [like((p.shape[0], model), bf16) for p in pieces]
    scratch = [pltpu.VMEM((count, n), bf16) for n in (model, extra, units, units, model)]
    scratch.append(pltpu.SemaphoreType.DMA((3 * len(pieces) + 2,)))
    body = functools.partial(expert_stage_body, len(pieces))
    outs = on_device(
        body, shapes, [], 6 * count * weights[0].size, kept=weights, far=pieces, scratch=scratch, direct=True
    )
    return outs[2:], (pieces, *outs[:2])


def expert_back_body(count, w_gate, w_up, w_down, *refs):
    ins, payloads, (gate_in, up_in) = refs[:count], refs[count : 2 * count], refs[2 * count : 2 * count + 2]
    grad_outs, outs = refs[2 * count + 2 : 2 * count + 5], refs[2 * count + 5 : 3 * count + 5]
    grads, extra, gate_held, up_held, *held_back, part, sems = refs[3 * count + 5 :]
    copies, leaving, first = Copies(sems), [], w_gate.shape[0]
    arriving = place(copies, ins, grads)
    at = 0
    for payload in payloads:
        size = payload.shape[0]
        arriving.append(
            copies.start(payload.at[:, pl.ds(first, extra.shape[1])], extra.at[pl.ds(at, size), :])
        )
        at += size
    arriving += [copies.start(gate_in, gate_held), copies.start(up_in, up_held)]
    for copy in arriving:
        copy.wait()
    scale = pair_gates(extra[...], w_gate.shape[1])
    grad_act = scale * dot_nt(grads[...], w_down[...])
    gate, up = wide(gate_held[...]), wide(up_held[...])
    sig = 1.0 / (1.0 + jnp.exp(-gate))
    silu = gate * sig
    low_gate = (grad_act * up * sig * (1.0 + gate * (1.0 - sig))).astype(bf16)
    low_up = (grad_act * silu).astype(bf16)
    for value, held_value, out in zip((low_gate, low_up, (scale * silu * up).astype(bf16)), held_back, grad_outs):
        held_value[...] = value
        leaving.append(copies.start(held_value, out))
    part[...] = (dot_nt(low_gate, w_gate[...]) + dot_nt(low_up, w_up[...])).astype(bf16)
    at = 0
    for out in outs:
        leaving.append(copies.start(part.at[pl.ds(at, out.shape[0]), :], out))
        at += out.shape[0]
    for copy in leaving:
        copy.wait()


def expert_back_stage(pieces, saved, *weights):
    payloads, gate_out, up_out = saved
    count = sum(p.shape[0] for p in pieces)
    model, units = weights[0].shape
    extra = payloads[0].shape[1] - model
    shapes = [like((count, units), bf16)] * 3 + [like((p.shape[0], model), bf16) for p in pieces]
    scratch = [pltpu.VMEM((count, n), bf16) for n in (model, extra, units, units, units, units, units, model)]
    scratch.append(pltpu.SemaphoreType.DMA((3 * len(pieces) + 5,)))
    body = functools.partial(expert_back_body, len(pieces))
    far = [*pieces, *payloads, gate_out, up_out]
    outs = on_device(
        body, shapes, [], 6 * count * weights[0].size, kept=weights, far=far, scratch=scratch, direct=True
    )
    return outs[3:], (payloads, pieces, *outs[:3])


def swept_products(swept, fixed, sums, swept_left, final):
    width = fixed[0][0].shape[1]
    step, steps = width // 2, 4
    rows = sum(t.shape[0] for t in swept)

    def body(*refs):
        refs = list(refs)
        left = jnp.concatenate([refs.pop(0)[...] for _ in swept], axis=0)
        rights = [jnp.concatenate([refs.pop(0)[...] for _ in group], axis=0) for group in fixed]
        totals = [refs.pop(0)[...] for _ in sums or ()] or [0.0] * len(fixed)
        others = []
        for total, right in zip(totals, rights):
            total = total + (dot_tn(left, right) if swept_left else dot_tn(right, left))
            if final:
                parts = (total[:, :step], total[:, step:]) if swept_left else (total[:step], total[step:])
                refs.pop(0)[...] = parts[0]
                others.append(parts[1].astype(bf16))
            else:
                refs.pop(0)[...] = total
        if final:
            refs.pop(0)[...] = jnp.concatenate(others, axis=1 if swept_left else 0)

    def spec(size):
        return pl.BlockSpec((step, size), lambda j: (j, 0)) if swept_left else pl.BlockSpec((size, step), lambda j: (0, j))

    def shape(size):
        return (step * steps, size) if swept_left else (size, step * steps)

    sizes = [(step if final else width, f32)] * len(fixed) + [(step * len(fixed), bf16)] * final
    shapes = [like(shape(size), dtype) for size, dtype in sizes]
    out_specs = [spec(size) for size, _ in sizes]
    in_specs = [pl.BlockSpec((t.shape[0], step), lambda j: (0, j)) for t in swept]
    in_specs += [pl.BlockSpec(t.shape, lambda j: (0, 0)) for group in fixed for t in group]
    in_specs += [spec(width) for _ in sums or ()]
    return pl.pallas_call(
        body,
        grid=(steps,),
        out_shape=shapes,
        in_specs=in_specs,
        out_specs=out_specs,
        compiler_params=pltpu.CompilerParams(vmem_limit_bytes=KERNEL_VMEM),
        cost_estimate=pl.CostEstimate(flops=COST * 2 * rows * width * step * steps * len(fixed), bytes_accessed=rows, transcendentals=0),
    )(*map(distant, [*swept, *[t for group in fixed for t in group], *(sums or ())]))


def expert_forward(rows, w_gate, w_up, w_down):
    gate_out = dot_nn(rows, w_gate)
    up_out = dot_nn(rows, w_up)
    act = (gate_out / (1.0 + jnp.exp(-gate_out)) * up_out).astype(bf16)
    part = dot_nn(act, w_down).astype(bf16)
    return part, (rows, gate_out.astype(bf16), up_out.astype(bf16))


def expert_backward(grad_rows, saved, w_gate, w_up, w_down):
    rows, gate_low, up_low = saved
    gate_out, up_out = wide(gate_low), wide(up_low)
    grad_act = dot_nt(grad_rows, w_down)
    sig = 1.0 / (1.0 + jnp.exp(-gate_out))
    silu = gate_out * sig
    grad_gate = (grad_act * up_out * sig * (1.0 + gate_out * (1.0 - sig))).astype(bf16)
    grad_up = (grad_act * silu).astype(bf16)
    act = (silu * up_out).astype(bf16)
    grad_in = (dot_nt(grad_gate, w_gate) + dot_nt(grad_up, w_up)).astype(bf16)
    return grad_in, (dot_tn(rows, grad_gate), dot_tn(rows, grad_up), dot_tn(act, grad_rows))


def halves(array):
    half = array.shape[0] // 2
    return array[:half], array[half:]


def owned_body(turns, groups, blocks, with_last, gains, *refs):
    refs = list(refs)
    lefts = [refs.pop(0) for _ in range(turns)]
    rights = [[refs.pop(0) for _ in range(turns + with_last)] for _ in range(groups)]
    last = [refs.pop(0) for _ in range(4 * with_last)]
    gains = [refs.pop(0)[...] for _ in range(gains)]
    outs, products, sems = refs[: 2 * len(blocks)], refs[-2], refs[-1]
    values = [t[...] for t in lefts]
    if with_last:
        grad, grad_two, hidden, gain = last
        total = hidden[...]
        back, _ = norm_back(total, norm_factor(total), gain[...], grad_two[...])
        values.append((wide(grad[...]) + back).astype(bf16))
    left = jnp.concatenate(values, axis=0)
    for g in range(groups):
        right = jnp.concatenate([t[...] for t in rights[g]], axis=0)
        products[g, :, : right.shape[1]] = dot_tn(left, right).astype(bf16)
        if gains:
            terms, at = [], right.shape[1]
            for gain in gains:
                high = gain.astype(bf16)
                terms += [high, (gain - wide(high)).astype(bf16)]
            rows = jnp.concatenate(terms + [jnp.zeros_like(terms[0])] * (-len(terms) % 16), axis=0)
            which = lax.broadcasted_iota(jnp.int32, (rows.shape[0], 128), 0)
            column = lax.broadcasted_iota(jnp.int32, (rows.shape[0], 128), 1)
            chosen = (column == (which // 2) % 2) & (which < len(terms))
            products[g, :, at : at + 128] = dot_tn(rows, jnp.where(chosen, 1.0, 0.0).astype(bf16)).astype(bf16)
    copies, leaving = Copies(sems), []
    me = lax.axis_index("dp")
    share = products.shape[1] // lax.axis_size("dp")
    for i, group in enumerate(blocks):
        for out, places in zip(outs[2 * i : 2 * i + 2], group):
            for j, (mask, side) in enumerate(places):
                rows = pl.ds(pl.multiple_of((me ^ mask) * share, share), share)
                leaving.append(copies.start(products.at[side, rows, :], out.at[pl.ds(j * share, share), :]))
    for copy in leaving:
        copy.wait()


def owned_products(cube, lefts, rights, last=(), gains=()):
    model, width = lefts[0].shape[1], rights[0][0].shape[1] + (128 if gains else 0)
    share = model // lax.axis_size("dp")
    stages = [[[(m ^ int(i), s) for m, s in side for i in cube.inner] for side in pair] for pair in cube.stages]
    own, near, middle, corner = stages
    blocks = [middle, [a + b + c for a, b, c in zip(own, near, corner)]]
    shapes = [like((len(places) * share, width), bf16) for pair in blocks for places in pair]
    scratch = [
        pltpu.VMEM((len(rights), model, width), bf16),
        pltpu.SemaphoreType.DMA((sum(len(places) for pair in blocks for places in pair),)),
    ]
    args = [*lefts, *[t for group in rights for t in group], *last, *gains]
    outs = pl.pallas_call(
        functools.partial(owned_body, len(lefts), len(rights), blocks, 1 if last else 0, len(gains)),
        out_shape=shapes,
        in_specs=[VMEM] * len(args),
        out_specs=[ANY] * len(shapes),
        scratch_shapes=scratch,
        compiler_params=pltpu.CompilerParams(vmem_limit_bytes=KERNEL_VMEM),
    )(*map(distant, args))
    return [(outs[2 * i], outs[2 * i + 1]) for i in range(len(blocks))]


class Blocks:
    def __init__(self, cube, weights):
        self.cube, self.weights = cube, weights

    def forward(self, payload, micro, side=()):
        saved = [None] * 4

        def work(stage, pieces):
            parts, saved[stage] = expert_stage(pieces, *self.weights)
            return parts

        return gather_rows(self.cube, payload, work, side), saved

    def backward(self, grad, micro, saved, side=()):
        keeps = [None] * 4

        def work(stage, pieces):
            parts, keeps[stage] = expert_back_stage(pieces, saved[stage], *self.weights)
            return parts

        return gather_rows(self.cube, grad, work, side), keeps

    def late_backward(self, pieces, saved):
        parts, keeps = [None] * 4, [None] * 4

        def run(*stages):
            def work(*gathered):
                for stage, rows in zip(stages, gathered):
                    parts[stage], keeps[stage] = expert_back_stage(rows, saved[stage], *self.weights)
                return [t for stage in stages for t in parts[stage]]

            return lambda: [pieces[stage] for stage in stages], work

        return run, parts, keeps

    def total_start(self, results, side=()):
        own, near, middle, corner = results
        arrived, corner, (own, near) = reduce_start(self.cube, middle, corner, (own, near), side)
        return arrived, corner, [[t] for t in near], own

    def total_finish(self, state, side=()):
        return reduce_finish(self.cube, *state, side)

    def total(self, results, side=()):
        return self.total_finish(self.total_start(results, side[:1]), side[1:])

    def weight_sums(self, slots, sums, final=False):
        def stages():
            return [stage for keeps in slots for stage in keeps]

        def hidden(*args):
            payloads, gates, ups = args
            sums[0] = swept_products(payloads, [gates, ups], sums[0], True, final)
            return sums[0]

        def down(*args):
            grads, acts = args
            sums[1] = swept_products(grads, [acts], sums[1], False, final)
            return sums[1]

        return [
            (lambda: [[t for s in stages() for t in s[0]], [s[2] for s in stages()], [s[3] for s in stages()]], hidden),
            (lambda: [[t for s in stages() for t in s[1]], [s[4] for s in stages()]], down),
        ]


def run_all(side):
    for thunk in side:
        if thunk is not None:
            thunk[1](*thunk[0]())


class Buckets:
    def __init__(self, cube, weights, routes, gates, capacity):
        self.cube, self.weights, self.capacity = cube, weights, capacity
        micros, self.rows, self.top = routes.shape
        self.experts = lax.axis_size("dp")
        self.tables = []
        for m in range(micros):
            flat = routes[m].reshape(-1)
            onehot = (flat[:, None] == jnp.arange(self.experts, dtype=jnp.int32)).astype(jnp.int32)
            earlier = jnp.cumsum(onehot, axis=0) - onehot
            target = flat * capacity + jnp.sum(earlier * onehot, axis=1)
            source = jnp.full((self.experts * capacity,), flat.shape[0], jnp.int32)
            source = source.at[target].set(jnp.arange(flat.shape[0], dtype=jnp.int32))
            self.tables.append((target, source, gates[m]))

    def table(self, micro):
        return jax.tree.map(lambda a, b: jnp.where(micro == 0, a, b), self.tables[0], self.tables[1])

    def exchange(self, rows):
        shape = (self.experts, self.capacity, rows.shape[1])
        moved = lax.all_to_all(rows.reshape(shape), "dp", split_axis=0, concat_axis=0, tiled=True)
        return moved.reshape(rows.shape)

    def whole(self, own):
        return jnp.concatenate([own, swap(own, self.cube.z)], axis=0)

    def forward(self, payload, micro, side=()):
        target, source, gates = self.table(micro)
        own = payload[:, : self.weights[0].shape[0]]
        padded = jnp.pad(self.whole(own), ((0, 1), (0, 0)))
        arrived = self.exchange(jnp.take(padded, source // self.top, axis=0))
        part, saved = expert_forward(arrived, *self.weights)
        picked = jnp.take(self.exchange(part), target, axis=0).reshape(self.rows, self.top, -1)
        run_all(side)
        return jnp.sum(gates[:, :, None] * picked, axis=1), saved

    def backward(self, grad, micro, saved, side=()):
        target, source, gates = self.table(micro)
        scaled = (gates[:, :, None] * wide(self.whole(grad))[:, None, :]).astype(bf16)
        padded = jnp.pad(scaled.reshape(self.rows * self.top, -1), ((0, 1), (0, 0)))
        arrived = self.exchange(jnp.take(padded, source, axis=0))
        grad_in, weights = expert_backward(arrived, saved, *self.weights)
        picked = jnp.take(self.exchange(grad_in), target, axis=0).reshape(self.rows, self.top, -1)
        run_all(side)
        return jnp.sum(picked, axis=1, dtype=f32), weights

    def total_start(self, results, side=()):
        run_all(side)
        return results

    def total_finish(self, results, side=()):
        own, other = halves(results.astype(bf16))
        run_all(side)
        return wide(own) + wide(swap(other, self.cube.z))

    def total(self, results, side=()):
        return self.total_finish(results, side)

    def weight_sums(self, slots, sums, final=False):
        def add(*slots):
            for weights in slots:
                for i, part in enumerate((list(weights[:2]), list(weights[2:]))):
                    sums[i] = part if sums[i] is None else [a + b for a, b in zip(sums[i], part)]

        return [None, (lambda: slots, add)]


def local(
    tokens, lengths, routes, gates, attn_gain, q_weight, key_projection, value_projection,
    o_weight, mlp_gain, expert_gate, expert_up, expert_down, cotangent,
):
    cube = Cube()
    section = lax.axis_index("section")
    shard = lax.axis_index("shard")
    me = lax.axis_index("dp")
    peers, shards = lax.axis_size("dp"), lax.axis_size("shard")
    _, block_rows, model = tokens.shape
    rows = block_rows // shards
    share = model // peers
    first = section == 0
    gain_one, gain_two = attn_gain[0][None], mlp_gain[0][None]
    weights = [q_weight[0], key_projection[0], value_projection[0], o_weight[0]]
    expert_w = (expert_gate[0, 0], expert_up[0, 0], expert_down[0, 0])
    capacity = 2 * block_rows * routes.shape[3] // peers
    whole_blocks = capacity >= block_rows

    def chosen(here, there):
        return jax.tree.map(lambda a, b: jnp.where(first, a, b), here, there)

    def begins(lens):
        lens = lens[:, 0]
        ends, longest = jnp.cumsum(lens, axis=1), jnp.argmax(lens, axis=1)
        return [ends[m, longest[m]] - lens[m, longest[m]] for m in range(2)]

    def turned(array, begin):
        doubled = jnp.concatenate([array, array], axis=0)
        return lax.dynamic_slice_in_dim(doubled, (begin + rows * shard) % block_rows, block_rows, 0)

    if not whole_blocks:
        early = begins(lengths)
        mixture = Buckets(
            cube,
            expert_w,
            jnp.stack([turned(routes[0, m], early[m]) for m in range(2)]),
            jnp.stack([turned(gates[0, m], early[m]) for m in range(2)]),
            capacity,
        )

    slices = [lax.dynamic_slice_in_dim(w, me * share, share, 0) for w in weights]
    qkv_slices = swap(jnp.concatenate(slices[:3], axis=1), cube.z)
    out_slices = slices[3]
    half_share = share // 2
    mask = cube.x[1] | cube.y[1]
    far_places = [2 * (me ^ mask), 2 * (me ^ mask) + 1]
    plane_places = [2 * (me ^ m) for m in (0, cube.x[1], cube.y[1])]
    mate_bit = cube.core[1]

    def mate_places(places):
        return [p ^ (2 * mate_bit) for p in places]

    def placed(own, m):
        half = model // shards
        kept = lax.dynamic_slice_in_dim(own, shard * half, half, 1)
        given = lax.dynamic_slice_in_dim(own, (1 - shard) * half, half, 1)
        got = swap(given, cube.z)
        low = jnp.where(shard == 0, kept, got)
        high = jnp.where(shard == 0, got, kept)
        return lax.dynamic_slice_in_dim(
            jnp.concatenate([low, high, low, high], axis=0), (block_rows - starts[m]) % block_rows, block_rows, 0
        )

    route_cols = [routes[0, m].T for m in range(2)]
    gate_cols = [gates[0, m].T for m in range(2)]
    cot_own, cot_other = turned_block(lengths, cotangent)
    opened, mask0 = opening(lengths, tokens, gain_one, weights)
    settled = [tokens, cotangent, route_cols, gate_cols]
    mate_w = [swap(w, cube.core) for w in expert_w] if whole_blocks else []
    opened, qkv_slices, cots, settled, mate_w = together(
        (opened, qkv_slices, (cot_own, cot_other), settled, mate_w)
    )
    inputs, part, qkv, heads, sent = opened
    cot_own, cot_other = cots
    own_near = [swap(cot_own, d) for d in (cube.x, cube.y)] if whole_blocks else []
    if whole_blocks:
        expert_w = pinned(list(zip(expert_w, mate_w)), (1, 1, 0))
    arrived, own_near, settled, expert_w = together(
        (swap(sent, cube.z), own_near, settle(lengths, *settled), expert_w)
    )
    fresh1, cot1, mask1, extra0, extra1, starts = settled
    hidden, payload = joined(part, arrived, gain_two, extra0)
    if whole_blocks:
        mixture = Blocks(cube, expert_w)
        plane = []

        def first_plane(qkv_slices, out_slices):
            near = [qkv_slices] + [swap(qkv_slices, d) for d in (cube.x, cube.y, ("dp", mask))]
            plane.extend([near, swap(out_slices, cube.z)])
            return plane

        side = [None, None, (lambda: [qkv_slices, out_slices], first_plane)]
        results, saved = mixture.forward(payload, 0, side)
        qkv_near, out_slices = plane
    else:
        results, saved = mixture.forward(payload, 0)
    first_mates = []

    def first_exchange(*near):
        first_mates.extend(swap(t, cube.core) for t in near)
        return first_mates

    mids = []

    def first_choice(*both_micros):
        mids.append(chosen(both_micros[2:], both_micros[:2]))
        return mids

    choice = (lambda: [mask0, extra0, mask1, extra1], first_choice)
    total = mixture.total(results, [both((lambda: qkv_near, first_exchange), choice) if whole_blocks else choice])
    result0 = (hidden + total).astype(bf16)
    if whole_blocks:
        result0, qkv_near, out_slices, cot_other = together((result0, qkv_near, out_slices, cot_other))
        arriving = lax.ppermute(result0, "section", [(0, 1)])
        out_near = [out_slices] + [swap(out_slices, d) for d in (cube.x, cube.y, ("dp", mask))]
        other_near = [swap(cot_other, d) for d in (cube.x, cube.y)]
        arriving, out_near, other_near, weights = together((arriving, out_near, other_near, pinned(weights)))
        qkv_mates, out_mates = first_mates, [swap(t, cube.core) for t in out_near]
        all_places = [*plane_places, far_places[0]]
        width = qkv_slices.shape[1]
        spans, pieces = [], []
        for group, places, column in (
            (qkv_near, all_places, 0), (qkv_mates, mate_places(all_places), 0),
            (out_near, all_places, width), (out_mates, mate_places(all_places), width),
        ):
            pieces += group
            spans += [(p, half_share, column) for p in places]
        packed = put_together(pieces, spans, (model, width + out_slices.shape[1]))
    else:
        arriving = lax.ppermute(result0, "section", [(0, 1)])
        packed = lax.all_gather(
            jnp.concatenate([qkv_slices, swap(out_slices, cube.z)], axis=1), "dp", axis=0, tiled=True
        )
    state0 = [inputs, hidden, mask0, None, saved]

    mask_mid, extra_mid = mids[0]

    inputs1, hidden1, payload, groups1 = attention_forward(
        fresh1, arriving, mask_mid, gain_one, gain_two, extra_mid, weights, packed
    )
    def first_groups(*args):
        groups = other_heads(*args)
        state0[3] = [(qkv, heads), tuple(groups)]
        return groups

    micro_mid = 1 - section
    late = []

    def cot_far(x0, y1):
        late.extend([swap(x0, cube.y), swap(y1, cube.x)])
        return late

    side = [(lambda: [inputs, mask0, gain_one, weights, packed], first_groups)]
    if whole_blocks:
        (x0, y0), (x1, y1) = own_near, other_near
        side += [None, (lambda: [x0, y1], cot_far)]
    results, saved1 = mixture.forward(payload, micro_mid, side)

    grad0 = cot_own
    if whole_blocks:
        pieces = [[cot_own], [x0, y0, cot_other], [late[0], y1, x1], [late[1]]]
        run, back_results, keeps0 = mixture.late_backward(pieces, saved1)
        total = mixture.total(results, [run(2), run(1, 0)])
        back_results[3] = run(3)
    else:
        back_results, keeps0 = mixture.backward(grad0, micro_mid, saved1)
        total = mixture.total(results)
    result1 = (hidden1 + total).astype(bf16)

    slot2 = []

    def last_attention(arriving):
        zero = jnp.zeros((rows, model), bf16)
        slot2.extend(
            attention_forward(zero, arriving, mask1, gain_one, gain_two, extra1, weights, packed)
        )
        return slot2

    arrived = []

    def second_handoff(result):
        arrived.append(lax.ppermute(result, "section", [(0, 1)]))
        return arrived

    if whole_blocks:
        result1, back_results[:3] = together((result1, back_results[:3]))
    else:
        result1, back_results = together((result1, back_results))
    state = mixture.total_start(back_results, [(lambda: [result1], second_handoff)])
    grad_two = mixture.total_finish(state, [(lambda: arrived, last_attention)])
    inputs2, hidden2, payload, groups2 = slot2

    def attention_turn(grad, grad_two, state):
        inputs, hidden, mask, groups, _ = state
        outs = attention_backward(
            grad, grad_two, inputs, hidden, mask, gain_one, gain_two, [g[0] for g in groups], weights, packed
        )
        grad_input, low, grad_low, normed, g0, g1, attn_g, mlp_g = outs
        factors = (normed, grad_low, (g0, g1), [g[1] for g in groups])
        return grad_input, low, factors, (attn_g, mlp_g)

    state1 = [inputs1, hidden1, mask_mid, groups1, saved1]
    turn0, returned = [], []

    def first_turn(grad_two):
        turn0.extend(attention_turn(grad0, grad_two, state1))
        return turn0

    def first_return(low):
        returned.append(lax.ppermute(low, "section", [(1, 0)]))
        return returned

    side = [(lambda: [grad_two], first_turn), None, (lambda: [turn0[1]], first_return)]
    results2, saved2 = mixture.forward(payload, 1, side)
    coming = returned[0]
    state2 = [inputs2, hidden2, mask1, groups2, saved2]

    sums = [None, None]
    if whole_blocks:
        *results2, corner = results2
        coming, results2, inputs = together((coming, results2, corner[0]()))
        corner = corner[1](*inputs)
        results2 = [*results2, (lambda: [corner], lambda t: t)]
    else:
        coming, results2, saved2 = together((coming, results2, saved2))
    state2[4] = saved2
    grad1 = coming + cot1
    state_mid = chosen(state0, state2)
    back_results, keeps1 = mixture.backward(grad1, section, state_mid[4])
    placings = {}

    def placing(name, micro, own):
        def work(rows):
            placings[name, micro] = placed(rows, micro)
            return placings[name, micro]

        return lambda: [own()], work

    hidden_work, down_work = mixture.weight_sums([keeps0, keeps1], sums)
    grad_two = mixture.total(back_results, [placing("out", 0, lambda: chosen(result0, result1)), hidden_work])
    grad_two, down_inputs = together((grad_two, down_work[0]())) if down_work else (grad_two, ())
    turn1 = attention_turn(grad1, grad_two, state_mid)
    if whole_blocks:
        low, results2[:3] = together((turn1[1], list(results2[:3])))
    else:
        low, results2 = together((turn1[1], results2))
    coming = lax.ppermute(low, "section", [(1, 0)])
    state = mixture.total_start(results2)
    grad2, state, _ = together((coming, state, down_work[1](*down_inputs) if down_work else ()))

    last_total = []

    def finish_last(*state):
        last_total.append(mixture.total_finish(state[0] if len(state) == 1 else state))
        return last_total

    side = [None, None, (lambda: [state] if not whole_blocks else list(state), finish_last)]
    back_results, keeps2 = mixture.backward(grad2, 1 - section, saved1, side)
    result2 = (hidden2 + last_total[0]).astype(bf16)
    placing_out = placing("out", 1, lambda: chosen(result1, result2))
    placing_grad = placing("grad", 0, lambda: chosen(turn1[0], turn0[0]))
    hidden_end, down_end = mixture.weight_sums([keeps2], sums, True)
    ends = [w for w in (hidden_end, down_end) if w]
    grad_two = mixture.total(back_results, [both(placing_out, placing_grad), both(*ends)])
    expert_sums = [*sums[0][:2], sums[1][0]]
    others = [t for group in sums for t in group if t.dtype == bf16]

    inputs, hidden, _, groups, _ = state1
    heads_all = [[t[2][3][g] for t in (turn0, turn1)] + [groups[g][1]] for g in range(shards)]
    grad_two, others = together((grad_two, others))
    others = [swap(t, cube.core) for t in others]
    out_pairs = owned_products(cube, [turn0[2][1], turn1[2][1]], heads_all, (grad2, grad_two, hidden, gain_two))
    out_pairs, others = together((out_pairs, others))
    turn2 = []

    def last_turn(grad_two):
        turn2.extend(attention_turn(grad2, grad_two, state1))
        return turn2

    def exchange(*others):
        return [swap(t, cube.core) for t in others]

    def sums_start(pairs, side):
        middle, rest = pairs
        size = middle[0].shape[0] // 3

        def blocks(*terms):
            return [[t[i : i + size] for t in terms] for i in range(0, terms[0].shape[0], size)]

        middle = [low_sum(*terms) for terms in blocks(middle[0], swap(middle[1], cube.core))]
        other = (lambda: [rest[1]], lambda t: [swap(t, cube.core)])
        arrived, other, mine = reduce_start(cube, middle, other, rest[0], side)
        own, *near, corner = blocks(mine, *other)
        return arrived, corner, near, own

    def run_both(*works):
        works = [w for w in works if w]
        return both(*works) if works else None

    out_state = sums_start(out_pairs, [(lambda: [grad_two], last_turn)])
    turns = (turn0, turn1, turn2)
    factors = [t[2] for t in turns]
    qkv_pairs = []

    def qkv_products(*_):
        rights = [[f[2][g] for f in factors] for g in range(shards)]
        gains = [g for t in turns for g in t[3]]
        qkv_pairs.extend(owned_products(cube, [f[0] for f in factors], rights, gains=gains))
        return qkv_pairs

    grad_o = reduce_finish(cube, *out_state, [(lambda: [], qkv_products)])
    qkv_pairs, grad_o = together((qkv_pairs, grad_o))

    def last_sums(*others):
        if others:
            (gate, up), down = jnp.split(others[0], 2, axis=1), others[1]
            expert_sums[:] = [mine + wide(other) for mine, other in zip(expert_sums, (gate, up, down))]
        return expert_sums

    last_rows = placing("grad", 1, lambda: chosen(turn2[0], turn1[0]))
    qkv_state = sums_start(qkv_pairs, [both(last_rows, (lambda: others, last_sums))])
    grad_qkv = reduce_finish(cube, *qkv_state)
    gate_total, up_total, down_total = expert_sums
    width = q_weight.shape[2]
    grad_q = grad_qkv[:, :width]
    grad_k = grad_qkv[:, width : width + HEAD_SIZE]
    grad_v = grad_qkv[:, width + HEAD_SIZE : width + 2 * HEAD_SIZE]
    gain_pair = [grad_qkv[:, width + 2 * HEAD_SIZE + i] for i in range(2)]
    section_out = jnp.stack([placings["out", 0], placings["out", 1]])
    input_grad = jnp.stack([placings["grad", 0], placings["grad", 1]])
    return (
        section_out[None],
        input_grad[None],
        gain_pair[0][None],
        grad_q[None],
        grad_k[None],
        grad_v[None],
        grad_o[None],
        gain_pair[1][None],
        gate_total[None, None],
        up_total[None, None],
        down_total[None, None],
    )


def solution(mesh):
    in_specs = (
        P(None, "dp", None),
        P(None, "dp", None),
        P("section", None, "dp", None),
        P("section", None, "dp", None),
        P("section", None),
        P("section", None, "shard"),
        P("section", None, "shard"),
        P("section", None, "shard"),
        P("section", None, "shard"),
        P("section", None),
        P("section", "dp", None, "shard"),
        P("section", "dp", None, "shard"),
        P("section", "dp", "shard", None),
        P(None, "dp", None),
    )
    out_specs = (
        P("section", None, "dp", "shard"),
        P("section", None, "dp", "shard"),
        P("section", "dp"),
        P("section", "dp", "shard"),
        P("section", "dp", "shard"),
        P("section", "dp", "shard"),
        P("section", "dp", "shard"),
        P("section", "dp"),
        P("section", "dp", None, "shard"),
        P("section", "dp", None, "shard"),
        P("section", "dp", "shard", None),
    )
    return jax.shard_map(local, mesh=mesh, in_specs=in_specs, out_specs=out_specs, check_vma=False)
```

```python
import functools

import jax
import jax.numpy as jnp
import numpy as np
from jax import lax
from jax.experimental import pallas as pl
from jax.experimental.pallas import tpu as pltpu
from jax.sharding import PartitionSpec as P

HEAD_SIZE = 128
epsilon = 1e-06
masked_value = -1e30
bf16 = jnp.bfloat16
f32 = jnp.float32


def wide(a):
    return a.astype(f32)


def dot_nn(a, b):
    return lax.dot_general(a, b, (((1,), (0,)), ((), ())), preferred_element_type=f32)


def dot_nt(a, b):
    return lax.dot_general(a, b, (((1,), (1,)), ((), ())), preferred_element_type=f32)


def dot_tn(a, b):
    return lax.dot_general(a, b, (((0,), (0,)), ((), ())), preferred_element_type=f32)


class Cube:
    def __init__(self):
        peers = lax.axis_size("dp")
        bits = [1 << i for i in range(peers.bit_length() - 1)]
        rest = bits[1:]
        self.core = ("dp", bits[0])
        self.x = ("dp", rest[0])
        self.y = ("dp", rest[len(rest) // 2])
        self.z = ("shard", 1)
        self.extra = [("dp", b) for b in rest if b not in (self.x[1], self.y[1])]
        inner = [0]
        for _, bit in self.extra:
            inner = inner + [m | bit for m in inner]
        self.inner = np.array(inner)
        x, y = self.x[1], self.y[1]
        self.corner = (x | y, 1)
        stages = [[(0, 0)], [(x, 0), (y, 0), (0, 1)], [(x | y, 0), (y, 1), (x, 1)], [self.corner]]
        self.stages = [(g, [(m | self.core[1], s) for m, s in g]) for g in stages]


def swap(value, direction):
    axis, bit = direction
    return lax.ppermute(value, axis, [(i, i ^ bit) for i in range(lax.axis_size(axis))])


def across(value, cube):
    mask, flip = cube.corner
    shards = lax.axis_size("shard")
    pairs = [
        (d * shards + s, (d ^ mask) * shards + (s ^ flip))
        for d in range(lax.axis_size("dp"))
        for s in range(shards)
    ]
    return lax.ppermute(value, ("dp", "shard"), pairs)


together = lax.optimization_barrier


def both(*thunks):
    def work(*groups):
        return [thunk[1](*group) for thunk, group in zip(thunks, groups)]

    return lambda: [thunk[0]() for thunk in thunks], work


def after(payload, thunks, step):
    if step >= len(thunks) or thunks[step] is None:
        return payload, lambda: ()
    inputs, work = thunks[step]
    payload, inputs = together((payload, inputs()))
    return payload, lambda: work(*inputs)


def gather_rows(cube, own, work, side=()):
    own, beside = after(own, side, 0)
    near = [swap(own, d) for d in (cube.x, cube.y, cube.z)]
    first = work(0, [own])
    near, first, _ = together((near, first, beside()))

    near, beside = after(near, side, 1)
    middle = [swap(block, d) for block, d in zip(near, (cube.y, cube.z, cube.x))]
    second = work(1, near)
    middle, second, _ = together((middle, second, beside()))

    middle, beside = after(middle, side, 2)
    corner = swap(middle[0], cube.z)
    third = work(2, middle)
    corner, third, _ = together((corner, third, beside()))
    return first, second, third, (lambda: [corner], lambda *blocks: work(3, list(blocks)))


def low_sum(*terms):
    return sum(wide(t) for t in terms).astype(bf16)


def reduce_start(cube, middle, corner, rest, side=()):
    (middle, rest), beside = after((middle, rest), side, 0)
    middle, inputs = together((middle, corner[0]()))
    arrived = [swap(t, d) for t, d in zip(middle, (cube.y, cube.z, cube.x))]
    return together((arrived, corner[1](*inputs), rest, beside()))[:3]


def reduce_finish(cube, arrived, corner, near, own, side=()):
    sent = [low_sum(*corner)] + [low_sum(*terms, a) for terms, a in zip(near, arrived)]
    sent, beside = after(sent, side, 0)
    arrived = [swap(t, d) for t, d in zip(sent[1:], (cube.x, cube.y, cube.z))] + [across(sent[0], cube)]
    arrived, own, _ = together((arrived, own, beside()))
    total = sum(wide(t) for t in [*own, *arrived])
    for direction in reversed(cube.extra):
        half = total.shape[0] // 2
        total = total[:half] + wide(swap(total[half:].astype(bf16), direction))
    return total


def norm_factor(values):
    return lax.rsqrt(jnp.mean(values * values, axis=1, keepdims=True) + epsilon)


def norm_back(values, factor, gain, grad):
    gain_grad = jnp.sum(grad * values * factor, axis=0, keepdims=True)
    scaled = grad * gain
    inner = jnp.mean(scaled * values, axis=1, keepdims=True)
    return factor * (scaled - values * factor * factor * inner), gain_grad


def stack_heads(rows):
    return jnp.concatenate(
        [rows[:, i : i + HEAD_SIZE] for i in range(0, rows.shape[1], HEAD_SIZE)], axis=0
    )


def spread_heads(stacked, rows):
    return jnp.concatenate(
        [stacked[i : i + rows] for i in range(0, stacked.shape[0], rows)], axis=1
    )


def head_probs(query, key, allowed):
    scores = jnp.where(allowed > 0.0, dot_nt(query, key) * HEAD_SIZE ** (-0.5), masked_value)
    exp_scores = jnp.exp(scores - jnp.max(scores, axis=1, keepdims=True))
    return exp_scores / jnp.sum(exp_scores, axis=1, keepdims=True)


def normed_rows(values, gain):
    return (values * norm_factor(values) * gain).astype(bf16)


def group_probs(qkv, allowed):
    width = qkv.shape[1] - 2 * HEAD_SIZE
    query = stack_heads(qkv[:, :width])
    key, value = qkv[:, width : width + HEAD_SIZE], qkv[:, width + HEAD_SIZE :]
    tiled = jnp.concatenate([allowed] * (width // HEAD_SIZE), axis=0)
    return query, key, value, head_probs(query, key, tiled)


def head_group(normed, allowed, weights, qkv, heads):
    *projections, w_out = weights
    at = 0
    for w in projections:
        part = dot_nn(normed, w()).astype(bf16)
        qkv[:, at : at + part.shape[1]] = part
        at += part.shape[1]
    _, _, value, probs = group_probs(qkv[...], allowed)
    heads[...] = spread_heads(dot_nn(probs.astype(bf16), value).astype(bf16), normed.shape[0])
    return dot_nt(heads[...], w_out())


VMEM = pl.BlockSpec(memory_space=pltpu.VMEM)
SMEM = pl.BlockSpec(memory_space=pltpu.SMEM)
ANY = pl.BlockSpec(memory_space=pl.ANY)
KERNEL_VMEM = 42 << 20
COST = 16


def held(shape, dtype):
    return pltpu.VMEM(shape, dtype)


def like(shape, dtype):
    return pltpu.HBM(shape, dtype)


def close(value):
    return pltpu.with_memory_space_constraint(value, pltpu.VMEM)


def distant(value):
    return pltpu.with_memory_space_constraint(value, pltpu.HBM)


def pinned(groups, axes=None):
    groups = [g if isinstance(g, (list, tuple)) else (g,) for g in groups]
    axes = axes or [0] * len(groups)
    values = [v for g in groups for v in g]
    shapes = [
        tuple(n * len(g) if i == axis else n for i, n in enumerate(g[0].shape)) for g, axis in zip(groups, axes)
    ]

    def body(*refs):
        ins, outs, sems = list(refs[: len(values)]), refs[len(values) : -1], refs[-1]
        copies, waits = Copies(sems), []
        for group, axis, out in zip(groups, axes, outs):
            for i, value in enumerate(group):
                size = value.shape[axis]
                place = [slice(None)] * axis + [pl.ds(i * size, size)]
                waits.append(copies.start(ins.pop(0), out.at[tuple(place)]))
        for copy in waits:
            copy.wait()

    return pl.pallas_call(
        body,
        out_shape=[held(shape, g[0].dtype) for g, shape in zip(groups, shapes)],
        in_specs=[ANY] * len(values),
        out_specs=[VMEM] * len(groups),
        scratch_shapes=[pltpu.SemaphoreType.DMA((len(values),))],
        compiler_params=pltpu.CompilerParams(vmem_limit_bytes=1 << 20),
    )(*map(distant, values))


def put_together(pieces, spans, shape):
    starts = jnp.stack([first for first, _, _ in spans]).astype(jnp.int32)

    def body(starts, *refs):
        ins, out, sems = refs[:-2], refs[-2], refs[-1]
        copies, waits = Copies(sems), []
        for i, (piece, (_, unit, column)) in enumerate(zip(ins, spans)):
            rows = pl.ds(pl.multiple_of(starts[i] * unit, unit), piece.shape[0])
            waits.append(copies.start(piece, out.at[rows, pl.ds(column, piece.shape[1])]))
        for copy in waits:
            copy.wait()

    return pl.pallas_call(
        body,
        out_shape=held(shape, pieces[0].dtype),
        in_specs=[SMEM] + [ANY] * len(pieces),
        out_specs=VMEM,
        scratch_shapes=[pltpu.SemaphoreType.DMA((len(pieces),))],
        compiler_params=pltpu.CompilerParams(vmem_limit_bytes=KERNEL_VMEM),
    )(starts, *map(distant, pieces))


class Copies:
    def __init__(self, sems):
        self.sems, self.count = sems, 0

    def start(self, source, target):
        copy = pltpu.make_async_copy(source, target, self.sems.at[self.count])
        self.count += 1
        copy.start()
        return copy

    def fetch(self, source, target):
        copy, waited = self.start(source, target), []

        def value():
            if not waited:
                copy.wait()
                waited.append(True)
            return target[...]

        return value


def on_device(body, outs, args, flops, scalars=(), kept=(), far=(), scratch=(), direct=False):
    moved = sum(a.size * a.dtype.itemsize for a in args)
    return pl.pallas_call(
        body,
        out_shape=outs,
        in_specs=[SMEM] * len(scalars) + [VMEM] * (len(args) + len(kept)) + [ANY] * len(far),
        out_specs=[SMEM if o.dtype == jnp.int32 else ANY if direct else VMEM for o in outs],
        scratch_shapes=scratch,
        compiler_params=pltpu.CompilerParams(vmem_limit_bytes=KERNEL_VMEM),
        cost_estimate=pl.CostEstimate(flops=COST * flops, bytes_accessed=moved, transcendentals=0),
    )(*scalars, *map(distant, args), *map(close, kept), *far)


def holders(*arrays):
    return [pltpu.VMEM(a.shape, a.dtype) for a in arrays] + [pltpu.SemaphoreType.DMA((len(arrays) + 1,))]


def geometry(lens, micro, side, rows, block):
    ends, total, best, start = [], 0, lens[micro, 0, 0], 0
    for i in range(lens.shape[2]):
        length = lens[micro, 0, i]
        if i:
            start = jnp.where(length > best, total, start)
            best = jnp.maximum(best, length)
        total = total + length
        ends.append(total)
    return ends, lax.rem(start + rows * side, block)


def positions(shape, axis, begin, block):
    place = lax.broadcasted_iota(jnp.int32, shape, axis) + begin
    return jnp.where(place >= block, place - block, place)


def selection(begin, rows, block):
    wanted = positions((rows, block), 0, begin, block)
    return (wanted == lax.broadcasted_iota(jnp.int32, (rows, block), 1)).astype(f32)


def sequence_mask(ends, begin, rows, block):
    row, col = [positions((rows, rows), axis, begin, block) for axis in (0, 1)]
    inside = sum(jnp.abs((row >= e).astype(jnp.int32) - (col >= e).astype(jnp.int32)) for e in ends)
    return ((inside == 0) & (col <= row)).astype(f32)


def gate_columns(pick, routes, gates):
    peers = lax.axis_size("dp")
    expert = lax.broadcasted_iota(jnp.int32, (128, routes.shape[1]), 0)
    table = jnp.zeros(expert.shape, f32)
    for k in range(routes.shape[0]):
        gate, route = gates[k : k + 1, :], routes[k : k + 1, :]
        high = wide(gate.astype(bf16))
        table += jnp.where(expert == route, high, 0.0) + jnp.where(expert == route + peers, gate - high, 0.0)
    return dot_nt(pick, table.astype(bf16)).astype(bf16)


def turned_body(lens, blocks, own, other, block_rows, sems):
    copy = Copies(sems).fetch(blocks.at[0], block_rows)
    block = block_rows.shape[0]
    here = jnp.where(lax.axis_index("section") == 0, 0.0, 1.0)
    shard = lax.axis_index("shard")
    for side, out in ((shard, own), (1 - shard, other)):
        _, begin = geometry(lens, 0, side, block // 2, block)
        out[...] = dot_nn((selection(begin, block // 2, block) * here).astype(bf16), copy()).astype(bf16)


def turned_block(lens, blocks):
    _, block, model = blocks.shape
    scratch = [pltpu.VMEM((block, model), bf16), pltpu.SemaphoreType.DMA((1,))]
    shapes = [like((block // 2, model), bf16)] * 2
    return on_device(
        turned_body, shapes, [], 2 * block * block * model, (lens,), far=[distant(blocks)], scratch=scratch
    )


def opening_body(lens, gain, tokens, *refs):
    wq, wk, wv, wo, inputs, part, qkv, heads, sent, qkv_other, heads_other, mask, *scratch, sems = refs
    copies = Copies(sems)
    sources = [tokens.at[0], wq, wk, wv, wo]
    block_rows, *weights = [copies.fetch(a, b) for a, b in zip(sources, scratch)]
    block = tokens.shape[1]
    rows = block // 2
    shard = lax.axis_index("shard")
    first = jnp.where(lax.axis_index("section") == 0, 1.0, 0.0)
    sides = []
    for side in (shard, 1 - shard):
        ends, begin = geometry(lens, 0, side, rows, block)
        sides.append((selection(begin, rows, block) * first, sequence_mask(ends, begin, rows, block)))
    values = dot_nn(jnp.concatenate([pick for pick, _ in sides], axis=0).astype(bf16), block_rows())
    inputs[...] = values[:rows].astype(bf16)
    mask[...] = sides[0][1]
    normed = normed_rows(values, gain[...])
    *projections, w_out = weights
    projected = jnp.concatenate([dot_nn(normed, w()).astype(bf16) for w in projections], axis=1)
    both_heads = []
    for i, (to_qkv, to_heads) in enumerate(((qkv, heads), (qkv_other, heads_other))):
        to_qkv[...] = projected[i * rows : (i + 1) * rows]
        _, _, value, probs = group_probs(to_qkv[...], sides[i][1])
        to_heads[...] = spread_heads(dot_nn(probs.astype(bf16), value).astype(bf16), rows)
        both_heads.append(to_heads[...])
    result = dot_nt(jnp.concatenate(both_heads, axis=0), w_out())
    part[...] = values[:rows] + result[:rows]
    sent[...] = result[rows:].astype(bf16)


def opening(lens, tokens, gain, weights):
    _, block, model = tokens.shape
    rows = block // 2
    width, out = sum(w.shape[1] for w in weights[:3]), weights[3].shape[1]
    shapes = [
        like((rows, model), bf16), like((rows, model), f32), like((rows, width), bf16), like((rows, out), bf16),
        like((rows, model), bf16), like((rows, width), bf16), like((rows, out), bf16), like((rows, rows), f32),
    ]
    scratch = [pltpu.VMEM((block, model), bf16), *holders(*weights)]
    outs = on_device(
        opening_body, shapes, [gain], 4 * rows * model * (width + out), (lens,), far=[distant(t) for t in (tokens, *weights)], scratch=scratch
    )
    return outs[:5], outs[7]


def settle_body(lens, routes0, gates0, routes1, gates1, tokens, grad, *refs):
    fresh, cot, mask, extra0, extra1, starts, token_rows, grad_rows, sems = refs
    copies = Copies(sems)
    for micro in range(2):
        _, starts[micro] = geometry(lens, micro, 0, tokens.shape[1] // 2, tokens.shape[1])
    token_rows = copies.fetch(tokens.at[1], token_rows)
    grad_rows = copies.fetch(grad.at[1], grad_rows)
    block = tokens.shape[1]
    rows = block // 2
    first = jnp.where(lax.axis_index("section") == 0, 1.0, 0.0)
    for micro, routes, gates, extra in ((0, routes0, gates0, extra0), (1, routes1, gates1, extra1)):
        ends, begin = geometry(lens, micro, lax.axis_index("shard"), rows, block)
        pick = selection(begin, rows, block)
        extra[...] = gate_columns(pick.astype(bf16), routes[...], gates[...])
    fresh[...] = dot_nn((pick * first).astype(bf16), token_rows()).astype(bf16)
    cot[...] = dot_nn((pick * (1.0 - first)).astype(bf16), grad_rows()).astype(bf16)
    mask[...] = sequence_mask(ends, begin, rows, block)


def settle(lens, tokens, grad, routes, gates):
    _, block, model = tokens.shape
    rows = block // 2
    shapes = [like((rows, model), bf16)] * 2 + [like((rows, rows), f32)] + [like((rows, 128), bf16)] * 2
    shapes.append(pltpu.SMEM((2,), jnp.int32))
    args = [routes[0], gates[0], routes[1], gates[1]]
    scratch = [pltpu.VMEM((block, model), bf16)] * 2 + [pltpu.SemaphoreType.DMA((2,))]
    return on_device(
        settle_body, shapes, args, 2 * block * block * model, (lens,), far=[distant(tokens), distant(grad)], scratch=scratch
    )


def joined_body(part, other, extra, gain, hidden, payload):
    total = part[...] + wide(other[...])
    hidden[...] = total
    model = total.shape[1]
    payload[:, :model] = normed_rows(total, gain[...])
    payload[:, model:] = extra[...]


def joined(part, other, gain, extra):
    rows, model = part.shape
    shapes = [like((rows, model), f32), like((rows, model + extra.shape[1]), bf16)]
    return on_device(joined_body, shapes, [part, other, extra, gain], 10 * rows * model)


def by_halves(refs):
    *own, packed, packed_out = refs
    widths = [w.shape[1] for w in own[:3]]
    firsts = [sum(widths[:i]) for i in range(3)]
    other = [lambda f=f, w=w: packed[:, f : f + w] for f, w in zip(firsts, widths)]
    return [lambda w=w: w[...] for w in own], [*other, lambda: packed_out[...]]


def attention_body(fresh, arriving, mask, extra, gain, gain_two, *refs):
    own, other = by_halves(refs[:6])
    inputs, hidden, payload, qkv0, qkv1, heads0, heads1 = refs[6:]
    rows = fresh[...] + arriving[...]
    inputs[...] = rows
    total = wide(rows)
    normed = normed_rows(total, gain[...])
    total = total + head_group(normed, mask[...], own, qkv0, heads0)
    total = total + head_group(normed, mask[...], other, qkv1, heads1)
    hidden[...] = total
    model = total.shape[1]
    payload[:, :model] = normed_rows(total, gain_two[...])
    payload[:, model:] = extra[...]


def attention_forward(fresh, arriving, mask, gain, gain_two, extra, weights, packed):
    rows, model = fresh.shape
    width, out = sum(w.shape[1] for w in weights[:3]), weights[3].shape[1]
    shapes = [
        like((rows, model), bf16), like((rows, model), f32), like((rows, model + extra.shape[1]), bf16),
        like((rows, width), bf16), like((rows, width), bf16), like((rows, out), bf16), like((rows, out), bf16),
    ]
    args = [fresh, arriving, mask, extra, gain, gain_two]
    outs = on_device(attention_body, shapes, args, 6 * rows * packed[0].size, kept=[*weights, *packed])
    inputs, hidden, payload, qkv0, qkv1, heads0, heads1 = outs
    return inputs, hidden, payload, [(qkv0, heads0), (qkv1, heads1)]


def attention_back_body(grad, grad_two, inputs, hidden, mask, q0, q1, gain, gain_two, *refs):
    own, other = by_halves(refs[:6])
    grad_input, grad_input_low, grad_low, normed, g0, g1, gain_grad, gain_two_grad = refs[6:]
    rows = inputs.shape[0]
    values = wide(inputs[...])
    normed[...] = normed_rows(values, gain[...])
    total = hidden[...]
    back, gain_two_grad[...] = norm_back(total, norm_factor(total), gain_two[...], grad_two[...])
    grad_hidden = wide(grad[...]) + back
    low = grad_hidden.astype(bf16)
    grad_low[...] = low
    grad_normed = jnp.zeros_like(grad_hidden)
    for qkv, weights, grad_qkv in ((q0, own, g0), (q1, other, g1)):
        query, key, value, probs = group_probs(qkv[...], mask[...])
        grad_heads = stack_heads(dot_nn(low, weights[3]()).astype(bf16))
        grad_probs = dot_nt(grad_heads, value)
        inner = jnp.sum(probs * grad_probs, axis=1, keepdims=True)
        grad_scores = (probs * (grad_probs - inner) * HEAD_SIZE ** (-0.5)).astype(bf16)
        grads = [
            spread_heads(dot_nn(grad_scores, key).astype(bf16), rows),
            dot_tn(grad_scores, query).astype(bf16),
            dot_tn(probs.astype(bf16), grad_heads).astype(bf16),
        ]
        at = 0
        for part, w in zip(grads, weights):
            grad_qkv[:, at : at + part.shape[1]] = part
            at += part.shape[1]
            grad_normed = grad_normed + dot_nt(part, w())
    back, gain_grad[...] = norm_back(values, norm_factor(values), gain[...], grad_normed)
    result = grad_hidden + back
    grad_input[...] = result
    grad_input_low[...] = result.astype(bf16)


def attention_backward(grad, grad_two, inputs, hidden, mask, gain, gain_two, projected, weights, packed):
    rows, model = inputs.shape
    width = projected[0].shape[1]
    shapes = [
        like((rows, model), f32), like((rows, model), bf16), like((rows, model), bf16),
        like((rows, model), bf16), like((rows, width), bf16), like((rows, width), bf16),
        like((1, model), f32), like((1, model), f32),
    ]
    args = [grad, grad_two, inputs, hidden, mask, *projected, gain, gain_two]
    return on_device(attention_back_body, shapes, args, 12 * rows * packed[0].size, kept=[*weights, *packed])


def place(copies, pieces, *targets):
    started, at = [], 0
    for piece in pieces:
        first, count = 0, piece.shape[0]
        for target in targets:
            source = piece.at[:, pl.ds(first, target.shape[1])]
            started.append(copies.start(source, target.at[pl.ds(at, count), :]))
            first += target.shape[1]
        at += count
    return started


def pair_gates(extra, width):
    me, peers = lax.axis_index("dp"), lax.axis_size("dp")
    lane = lax.broadcasted_iota(jnp.int32, extra.shape, 1)

    def gate(expert):
        return jnp.sum(jnp.where((lane == expert) | (lane == expert + peers), wide(extra), 0.0), axis=1, keepdims=True)

    column = lax.broadcasted_iota(jnp.int32, (extra.shape[0], width), 1)
    return jnp.where(column < width // 2, gate(me), gate(me ^ 1))


def expert_stage_body(count, w_gate, w_up, w_down, *refs):
    ins, (gate_out, up_out), outs = refs[:count], refs[count : count + 2], refs[count + 2 : 2 * count + 2]
    rows, extra, gate_held, up_held, part, sems = refs[2 * count + 2 :]
    copies, leaving = Copies(sems), []
    for copy in place(copies, ins, rows, extra):
        copy.wait()
    values = rows[...]
    gate = dot_nn(values, w_gate[...])
    up = dot_nn(values, w_up[...])
    gate_held[...] = gate.astype(bf16)
    leaving.append(copies.start(gate_held, gate_out))
    up_held[...] = up.astype(bf16)
    leaving.append(copies.start(up_held, up_out))
    act = gate / (1.0 + jnp.exp(-gate)) * up * pair_gates(extra[...], gate.shape[1])
    part[...] = dot_nn(act.astype(bf16), w_down[...]).astype(bf16)
    at = 0
    for out in outs:
        leaving.append(copies.start(part.at[pl.ds(at, out.shape[0]), :], out))
        at += out.shape[0]
    for copy in leaving:
        copy.wait()


def expert_stage(pieces, *weights):
    count = sum(p.shape[0] for p in pieces)
    model, units = weights[0].shape
    extra = pieces[0].shape[1] - model
    shapes = [like((count, units), bf16)] * 2 + [like((p.shape[0], model), bf16) for p in pieces]
    scratch = [pltpu.VMEM((count, n), bf16) for n in (model, extra, units, units, model)]
    scratch.append(pltpu.SemaphoreType.DMA((3 * len(pieces) + 2,)))
    body = functools.partial(expert_stage_body, len(pieces))
    outs = on_device(
        body, shapes, [], 6 * count * weights[0].size, kept=weights, far=pieces, scratch=scratch, direct=True
    )
    return outs[2:], (pieces, *outs[:2])


def expert_back_body(count, w_gate, w_up, w_down, *refs):
    ins, payloads, (gate_in, up_in) = refs[:count], refs[count : 2 * count], refs[2 * count : 2 * count + 2]
    grad_outs, outs = refs[2 * count + 2 : 2 * count + 5], refs[2 * count + 5 : 3 * count + 5]
    grads, extra, gate_held, up_held, *held_back, part, sems = refs[3 * count + 5 :]
    copies, leaving, first = Copies(sems), [], w_gate.shape[0]
    arriving = place(copies, ins, grads)
    at = 0
    for payload in payloads:
        size = payload.shape[0]
        arriving.append(
            copies.start(payload.at[:, pl.ds(first, extra.shape[1])], extra.at[pl.ds(at, size), :])
        )
        at += size
    arriving += [copies.start(gate_in, gate_held), copies.start(up_in, up_held)]
    for copy in arriving:
        copy.wait()
    scale = pair_gates(extra[...], w_gate.shape[1])
    grad_act = scale * dot_nt(grads[...], w_down[...])
    gate, up = wide(gate_held[...]), wide(up_held[...])
    sig = 1.0 / (1.0 + jnp.exp(-gate))
    silu = gate * sig
    low_gate = (grad_act * up * sig * (1.0 + gate * (1.0 - sig))).astype(bf16)
    low_up = (grad_act * silu).astype(bf16)
    for value, held_value, out in zip((low_gate, low_up, (scale * silu * up).astype(bf16)), held_back, grad_outs):
        held_value[...] = value
        leaving.append(copies.start(held_value, out))
    part[...] = (dot_nt(low_gate, w_gate[...]) + dot_nt(low_up, w_up[...])).astype(bf16)
    at = 0
    for out in outs:
        leaving.append(copies.start(part.at[pl.ds(at, out.shape[0]), :], out))
        at += out.shape[0]
    for copy in leaving:
        copy.wait()


def expert_back_stage(pieces, saved, *weights):
    payloads, gate_out, up_out = saved
    count = sum(p.shape[0] for p in pieces)
    model, units = weights[0].shape
    extra = payloads[0].shape[1] - model
    shapes = [like((count, units), bf16)] * 3 + [like((p.shape[0], model), bf16) for p in pieces]
    scratch = [pltpu.VMEM((count, n), bf16) for n in (model, extra, units, units, units, units, units, model)]
    scratch.append(pltpu.SemaphoreType.DMA((3 * len(pieces) + 5,)))
    body = functools.partial(expert_back_body, len(pieces))
    far = [*pieces, *payloads, gate_out, up_out]
    outs = on_device(
        body, shapes, [], 6 * count * weights[0].size, kept=weights, far=far, scratch=scratch, direct=True
    )
    return outs[3:], (payloads, pieces, *outs[:3])


def swept_products(swept, fixed, sums, swept_left, final):
    width = fixed[0][0].shape[1]
    step, steps = width // 2, 4
    rows = sum(t.shape[0] for t in swept)

    def body(*refs):
        refs = list(refs)
        left = jnp.concatenate([refs.pop(0)[...] for _ in swept], axis=0)
        rights = [jnp.concatenate([refs.pop(0)[...] for _ in group], axis=0) for group in fixed]
        totals = [refs.pop(0)[...] for _ in sums or ()] or [0.0] * len(fixed)
        others = []
        for total, right in zip(totals, rights):
            total = total + (dot_tn(left, right) if swept_left else dot_tn(right, left))
            if final:
                parts = (total[:, :step], total[:, step:]) if swept_left else (total[:step], total[step:])
                refs.pop(0)[...] = parts[0]
                others.append(parts[1].astype(bf16))
            else:
                refs.pop(0)[...] = total
        if final:
            refs.pop(0)[...] = jnp.concatenate(others, axis=1 if swept_left else 0)

    def spec(size):
        return pl.BlockSpec((step, size), lambda j: (j, 0)) if swept_left else pl.BlockSpec((size, step), lambda j: (0, j))

    def shape(size):
        return (step * steps, size) if swept_left else (size, step * steps)

    sizes = [(step if final else width, f32)] * len(fixed) + [(step * len(fixed), bf16)] * final
    shapes = [like(shape(size), dtype) for size, dtype in sizes]
    out_specs = [spec(size) for size, _ in sizes]
    in_specs = [pl.BlockSpec((t.shape[0], step), lambda j: (0, j)) for t in swept]
    in_specs += [pl.BlockSpec(t.shape, lambda j: (0, 0)) for group in fixed for t in group]
    in_specs += [spec(width) for _ in sums or ()]
    return pl.pallas_call(
        body,
        grid=(steps,),
        out_shape=shapes,
        in_specs=in_specs,
        out_specs=out_specs,
        compiler_params=pltpu.CompilerParams(vmem_limit_bytes=KERNEL_VMEM),
        cost_estimate=pl.CostEstimate(flops=COST * 2 * rows * width * step * steps * len(fixed), bytes_accessed=rows, transcendentals=0),
    )(*map(distant, [*swept, *[t for group in fixed for t in group], *(sums or ())]))


def expert_forward(rows, w_gate, w_up, w_down):
    gate_out = dot_nn(rows, w_gate)
    up_out = dot_nn(rows, w_up)
    act = (gate_out / (1.0 + jnp.exp(-gate_out)) * up_out).astype(bf16)
    part = dot_nn(act, w_down).astype(bf16)
    return part, (rows, gate_out.astype(bf16), up_out.astype(bf16))


def expert_backward(grad_rows, saved, w_gate, w_up, w_down):
    rows, gate_low, up_low = saved
    gate_out, up_out = wide(gate_low), wide(up_low)
    grad_act = dot_nt(grad_rows, w_down)
    sig = 1.0 / (1.0 + jnp.exp(-gate_out))
    silu = gate_out * sig
    grad_gate = (grad_act * up_out * sig * (1.0 + gate_out * (1.0 - sig))).astype(bf16)
    grad_up = (grad_act * silu).astype(bf16)
    act = (silu * up_out).astype(bf16)
    grad_in = (dot_nt(grad_gate, w_gate) + dot_nt(grad_up, w_up)).astype(bf16)
    return grad_in, (dot_tn(rows, grad_gate), dot_tn(rows, grad_up), dot_tn(act, grad_rows))


def halves(array):
    half = array.shape[0] // 2
    return array[:half], array[half:]


def owned_body(turns, groups, blocks, with_last, gains, *refs):
    refs = list(refs)
    lefts = [refs.pop(0) for _ in range(turns)]
    rights = [[refs.pop(0) for _ in range(turns + with_last)] for _ in range(groups)]
    last = [refs.pop(0) for _ in range(4 * with_last)]
    gains = [refs.pop(0)[...] for _ in range(gains)]
    outs, products, sems = refs[: 2 * len(blocks)], refs[-2], refs[-1]
    values = [t[...] for t in lefts]
    if with_last:
        grad, grad_two, hidden, gain = last
        total = hidden[...]
        back, _ = norm_back(total, norm_factor(total), gain[...], grad_two[...])
        values.append((wide(grad[...]) + back).astype(bf16))
    left = jnp.concatenate(values, axis=0)
    for g in range(groups):
        right = jnp.concatenate([t[...] for t in rights[g]], axis=0)
        products[g, :, : right.shape[1]] = dot_tn(left, right).astype(bf16)
        if gains:
            terms, at = [], right.shape[1]
            for gain in gains:
                high = gain.astype(bf16)
                terms += [high, (gain - wide(high)).astype(bf16)]
            rows = jnp.concatenate(terms + [jnp.zeros_like(terms[0])] * (-len(terms) % 16), axis=0)
            which = lax.broadcasted_iota(jnp.int32, (rows.shape[0], 128), 0)
            column = lax.broadcasted_iota(jnp.int32, (rows.shape[0], 128), 1)
            chosen = (column == (which // 2) % 2) & (which < len(terms))
            products[g, :, at : at + 128] = dot_tn(rows, jnp.where(chosen, 1.0, 0.0).astype(bf16)).astype(bf16)
    copies, leaving = Copies(sems), []
    me = lax.axis_index("dp")
    share = products.shape[1] // lax.axis_size("dp")
    for i, group in enumerate(blocks):
        for out, places in zip(outs[2 * i : 2 * i + 2], group):
            for j, (mask, side) in enumerate(places):
                rows = pl.ds(pl.multiple_of((me ^ mask) * share, share), share)
                leaving.append(copies.start(products.at[side, rows, :], out.at[pl.ds(j * share, share), :]))
    for copy in leaving:
        copy.wait()


def owned_products(cube, lefts, rights, last=(), gains=()):
    model, width = lefts[0].shape[1], rights[0][0].shape[1] + (128 if gains else 0)
    share = model // lax.axis_size("dp")
    stages = [[[(m ^ int(i), s) for m, s in side for i in cube.inner] for side in pair] for pair in cube.stages]
    own, near, middle, corner = stages
    blocks = [middle, [a + b + c for a, b, c in zip(own, near, corner)]]
    shapes = [like((len(places) * share, width), bf16) for pair in blocks for places in pair]
    scratch = [
        pltpu.VMEM((len(rights), model, width), bf16),
        pltpu.SemaphoreType.DMA((sum(len(places) for pair in blocks for places in pair),)),
    ]
    args = [*lefts, *[t for group in rights for t in group], *last, *gains]
    outs = pl.pallas_call(
        functools.partial(owned_body, len(lefts), len(rights), blocks, 1 if last else 0, len(gains)),
        out_shape=shapes,
        in_specs=[VMEM] * len(args),
        out_specs=[ANY] * len(shapes),
        scratch_shapes=scratch,
        compiler_params=pltpu.CompilerParams(vmem_limit_bytes=KERNEL_VMEM),
    )(*map(distant, args))
    return [(outs[2 * i], outs[2 * i + 1]) for i in range(len(blocks))]


class Blocks:
    def __init__(self, cube, weights):
        self.cube, self.weights = cube, weights

    def forward(self, payload, micro, side=()):
        saved = [None] * 4

        def work(stage, pieces):
            parts, saved[stage] = expert_stage(pieces, *self.weights)
            return parts

        return gather_rows(self.cube, payload, work, side), saved

    def backward(self, grad, micro, saved, side=()):
        keeps = [None] * 4

        def work(stage, pieces):
            parts, keeps[stage] = expert_back_stage(pieces, saved[stage], *self.weights)
            return parts

        return gather_rows(self.cube, grad, work, side), keeps

    def late_backward(self, pieces, saved):
        parts, keeps = [None] * 4, [None] * 4

        def run(*stages):
            def work(*gathered):
                for stage, rows in zip(stages, gathered):
                    parts[stage], keeps[stage] = expert_back_stage(rows, saved[stage], *self.weights)
                return [t for stage in stages for t in parts[stage]]

            return lambda: [pieces[stage] for stage in stages], work

        return run, parts, keeps

    def total_start(self, results, side=()):
        own, near, middle, corner = results
        arrived, corner, (own, near) = reduce_start(self.cube, middle, corner, (own, near), side)
        return arrived, corner, [[t] for t in near], own

    def total_finish(self, state, side=()):
        return reduce_finish(self.cube, *state, side)

    def total(self, results, side=()):
        return self.total_finish(self.total_start(results, side[:1]), side[1:])

    def weight_sums(self, slots, sums, final=False):
        def stages():
            return [stage for keeps in slots for stage in keeps]

        def hidden(*args):
            payloads, gates, ups = args
            sums[0] = swept_products(payloads, [gates, ups], sums[0], True, final)
            return sums[0]

        def down(*args):
            grads, acts = args
            sums[1] = swept_products(grads, [acts], sums[1], False, final)
            return sums[1]

        return [
            (lambda: [[t for s in stages() for t in s[0]], [s[2] for s in stages()], [s[3] for s in stages()]], hidden),
            (lambda: [[t for s in stages() for t in s[1]], [s[4] for s in stages()]], down),
        ]


def run_all(side):
    for thunk in side:
        if thunk is not None:
            thunk[1](*thunk[0]())


class Buckets:
    def __init__(self, cube, weights, routes, gates, capacity):
        self.cube, self.weights, self.capacity = cube, weights, capacity
        micros, self.rows, self.top = routes.shape
        self.experts = lax.axis_size("dp")
        self.tables = []
        for m in range(micros):
            flat = routes[m].reshape(-1)
            onehot = (flat[:, None] == jnp.arange(self.experts, dtype=jnp.int32)).astype(jnp.int32)
            earlier = jnp.cumsum(onehot, axis=0) - onehot
            target = flat * capacity + jnp.sum(earlier * onehot, axis=1)
            source = jnp.full((self.experts * capacity,), flat.shape[0], jnp.int32)
            source = source.at[target].set(jnp.arange(flat.shape[0], dtype=jnp.int32))
            self.tables.append((target, source, gates[m]))

    def table(self, micro):
        return jax.tree.map(lambda a, b: jnp.where(micro == 0, a, b), self.tables[0], self.tables[1])

    def exchange(self, rows):
        shape = (self.experts, self.capacity, rows.shape[1])
        moved = lax.all_to_all(rows.reshape(shape), "dp", split_axis=0, concat_axis=0, tiled=True)
        return moved.reshape(rows.shape)

    def whole(self, own):
        return jnp.concatenate([own, swap(own, self.cube.z)], axis=0)

    def forward(self, payload, micro, side=()):
        target, source, gates = self.table(micro)
        own = payload[:, : self.weights[0].shape[0]]
        padded = jnp.pad(self.whole(own), ((0, 1), (0, 0)))
        arrived = self.exchange(jnp.take(padded, source // self.top, axis=0))
        part, saved = expert_forward(arrived, *self.weights)
        picked = jnp.take(self.exchange(part), target, axis=0).reshape(self.rows, self.top, -1)
        run_all(side)
        return jnp.sum(gates[:, :, None] * picked, axis=1), saved

    def backward(self, grad, micro, saved, side=()):
        target, source, gates = self.table(micro)
        scaled = (gates[:, :, None] * wide(self.whole(grad))[:, None, :]).astype(bf16)
        padded = jnp.pad(scaled.reshape(self.rows * self.top, -1), ((0, 1), (0, 0)))
        arrived = self.exchange(jnp.take(padded, source, axis=0))
        grad_in, weights = expert_backward(arrived, saved, *self.weights)
        picked = jnp.take(self.exchange(grad_in), target, axis=0).reshape(self.rows, self.top, -1)
        run_all(side)
        return jnp.sum(picked, axis=1, dtype=f32), weights

    def total_start(self, results, side=()):
        run_all(side)
        return results

    def total_finish(self, results, side=()):
        own, other = halves(results.astype(bf16))
        run_all(side)
        return wide(own) + wide(swap(other, self.cube.z))

    def total(self, results, side=()):
        return self.total_finish(results, side)

    def weight_sums(self, slots, sums, final=False):
        def add(*slots):
            for weights in slots:
                for i, part in enumerate((list(weights[:2]), list(weights[2:]))):
                    sums[i] = part if sums[i] is None else [a + b for a, b in zip(sums[i], part)]

        return [None, (lambda: slots, add)]


def local(
    tokens, lengths, routes, gates, attn_gain, q_weight, key_projection, value_projection,
    o_weight, mlp_gain, expert_gate, expert_up, expert_down, cotangent,
):
    cube = Cube()
    section = lax.axis_index("section")
    shard = lax.axis_index("shard")
    me = lax.axis_index("dp")
    peers, shards = lax.axis_size("dp"), lax.axis_size("shard")
    _, block_rows, model = tokens.shape
    rows = block_rows // shards
    share = model // peers
    first = section == 0
    gain_one, gain_two = attn_gain[0][None], mlp_gain[0][None]
    weights = [q_weight[0], key_projection[0], value_projection[0], o_weight[0]]
    expert_w = (expert_gate[0, 0], expert_up[0, 0], expert_down[0, 0])
    capacity = 2 * block_rows * routes.shape[3] // peers
    whole_blocks = capacity >= block_rows

    def chosen(here, there):
        return jax.tree.map(lambda a, b: jnp.where(first, a, b), here, there)

    def begins(lens):
        lens = lens[:, 0]
        ends, longest = jnp.cumsum(lens, axis=1), jnp.argmax(lens, axis=1)
        return [ends[m, longest[m]] - lens[m, longest[m]] for m in range(2)]

    def turned(array, begin):
        doubled = jnp.concatenate([array, array], axis=0)
        return lax.dynamic_slice_in_dim(doubled, (begin + rows * shard) % block_rows, block_rows, 0)

    if not whole_blocks:
        early = begins(lengths)
        mixture = Buckets(
            cube,
            expert_w,
            jnp.stack([turned(routes[0, m], early[m]) for m in range(2)]),
            jnp.stack([turned(gates[0, m], early[m]) for m in range(2)]),
            capacity,
        )

    slices = [lax.dynamic_slice_in_dim(w, me * share, share, 0) for w in weights]
    qkv_slices = swap(jnp.concatenate(slices[:3], axis=1), cube.z)
    out_slices = slices[3]
    half_share = share // 2
    mask = cube.x[1] | cube.y[1]
    far_places = [2 * (me ^ mask), 2 * (me ^ mask) + 1]
    plane_places = [2 * (me ^ m) for m in (0, cube.x[1], cube.y[1])]
    mate_bit = cube.core[1]

    def mate_places(places):
        return [p ^ (2 * mate_bit) for p in places]

    def parted(own):
        half = model // shards
        given = lax.dynamic_slice_in_dim(own, (1 - shard) * half, half, 1)
        return lax.dynamic_slice_in_dim(own, shard * half, half, 1), given.astype(bf16)

    def placed(parts, m):
        kept, given = parts
        got = swap(given, cube.z).astype(kept.dtype)
        low = jnp.where(shard == 0, kept, got)
        high = jnp.where(shard == 0, got, kept)
        return lax.dynamic_slice_in_dim(
            jnp.concatenate([low, high, low, high], axis=0), (block_rows - starts[m]) % block_rows, block_rows, 0
        )

    cot_own, cot_other = turned_block(lengths, cotangent)
    own_near = [swap(cot_own, d) for d in (cube.x, cube.y)] if whole_blocks else []
    opened, mask0 = opening(lengths, tokens, gain_one, weights)
    settled = [tokens, cotangent, routes, gates]
    mates = [swap(expert_w[0], cube.core)] if whole_blocks else []
    opened, qkv_slices, own_near, cot_other, settled, mates, expert_w = together(
        (opened, qkv_slices, own_near, cot_other, settled, mates, expert_w)
    )
    inputs, part, qkv, heads, sent = opened
    *settled, route_rows, gate_rows = settled
    settled += [[t[0, m].T for m in range(2)] for t in (route_rows, gate_rows)]
    other_near = [swap(cot_other, d) for d in (cube.x, cube.y)] if whole_blocks else []
    if whole_blocks:
        mates.append(swap(expert_w[1], cube.core))
    arrived, other_near, settled, mates, expert_w = together(
        (swap(sent, cube.z), other_near, settle(lengths, *settled), mates, expert_w)
    )
    fresh1, cot1, mask1, extra0, extra1, starts = settled
    hidden, payload = joined(part, arrived, gain_two, extra0)
    if whole_blocks:
        payload, expert_w, mates = together((payload, expert_w, mates))
        mates.append(swap(expert_w[2], cube.core))
        expert_w = pinned(list(zip(expert_w, mates)), (1, 1, 0))
        mixture = Blocks(cube, expert_w)
        plane = []

        def first_plane(qkv_slices, out_slices):
            near = [qkv_slices] + [swap(qkv_slices, d) for d in (cube.x, cube.y, ("dp", mask))]
            plane.extend([near, swap(out_slices, cube.z)])
            return plane

        side = [None, None, (lambda: [qkv_slices, out_slices], first_plane)]
        results, saved = mixture.forward(payload, 0, side)
        qkv_near, out_slices = plane
    else:
        results, saved = mixture.forward(payload, 0)
    first_mates = []

    def first_exchange(*near):
        first_mates.extend(swap(t, cube.core) for t in near)
        return first_mates

    mids = []

    def first_choice(*both_micros):
        mids.append(chosen(both_micros[2:], both_micros[:2]))
        mids.append(chosen(both_micros[:2], both_micros[2:]))
        return mids

    choice = (lambda: [mask0, extra0, mask1, extra1], first_choice)
    total = mixture.total(results, [both((lambda: qkv_near, first_exchange), choice) if whole_blocks else choice])
    result0 = (hidden + total).astype(bf16)
    if whole_blocks:
        result0, qkv_near, out_slices = together((result0, qkv_near, out_slices))
        arriving = lax.ppermute(result0, "section", [(0, 1)])
        out_near = [out_slices] + [swap(out_slices, d) for d in (cube.x, cube.y, ("dp", mask))]
        all_places = [*plane_places, far_places[0]]
        places = [*all_places, *mate_places(all_places)]

        def assembled(pieces):
            spans = [(p, half_share, 0) for p in places]
            return put_together(pieces, spans, (model, pieces[0].shape[1]))

        arriving, out_near, weights, qkv_packed = together(
            (arriving, out_near, pinned(weights), assembled([*qkv_near, *first_mates]))
        )
        packed = [qkv_packed, assembled([*out_near, *[swap(t, cube.core) for t in out_near]])]
    else:
        arriving = lax.ppermute(result0, "section", [(0, 1)])
        packed = [
            lax.all_gather(t, "dp", axis=0, tiled=True) for t in (qkv_slices, swap(out_slices, cube.z))
        ]

    (mask_mid, extra_mid), (mask_last, extra_last) = mids

    inputs1, hidden1, payload, groups1 = attention_forward(
        fresh1, arriving, mask_mid, gain_one, gain_two, extra_mid, weights, packed
    )
    micro_mid = 1 - section
    late = []

    def cot_far(x0, y1):
        late.extend([swap(x0, cube.y), swap(y1, cube.x)])
        return late

    side = []
    if whole_blocks:
        (x0, y0), (x1, y1) = own_near, other_near
        side = [None, None, (lambda: [x0, y1], cot_far)]
    results, saved1 = mixture.forward(payload, micro_mid, side)

    grad0 = cot_own
    if whole_blocks:
        pieces = [[cot_own], [x0, y0, cot_other], [late[0], y1, x1], [late[1]]]
        run, back_results, keeps0 = mixture.late_backward(pieces, saved1)
        total = mixture.total(results, [run(2), run(1, 0)])
        back_results[3] = run(3)
    else:
        back_results, keeps0 = mixture.backward(grad0, micro_mid, saved1)
        total = mixture.total(results)
    result1 = (hidden1 + total).astype(bf16)

    slot2 = []

    def last_attention(arriving):
        slot2.extend(
            attention_forward(inputs, arriving, mask_last, gain_one, gain_two, extra_last, weights, packed)
        )
        return slot2

    arrived = []

    def second_handoff(result):
        arrived.append(lax.ppermute(result, "section", [(0, 1)]))
        return arrived

    if whole_blocks:
        result1, back_results[:3] = together((result1, back_results[:3]))
    else:
        result1, back_results = together((result1, back_results))
    state = mixture.total_start(back_results, [(lambda: [result1], second_handoff)])
    grad_two = mixture.total_finish(state, [(lambda: arrived, last_attention)])
    inputs2, hidden2, payload, groups2 = slot2

    def attention_turn(grad, grad_two, state):
        inputs, hidden, mask, groups, _ = state
        outs = attention_backward(
            grad, grad_two, inputs, hidden, mask, gain_one, gain_two, [g[0] for g in groups], weights, packed
        )
        grad_input, low, grad_low, normed, g0, g1, attn_g, mlp_g = outs
        factors = (normed, grad_low, (g0, g1), [g[1] for g in groups])
        return grad_input, low, factors, (attn_g, mlp_g)

    state1 = [inputs1, hidden1, mask_mid, groups1, saved1]
    turn0, returned = [], []

    def first_turn(grad_two):
        turn0.extend(attention_turn(grad0, grad_two, state1))
        return turn0

    def first_return(low):
        returned.append(lax.ppermute(low, "section", [(1, 0)]))
        return returned

    side = [(lambda: [grad_two], first_turn), None, (lambda: [turn0[1]], first_return)]
    results2, saved2 = mixture.forward(payload, section, side)
    coming = returned[0]

    sums = [None, None]
    if whole_blocks:
        *results2, corner = results2
        coming, results2, inputs = together((coming, results2, corner[0]()))
        corner = corner[1](*inputs)
        results2 = [*results2, (lambda: [corner], lambda t: t)]
    else:
        coming, results2, saved2 = together((coming, results2, saved2))
    grad1 = coming + cot1
    state2 = [inputs2, hidden2, mask_last, groups2, saved2]
    back_results, keeps1 = mixture.backward(grad1, section, saved2)
    def run_both(*works):
        works = [w for w in works if w]
        return both(*works) if works else None

    placings = {}

    def placing(name, micro, own):
        def work(rows):
            placings[name, micro] = placed(parted(rows), micro)
            return placings[name, micro]

        return lambda: [own()], work

    hidden_work, _ = mixture.weight_sums([keeps0], sums)
    _, down_work = mixture.weight_sums([keeps0, keeps1], sums)
    place_first = placing("out", 0, lambda: chosen(result0, result1))
    grad_two = mixture.total(back_results, [run_both(place_first, hidden_work)])
    grad_two, down_inputs = together((grad_two, down_work[0]())) if down_work else (grad_two, ())
    turn1 = attention_turn(grad1, grad_two, state2)
    if whole_blocks:
        low, results2[:3] = together((turn1[1], list(results2[:3])))
    else:
        low, results2 = together((turn1[1], results2))
    coming = lax.ppermute(low, "section", [(1, 0)])
    state = mixture.total_start(results2)
    grad2, state, _ = together((coming, state, down_work[1](*down_inputs) if down_work else ()))

    last_total = []

    def finish_last(*state):
        last_total.append(mixture.total_finish(state[0] if len(state) == 1 else state))
        return last_total

    hidden_work, _ = mixture.weight_sums([keeps1], sums)
    side = [None, None, run_both((lambda: [state] if not whole_blocks else list(state), finish_last), hidden_work)]
    back_results, keeps2 = mixture.backward(grad2, 1 - section, saved1, side)
    result2 = (hidden2 + last_total[0]).astype(bf16)
    placing_out = placing("out", 1, lambda: chosen(result1, result2))
    placing_grad = placing("grad", 0, lambda: chosen(turn1[0], turn0[0]))
    hidden_end, down_end = mixture.weight_sums([keeps2], sums, True)
    waiting = []

    def part_both(out, grad):
        waiting.extend([parted(out), parted(grad)])
        return waiting

    part_work = (lambda: [chosen(result1, result2), chosen(turn1[0], turn0[0])], part_both)
    grad_two = mixture.total(back_results, [part_work, run_both(hidden_end or down_end)])

    _, hidden, _, groups, _ = state1
    others = [t for t in sums[0] if t.dtype == bf16]
    grad_two, others, waiting = together((grad_two, others, waiting))
    others = [swap(t, cube.core) for t in others]
    placings["out", 1], placings["grad", 0] = placed(waiting[0], 1), placed(waiting[1], 0)
    heads_all = [[groups1[g][1], groups2[g][1], groups1[g][1]] for g in range(shards)]
    out_pairs = owned_products(cube, [turn0[2][1], turn1[2][1]], heads_all, (grad2, grad_two, hidden, gain_two))
    out_pairs, others, placings = together((out_pairs, others, placings))
    turn2 = []

    def last_turn(grad_two):
        turn2.extend(attention_turn(grad2, grad_two, state1))
        return turn2

    def exchange(*others):
        return [swap(t, cube.core) for t in others]

    def sums_start(pairs, side):
        middle, rest = pairs
        size = middle[0].shape[0] // 3

        def blocks(*terms):
            return [[t[i : i + size] for t in terms] for i in range(0, terms[0].shape[0], size)]

        middle = [low_sum(*terms) for terms in blocks(middle[0], swap(middle[1], cube.core))]
        other = (lambda: [rest[1]], lambda t: [swap(t, cube.core)])
        arrived, other, mine = reduce_start(cube, middle, other, rest[0], side)
        own, *near, corner = blocks(mine, *other)
        return arrived, corner, near, own

    out_state = sums_start(out_pairs, [(lambda: [grad_two], last_turn)])
    turns = (turn0, turn1, turn2)
    factors = [t[2] for t in turns]
    qkv_pairs = []

    def qkv_products(*_):
        rights = [[f[2][g] for f in factors] for g in range(shards)]
        gains = [g for t in turns for g in t[3]]
        qkv_pairs.extend(owned_products(cube, [f[0] for f in factors], rights, gains=gains))
        return qkv_pairs

    grad_o = reduce_finish(cube, *out_state, [(lambda: [], qkv_products)])
    qkv_pairs, grad_o = together((qkv_pairs, grad_o))

    expert_sums = list(sums[0][:2])

    def hidden_sums(*others):
        for other in others:
            expert_sums[:] = [mine + wide(t) for mine, t in zip(expert_sums, jnp.split(other, 2, axis=1))]
        return expert_sums

    def down_sums(*others):
        for other in others:
            expert_sums[2] = expert_sums[2] + wide(swap(other, cube.core))
        return expert_sums[2]

    last_rows = placing("grad", 1, lambda: chosen(turn2[0], turn1[0]))
    last_end = down_end if whole_blocks else None
    qkv_state = sums_start(qkv_pairs, [run_both(last_rows, (lambda: others, hidden_sums), last_end)])
    expert_sums.append(sums[1][0])
    grad_qkv = reduce_finish(cube, *qkv_state, [(lambda: sums[1][1:], down_sums)])
    gate_total, up_total, down_total = expert_sums
    width = q_weight.shape[2]
    grad_q = grad_qkv[:, :width]
    grad_k = grad_qkv[:, width : width + HEAD_SIZE]
    grad_v = grad_qkv[:, width + HEAD_SIZE : width + 2 * HEAD_SIZE]
    gain_pair = [grad_qkv[:, width + 2 * HEAD_SIZE + i] for i in range(2)]
    section_out = jnp.stack([placings["out", 0], placings["out", 1]])
    input_grad = jnp.stack([placings["grad", 0], placings["grad", 1]])
    return (
        section_out[None],
        input_grad[None],
        gain_pair[0][None],
        grad_q[None],
        grad_k[None],
        grad_v[None],
        grad_o[None],
        gain_pair[1][None],
        gate_total[None, None],
        up_total[None, None],
        down_total[None, None],
    )


def solution(mesh):
    in_specs = (
        P(None, "dp", None),
        P(None, "dp", None),
        P("section", None, "dp", None),
        P("section", None, "dp", None),
        P("section", None),
        P("section", None, "shard"),
        P("section", None, "shard"),
        P("section", None, "shard"),
        P("section", None, "shard"),
        P("section", None),
        P("section", "dp", None, "shard"),
        P("section", "dp", None, "shard"),
        P("section", "dp", "shard", None),
        P(None, "dp", None),
    )
    out_specs = (
        P("section", None, "dp", "shard"),
        P("section", None, "dp", "shard"),
        P("section", "dp"),
        P("section", "dp", "shard"),
        P("section", "dp", "shard"),
        P("section", "dp", "shard"),
        P("section", "dp", "shard"),
        P("section", "dp"),
        P("section", "dp", None, "shard"),
        P("section", "dp", None, "shard"),
        P("section", "dp", "shard", None),
    )
    return jax.shard_map(local, mesh=mesh, in_specs=in_specs, out_specs=out_specs, check_vma=False)
```

```python
import functools

import jax
import jax.numpy as jnp
import numpy as np
from jax import lax
from jax.experimental import pallas as pl
from jax.experimental.pallas import tpu as pltpu
from jax.sharding import PartitionSpec as P

HEAD_SIZE = 128
epsilon = 1e-06
masked_value = -1e30
bf16 = jnp.bfloat16
f32 = jnp.float32


def wide(a):
    return a.astype(f32)


def dot_nn(a, b):
    return lax.dot_general(a, b, (((1,), (0,)), ((), ())), preferred_element_type=f32)


def dot_nt(a, b):
    return lax.dot_general(a, b, (((1,), (1,)), ((), ())), preferred_element_type=f32)


def dot_tn(a, b):
    return lax.dot_general(a, b, (((0,), (0,)), ((), ())), preferred_element_type=f32)


class Cube:
    def __init__(self):
        peers = lax.axis_size("dp")
        bits = [1 << i for i in range(peers.bit_length() - 1)]
        rest = bits[1:]
        self.core = ("dp", bits[0])
        self.x = ("dp", rest[0])
        self.y = ("dp", rest[len(rest) // 2])
        self.z = ("shard", 1)
        self.extra = [("dp", b) for b in rest if b not in (self.x[1], self.y[1])]
        inner = [0]
        for _, bit in self.extra:
            inner = inner + [m | bit for m in inner]
        self.inner = np.array(inner)
        x, y = self.x[1], self.y[1]
        self.corner = (x | y, 1)
        stages = [[(0, 0)], [(x, 0), (y, 0), (0, 1)], [(x | y, 0), (y, 1), (x, 1)], [self.corner]]
        self.stages = [(g, [(m | self.core[1], s) for m, s in g]) for g in stages]


def swap(value, direction):
    axis, bit = direction
    return lax.ppermute(value, axis, [(i, i ^ bit) for i in range(lax.axis_size(axis))])


def across(value, cube):
    mask, flip = cube.corner
    shards = lax.axis_size("shard")
    pairs = [
        (d * shards + s, (d ^ mask) * shards + (s ^ flip))
        for d in range(lax.axis_size("dp"))
        for s in range(shards)
    ]
    return lax.ppermute(value, ("dp", "shard"), pairs)


together = lax.optimization_barrier


def both(*thunks):
    def work(*groups):
        return [thunk[1](*group) for thunk, group in zip(thunks, groups)]

    return lambda: [thunk[0]() for thunk in thunks], work


def after(payload, thunks, step):
    if step >= len(thunks) or thunks[step] is None:
        return payload, lambda: ()
    inputs, work = thunks[step]
    payload, inputs = together((payload, inputs()))
    return payload, lambda: work(*inputs)


def gather_rows(cube, own, work, side=()):
    own, beside = after(own, side, 0)
    near = [swap(own, d) for d in (cube.x, cube.y, cube.z)]
    first = work(0, [own])
    near, first, _ = together((near, first, beside()))

    near, beside = after(near, side, 1)
    middle = [swap(block, d) for block, d in zip(near, (cube.y, cube.z, cube.x))]
    second = work(1, near)
    middle, second, _ = together((middle, second, beside()))

    middle, beside = after(middle, side, 2)
    corner = swap(middle[0], cube.z)
    third = work(2, middle)
    corner, third, _ = together((corner, third, beside()))
    return first, second, third, (lambda: [corner], lambda *blocks: work(3, list(blocks)))


def low_sum(*terms):
    return sum(wide(t) for t in terms).astype(bf16)


def reduce_start(cube, middle, corner, rest, side=()):
    (middle, rest), beside = after((middle, rest), side, 0)
    middle, inputs = together((middle, corner[0]()))
    arrived = [swap(t, d) for t, d in zip(middle, (cube.y, cube.z, cube.x))]
    return together((arrived, corner[1](*inputs), rest, beside()))[:3]


def reduce_finish(cube, arrived, corner, near, own, side=()):
    sent = [low_sum(*terms) for terms in [*([corner] if corner else []), *[[*t, a] for t, a in zip(near, arrived)]]]
    sent, beside = after(sent, side, 0)
    arrived = [swap(t, d) for t, d in zip(sent[-3:], (cube.x, cube.y, cube.z))]
    arrived += [across(t, cube) for t in sent[:-3]]
    arrived, own, _ = together((arrived, own, beside()))
    total = sum(wide(t) for t in [*own, *arrived])
    for direction in reversed(cube.extra):
        half = total.shape[0] // 2
        total = total[:half] + wide(swap(total[half:].astype(bf16), direction))
    return total


def norm_factor(values):
    return lax.rsqrt(jnp.mean(values * values, axis=1, keepdims=True) + epsilon)


def norm_back(values, factor, gain, grad):
    gain_grad = jnp.sum(grad * values * factor, axis=0, keepdims=True)
    scaled = grad * gain
    inner = jnp.mean(scaled * values, axis=1, keepdims=True)
    return factor * (scaled - values * factor * factor * inner), gain_grad


def stack_heads(rows):
    return jnp.concatenate(
        [rows[:, i : i + HEAD_SIZE] for i in range(0, rows.shape[1], HEAD_SIZE)], axis=0
    )


def spread_heads(stacked, rows):
    return jnp.concatenate(
        [stacked[i : i + rows] for i in range(0, stacked.shape[0], rows)], axis=1
    )


def head_probs(query, key, allowed):
    scores = jnp.where(allowed > 0.0, dot_nt(query, key) * HEAD_SIZE ** (-0.5), masked_value)
    exp_scores = jnp.exp(scores - jnp.max(scores, axis=1, keepdims=True))
    return exp_scores / jnp.sum(exp_scores, axis=1, keepdims=True)


def normed_rows(values, gain):
    return (values * norm_factor(values) * gain).astype(bf16)


def group_probs(qkv, allowed):
    width = qkv.shape[1] - 2 * HEAD_SIZE
    query = stack_heads(qkv[:, :width])
    key, value = qkv[:, width : width + HEAD_SIZE], qkv[:, width + HEAD_SIZE :]
    tiled = jnp.concatenate([allowed] * (width // HEAD_SIZE), axis=0)
    return query, key, value, head_probs(query, key, tiled)


def head_group(normed, allowed, weights, qkv, heads):
    *projections, w_out = weights
    at = 0
    for w in projections:
        part = dot_nn(normed, w()).astype(bf16)
        qkv[:, at : at + part.shape[1]] = part
        at += part.shape[1]
    _, _, value, probs = group_probs(qkv[...], allowed)
    heads[...] = spread_heads(dot_nn(probs.astype(bf16), value).astype(bf16), normed.shape[0])
    return dot_nt(heads[...], w_out())


VMEM = pl.BlockSpec(memory_space=pltpu.VMEM)
SMEM = pl.BlockSpec(memory_space=pltpu.SMEM)
ANY = pl.BlockSpec(memory_space=pl.ANY)
KERNEL_VMEM = 42 << 20
COST = 16
HELD = True


def held(shape, dtype):
    return pltpu.VMEM(shape, dtype)


def like(shape, dtype):
    return pltpu.HBM(shape, dtype)


def close(value):
    return pltpu.with_memory_space_constraint(value, pltpu.VMEM)


def distant(value):
    return pltpu.with_memory_space_constraint(value, pltpu.HBM)


def pinned(groups, axes=None):
    groups = [g if isinstance(g, (list, tuple)) else (g,) for g in groups]
    axes = axes or [0] * len(groups)
    values = [v for g in groups for v in g]
    shapes = [
        tuple(n * len(g) if i == axis else n for i, n in enumerate(g[0].shape)) for g, axis in zip(groups, axes)
    ]

    def body(*refs):
        ins, outs, sems = list(refs[: len(values)]), refs[len(values) : -1], refs[-1]
        copies, waits = Copies(sems), []
        for group, axis, out in zip(groups, axes, outs):
            for i, value in enumerate(group):
                size = value.shape[axis]
                place = [slice(None)] * axis + [pl.ds(i * size, size)]
                waits.append(copies.start(ins.pop(0), out.at[tuple(place)]))
        for copy in waits:
            copy.wait()

    return pl.pallas_call(
        body,
        out_shape=[held(shape, g[0].dtype) for g, shape in zip(groups, shapes)],
        in_specs=[ANY] * len(values),
        out_specs=[VMEM] * len(groups),
        scratch_shapes=[pltpu.SemaphoreType.DMA((len(values),))],
        compiler_params=pltpu.CompilerParams(vmem_limit_bytes=1 << 20),
    )(*map(distant, values))


def put_together(pieces, spans, shape):
    starts = jnp.stack([first for first, _, _ in spans]).astype(jnp.int32)

    def body(starts, *refs):
        ins, out, sems = refs[:-2], refs[-2], refs[-1]
        copies, waits = Copies(sems), []
        for i, (piece, (_, unit, column)) in enumerate(zip(ins, spans)):
            rows = pl.ds(pl.multiple_of(starts[i] * unit, unit), piece.shape[0])
            waits.append(copies.start(piece, out.at[rows, pl.ds(column, piece.shape[1])]))
        for copy in waits:
            copy.wait()

    return pl.pallas_call(
        body,
        out_shape=held(shape, pieces[0].dtype),
        in_specs=[SMEM] + [ANY] * len(pieces),
        out_specs=VMEM,
        scratch_shapes=[pltpu.SemaphoreType.DMA((len(pieces),))],
        compiler_params=pltpu.CompilerParams(vmem_limit_bytes=KERNEL_VMEM),
    )(starts, *map(distant, pieces))


class Copies:
    def __init__(self, sems):
        self.sems, self.count = sems, 0

    def start(self, source, target):
        copy = pltpu.make_async_copy(source, target, self.sems.at[self.count])
        self.count += 1
        copy.start()
        return copy

    def fetch(self, source, target):
        copy, waited = self.start(source, target), []

        def value():
            if not waited:
                copy.wait()
                waited.append(True)
            return target[...]

        return value


def on_device(body, outs, args, flops, scalars=(), kept=(), far=(), scratch=(), direct=False):
    moved = sum(a.size * a.dtype.itemsize for a in args)
    return pl.pallas_call(
        body,
        out_shape=outs,
        in_specs=[SMEM] * len(scalars) + [VMEM] * (len(args) + len(kept)) + [ANY] * len(far),
        out_specs=[SMEM if o.dtype == jnp.int32 else ANY if direct else VMEM for o in outs],
        scratch_shapes=scratch,
        compiler_params=pltpu.CompilerParams(vmem_limit_bytes=KERNEL_VMEM),
        cost_estimate=pl.CostEstimate(flops=COST * flops, bytes_accessed=moved, transcendentals=0),
    )(*scalars, *map(distant, args), *map(close, kept), *far)


def holders(*arrays):
    return [pltpu.VMEM(a.shape, a.dtype) for a in arrays] + [pltpu.SemaphoreType.DMA((len(arrays) + 1,))]


def geometry(lens, micro, side, rows, block):
    ends, total, best, start = [], 0, lens[micro, 0, 0], 0
    for i in range(lens.shape[2]):
        length = lens[micro, 0, i]
        if i:
            start = jnp.where(length > best, total, start)
            best = jnp.maximum(best, length)
        total = total + length
        ends.append(total)
    return ends, lax.rem(start + rows * side, block)


def positions(shape, axis, begin, block):
    place = lax.broadcasted_iota(jnp.int32, shape, axis) + begin
    return jnp.where(place >= block, place - block, place)


def selection(begin, rows, block):
    wanted = positions((rows, block), 0, begin, block)
    return (wanted == lax.broadcasted_iota(jnp.int32, (rows, block), 1)).astype(f32)


def sequence_mask(ends, begin, rows, block):
    row, col = [positions((rows, rows), axis, begin, block) for axis in (0, 1)]
    inside = sum(jnp.abs((row >= e).astype(jnp.int32) - (col >= e).astype(jnp.int32)) for e in ends)
    return ((inside == 0) & (col <= row)).astype(f32)


def gate_columns(pick, routes, gates):
    peers = lax.axis_size("dp")
    expert = lax.broadcasted_iota(jnp.int32, (128, routes.shape[1]), 0)
    table = jnp.zeros(expert.shape, f32)
    for k in range(routes.shape[0]):
        gate, route = gates[k : k + 1, :], routes[k : k + 1, :]
        high = wide(gate.astype(bf16))
        table += jnp.where(expert == route, high, 0.0) + jnp.where(expert == route + peers, gate - high, 0.0)
    return dot_nt(pick, table.astype(bf16)).astype(bf16)


def turned_body(lens, blocks, own, other, block_rows, sems):
    copy = Copies(sems).fetch(blocks.at[0], block_rows)
    block = block_rows.shape[0]
    here = jnp.where(lax.axis_index("section") == 0, 0.0, 1.0)
    shard = lax.axis_index("shard")
    for side, out in ((shard, own), (1 - shard, other)):
        _, begin = geometry(lens, 0, side, block // 2, block)
        out[...] = dot_nn((selection(begin, block // 2, block) * here).astype(bf16), copy()).astype(bf16)


def turned_block(lens, blocks):
    _, block, model = blocks.shape
    scratch = [pltpu.VMEM((block, model), bf16), pltpu.SemaphoreType.DMA((1,))]
    shapes = [like((block // 2, model), bf16)] * 2
    return on_device(
        turned_body, shapes, [], 2 * block * block * model, (lens,), far=[distant(blocks)], scratch=scratch
    )


def opening_body(lens, gain, tokens, *refs):
    wq, wk, wv, wo, inputs, part, qkv, heads, sent, qkv_other, heads_other, mask, *scratch, sems = refs
    copies = Copies(sems)
    sources = [tokens.at[0], wq, wk, wv, wo]
    block_rows, *weights = [copies.fetch(a, b) for a, b in zip(sources, scratch)]
    block = tokens.shape[1]
    rows = block // 2
    shard = lax.axis_index("shard")
    first = jnp.where(lax.axis_index("section") == 0, 1.0, 0.0)
    sides = []
    for side in (shard, 1 - shard):
        ends, begin = geometry(lens, 0, side, rows, block)
        sides.append((selection(begin, rows, block) * first, sequence_mask(ends, begin, rows, block)))
    values = dot_nn(jnp.concatenate([pick for pick, _ in sides], axis=0).astype(bf16), block_rows())
    inputs[...] = values[:rows].astype(bf16)
    mask[...] = sides[0][1]
    normed = normed_rows(values, gain[...])
    *projections, w_out = weights
    projected = jnp.concatenate([dot_nn(normed, w()).astype(bf16) for w in projections], axis=1)
    both_heads = []
    for i, (to_qkv, to_heads) in enumerate(((qkv, heads), (qkv_other, heads_other))):
        to_qkv[...] = projected[i * rows : (i + 1) * rows]
        _, _, value, probs = group_probs(to_qkv[...], sides[i][1])
        to_heads[...] = spread_heads(dot_nn(probs.astype(bf16), value).astype(bf16), rows)
        both_heads.append(to_heads[...])
    result = dot_nt(jnp.concatenate(both_heads, axis=0), w_out())
    part[...] = values[:rows] + result[:rows]
    sent[...] = result[rows:].astype(bf16)


def opening(lens, tokens, gain, weights):
    _, block, model = tokens.shape
    rows = block // 2
    width, out = sum(w.shape[1] for w in weights[:3]), weights[3].shape[1]
    shapes = [
        like((rows, model), bf16), like((rows, model), f32), like((rows, width), bf16), like((rows, out), bf16),
        like((rows, model), bf16), like((rows, width), bf16), like((rows, out), bf16), like((rows, rows), f32),
    ]
    scratch = [pltpu.VMEM((block, model), bf16), *holders(*weights)]
    outs = on_device(
        opening_body, shapes, [gain], 4 * rows * model * (width + out), (lens,), far=[distant(t) for t in (tokens, *weights)], scratch=scratch
    )
    return outs[:5], outs[7]


def settle_body(lens, routes0, gates0, routes1, gates1, tokens, grad, *refs):
    fresh, cot, mask, extra0, extra1, starts, token_rows, grad_rows, sems = refs
    copies = Copies(sems)
    for micro in range(2):
        _, starts[micro] = geometry(lens, micro, 0, tokens.shape[1] // 2, tokens.shape[1])
    token_rows = copies.fetch(tokens.at[1], token_rows)
    grad_rows = copies.fetch(grad.at[1], grad_rows)
    block = tokens.shape[1]
    rows = block // 2
    first = jnp.where(lax.axis_index("section") == 0, 1.0, 0.0)
    for micro, routes, gates, extra in ((0, routes0, gates0, extra0), (1, routes1, gates1, extra1)):
        ends, begin = geometry(lens, micro, lax.axis_index("shard"), rows, block)
        pick = selection(begin, rows, block)
        extra[...] = gate_columns(pick.astype(bf16), routes[...], gates[...])
    fresh[...] = dot_nn((pick * first).astype(bf16), token_rows()).astype(bf16)
    cot[...] = dot_nn((pick * (1.0 - first)).astype(bf16), grad_rows()).astype(bf16)
    mask[...] = sequence_mask(ends, begin, rows, block)


def settle(lens, tokens, grad, routes, gates):
    _, block, model = tokens.shape
    rows = block // 2
    shapes = [like((rows, model), bf16)] * 2 + [like((rows, rows), f32)] + [like((rows, 128), bf16)] * 2
    shapes.append(pltpu.SMEM((2,), jnp.int32))
    args = [routes[0], gates[0], routes[1], gates[1]]
    scratch = [pltpu.VMEM((block, model), bf16)] * 2 + [pltpu.SemaphoreType.DMA((2,))]
    return on_device(
        settle_body, shapes, args, 2 * block * block * model, (lens,), far=[distant(tokens), distant(grad)], scratch=scratch
    )


def joined_body(part, other, extra, gain, hidden, payload):
    total = part[...] + wide(other[...])
    hidden[...] = total
    model = total.shape[1]
    payload[:, :model] = normed_rows(total, gain[...])
    payload[:, model:] = extra[...]


def joined(part, other, gain, extra):
    rows, model = part.shape
    shapes = [like((rows, model), f32), like((rows, model + extra.shape[1]), bf16)]
    return on_device(joined_body, shapes, [part, other, extra, gain], 10 * rows * model)


def by_halves(refs):
    *own, packed, packed_out = refs
    widths = [w.shape[1] for w in own[:3]]
    firsts = [sum(widths[:i]) for i in range(3)]
    other = [lambda f=f, w=w: packed[:, f : f + w] for f, w in zip(firsts, widths)]
    return [lambda w=w: w[...] for w in own], [*other, lambda: packed_out[...]]


def attention_body(fresh, arriving, mask, extra, gain, gain_two, *refs):
    own, other = by_halves(refs[:6])
    inputs, hidden, payload, qkv0, qkv1, heads0, heads1 = refs[6:]
    rows = fresh[...] + arriving[...]
    inputs[...] = rows
    total = wide(rows)
    normed = normed_rows(total, gain[...])
    total = total + head_group(normed, mask[...], own, qkv0, heads0)
    total = total + head_group(normed, mask[...], other, qkv1, heads1)
    hidden[...] = total
    model = total.shape[1]
    payload[:, :model] = normed_rows(total, gain_two[...])
    payload[:, model:] = extra[...]


def attention_forward(fresh, arriving, mask, gain, gain_two, extra, weights, packed):
    rows, model = fresh.shape
    width, out = sum(w.shape[1] for w in weights[:3]), weights[3].shape[1]
    shapes = [
        like((rows, model), bf16), like((rows, model), f32), like((rows, model + extra.shape[1]), bf16),
        like((rows, width), bf16), like((rows, width), bf16), like((rows, out), bf16), like((rows, out), bf16),
    ]
    args = [fresh, arriving, mask, extra, gain, gain_two]
    outs = on_device(attention_body, shapes, args, 6 * rows * packed[0].size, kept=[*weights, *packed])
    inputs, hidden, payload, qkv0, qkv1, heads0, heads1 = outs
    return inputs, hidden, payload, [(qkv0, heads0), (qkv1, heads1)]


def attention_back_body(grad, grad_two, inputs, hidden, mask, q0, q1, gain, gain_two, *refs):
    own, other = by_halves(refs[:6])
    grad_input, grad_input_low, grad_low, normed, g0, g1, gain_grad, gain_two_grad = refs[6:]
    rows = inputs.shape[0]
    values = wide(inputs[...])
    normed[...] = normed_rows(values, gain[...])
    total = hidden[...]
    back, gain_two_grad[...] = norm_back(total, norm_factor(total), gain_two[...], grad_two[...])
    grad_hidden = wide(grad[...]) + back
    low = grad_hidden.astype(bf16)
    grad_low[...] = low
    grad_normed = jnp.zeros_like(grad_hidden)
    for qkv, weights, grad_qkv in ((q0, own, g0), (q1, other, g1)):
        query, key, value, probs = group_probs(qkv[...], mask[...])
        grad_heads = stack_heads(dot_nn(low, weights[3]()).astype(bf16))
        grad_probs = dot_nt(grad_heads, value)
        inner = jnp.sum(probs * grad_probs, axis=1, keepdims=True)
        grad_scores = (probs * (grad_probs - inner) * HEAD_SIZE ** (-0.5)).astype(bf16)
        grads = [
            spread_heads(dot_nn(grad_scores, key).astype(bf16), rows),
            dot_tn(grad_scores, query).astype(bf16),
            dot_tn(probs.astype(bf16), grad_heads).astype(bf16),
        ]
        at = 0
        for part, w in zip(grads, weights):
            grad_qkv[:, at : at + part.shape[1]] = part
            at += part.shape[1]
            grad_normed = grad_normed + dot_nt(part, w())
    back, gain_grad[...] = norm_back(values, norm_factor(values), gain[...], grad_normed)
    result = grad_hidden + back
    grad_input[...] = result
    grad_input_low[...] = result.astype(bf16)


def attention_backward(grad, grad_two, inputs, hidden, mask, gain, gain_two, projected, weights, packed):
    rows, model = inputs.shape
    width = projected[0].shape[1]
    shapes = [
        like((rows, model), f32), like((rows, model), bf16), like((rows, model), bf16),
        like((rows, model), bf16), like((rows, width), bf16), like((rows, width), bf16),
        like((1, model), f32), like((1, model), f32),
    ]
    args = [grad, grad_two, inputs, hidden, mask, *projected, gain, gain_two]
    return on_device(attention_back_body, shapes, args, 12 * rows * packed[0].size, kept=[*weights, *packed])


def place(copies, pieces, *targets):
    started, at = [], 0
    for piece in pieces:
        first, count = 0, piece.shape[0]
        for target in targets:
            source = piece.at[:, pl.ds(first, target.shape[1])]
            started.append(copies.start(source, target.at[pl.ds(at, count), :]))
            first += target.shape[1]
        at += count
    return started


def pair_gates(extra, width):
    me, peers = lax.axis_index("dp"), lax.axis_size("dp")
    lane = lax.broadcasted_iota(jnp.int32, extra.shape, 1)

    def gate(expert):
        return jnp.sum(jnp.where((lane == expert) | (lane == expert + peers), wide(extra), 0.0), axis=1, keepdims=True)

    column = lax.broadcasted_iota(jnp.int32, (extra.shape[0], width), 1)
    return jnp.where(column < width // 2, gate(me), gate(me ^ 1))


def expert_stage_body(count, w_gate, w_up, w_down, *refs):
    ins, (gate_out, up_out), outs = refs[:count], refs[count : count + 2], refs[count + 2 : 2 * count + 2]
    rows, extra, gate_held, up_held, part, sems = refs[2 * count + 2 :]
    copies, leaving = Copies(sems), []
    for copy in place(copies, ins, rows, extra):
        copy.wait()
    values = rows[...]
    gate = dot_nn(values, w_gate[...])
    up = dot_nn(values, w_up[...])
    gate_held[...] = gate.astype(bf16)
    leaving.append(copies.start(gate_held, gate_out))
    up_held[...] = up.astype(bf16)
    leaving.append(copies.start(up_held, up_out))
    act = gate / (1.0 + jnp.exp(-gate)) * up * pair_gates(extra[...], gate.shape[1])
    part[...] = dot_nn(act.astype(bf16), w_down[...]).astype(bf16)
    at = 0
    for out in outs:
        leaving.append(copies.start(part.at[pl.ds(at, out.shape[0]), :], out))
        at += out.shape[0]
    for copy in leaving:
        copy.wait()


def expert_stage(pieces, *weights):
    count = sum(p.shape[0] for p in pieces)
    model, units = weights[0].shape
    extra = pieces[0].shape[1] - model
    kind = held if HELD and len(pieces) == 3 else like
    shapes = [like((count, units), bf16)] * 2 + [kind((p.shape[0], model), bf16) for p in pieces]
    scratch = [pltpu.VMEM((count, n), bf16) for n in (model, extra, units, units, model)]
    scratch.append(pltpu.SemaphoreType.DMA((3 * len(pieces) + 2,)))
    body = functools.partial(expert_stage_body, len(pieces))
    outs = on_device(
        body, shapes, [], 6 * count * weights[0].size, kept=weights, far=pieces, scratch=scratch, direct=True
    )
    return outs[2:], (pieces, *outs[:2])


def expert_back_body(count, w_gate, w_up, w_down, *refs):
    ins, payloads, (gate_in, up_in) = refs[:count], refs[count : 2 * count], refs[2 * count : 2 * count + 2]
    grad_outs, outs = refs[2 * count + 2 : 2 * count + 5], refs[2 * count + 5 : 3 * count + 5]
    grads, extra, gate_held, up_held, *held_back, part, sems = refs[3 * count + 5 :]
    copies, leaving, first = Copies(sems), [], w_gate.shape[0]
    arriving = place(copies, ins, grads)
    at = 0
    for payload in payloads:
        size = payload.shape[0]
        arriving.append(
            copies.start(payload.at[:, pl.ds(first, extra.shape[1])], extra.at[pl.ds(at, size), :])
        )
        at += size
    arriving += [copies.start(gate_in, gate_held), copies.start(up_in, up_held)]
    for copy in arriving:
        copy.wait()
    scale = pair_gates(extra[...], w_gate.shape[1])
    grad_act = scale * dot_nt(grads[...], w_down[...])
    gate, up = wide(gate_held[...]), wide(up_held[...])
    sig = 1.0 / (1.0 + jnp.exp(-gate))
    silu = gate * sig
    low_gate = (grad_act * up * sig * (1.0 + gate * (1.0 - sig))).astype(bf16)
    low_up = (grad_act * silu).astype(bf16)
    for value, held_value, out in zip((low_gate, low_up, (scale * silu * up).astype(bf16)), held_back, grad_outs):
        held_value[...] = value
        leaving.append(copies.start(held_value, out))
    part[...] = (dot_nt(low_gate, w_gate[...]) + dot_nt(low_up, w_up[...])).astype(bf16)
    at = 0
    for out in outs:
        leaving.append(copies.start(part.at[pl.ds(at, out.shape[0]), :], out))
        at += out.shape[0]
    for copy in leaving:
        copy.wait()


def expert_back_stage(pieces, saved, *weights):
    payloads, gate_out, up_out = saved
    count = sum(p.shape[0] for p in pieces)
    model, units = weights[0].shape
    extra = payloads[0].shape[1] - model
    kind = held if HELD and len(pieces) == 3 else like
    shapes = [like((count, units), bf16)] * 3 + [kind((p.shape[0], model), bf16) for p in pieces]
    scratch = [pltpu.VMEM((count, n), bf16) for n in (model, extra, units, units, units, units, units, model)]
    scratch.append(pltpu.SemaphoreType.DMA((3 * len(pieces) + 5,)))
    body = functools.partial(expert_back_body, len(pieces))
    far = [*pieces, *payloads, gate_out, up_out]
    outs = on_device(
        body, shapes, [], 6 * count * weights[0].size, kept=weights, far=far, scratch=scratch, direct=True
    )
    return outs[3:], (payloads, pieces, *outs[:3])


def swept_products(swept, fixed, sums, swept_left, final):
    width = fixed[0][0].shape[1]
    step, steps = width // 2, 4
    rows = sum(t.shape[0] for t in swept)

    def body(*refs):
        refs = list(refs)
        left = jnp.concatenate([refs.pop(0)[...] for _ in swept], axis=0)
        rights = [jnp.concatenate([refs.pop(0)[...] for _ in group], axis=0) for group in fixed]
        totals = [refs.pop(0)[...] for _ in sums or ()] or [0.0] * len(fixed)
        others = []
        for total, right in zip(totals, rights):
            total = total + (dot_tn(left, right) if swept_left else dot_tn(right, left))
            if final:
                parts = (total[:, :step], total[:, step:]) if swept_left else (total[:step], total[step:])
                refs.pop(0)[...] = parts[0]
                others.append(parts[1].astype(bf16))
            else:
                refs.pop(0)[...] = total
        if final:
            refs.pop(0)[...] = jnp.concatenate(others, axis=1 if swept_left else 0)

    def spec(size):
        return pl.BlockSpec((step, size), lambda j: (j, 0)) if swept_left else pl.BlockSpec((size, step), lambda j: (0, j))

    def shape(size):
        return (step * steps, size) if swept_left else (size, step * steps)

    sizes = [(step if final else width, f32)] * len(fixed) + [(step * len(fixed), bf16)] * final
    shapes = [like(shape(size), dtype) for size, dtype in sizes]
    out_specs = [spec(size) for size, _ in sizes]
    in_specs = [pl.BlockSpec((t.shape[0], step), lambda j: (0, j)) for t in swept]
    in_specs += [pl.BlockSpec(t.shape, lambda j: (0, 0)) for group in fixed for t in group]
    in_specs += [spec(width) for _ in sums or ()]
    return pl.pallas_call(
        body,
        grid=(steps,),
        out_shape=shapes,
        in_specs=in_specs,
        out_specs=out_specs,
        compiler_params=pltpu.CompilerParams(vmem_limit_bytes=KERNEL_VMEM),
        cost_estimate=pl.CostEstimate(flops=COST * 2 * rows * width * step * steps * len(fixed), bytes_accessed=rows, transcendentals=0),
    )(*map(distant, [*swept, *[t for group in fixed for t in group], *(sums or ())]))


def expert_forward(rows, w_gate, w_up, w_down):
    gate_out = dot_nn(rows, w_gate)
    up_out = dot_nn(rows, w_up)
    act = (gate_out / (1.0 + jnp.exp(-gate_out)) * up_out).astype(bf16)
    part = dot_nn(act, w_down).astype(bf16)
    return part, (rows, gate_out.astype(bf16), up_out.astype(bf16))


def expert_backward(grad_rows, saved, w_gate, w_up, w_down):
    rows, gate_low, up_low = saved
    gate_out, up_out = wide(gate_low), wide(up_low)
    grad_act = dot_nt(grad_rows, w_down)
    sig = 1.0 / (1.0 + jnp.exp(-gate_out))
    silu = gate_out * sig
    grad_gate = (grad_act * up_out * sig * (1.0 + gate_out * (1.0 - sig))).astype(bf16)
    grad_up = (grad_act * silu).astype(bf16)
    act = (silu * up_out).astype(bf16)
    grad_in = (dot_nt(grad_gate, w_gate) + dot_nt(grad_up, w_up)).astype(bf16)
    return grad_in, (dot_tn(rows, grad_gate), dot_tn(rows, grad_up), dot_tn(act, grad_rows))


def halves(array):
    half = array.shape[0] // 2
    return array[:half], array[half:]


def owned_body(turns, groups, blocks, with_last, gains, *refs):
    refs = list(refs)
    lefts = [refs.pop(0) for _ in range(turns)]
    rights = [[refs.pop(0) for _ in range(turns + with_last)] for _ in range(groups)]
    last = [refs.pop(0) for _ in range(4 * with_last)]
    gains = [refs.pop(0)[...] for _ in range(gains)]
    outs, products, sems = refs[: 2 * len(blocks)], refs[-2], refs[-1]
    values = [t[...] for t in lefts]
    if with_last:
        grad, grad_two, hidden, gain = last
        total = hidden[...]
        back, _ = norm_back(total, norm_factor(total), gain[...], grad_two[...])
        values.append((wide(grad[...]) + back).astype(bf16))
    left = jnp.concatenate(values, axis=0)
    for g in range(groups):
        right = jnp.concatenate([t[...] for t in rights[g]], axis=0)
        products[g, :, : right.shape[1]] = dot_tn(left, right).astype(bf16)
        if gains:
            terms, at = [], right.shape[1]
            for gain in gains:
                high = gain.astype(bf16)
                terms += [high, (gain - wide(high)).astype(bf16)]
            rows = jnp.concatenate(terms + [jnp.zeros_like(terms[0])] * (-len(terms) % 16), axis=0)
            which = lax.broadcasted_iota(jnp.int32, (rows.shape[0], 128), 0)
            column = lax.broadcasted_iota(jnp.int32, (rows.shape[0], 128), 1)
            chosen = (column == (which // 2) % 2) & (which < len(terms))
            products[g, :, at : at + 128] = dot_tn(rows, jnp.where(chosen, 1.0, 0.0).astype(bf16)).astype(bf16)
    copies, leaving = Copies(sems), []
    me = lax.axis_index("dp")
    share = products.shape[1] // lax.axis_size("dp")
    for i, group in enumerate(blocks):
        for out, places in zip(outs[2 * i : 2 * i + 2], group):
            for j, (mask, side) in enumerate(places):
                rows = pl.ds(pl.multiple_of((me ^ mask) * share, share), share)
                leaving.append(copies.start(products.at[side, rows, :], out.at[pl.ds(j * share, share), :]))
    for copy in leaving:
        copy.wait()


def owned_products(cube, lefts, rights, last=(), gains=()):
    model, width = lefts[0].shape[1], rights[0][0].shape[1] + (128 if gains else 0)
    share = model // lax.axis_size("dp")
    stages = [[[(m ^ int(i), s) for m, s in side for i in cube.inner] for side in pair] for pair in cube.stages]
    own, near, middle, corner = stages
    blocks = [middle, [a + b + c for a, b, c in zip(own, near, corner)]]
    shapes = [like((len(places) * share, width), bf16) for pair in blocks for places in pair]
    scratch = [
        pltpu.VMEM((len(rights), model, width), bf16),
        pltpu.SemaphoreType.DMA((sum(len(places) for pair in blocks for places in pair),)),
    ]
    args = [*lefts, *[t for group in rights for t in group], *last, *gains]
    outs = pl.pallas_call(
        functools.partial(owned_body, len(lefts), len(rights), blocks, 1 if last else 0, len(gains)),
        out_shape=shapes,
        in_specs=[VMEM] * len(args),
        out_specs=[ANY] * len(shapes),
        scratch_shapes=scratch,
        compiler_params=pltpu.CompilerParams(vmem_limit_bytes=KERNEL_VMEM),
    )(*map(distant, args))
    return [(outs[2 * i], outs[2 * i + 1]) for i in range(len(blocks))]


class Blocks:
    def __init__(self, cube, weights):
        self.cube, self.weights = cube, weights

    def forward(self, payload, micro, side=()):
        saved = [None] * 4

        def work(stage, pieces):
            parts, saved[stage] = expert_stage(pieces, *self.weights)
            return parts

        return gather_rows(self.cube, payload, work, side), saved

    def backward(self, grad, micro, saved, side=()):
        keeps = [None] * 4

        def work(stage, pieces):
            parts, keeps[stage] = expert_back_stage(pieces, saved[stage], *self.weights)
            return parts

        return gather_rows(self.cube, grad, work, side), keeps

    def late_backward(self, pieces, saved):
        parts, keeps = [None] * 4, [None] * 4

        def run(*stages):
            def work(*gathered):
                for stage, rows in zip(stages, gathered):
                    parts[stage], keeps[stage] = expert_back_stage(rows, saved[stage], *self.weights)
                return [t for stage in stages for t in parts[stage]]

            return lambda: [pieces[stage] for stage in stages], work

        return run, parts, keeps

    def total_start(self, results, side=()):
        own, near, middle, corner = results
        arrived, corner, (own, near) = reduce_start(self.cube, middle, corner, (own, near), side)
        return arrived, corner, [[t] for t in near], own

    def total_finish(self, state, side=()):
        return reduce_finish(self.cube, *state, side)

    def total(self, results, side=()):
        return self.total_finish(self.total_start(results, side[:1]), side[1:])

    def weight_sums(self, slots, sums, final=False):
        def stages():
            return [stage for keeps in slots for stage in keeps]

        def hidden(*args):
            payloads, gates, ups = args
            sums[0] = swept_products(payloads, [gates, ups], sums[0], True, final)
            return sums[0]

        def down(*args):
            grads, acts = args
            sums[1] = swept_products(grads, [acts], sums[1], False, final)
            return sums[1]

        return [
            (lambda: [[t for s in stages() for t in s[0]], [s[2] for s in stages()], [s[3] for s in stages()]], hidden),
            (lambda: [[t for s in stages() for t in s[1]], [s[4] for s in stages()]], down),
        ]


def run_all(side):
    for thunk in side:
        if thunk is not None:
            thunk[1](*thunk[0]())


class Buckets:
    def __init__(self, cube, weights, routes, gates, capacity):
        self.cube, self.weights, self.capacity = cube, weights, capacity
        micros, self.rows, self.top = routes.shape
        self.experts = lax.axis_size("dp")
        self.tables = []
        for m in range(micros):
            flat = routes[m].reshape(-1)
            onehot = (flat[:, None] == jnp.arange(self.experts, dtype=jnp.int32)).astype(jnp.int32)
            earlier = jnp.cumsum(onehot, axis=0) - onehot
            target = flat * capacity + jnp.sum(earlier * onehot, axis=1)
            source = jnp.full((self.experts * capacity,), flat.shape[0], jnp.int32)
            source = source.at[target].set(jnp.arange(flat.shape[0], dtype=jnp.int32))
            self.tables.append((target, source, gates[m]))

    def table(self, micro):
        return jax.tree.map(lambda a, b: jnp.where(micro == 0, a, b), self.tables[0], self.tables[1])

    def exchange(self, rows):
        shape = (self.experts, self.capacity, rows.shape[1])
        moved = lax.all_to_all(rows.reshape(shape), "dp", split_axis=0, concat_axis=0, tiled=True)
        return moved.reshape(rows.shape)

    def whole(self, own):
        return jnp.concatenate([own, swap(own, self.cube.z)], axis=0)

    def forward(self, payload, micro, side=()):
        target, source, gates = self.table(micro)
        own = payload[:, : self.weights[0].shape[0]]
        padded = jnp.pad(self.whole(own), ((0, 1), (0, 0)))
        arrived = self.exchange(jnp.take(padded, source // self.top, axis=0))
        part, saved = expert_forward(arrived, *self.weights)
        picked = jnp.take(self.exchange(part), target, axis=0).reshape(self.rows, self.top, -1)
        run_all(side)
        return jnp.sum(gates[:, :, None] * picked, axis=1), saved

    def backward(self, grad, micro, saved, side=()):
        target, source, gates = self.table(micro)
        scaled = (gates[:, :, None] * wide(self.whole(grad))[:, None, :]).astype(bf16)
        padded = jnp.pad(scaled.reshape(self.rows * self.top, -1), ((0, 1), (0, 0)))
        arrived = self.exchange(jnp.take(padded, source, axis=0))
        grad_in, weights = expert_backward(arrived, saved, *self.weights)
        picked = jnp.take(self.exchange(grad_in), target, axis=0).reshape(self.rows, self.top, -1)
        run_all(side)
        return jnp.sum(picked, axis=1, dtype=f32), weights

    def total_start(self, results, side=()):
        run_all(side)
        return results

    def total_finish(self, results, side=()):
        own, other = halves(results.astype(bf16))
        run_all(side)
        return wide(own) + wide(swap(other, self.cube.z))

    def total(self, results, side=()):
        return self.total_finish(results, side)

    def weight_sums(self, slots, sums, final=False):
        def add(*slots):
            for weights in slots:
                for i, part in enumerate((list(weights[:2]), list(weights[2:]))):
                    sums[i] = part if sums[i] is None else [a + b for a, b in zip(sums[i], part)]

        return [None, (lambda: slots, add)]


def local(
    tokens, lengths, routes, gates, attn_gain, q_weight, key_projection, value_projection,
    o_weight, mlp_gain, expert_gate, expert_up, expert_down, cotangent,
):
    cube = Cube()
    section = lax.axis_index("section")
    shard = lax.axis_index("shard")
    me = lax.axis_index("dp")
    peers, shards = lax.axis_size("dp"), lax.axis_size("shard")
    _, block_rows, model = tokens.shape
    rows = block_rows // shards
    share = model // peers
    first = section == 0
    gain_one, gain_two = attn_gain[0][None], mlp_gain[0][None]
    weights = [q_weight[0], key_projection[0], value_projection[0], o_weight[0]]
    expert_w = (expert_gate[0, 0], expert_up[0, 0], expert_down[0, 0])
    capacity = 2 * block_rows * routes.shape[3] // peers
    whole_blocks = capacity >= block_rows

    def chosen(here, there):
        return jax.tree.map(lambda a, b: jnp.where(first, a, b), here, there)

    def begins(lens):
        lens = lens[:, 0]
        ends, longest = jnp.cumsum(lens, axis=1), jnp.argmax(lens, axis=1)
        return [ends[m, longest[m]] - lens[m, longest[m]] for m in range(2)]

    def turned(array, begin):
        doubled = jnp.concatenate([array, array], axis=0)
        return lax.dynamic_slice_in_dim(doubled, (begin + rows * shard) % block_rows, block_rows, 0)

    if not whole_blocks:
        early = begins(lengths)
        mixture = Buckets(
            cube,
            expert_w,
            jnp.stack([turned(routes[0, m], early[m]) for m in range(2)]),
            jnp.stack([turned(gates[0, m], early[m]) for m in range(2)]),
            capacity,
        )

    slices = [lax.dynamic_slice_in_dim(w, me * share, share, 0) for w in weights[:3]]
    qkv_slices = swap(jnp.concatenate(slices, axis=1), cube.z)
    half_share = share // 2
    mask = cube.x[1] | cube.y[1]
    far_places = [2 * (me ^ mask), 2 * (me ^ mask) + 1]
    plane_places = [2 * (me ^ m) for m in (0, cube.x[1], cube.y[1])]
    mate_bit = cube.core[1]

    def mate_places(places):
        return [p ^ (2 * mate_bit) for p in places]

    def parted(own):
        half = model // shards
        given = lax.dynamic_slice_in_dim(own, (1 - shard) * half, half, 1)
        return lax.dynamic_slice_in_dim(own, shard * half, half, 1), given.astype(bf16)

    def placed(parts, m, got=None):
        kept, given = parts
        got = (swap(given, cube.z) if got is None else got).astype(kept.dtype)
        low = jnp.where(shard == 0, kept, got)
        high = jnp.where(shard == 0, got, kept)
        return lax.dynamic_slice_in_dim(
            jnp.concatenate([low, high, low, high], axis=0), (block_rows - starts[m]) % block_rows, block_rows, 0
        )

    cot_own, cot_other = turned_block(lengths, cotangent)
    own_near = [swap(cot_own, d) for d in (cube.x, cube.y)] if whole_blocks else []
    opened, mask0 = opening(lengths, tokens, gain_one, weights)
    settled = [tokens, cotangent, routes, gates]
    out_raw = weights[3]
    mates = [swap(expert_w[0], cube.core)] if whole_blocks else []
    opened, qkv_slices, own_near, cot_other, settled, mates, expert_w, out_raw = together(
        (opened, qkv_slices, own_near, cot_other, settled, mates, expert_w, out_raw)
    )
    out_slices = lax.dynamic_slice_in_dim(out_raw, me * share, share, 0)
    inputs, part, qkv, heads, sent = opened
    *settled, route_rows, gate_rows = settled
    settled += [[t[0, m].T for m in range(2)] for t in (route_rows, gate_rows)]
    other_near = [swap(cot_other, d) for d in (cube.x, cube.y)] if whole_blocks else []
    if whole_blocks:
        mates.append(swap(expert_w[1], cube.core))
    arrived, other_near, settled, mates, expert_w, out_slices = together(
        (swap(sent, cube.z), other_near, settle(lengths, *settled), mates, expert_w, out_slices)
    )
    fresh1, cot1, mask1, extra0, extra1, starts = settled
    hidden, payload = joined(part, arrived, gain_two, extra0)
    if whole_blocks:
        payload, expert_w, mates = together((payload, expert_w, mates))
        mates.append(swap(expert_w[2], cube.core))
        expert_w = pinned(list(zip(expert_w, mates)), (1, 1, 0))
        mixture = Blocks(cube, expert_w)
        plane = []

        def first_plane(qkv_slices, out_slices):
            near = [qkv_slices] + [swap(qkv_slices, d) for d in (cube.x, cube.y, ("dp", mask))]
            plane.extend([near, swap(out_slices, cube.z)])
            return plane

        side = [None, None, (lambda: [qkv_slices, out_slices], first_plane)]
        results, saved = mixture.forward(payload, 0, side)
        qkv_near, out_slices = plane
    else:
        results, saved = mixture.forward(payload, 0)
    first_mates = []

    def first_exchange(*near):
        first_mates.extend(swap(t, cube.core) for t in near)
        return first_mates

    mids = []

    def first_choice(*both_micros):
        mids.append(chosen(both_micros[2:], both_micros[:2]))
        mids.append(chosen(both_micros[:2], both_micros[2:]))
        return mids

    choice = (lambda: [mask0, extra0, mask1, extra1], first_choice)
    total = mixture.total(results, [both((lambda: qkv_near, first_exchange), choice) if whole_blocks else choice])
    result0 = (hidden + total).astype(bf16)
    if whole_blocks:
        result0, qkv_near, out_slices = together((result0, qkv_near, out_slices))
        arriving = lax.ppermute(result0, "section", [(0, 1)])
        out_near = [out_slices] + [swap(out_slices, d) for d in (cube.x, cube.y, ("dp", mask))]
        all_places = [*plane_places, far_places[0]]
        places = [*all_places, *mate_places(all_places)]

        def assembled(pieces):
            spans = [(p, half_share, 0) for p in places]
            return put_together(pieces, spans, (model, pieces[0].shape[1]))

        arriving, out_near, weights, qkv_packed = together(
            (arriving, out_near, pinned(weights), assembled([*qkv_near, *first_mates]))
        )
        packed = [qkv_packed, assembled([*out_near, *[swap(t, cube.core) for t in out_near]])]
    else:
        arriving = lax.ppermute(result0, "section", [(0, 1)])
        packed = [
            lax.all_gather(t, "dp", axis=0, tiled=True) for t in (qkv_slices, swap(out_slices, cube.z))
        ]

    (mask_mid, extra_mid), (mask_last, extra_last) = mids

    inputs1, hidden1, payload, groups1 = attention_forward(
        fresh1, arriving, mask_mid, gain_one, gain_two, extra_mid, weights, packed
    )
    micro_mid = 1 - section
    late = []

    def cot_far(x0, y1):
        late.extend([swap(x0, cube.y), swap(y1, cube.x)])
        return late

    side = []
    if whole_blocks:
        (x0, y0), (x1, y1) = own_near, other_near
        side = [None, None, (lambda: [x0, y1], cot_far)]
    results, saved1 = mixture.forward(payload, micro_mid, side)

    grad0 = cot_own
    if whole_blocks:
        pieces = [[cot_own], [x0, y0, cot_other], [late[0], y1, x1], [late[1]]]
        run, back_results, keeps0 = mixture.late_backward(pieces, saved1)
        total = mixture.total(results, [run(2), run(1, 0)])
        back_results[3] = run(3)
    else:
        back_results, keeps0 = mixture.backward(grad0, micro_mid, saved1)
        total = mixture.total(results)
    result1 = (hidden1 + total).astype(bf16)

    slot2 = []

    def last_attention(arriving):
        slot2.extend(
            attention_forward(inputs, arriving, mask_last, gain_one, gain_two, extra_last, weights, packed)
        )
        return slot2

    arrived = []

    def second_handoff(result):
        arrived.append(lax.ppermute(result, "section", [(0, 1)]))
        return arrived

    if whole_blocks:
        result1, back_results[:3] = together((result1, back_results[:3]))
    else:
        result1, back_results = together((result1, back_results))
    state = mixture.total_start(back_results, [(lambda: [result1], second_handoff)])
    grad_two = mixture.total_finish(state, [(lambda: arrived, last_attention)])
    inputs2, hidden2, payload, groups2 = slot2

    def attention_turn(grad, grad_two, state):
        inputs, hidden, mask, groups, _ = state
        outs = attention_backward(
            grad, grad_two, inputs, hidden, mask, gain_one, gain_two, [g[0] for g in groups], weights, packed
        )
        grad_input, low, grad_low, normed, g0, g1, attn_g, mlp_g = outs
        factors = (normed, grad_low, (g0, g1), [g[1] for g in groups])
        return grad_input, low, factors, (attn_g, mlp_g)

    state1 = [inputs1, hidden1, mask_mid, groups1, saved1]
    turn0, returned = [], []

    def first_turn(grad_two):
        turn0.extend(attention_turn(grad0, grad_two, state1))
        return turn0

    def first_return(low):
        returned.append(lax.ppermute(low, "section", [(1, 0)]))
        return returned

    side = [(lambda: [grad_two], first_turn), None, (lambda: [turn0[1]], first_return)]
    results2, saved2 = mixture.forward(payload, section, side)
    coming = returned[0]

    sums = [None, None]
    if whole_blocks:
        *results2, corner = results2
        coming, results2, inputs = together((coming, results2, corner[0]()))
        corner = corner[1](*inputs)
        results2 = [*results2, (lambda: [corner], lambda t: t)]
    else:
        coming, results2, saved2 = together((coming, results2, saved2))
    grad1 = coming + cot1
    state2 = [inputs2, hidden2, mask_last, groups2, saved2]
    back_results, keeps1 = mixture.backward(grad1, section, saved2)
    def run_both(*works):
        works = [w for w in works if w]
        return both(*works) if works else None

    placings = {}

    def placing(name, micro, own):
        def work(rows):
            placings[name, micro] = placed(parted(rows), micro)
            return placings[name, micro]

        return lambda: [own()], work

    hidden_work, _ = mixture.weight_sums([keeps0], sums)
    _, down_work = mixture.weight_sums([keeps0, keeps1], sums)
    place_first = placing("out", 0, lambda: chosen(result0, result1))
    grad_two = mixture.total(back_results, [run_both(place_first, hidden_work)])
    grad_two, down_inputs = together((grad_two, down_work[0]())) if down_work else (grad_two, ())
    turn1 = attention_turn(grad1, grad_two, state2)
    if whole_blocks:
        low, results2[:3] = together((turn1[1], list(results2[:3])))
    else:
        low, results2 = together((turn1[1], results2))
    coming = lax.ppermute(low, "section", [(1, 0)])
    state = mixture.total_start(results2)
    grad2, state, _ = together((coming, state, down_work[1](*down_inputs) if down_work else ()))

    last_total = []

    def finish_last(*state):
        last_total.append(mixture.total_finish(state[0] if len(state) == 1 else state))
        return last_total

    hidden_work, _ = mixture.weight_sums([keeps1], sums)
    side = [None, None, run_both((lambda: [state] if not whole_blocks else list(state), finish_last), hidden_work)]
    back_results, keeps2 = mixture.backward(grad2, 1 - section, saved1, side)
    result2 = (hidden2 + last_total[0]).astype(bf16)
    placing_out = placing("out", 1, lambda: chosen(result1, result2))
    placing_grad = placing("grad", 0, lambda: chosen(turn1[0], turn0[0]))
    hidden_end, down_end = mixture.weight_sums([keeps2], sums, True)
    waiting = []

    def part_both(out, grad):
        waiting.extend([parted(out), parted(grad)])
        return waiting

    part_work = (lambda: [chosen(result1, result2), chosen(turn1[0], turn0[0])], part_both)
    grad_two = mixture.total(back_results, [part_work, run_both(hidden_end or down_end)])

    _, hidden, _, groups, _ = state1
    others = [t for t in sums[0] if t.dtype == bf16]
    grad_two, others, waiting = together((grad_two, others, waiting))
    others = [swap(t, cube.core) for t in others]
    received = [swap(given, cube.z) for _, given in waiting]
    heads_all = [[groups1[g][1], groups2[g][1], groups1[g][1]] for g in range(shards)]
    out_pairs = owned_products(cube, [turn0[2][1], turn1[2][1]], heads_all, (grad2, grad_two, hidden, gain_two))
    out_pairs, others, received = together((out_pairs, others, received))
    turn2 = []

    def last_turn(grad_two):
        turn2.extend(attention_turn(grad2, grad_two, state1))
        return turn2

    def exchange(*others):
        return [swap(t, cube.core) for t in others]

    def sums_start(pairs, side):
        middle, rest = pairs
        size = middle[0].shape[0] // 3

        def blocks(*terms):
            return [[t[i : i + size] for t in terms] for i in range(0, terms[0].shape[0], size)]

        middle = [low_sum(*terms) for terms in blocks(middle[0], swap(middle[1], cube.core))]
        other = (lambda: [rest[1]], lambda t: [swap(t, cube.core)])
        arrived, other, mine = reduce_start(cube, middle, other, rest[0], side)
        own, *near, corner = blocks(mine, *other)
        return arrived, corner, near, own

    out_state = sums_start(out_pairs, [(lambda: [grad_two], last_turn)])
    turns = (turn0, turn1, turn2)
    factors = [t[2] for t in turns]
    qkv_pairs = []

    def qkv_products(*_):
        rights = [[f[2][g] for f in factors] for g in range(shards)]
        gains = [g for t in turns for g in t[3]]
        qkv_pairs.extend(owned_products(cube, [f[0] for f in factors], rights, gains=gains))
        return qkv_pairs

    grad_o = reduce_finish(cube, *out_state, [(lambda: [], qkv_products)])
    qkv_pairs, grad_o = together((qkv_pairs, grad_o))

    expert_sums = list(sums[0][:2])

    def hidden_sums(*others):
        for other in others:
            expert_sums[:2] = [mine + wide(t) for mine, t in zip(expert_sums, jnp.split(other, 2, axis=1))]
        return expert_sums

    def down_sums(*others):
        for other in others:
            expert_sums[2] = expert_sums[2] + wide(swap(other, cube.core))
        return expert_sums[2]

    def waited(*got):
        placings["out", 1], placings["grad", 0] = placed(waiting[0], 1, got[0]), placed(waiting[1], 0, got[1])
        return placings["out", 1], placings["grad", 0]

    last_rows = placing("grad", 1, lambda: chosen(turn2[0], turn1[0]))
    last_end = down_end if whole_blocks else None
    qkv_state = sums_start(qkv_pairs, [run_both(last_rows, last_end)])
    expert_sums.append(sums[1][0])
    last_side = run_both((lambda: sums[1][1:], down_sums), (lambda: others, hidden_sums), (lambda: received, waited))
    grad_qkv = reduce_finish(cube, *qkv_state, [last_side])
    gate_total, up_total, down_total = expert_sums
    width = q_weight.shape[2]
    grad_q = grad_qkv[:, :width]
    grad_k = grad_qkv[:, width : width + HEAD_SIZE]
    grad_v = grad_qkv[:, width + HEAD_SIZE : width + 2 * HEAD_SIZE]
    gain_pair = [grad_qkv[:, width + 2 * HEAD_SIZE + i] for i in range(2)]
    section_out = jnp.stack([placings["out", 0], placings["out", 1]])
    input_grad = jnp.stack([placings["grad", 0], placings["grad", 1]])
    return (
        section_out[None],
        input_grad[None],
        gain_pair[0][None],
        grad_q[None],
        grad_k[None],
        grad_v[None],
        grad_o[None],
        gain_pair[1][None],
        gate_total[None, None],
        up_total[None, None],
        down_total[None, None],
    )


def solution(mesh):
    in_specs = (
        P(None, "dp", None),
        P(None, "dp", None),
        P("section", None, "dp", None),
        P("section", None, "dp", None),
        P("section", None),
        P("section", None, "shard"),
        P("section", None, "shard"),
        P("section", None, "shard"),
        P("section", None, "shard"),
        P("section", None),
        P("section", "dp", None, "shard"),
        P("section", "dp", None, "shard"),
        P("section", "dp", "shard", None),
        P(None, "dp", None),
    )
    out_specs = (
        P("section", None, "dp", "shard"),
        P("section", None, "dp", "shard"),
        P("section", "dp"),
        P("section", "dp", "shard"),
        P("section", "dp", "shard"),
        P("section", "dp", "shard"),
        P("section", "dp", "shard"),
        P("section", "dp"),
        P("section", "dp", None, "shard"),
        P("section", "dp", None, "shard"),
        P("section", "dp", "shard", None),
    )
    return jax.shard_map(local, mesh=mesh, in_specs=in_specs, out_specs=out_specs, check_vma=False)
```

```python
import functools

import jax
import jax.numpy as jnp
import numpy as np
from jax import lax
from jax.experimental import pallas as pl
from jax.experimental.pallas import tpu as pltpu
from jax.sharding import PartitionSpec as P

HEAD_SIZE = 128
epsilon = 1e-06
masked_value = -1e30
bf16 = jnp.bfloat16
f32 = jnp.float32


def wide(a):
    return a.astype(f32)


def dot_nn(a, b):
    return lax.dot_general(a, b, (((1,), (0,)), ((), ())), preferred_element_type=f32)


def dot_nt(a, b):
    return lax.dot_general(a, b, (((1,), (1,)), ((), ())), preferred_element_type=f32)


def dot_tn(a, b):
    return lax.dot_general(a, b, (((0,), (0,)), ((), ())), preferred_element_type=f32)


class Cube:
    def __init__(self):
        peers = lax.axis_size("dp")
        bits = [1 << i for i in range(peers.bit_length() - 1)]
        rest = bits[1:]
        self.core = ("dp", bits[0])
        self.x = ("dp", rest[0])
        self.y = ("dp", rest[len(rest) // 2])
        self.z = ("shard", 1)
        self.extra = [("dp", b) for b in rest if b not in (self.x[1], self.y[1])]
        inner = [0]
        for _, bit in self.extra:
            inner = inner + [m | bit for m in inner]
        self.inner = np.array(inner)
        x, y = self.x[1], self.y[1]
        self.corner = (x | y, 1)
        stages = [[(0, 0)], [(x, 0), (y, 0), (0, 1)], [(x | y, 0), (y, 1), (x, 1)], [self.corner]]
        self.stages = [(g, [(m | self.core[1], s) for m, s in g]) for g in stages]


def swap(value, direction):
    axis, bit = direction
    return lax.ppermute(value, axis, [(i, i ^ bit) for i in range(lax.axis_size(axis))])


def across(value, cube):
    mask, flip = cube.corner
    shards = lax.axis_size("shard")
    pairs = [
        (d * shards + s, (d ^ mask) * shards + (s ^ flip))
        for d in range(lax.axis_size("dp"))
        for s in range(shards)
    ]
    return lax.ppermute(value, ("dp", "shard"), pairs)


together = lax.optimization_barrier


def both(*thunks):
    def work(*groups):
        return [thunk[1](*group) for thunk, group in zip(thunks, groups)]

    return lambda: [thunk[0]() for thunk in thunks], work


def after(payload, thunks, step):
    if step >= len(thunks) or thunks[step] is None:
        return payload, lambda: ()
    inputs, work = thunks[step]
    payload, inputs = together((payload, inputs()))
    return payload, lambda: work(*inputs)


def gather_rows(cube, own, work, side=()):
    own, beside = after(own, side, 0)
    near = [swap(own, d) for d in (cube.x, cube.y, cube.z)]
    first = work(0, [own])
    near, first, _ = together((near, first, beside()))

    near, beside = after(near, side, 1)
    middle = [swap(block, d) for block, d in zip(near, (cube.y, cube.z, cube.x))]
    second = work(1, near)
    middle, second, _ = together((middle, second, beside()))

    middle, beside = after(middle, side, 2)
    corner = swap(middle[0], cube.z)
    third = work(2, middle)
    corner, third, _ = together((corner, third, beside()))
    return first, second, third, (lambda: [corner], lambda *blocks: work(3, list(blocks)))


def low_sum(*terms):
    return sum(wide(t) for t in terms).astype(bf16)


def reduce_start(cube, middle, corner, rest, side=()):
    (middle, rest), beside = after((middle, rest), side, 0)
    middle, inputs = together((middle, corner[0]()))
    arrived = [swap(t, d) for t, d in zip(middle, (cube.y, cube.z, cube.x))]
    return together((arrived, corner[1](*inputs), rest, beside()))[:3]


def reduce_finish(cube, arrived, corner, near, own, side=()):
    sent = [low_sum(*terms) for terms in [*([corner] if corner else []), *[[*t, a] for t, a in zip(near, arrived)]]]
    sent, beside = after(sent, side, 0)
    arrived = [swap(t, d) for t, d in zip(sent[-3:], (cube.x, cube.y, cube.z))]
    arrived += [across(t, cube) for t in sent[:-3]]
    arrived, own, _ = together((arrived, own, beside()))
    total = sum(wide(t) for t in [*own, *arrived])
    for direction in reversed(cube.extra):
        half = total.shape[0] // 2
        total = total[:half] + wide(swap(total[half:].astype(bf16), direction))
    return total


def norm_factor(values):
    return lax.rsqrt(jnp.mean(values * values, axis=1, keepdims=True) + epsilon)


def norm_back(values, factor, gain, grad):
    gain_grad = jnp.sum(grad * values * factor, axis=0, keepdims=True)
    scaled = grad * gain
    inner = jnp.mean(scaled * values, axis=1, keepdims=True)
    return factor * (scaled - values * factor * factor * inner), gain_grad


def stack_heads(rows):
    return jnp.concatenate(
        [rows[:, i : i + HEAD_SIZE] for i in range(0, rows.shape[1], HEAD_SIZE)], axis=0
    )


def spread_heads(stacked, rows):
    return jnp.concatenate(
        [stacked[i : i + rows] for i in range(0, stacked.shape[0], rows)], axis=1
    )


def head_probs(query, key, allowed):
    scores = jnp.where(allowed > 0.0, dot_nt(query, key) * HEAD_SIZE ** (-0.5), masked_value)
    exp_scores = jnp.exp(scores - jnp.max(scores, axis=1, keepdims=True))
    return exp_scores / jnp.sum(exp_scores, axis=1, keepdims=True)


def normed_rows(values, gain):
    return (values * norm_factor(values) * gain).astype(bf16)


def group_probs(qkv, allowed):
    width = qkv.shape[1] - 2 * HEAD_SIZE
    query = stack_heads(qkv[:, :width])
    key, value = qkv[:, width : width + HEAD_SIZE], qkv[:, width + HEAD_SIZE :]
    tiled = jnp.concatenate([allowed] * (width // HEAD_SIZE), axis=0)
    return query, key, value, head_probs(query, key, tiled)


def head_group(normed, allowed, weights, qkv, heads):
    *projections, w_out = weights
    at = 0
    for w in projections:
        part = dot_nn(normed, w()).astype(bf16)
        qkv[:, at : at + part.shape[1]] = part
        at += part.shape[1]
    _, _, value, probs = group_probs(qkv[...], allowed)
    heads[...] = spread_heads(dot_nn(probs.astype(bf16), value).astype(bf16), normed.shape[0])
    return dot_nt(heads[...], w_out())


VMEM = pl.BlockSpec(memory_space=pltpu.VMEM)
SMEM = pl.BlockSpec(memory_space=pltpu.SMEM)
ANY = pl.BlockSpec(memory_space=pl.ANY)
KERNEL_VMEM = 42 << 20
COST = 16
HELD = True


def held(shape, dtype):
    return pltpu.VMEM(shape, dtype)


def like(shape, dtype):
    return pltpu.HBM(shape, dtype)


def close(value):
    return pltpu.with_memory_space_constraint(value, pltpu.VMEM)


def distant(value):
    return pltpu.with_memory_space_constraint(value, pltpu.HBM)


def pinned(groups, axes=None):
    groups = [g if isinstance(g, (list, tuple)) else (g,) for g in groups]
    axes = axes or [0] * len(groups)
    values = [v for g in groups for v in g]
    shapes = [
        tuple(n * len(g) if i == axis else n for i, n in enumerate(g[0].shape)) for g, axis in zip(groups, axes)
    ]

    def body(*refs):
        ins, outs, sems = list(refs[: len(values)]), refs[len(values) : -1], refs[-1]
        copies, waits = Copies(sems), []
        for group, axis, out in zip(groups, axes, outs):
            for i, value in enumerate(group):
                size = value.shape[axis]
                place = [slice(None)] * axis + [pl.ds(i * size, size)]
                waits.append(copies.start(ins.pop(0), out.at[tuple(place)]))
        for copy in waits:
            copy.wait()

    return pl.pallas_call(
        body,
        out_shape=[held(shape, g[0].dtype) for g, shape in zip(groups, shapes)],
        in_specs=[ANY] * len(values),
        out_specs=[VMEM] * len(groups),
        scratch_shapes=[pltpu.SemaphoreType.DMA((len(values),))],
        compiler_params=pltpu.CompilerParams(vmem_limit_bytes=1 << 20),
    )(*map(distant, values))


def put_together(pieces, spans, shape):
    starts = jnp.stack([first for first, _, _ in spans]).astype(jnp.int32)

    def body(starts, *refs):
        ins, out, sems = refs[:-2], refs[-2], refs[-1]
        copies, waits = Copies(sems), []
        for i, (piece, (_, unit, column)) in enumerate(zip(ins, spans)):
            rows = pl.ds(pl.multiple_of(starts[i] * unit, unit), piece.shape[0])
            waits.append(copies.start(piece, out.at[rows, pl.ds(column, piece.shape[1])]))
        for copy in waits:
            copy.wait()

    return pl.pallas_call(
        body,
        out_shape=held(shape, pieces[0].dtype),
        in_specs=[SMEM] + [ANY] * len(pieces),
        out_specs=VMEM,
        scratch_shapes=[pltpu.SemaphoreType.DMA((len(pieces),))],
        compiler_params=pltpu.CompilerParams(vmem_limit_bytes=KERNEL_VMEM),
    )(starts, *map(distant, pieces))


class Copies:
    def __init__(self, sems):
        self.sems, self.count = sems, 0

    def start(self, source, target):
        copy = pltpu.make_async_copy(source, target, self.sems.at[self.count])
        self.count += 1
        copy.start()
        return copy

    def fetch(self, source, target):
        copy, waited = self.start(source, target), []

        def value():
            if not waited:
                copy.wait()
                waited.append(True)
            return target[...]

        return value


def on_device(body, outs, args, flops, scalars=(), kept=(), far=(), scratch=(), direct=False):
    moved = sum(a.size * a.dtype.itemsize for a in args)
    return pl.pallas_call(
        body,
        out_shape=outs,
        in_specs=[SMEM] * len(scalars) + [VMEM] * (len(args) + len(kept)) + [ANY] * len(far),
        out_specs=[SMEM if o.dtype == jnp.int32 else ANY if direct else VMEM for o in outs],
        scratch_shapes=scratch,
        compiler_params=pltpu.CompilerParams(vmem_limit_bytes=KERNEL_VMEM),
        cost_estimate=pl.CostEstimate(flops=COST * flops, bytes_accessed=moved, transcendentals=0),
    )(*scalars, *map(distant, args), *map(close, kept), *far)


def holders(*arrays):
    return [pltpu.VMEM(a.shape, a.dtype) for a in arrays] + [pltpu.SemaphoreType.DMA((len(arrays) + 1,))]


def geometry(lens, micro, side, rows, block):
    ends, total, best, start = [], 0, lens[micro, 0, 0], 0
    for i in range(lens.shape[2]):
        length = lens[micro, 0, i]
        if i:
            start = jnp.where(length > best, total, start)
            best = jnp.maximum(best, length)
        total = total + length
        ends.append(total)
    return ends, lax.rem(start + rows * side, block)


def positions(shape, axis, begin, block):
    place = lax.broadcasted_iota(jnp.int32, shape, axis) + begin
    return jnp.where(place >= block, place - block, place)


def selection(begin, rows, block):
    wanted = positions((rows, block), 0, begin, block)
    return (wanted == lax.broadcasted_iota(jnp.int32, (rows, block), 1)).astype(f32)


def sequence_mask(ends, begin, rows, block):
    row, col = [positions((rows, rows), axis, begin, block) for axis in (0, 1)]
    inside = sum(jnp.abs((row >= e).astype(jnp.int32) - (col >= e).astype(jnp.int32)) for e in ends)
    return ((inside == 0) & (col <= row)).astype(f32)


def gate_columns(pick, routes, gates):
    peers = lax.axis_size("dp")
    expert = lax.broadcasted_iota(jnp.int32, (128, routes.shape[1]), 0)
    table = jnp.zeros(expert.shape, f32)
    for k in range(routes.shape[0]):
        gate, route = gates[k : k + 1, :], routes[k : k + 1, :]
        high = wide(gate.astype(bf16))
        table += jnp.where(expert == route, high, 0.0) + jnp.where(expert == route + peers, gate - high, 0.0)
    return dot_nt(pick, table.astype(bf16)).astype(bf16)


def turned_body(lens, blocks, own, other, block_rows, sems):
    copy = Copies(sems).fetch(blocks.at[0], block_rows)
    block = block_rows.shape[0]
    here = jnp.where(lax.axis_index("section") == 0, 0.0, 1.0)
    shard = lax.axis_index("shard")
    for side, out in ((shard, own), (1 - shard, other)):
        _, begin = geometry(lens, 0, side, block // 2, block)
        out[...] = dot_nn((selection(begin, block // 2, block) * here).astype(bf16), copy()).astype(bf16)


def turned_block(lens, blocks):
    _, block, model = blocks.shape
    scratch = [pltpu.VMEM((block, model), bf16), pltpu.SemaphoreType.DMA((1,))]
    shapes = [like((block // 2, model), bf16)] * 2
    return on_device(
        turned_body, shapes, [], 2 * block * block * model, (lens,), far=[distant(blocks)], scratch=scratch
    )


def opening_body(lens, gain, tokens, *refs):
    wq, wk, wv, wo, inputs, part, sent, mask, qkv, heads, *scratch, sems = refs
    copies = Copies(sems)
    sources = [tokens.at[0], wq, wk, wv, wo]
    block_rows, *weights = [copies.fetch(a, b) for a, b in zip(sources, scratch)]
    block = tokens.shape[1]
    rows = block // 2
    shard = lax.axis_index("shard")
    first = jnp.where(lax.axis_index("section") == 0, 1.0, 0.0)
    sides = []
    for side in (shard, 1 - shard):
        ends, begin = geometry(lens, 0, side, rows, block)
        sides.append((selection(begin, rows, block) * first, sequence_mask(ends, begin, rows, block)))
    values = dot_nn(jnp.concatenate([pick for pick, _ in sides], axis=0).astype(bf16), block_rows())
    inputs[...] = values[:rows].astype(bf16)
    mask[...] = sides[0][1]
    normed = normed_rows(values, gain[...])
    *projections, w_out = weights
    projected = jnp.concatenate([dot_nn(normed, w()).astype(bf16) for w in projections], axis=1)
    for i, (_, allowed) in enumerate(sides):
        here = pl.ds(i * rows, rows)
        qkv[here, :] = projected[i * rows : (i + 1) * rows]
        _, _, value, probs = group_probs(qkv[here, :], allowed)
        heads[here, :] = spread_heads(dot_nn(probs.astype(bf16), value).astype(bf16), rows)
    result = dot_nt(heads[...], w_out())
    part[...] = values[:rows] + result[:rows]
    sent[...] = result[rows:].astype(bf16)


def opening(lens, tokens, gain, weights):
    _, block, model = tokens.shape
    rows = block // 2
    width, out = sum(w.shape[1] for w in weights[:3]), weights[3].shape[1]
    shapes = [
        like((rows, model), bf16), like((rows, model), f32), like((rows, model), bf16), like((rows, rows), f32)
    ]
    scratch = [pltpu.VMEM((block, n), bf16) for n in (width, out, model)] + holders(*weights)
    return on_device(
        opening_body, shapes, [gain], 4 * rows * model * (width + out), (lens,),
        far=[distant(t) for t in (tokens, *weights)], scratch=scratch,
    )


def settle_body(lens, routes0, gates0, routes1, gates1, tokens, grad, *refs):
    fresh, cot, mask, extra0, extra1, starts, token_rows, grad_rows, sems = refs
    copies = Copies(sems)
    for micro in range(2):
        _, starts[micro] = geometry(lens, micro, 0, tokens.shape[1] // 2, tokens.shape[1])
    token_rows = copies.fetch(tokens.at[1], token_rows)
    grad_rows = copies.fetch(grad.at[1], grad_rows)
    block = tokens.shape[1]
    rows = block // 2
    first = jnp.where(lax.axis_index("section") == 0, 1.0, 0.0)
    for micro, routes, gates, extra in ((0, routes0, gates0, extra0), (1, routes1, gates1, extra1)):
        ends, begin = geometry(lens, micro, lax.axis_index("shard"), rows, block)
        pick = selection(begin, rows, block)
        extra[...] = gate_columns(pick.astype(bf16), routes[...], gates[...])
    fresh[...] = dot_nn((pick * first).astype(bf16), token_rows()).astype(bf16)
    cot[...] = dot_nn((pick * (1.0 - first)).astype(bf16), grad_rows()).astype(bf16)
    mask[...] = sequence_mask(ends, begin, rows, block)


def settle(lens, tokens, grad, routes, gates):
    _, block, model = tokens.shape
    rows = block // 2
    shapes = [like((rows, model), bf16)] * 2 + [like((rows, rows), f32)] + [like((rows, 128), bf16)] * 2
    shapes.append(pltpu.SMEM((2,), jnp.int32))
    args = [routes[0], gates[0], routes[1], gates[1]]
    scratch = [pltpu.VMEM((block, model), bf16)] * 2 + [pltpu.SemaphoreType.DMA((2,))]
    return on_device(
        settle_body, shapes, args, 2 * block * block * model, (lens,), far=[distant(tokens), distant(grad)], scratch=scratch
    )


def joined_body(part, other, extra, gain, hidden, payload):
    total = part[...] + wide(other[...])
    hidden[...] = total
    model = total.shape[1]
    payload[:, :model] = normed_rows(total, gain[...])
    payload[:, model:] = extra[...]


def joined(part, other, gain, extra):
    rows, model = part.shape
    shapes = [like((rows, model), f32), like((rows, model + extra.shape[1]), bf16)]
    return on_device(joined_body, shapes, [part, other, extra, gain], 10 * rows * model)


def by_halves(refs):
    *own, packed, packed_out = refs
    widths = [w.shape[1] for w in own[:3]]
    firsts = [sum(widths[:i]) for i in range(3)]
    other = [lambda f=f, w=w: packed[:, f : f + w] for f, w in zip(firsts, widths)]
    return [lambda w=w: w[...] for w in own], [*other, lambda: packed_out[...]]


def attention_body(fresh, arriving, mask, extra, gain, gain_two, *refs):
    own, other = by_halves(refs[:6])
    inputs, hidden, payload, qkv0, qkv1, heads0, heads1 = refs[6:]
    rows = fresh[...] + arriving[...]
    inputs[...] = rows
    total = wide(rows)
    normed = normed_rows(total, gain[...])
    total = total + head_group(normed, mask[...], own, qkv0, heads0)
    total = total + head_group(normed, mask[...], other, qkv1, heads1)
    hidden[...] = total
    model = total.shape[1]
    payload[:, :model] = normed_rows(total, gain_two[...])
    payload[:, model:] = extra[...]


def attention_forward(fresh, arriving, mask, gain, gain_two, extra, weights, packed):
    rows, model = fresh.shape
    width, out = sum(w.shape[1] for w in weights[:3]), weights[3].shape[1]
    shapes = [
        like((rows, model), bf16), like((rows, model), f32), like((rows, model + extra.shape[1]), bf16),
        like((rows, width), bf16), like((rows, width), bf16), like((rows, out), bf16), like((rows, out), bf16),
    ]
    args = [fresh, arriving, mask, extra, gain, gain_two]
    outs = on_device(attention_body, shapes, args, 6 * rows * packed[0].size, kept=[*weights, *packed])
    inputs, hidden, payload, qkv0, qkv1, heads0, heads1 = outs
    return inputs, hidden, payload, [(qkv0, heads0), (qkv1, heads1)]


def attention_back_body(grad, grad_two, inputs, hidden, mask, q0, q1, gain, gain_two, *refs):
    own, other = by_halves(refs[:6])
    grad_input, grad_input_low, grad_low, normed, g0, g1, gain_grad, gain_two_grad = refs[6:]
    rows = inputs.shape[0]
    values = wide(inputs[...])
    normed[...] = normed_rows(values, gain[...])
    total = hidden[...]
    back, gain_two_grad[...] = norm_back(total, norm_factor(total), gain_two[...], grad_two[...])
    grad_hidden = wide(grad[...]) + back
    low = grad_hidden.astype(bf16)
    grad_low[...] = low
    grad_normed = jnp.zeros_like(grad_hidden)
    for qkv, weights, grad_qkv in ((q0, own, g0), (q1, other, g1)):
        query, key, value, probs = group_probs(qkv[...], mask[...])
        grad_heads = stack_heads(dot_nn(low, weights[3]()).astype(bf16))
        grad_probs = dot_nt(grad_heads, value)
        inner = jnp.sum(probs * grad_probs, axis=1, keepdims=True)
        grad_scores = (probs * (grad_probs - inner) * HEAD_SIZE ** (-0.5)).astype(bf16)
        grads = [
            spread_heads(dot_nn(grad_scores, key).astype(bf16), rows),
            dot_tn(grad_scores, query).astype(bf16),
            dot_tn(probs.astype(bf16), grad_heads).astype(bf16),
        ]
        at = 0
        for part, w in zip(grads, weights):
            grad_qkv[:, at : at + part.shape[1]] = part
            at += part.shape[1]
            grad_normed = grad_normed + dot_nt(part, w())
    back, gain_grad[...] = norm_back(values, norm_factor(values), gain[...], grad_normed)
    result = grad_hidden + back
    grad_input[...] = result
    grad_input_low[...] = result.astype(bf16)


def attention_backward(grad, grad_two, inputs, hidden, mask, gain, gain_two, projected, weights, packed):
    rows, model = inputs.shape
    width = projected[0].shape[1]
    shapes = [
        like((rows, model), f32), like((rows, model), bf16), like((rows, model), bf16),
        like((rows, model), bf16), like((rows, width), bf16), like((rows, width), bf16),
        like((1, model), f32), like((1, model), f32),
    ]
    args = [grad, grad_two, inputs, hidden, mask, *projected, gain, gain_two]
    return on_device(attention_back_body, shapes, args, 12 * rows * packed[0].size, kept=[*weights, *packed])


def place(copies, pieces, *targets):
    started, at = [], 0
    for piece in pieces:
        first, count = 0, piece.shape[0]
        for target in targets:
            source = piece.at[:, pl.ds(first, target.shape[1])]
            started.append(copies.start(source, target.at[pl.ds(at, count), :]))
            first += target.shape[1]
        at += count
    return started


def pair_gates(extra, width):
    me, peers = lax.axis_index("dp"), lax.axis_size("dp")
    lane = lax.broadcasted_iota(jnp.int32, extra.shape, 1)

    def gate(expert):
        return jnp.sum(jnp.where((lane == expert) | (lane == expert + peers), wide(extra), 0.0), axis=1, keepdims=True)

    column = lax.broadcasted_iota(jnp.int32, (extra.shape[0], width), 1)
    return jnp.where(column < width // 2, gate(me), gate(me ^ 1))


def expert_stage_body(count, w_gate, w_up, w_down, *refs):
    ins, (gate_out, up_out), outs = refs[:count], refs[count : count + 2], refs[count + 2 : 2 * count + 2]
    rows, extra, gate_held, up_held, part, sems = refs[2 * count + 2 :]
    copies, leaving = Copies(sems), []
    for copy in place(copies, ins, rows, extra):
        copy.wait()
    values = rows[...]
    gate = dot_nn(values, w_gate[...])
    up = dot_nn(values, w_up[...])
    gate_held[...] = gate.astype(bf16)
    leaving.append(copies.start(gate_held, gate_out))
    up_held[...] = up.astype(bf16)
    leaving.append(copies.start(up_held, up_out))
    act = gate / (1.0 + jnp.exp(-gate)) * up * pair_gates(extra[...], gate.shape[1])
    part[...] = dot_nn(act.astype(bf16), w_down[...]).astype(bf16)
    at = 0
    for out in outs:
        leaving.append(copies.start(part.at[pl.ds(at, out.shape[0]), :], out))
        at += out.shape[0]
    for copy in leaving:
        copy.wait()


def expert_stage(pieces, *weights):
    count = sum(p.shape[0] for p in pieces)
    model, units = weights[0].shape
    extra = pieces[0].shape[1] - model
    kind = held if HELD and len(pieces) == 3 else like
    shapes = [like((count, units), bf16)] * 2 + [kind((p.shape[0], model), bf16) for p in pieces]
    scratch = [pltpu.VMEM((count, n), bf16) for n in (model, extra, units, units, model)]
    scratch.append(pltpu.SemaphoreType.DMA((3 * len(pieces) + 2,)))
    body = functools.partial(expert_stage_body, len(pieces))
    outs = on_device(
        body, shapes, [], 6 * count * weights[0].size, kept=weights, far=pieces, scratch=scratch, direct=True
    )
    return outs[2:], (pieces, *outs[:2])


def expert_back_body(count, w_gate, w_up, w_down, *refs):
    ins, payloads, (gate_in, up_in) = refs[:count], refs[count : 2 * count], refs[2 * count : 2 * count + 2]
    grad_outs, outs = refs[2 * count + 2 : 2 * count + 5], refs[2 * count + 5 : 3 * count + 5]
    grads, extra, gate_held, up_held, *held_back, part, sems = refs[3 * count + 5 :]
    copies, leaving, first = Copies(sems), [], w_gate.shape[0]
    arriving = place(copies, ins, grads)
    at = 0
    for payload in payloads:
        size = payload.shape[0]
        arriving.append(
            copies.start(payload.at[:, pl.ds(first, extra.shape[1])], extra.at[pl.ds(at, size), :])
        )
        at += size
    arriving += [copies.start(gate_in, gate_held), copies.start(up_in, up_held)]
    for copy in arriving:
        copy.wait()
    scale = pair_gates(extra[...], w_gate.shape[1])
    grad_act = scale * dot_nt(grads[...], w_down[...])
    gate, up = wide(gate_held[...]), wide(up_held[...])
    sig = 1.0 / (1.0 + jnp.exp(-gate))
    silu = gate * sig
    low_gate = (grad_act * up * sig * (1.0 + gate * (1.0 - sig))).astype(bf16)
    low_up = (grad_act * silu).astype(bf16)
    for value, held_value, out in zip((low_gate, low_up, (scale * silu * up).astype(bf16)), held_back, grad_outs):
        held_value[...] = value
        leaving.append(copies.start(held_value, out))
    part[...] = (dot_nt(low_gate, w_gate[...]) + dot_nt(low_up, w_up[...])).astype(bf16)
    at = 0
    for out in outs:
        leaving.append(copies.start(part.at[pl.ds(at, out.shape[0]), :], out))
        at += out.shape[0]
    for copy in leaving:
        copy.wait()


def expert_back_stage(pieces, saved, *weights):
    payloads, gate_out, up_out = saved
    count = sum(p.shape[0] for p in pieces)
    model, units = weights[0].shape
    extra = payloads[0].shape[1] - model
    kind = held if HELD and len(pieces) == 3 else like
    shapes = [like((count, units), bf16)] * 3 + [kind((p.shape[0], model), bf16) for p in pieces]
    scratch = [pltpu.VMEM((count, n), bf16) for n in (model, extra, units, units, units, units, units, model)]
    scratch.append(pltpu.SemaphoreType.DMA((3 * len(pieces) + 5,)))
    body = functools.partial(expert_back_body, len(pieces))
    far = [*pieces, *payloads, gate_out, up_out]
    outs = on_device(
        body, shapes, [], 6 * count * weights[0].size, kept=weights, far=far, scratch=scratch, direct=True
    )
    return outs[3:], (payloads, pieces, *outs[:3])


def swept_products(swept, fixed, sums, swept_left, final):
    width = fixed[0][0].shape[1]
    step, steps = width // 2, 4
    rows = sum(t.shape[0] for t in swept)

    def body(*refs):
        refs = list(refs)
        left = jnp.concatenate([refs.pop(0)[...] for _ in swept], axis=0)
        rights = [jnp.concatenate([refs.pop(0)[...] for _ in group], axis=0) for group in fixed]
        totals = [refs.pop(0)[...] for _ in sums or ()] or [0.0] * len(fixed)
        others = []
        for total, right in zip(totals, rights):
            total = total + (dot_tn(left, right) if swept_left else dot_tn(right, left))
            if final:
                parts = (total[:, :step], total[:, step:]) if swept_left else (total[:step], total[step:])
                refs.pop(0)[...] = parts[0]
                others.append(parts[1].astype(bf16))
            else:
                refs.pop(0)[...] = total
        if final:
            refs.pop(0)[...] = jnp.concatenate(others, axis=1 if swept_left else 0)

    def spec(size):
        return pl.BlockSpec((step, size), lambda j: (j, 0)) if swept_left else pl.BlockSpec((size, step), lambda j: (0, j))

    def shape(size):
        return (step * steps, size) if swept_left else (size, step * steps)

    sizes = [(step if final else width, f32)] * len(fixed) + [(step * len(fixed), bf16)] * final
    shapes = [like(shape(size), dtype) for size, dtype in sizes]
    out_specs = [spec(size) for size, _ in sizes]
    in_specs = [pl.BlockSpec((t.shape[0], step), lambda j: (0, j)) for t in swept]
    in_specs += [pl.BlockSpec(t.shape, lambda j: (0, 0)) for group in fixed for t in group]
    in_specs += [spec(width) for _ in sums or ()]
    return pl.pallas_call(
        body,
        grid=(steps,),
        out_shape=shapes,
        in_specs=in_specs,
        out_specs=out_specs,
        compiler_params=pltpu.CompilerParams(vmem_limit_bytes=KERNEL_VMEM),
        cost_estimate=pl.CostEstimate(flops=COST * 2 * rows * width * step * steps * len(fixed), bytes_accessed=rows, transcendentals=0),
    )(*map(distant, [*swept, *[t for group in fixed for t in group], *(sums or ())]))


def expert_forward(rows, w_gate, w_up, w_down):
    gate_out = dot_nn(rows, w_gate)
    up_out = dot_nn(rows, w_up)
    act = (gate_out / (1.0 + jnp.exp(-gate_out)) * up_out).astype(bf16)
    part = dot_nn(act, w_down).astype(bf16)
    return part, (rows, gate_out.astype(bf16), up_out.astype(bf16))


def expert_backward(grad_rows, saved, w_gate, w_up, w_down):
    rows, gate_low, up_low = saved
    gate_out, up_out = wide(gate_low), wide(up_low)
    grad_act = dot_nt(grad_rows, w_down)
    sig = 1.0 / (1.0 + jnp.exp(-gate_out))
    silu = gate_out * sig
    grad_gate = (grad_act * up_out * sig * (1.0 + gate_out * (1.0 - sig))).astype(bf16)
    grad_up = (grad_act * silu).astype(bf16)
    act = (silu * up_out).astype(bf16)
    grad_in = (dot_nt(grad_gate, w_gate) + dot_nt(grad_up, w_up)).astype(bf16)
    return grad_in, (dot_tn(rows, grad_gate), dot_tn(rows, grad_up), dot_tn(act, grad_rows))


def halves(array):
    half = array.shape[0] // 2
    return array[:half], array[half:]


def owned_body(turns, groups, blocks, with_last, gains, *refs):
    refs = list(refs)
    lefts = [refs.pop(0) for _ in range(turns)]
    rights = [[refs.pop(0) for _ in range(turns + with_last)] for _ in range(groups)]
    last = [refs.pop(0) for _ in range(4 * with_last)]
    gains = [refs.pop(0)[...] for _ in range(gains)]
    outs, products, sems = refs[: 2 * len(blocks)], refs[-2], refs[-1]
    values = [t[...] for t in lefts]
    if with_last:
        grad, grad_two, hidden, gain = last
        total = hidden[...]
        back, _ = norm_back(total, norm_factor(total), gain[...], grad_two[...])
        values.append((wide(grad[...]) + back).astype(bf16))
    left = jnp.concatenate(values, axis=0)
    for g in range(groups):
        right = jnp.concatenate([t[...] for t in rights[g]], axis=0)
        products[g, :, : right.shape[1]] = dot_tn(left, right).astype(bf16)
        if gains:
            terms, at = [], right.shape[1]
            for gain in gains:
                high = gain.astype(bf16)
                terms += [high, (gain - wide(high)).astype(bf16)]
            rows = jnp.concatenate(terms + [jnp.zeros_like(terms[0])] * (-len(terms) % 16), axis=0)
            which = lax.broadcasted_iota(jnp.int32, (rows.shape[0], 128), 0)
            column = lax.broadcasted_iota(jnp.int32, (rows.shape[0], 128), 1)
            chosen = (column == (which // 2) % 2) & (which < len(terms))
            products[g, :, at : at + 128] = dot_tn(rows, jnp.where(chosen, 1.0, 0.0).astype(bf16)).astype(bf16)
    copies, leaving = Copies(sems), []
    me = lax.axis_index("dp")
    share = products.shape[1] // lax.axis_size("dp")
    for i, group in enumerate(blocks):
        for out, places in zip(outs[2 * i : 2 * i + 2], group):
            for j, (mask, side) in enumerate(places):
                rows = pl.ds(pl.multiple_of((me ^ mask) * share, share), share)
                leaving.append(copies.start(products.at[side, rows, :], out.at[pl.ds(j * share, share), :]))
    for copy in leaving:
        copy.wait()


def owned_products(cube, lefts, rights, last=(), gains=()):
    model, width = lefts[0].shape[1], rights[0][0].shape[1] + (128 if gains else 0)
    share = model // lax.axis_size("dp")
    stages = [[[(m ^ int(i), s) for m, s in side for i in cube.inner] for side in pair] for pair in cube.stages]
    own, near, middle, corner = stages
    blocks = [middle, [a + b + c for a, b, c in zip(own, near, corner)]]
    shapes = [like((len(places) * share, width), bf16) for pair in blocks for places in pair]
    scratch = [
        pltpu.VMEM((len(rights), model, width), bf16),
        pltpu.SemaphoreType.DMA((sum(len(places) for pair in blocks for places in pair),)),
    ]
    args = [*lefts, *[t for group in rights for t in group], *last, *gains]
    outs = pl.pallas_call(
        functools.partial(owned_body, len(lefts), len(rights), blocks, 1 if last else 0, len(gains)),
        out_shape=shapes,
        in_specs=[VMEM] * len(args),
        out_specs=[ANY] * len(shapes),
        scratch_shapes=scratch,
        compiler_params=pltpu.CompilerParams(vmem_limit_bytes=KERNEL_VMEM),
    )(*map(distant, args))
    return [(outs[2 * i], outs[2 * i + 1]) for i in range(len(blocks))]


class Blocks:
    def __init__(self, cube, weights):
        self.cube, self.weights = cube, weights

    def forward(self, payload, micro, side=()):
        saved = [None] * 4

        def work(stage, pieces):
            parts, saved[stage] = expert_stage(pieces, *self.weights)
            return parts

        return gather_rows(self.cube, payload, work, side), saved

    def backward(self, grad, micro, saved, side=()):
        keeps = [None] * 4

        def work(stage, pieces):
            parts, keeps[stage] = expert_back_stage(pieces, saved[stage], *self.weights)
            return parts

        return gather_rows(self.cube, grad, work, side), keeps

    def late_backward(self, pieces, saved):
        parts, keeps = [None] * 4, [None] * 4

        def run(*stages):
            def work(*gathered):
                for stage, rows in zip(stages, gathered):
                    parts[stage], keeps[stage] = expert_back_stage(rows, saved[stage], *self.weights)
                return [t for stage in stages for t in parts[stage]]

            return lambda: [pieces[stage] for stage in stages], work

        return run, parts, keeps

    def total_start(self, results, side=()):
        own, near, middle, corner = results
        arrived, corner, (own, near) = reduce_start(self.cube, middle, corner, (own, near), side)
        return arrived, corner, [[t] for t in near], own

    def total_finish(self, state, side=()):
        return reduce_finish(self.cube, *state, side)

    def total(self, results, side=()):
        return self.total_finish(self.total_start(results, side[:1]), side[1:])

    def weight_sums(self, slots, sums, final=False):
        def stages():
            return [stage for keeps in slots for stage in keeps]

        def hidden(*args):
            payloads, gates, ups = args
            sums[0] = swept_products(payloads, [gates, ups], sums[0], True, final)
            return sums[0]

        def down(*args):
            grads, acts = args
            sums[1] = swept_products(grads, [acts], sums[1], False, final)
            return sums[1]

        return [
            (lambda: [[t for s in stages() for t in s[0]], [s[2] for s in stages()], [s[3] for s in stages()]], hidden),
            (lambda: [[t for s in stages() for t in s[1]], [s[4] for s in stages()]], down),
        ]


def run_all(side):
    for thunk in side:
        if thunk is not None:
            thunk[1](*thunk[0]())


class Buckets:
    def __init__(self, cube, weights, routes, gates, capacity):
        self.cube, self.weights, self.capacity = cube, weights, capacity
        micros, self.rows, self.top = routes.shape
        self.experts = lax.axis_size("dp")
        self.tables = []
        for m in range(micros):
            flat = routes[m].reshape(-1)
            onehot = (flat[:, None] == jnp.arange(self.experts, dtype=jnp.int32)).astype(jnp.int32)
            earlier = jnp.cumsum(onehot, axis=0) - onehot
            target = flat * capacity + jnp.sum(earlier * onehot, axis=1)
            source = jnp.full((self.experts * capacity,), flat.shape[0], jnp.int32)
            source = source.at[target].set(jnp.arange(flat.shape[0], dtype=jnp.int32))
            self.tables.append((target, source, gates[m]))

    def table(self, micro):
        return jax.tree.map(lambda a, b: jnp.where(micro == 0, a, b), self.tables[0], self.tables[1])

    def exchange(self, rows):
        shape = (self.experts, self.capacity, rows.shape[1])
        moved = lax.all_to_all(rows.reshape(shape), "dp", split_axis=0, concat_axis=0, tiled=True)
        return moved.reshape(rows.shape)

    def whole(self, own):
        return jnp.concatenate([own, swap(own, self.cube.z)], axis=0)

    def forward(self, payload, micro, side=()):
        target, source, gates = self.table(micro)
        own = payload[:, : self.weights[0].shape[0]]
        padded = jnp.pad(self.whole(own), ((0, 1), (0, 0)))
        arrived = self.exchange(jnp.take(padded, source // self.top, axis=0))
        part, saved = expert_forward(arrived, *self.weights)
        picked = jnp.take(self.exchange(part), target, axis=0).reshape(self.rows, self.top, -1)
        run_all(side)
        return jnp.sum(gates[:, :, None] * picked, axis=1), saved

    def backward(self, grad, micro, saved, side=()):
        target, source, gates = self.table(micro)
        scaled = (gates[:, :, None] * wide(self.whole(grad))[:, None, :]).astype(bf16)
        padded = jnp.pad(scaled.reshape(self.rows * self.top, -1), ((0, 1), (0, 0)))
        arrived = self.exchange(jnp.take(padded, source, axis=0))
        grad_in, weights = expert_backward(arrived, saved, *self.weights)
        picked = jnp.take(self.exchange(grad_in), target, axis=0).reshape(self.rows, self.top, -1)
        run_all(side)
        return jnp.sum(picked, axis=1, dtype=f32), weights

    def total_start(self, results, side=()):
        run_all(side)
        return results

    def total_finish(self, results, side=()):
        own, other = halves(results.astype(bf16))
        run_all(side)
        return wide(own) + wide(swap(other, self.cube.z))

    def total(self, results, side=()):
        return self.total_finish(results, side)

    def weight_sums(self, slots, sums, final=False):
        def add(*slots):
            for weights in slots:
                for i, part in enumerate((list(weights[:2]), list(weights[2:]))):
                    sums[i] = part if sums[i] is None else [a + b for a, b in zip(sums[i], part)]

        return [None, (lambda: slots, add)]


def local(
    tokens, lengths, routes, gates, attn_gain, q_weight, key_projection, value_projection,
    o_weight, mlp_gain, expert_gate, expert_up, expert_down, cotangent,
):
    cube = Cube()
    section = lax.axis_index("section")
    shard = lax.axis_index("shard")
    me = lax.axis_index("dp")
    peers, shards = lax.axis_size("dp"), lax.axis_size("shard")
    _, block_rows, model = tokens.shape
    rows = block_rows // shards
    share = model // peers
    first = section == 0
    gain_one, gain_two = attn_gain[0][None], mlp_gain[0][None]
    weights = [q_weight[0], key_projection[0], value_projection[0], o_weight[0]]
    expert_w = (expert_gate[0, 0], expert_up[0, 0], expert_down[0, 0])
    capacity = 2 * block_rows * routes.shape[3] // peers
    whole_blocks = capacity >= block_rows

    def chosen(here, there):
        return jax.tree.map(lambda a, b: jnp.where(first, a, b), here, there)

    def begins(lens):
        lens = lens[:, 0]
        ends, longest = jnp.cumsum(lens, axis=1), jnp.argmax(lens, axis=1)
        return [ends[m, longest[m]] - lens[m, longest[m]] for m in range(2)]

    def turned(array, begin):
        doubled = jnp.concatenate([array, array], axis=0)
        return lax.dynamic_slice_in_dim(doubled, (begin + rows * shard) % block_rows, block_rows, 0)

    if not whole_blocks:
        early = begins(lengths)
        mixture = Buckets(
            cube,
            expert_w,
            jnp.stack([turned(routes[0, m], early[m]) for m in range(2)]),
            jnp.stack([turned(gates[0, m], early[m]) for m in range(2)]),
            capacity,
        )

    slices = [lax.dynamic_slice_in_dim(w, me * share, share, 0) for w in weights[:3]]
    qkv_slices = swap(jnp.concatenate(slices, axis=1), cube.z)
    half_share = share // 2
    mask = cube.x[1] | cube.y[1]
    far_places = [2 * (me ^ mask), 2 * (me ^ mask) + 1]
    plane_places = [2 * (me ^ m) for m in (0, cube.x[1], cube.y[1])]
    mate_bit = cube.core[1]

    def mate_places(places):
        return [p ^ (2 * mate_bit) for p in places]

    def parted(own):
        half = model // shards
        given = lax.dynamic_slice_in_dim(own, (1 - shard) * half, half, 1)
        return lax.dynamic_slice_in_dim(own, shard * half, half, 1), given.astype(bf16)

    def placed(parts, m, got=None):
        kept, given = parts
        got = (swap(given, cube.z) if got is None else got).astype(kept.dtype)
        low = jnp.where(shard == 0, kept, got)
        high = jnp.where(shard == 0, got, kept)
        return lax.dynamic_slice_in_dim(
            jnp.concatenate([low, high, low, high], axis=0), (block_rows - starts[m]) % block_rows, block_rows, 0
        )

    cot_own, cot_other = turned_block(lengths, cotangent)
    own_near = [swap(cot_own, d) for d in (cube.x, cube.y)] if whole_blocks else []
    opened = opening(lengths, tokens, gain_one, weights)
    settled = [tokens, cotangent, routes, gates]
    out_raw = weights[3]
    mates = [swap(expert_w[0], cube.core)] if whole_blocks else []
    opened, qkv_slices, own_near, cot_other, settled, mates, expert_w, out_raw = together(
        (opened, qkv_slices, own_near, cot_other, settled, mates, expert_w, out_raw)
    )
    out_slices = lax.dynamic_slice_in_dim(out_raw, me * share, share, 0)
    inputs, part, sent, mask0 = opened
    *settled, route_rows, gate_rows = settled
    settled += [[t[0, m].T for m in range(2)] for t in (route_rows, gate_rows)]
    other_near = [swap(cot_other, d) for d in (cube.x, cube.y)] if whole_blocks else []
    if whole_blocks:
        mates.append(swap(expert_w[1], cube.core))
    arrived, other_near, settled, mates, expert_w, out_slices = together(
        (swap(sent, cube.z), other_near, settle(lengths, *settled), mates, expert_w, out_slices)
    )
    fresh1, cot1, mask1, extra0, extra1, starts = settled
    hidden, payload = joined(part, arrived, gain_two, extra0)
    if whole_blocks:
        payload, expert_w, mates = together((payload, expert_w, mates))
        mates.append(swap(expert_w[2], cube.core))
        expert_w = pinned(list(zip(expert_w, mates)), (1, 1, 0))
        mixture = Blocks(cube, expert_w)
        plane = []

        def first_plane(qkv_slices, out_slices):
            near = [qkv_slices] + [swap(qkv_slices, d) for d in (cube.x, cube.y, ("dp", mask))]
            plane.extend([near, swap(out_slices, cube.z)])
            return plane

        side = [None, None, (lambda: [qkv_slices, out_slices], first_plane)]
        results, saved = mixture.forward(payload, 0, side)
        qkv_near, out_slices = plane
    else:
        results, saved = mixture.forward(payload, 0)
    first_mates = []

    def first_exchange(*near):
        first_mates.extend(swap(t, cube.core) for t in near)
        return first_mates

    mids = []

    def first_choice(*both_micros):
        mids.append(chosen(both_micros[2:], both_micros[:2]))
        mids.append(chosen(both_micros[:2], both_micros[2:]))
        return mids

    choice = (lambda: [mask0, extra0, mask1, extra1], first_choice)
    total = mixture.total(results, [both((lambda: qkv_near, first_exchange), choice) if whole_blocks else choice])
    result0 = (hidden + total).astype(bf16)
    if whole_blocks:
        result0, qkv_near, out_slices = together((result0, qkv_near, out_slices))
        arriving = lax.ppermute(result0, "section", [(0, 1)])
        out_near = [out_slices] + [swap(out_slices, d) for d in (cube.x, cube.y, ("dp", mask))]
        all_places = [*plane_places, far_places[0]]
        places = [*all_places, *mate_places(all_places)]

        def assembled(pieces):
            spans = [(p, half_share, 0) for p in places]
            return put_together(pieces, spans, (model, pieces[0].shape[1]))

        arriving, out_near, weights, qkv_packed = together(
            (arriving, out_near, pinned(weights), assembled([*qkv_near, *first_mates]))
        )
        packed = [qkv_packed, assembled([*out_near, *[swap(t, cube.core) for t in out_near]])]
    else:
        arriving = lax.ppermute(result0, "section", [(0, 1)])
        packed = [
            lax.all_gather(t, "dp", axis=0, tiled=True) for t in (qkv_slices, swap(out_slices, cube.z))
        ]

    (mask_mid, extra_mid), (mask_last, extra_last) = mids

    inputs1, hidden1, payload, groups1 = attention_forward(
        fresh1, arriving, mask_mid, gain_one, gain_two, extra_mid, weights, packed
    )
    micro_mid = 1 - section
    late = []

    def cot_far(x0, y1):
        late.extend([swap(x0, cube.y), swap(y1, cube.x)])
        return late

    side = []
    if whole_blocks:
        (x0, y0), (x1, y1) = own_near, other_near
        side = [None, None, (lambda: [x0, y1], cot_far)]
    results, saved1 = mixture.forward(payload, micro_mid, side)

    grad0 = cot_own
    if whole_blocks:
        pieces = [[cot_own], [x0, y0, cot_other], [late[0], y1, x1], [late[1]]]
        run, back_results, keeps0 = mixture.late_backward(pieces, saved1)
        total = mixture.total(results, [run(2), run(1, 0)])
        back_results[3] = run(3)
    else:
        back_results, keeps0 = mixture.backward(grad0, micro_mid, saved1)
        total = mixture.total(results)
    result1 = (hidden1 + total).astype(bf16)

    slot2 = []

    def last_attention(arriving):
        slot2.extend(
            attention_forward(inputs, arriving, mask_last, gain_one, gain_two, extra_last, weights, packed)
        )
        return slot2

    arrived = []

    def second_handoff(result):
        arrived.append(lax.ppermute(result, "section", [(0, 1)]))
        return arrived

    if whole_blocks:
        result1, back_results[:3] = together((result1, back_results[:3]))
    else:
        result1, back_results = together((result1, back_results))
    state = mixture.total_start(back_results, [(lambda: [result1], second_handoff)])
    grad_two = mixture.total_finish(state, [(lambda: arrived, last_attention)])
    inputs2, hidden2, payload, groups2 = slot2

    def attention_turn(grad, grad_two, state):
        inputs, hidden, mask, groups, _ = state
        outs = attention_backward(
            grad, grad_two, inputs, hidden, mask, gain_one, gain_two, [g[0] for g in groups], weights, packed
        )
        grad_input, low, grad_low, normed, g0, g1, attn_g, mlp_g = outs
        factors = (normed, grad_low, (g0, g1), [g[1] for g in groups])
        return grad_input, low, factors, (attn_g, mlp_g)

    state1 = [inputs1, hidden1, mask_mid, groups1, saved1]
    turn0, returned = [], []

    def first_turn(grad_two):
        turn0.extend(attention_turn(grad0, grad_two, state1))
        return turn0

    def first_return(low):
        returned.append(lax.ppermute(low, "section", [(1, 0)]))
        return returned

    side = [(lambda: [grad_two], first_turn), None, (lambda: [turn0[1]], first_return)]
    results2, saved2 = mixture.forward(payload, section, side)
    coming = returned[0]

    sums = [None, None]
    if whole_blocks:
        *results2, corner = results2
        coming, results2, inputs = together((coming, results2, corner[0]()))
        corner = corner[1](*inputs)
        results2 = [*results2, (lambda: [], lambda: [])]
    else:
        coming, results2, saved2 = together((coming, results2, saved2))
    grad1 = coming + cot1
    state2 = [inputs2, hidden2, mask_last, groups2, saved2]
    def run_both(*works):
        works = [w for w in works if w]
        return both(*works) if works else None

    placings = {}

    def placing(name, micro, own):
        def work(rows):
            placings[name, micro] = placed(parted(rows), micro)
            return placings[name, micro]

        return lambda: [own()], work

    place_first = placing("out", 0, lambda: chosen(result0, result1))
    back_results, keeps1 = mixture.backward(grad1, section, saved2, [None, None, place_first])
    corner_sums = []

    def corner_sum(t):
        corner_sums.append(across(t, cube))
        return corner_sums

    corner_work = (lambda: corner, corner_sum) if whole_blocks else None
    hidden_work, _ = mixture.weight_sums([keeps0], sums)
    _, down_work = mixture.weight_sums([keeps0, keeps1], sums)
    hidden_next, _ = mixture.weight_sums([keeps1], sums)
    grad_two = mixture.total(back_results, [run_both(hidden_work, corner_work), run_both(hidden_next)])
    grad_two, down_inputs = together((grad_two, down_work[0]())) if down_work else (grad_two, ())
    turn1 = attention_turn(grad1, grad_two, state2)
    if whole_blocks:
        low, results2[:3] = together((turn1[1], list(results2[:3])))
    else:
        low, results2 = together((turn1[1], results2))
    coming = lax.ppermute(low, "section", [(1, 0)])
    state = mixture.total_start(results2)
    if whole_blocks:
        state = (*state[:3], [*state[3], *corner_sums])
    grad2, state, _ = together((coming, state, down_work[1](*down_inputs) if down_work else ()))

    last_total = []

    def finish_last(*state):
        last_total.append(mixture.total_finish(state[0] if len(state) == 1 else state))
        return last_total

    side = [None, None, (lambda: [state] if not whole_blocks else list(state), finish_last)]
    back_results, keeps2 = mixture.backward(grad2, 1 - section, saved1, side)
    result2 = (hidden2 + last_total[0]).astype(bf16)
    placing_out = placing("out", 1, lambda: chosen(result1, result2))
    placing_grad = placing("grad", 0, lambda: chosen(turn1[0], turn0[0]))
    hidden_end, down_end = mixture.weight_sums([keeps2], sums, True)
    waiting = []

    def part_both(out, grad):
        waiting.extend([parted(out), parted(grad)])
        return waiting

    part_work = (lambda: [chosen(result1, result2), chosen(turn1[0], turn0[0])], part_both)
    grad_two = mixture.total(back_results, [part_work, run_both(hidden_end or down_end)])

    _, hidden, _, groups, _ = state1
    others = [t for t in sums[0] if t.dtype == bf16]
    grad_two, others, waiting = together((grad_two, others, waiting))
    others = [swap(t, cube.core) for t in others]
    received = [swap(given, cube.z) for _, given in waiting]
    heads_all = [[groups1[g][1], groups2[g][1], groups1[g][1]] for g in range(shards)]
    out_pairs = owned_products(cube, [turn0[2][1], turn1[2][1]], heads_all, (grad2, grad_two, hidden, gain_two))
    out_pairs, others, received = together((out_pairs, others, received))
    turn2 = []

    def last_turn(grad_two):
        turn2.extend(attention_turn(grad2, grad_two, state1))
        return turn2

    def exchange(*others):
        return [swap(t, cube.core) for t in others]

    def sums_start(pairs, side):
        middle, rest = pairs
        size = middle[0].shape[0] // 3

        def blocks(*terms):
            return [[t[i : i + size] for t in terms] for i in range(0, terms[0].shape[0], size)]

        middle = [low_sum(*terms) for terms in blocks(middle[0], swap(middle[1], cube.core))]
        other = (lambda: [rest[1]], lambda t: [swap(t, cube.core)])
        arrived, other, mine = reduce_start(cube, middle, other, rest[0], side)
        own, *near, corner = blocks(mine, *other)
        return arrived, corner, near, own

    out_state = sums_start(out_pairs, [(lambda: [grad_two], last_turn)])
    turns = (turn0, turn1, turn2)
    factors = [t[2] for t in turns]
    qkv_pairs = []

    def qkv_products(*_):
        rights = [[f[2][g] for f in factors] for g in range(shards)]
        gains = [g for t in turns for g in t[3]]
        qkv_pairs.extend(owned_products(cube, [f[0] for f in factors], rights, gains=gains))
        return qkv_pairs

    grad_o = reduce_finish(cube, *out_state, [(lambda: [], qkv_products)])
    qkv_pairs, grad_o = together((qkv_pairs, grad_o))

    expert_sums = list(sums[0][:2])

    def hidden_sums(*others):
        for other in others:
            expert_sums[:2] = [mine + wide(t) for mine, t in zip(expert_sums, jnp.split(other, 2, axis=1))]
        return expert_sums

    def down_sums(*others):
        for other in others:
            expert_sums[2] = expert_sums[2] + wide(swap(other, cube.core))
        return expert_sums[2]

    def waited(*got):
        placings["out", 1], placings["grad", 0] = placed(waiting[0], 1, got[0]), placed(waiting[1], 0, got[1])
        return placings["out", 1], placings["grad", 0]

    last_rows = placing("grad", 1, lambda: chosen(turn2[0], turn1[0]))
    last_end = down_end if whole_blocks else None
    qkv_state = sums_start(qkv_pairs, [run_both(last_rows, last_end)])
    expert_sums.append(sums[1][0])
    last_side = run_both((lambda: sums[1][1:], down_sums), (lambda: others, hidden_sums), (lambda: received, waited))
    grad_qkv = reduce_finish(cube, *qkv_state, [last_side])
    gate_total, up_total, down_total = expert_sums
    width = q_weight.shape[2]
    grad_q = grad_qkv[:, :width]
    grad_k = grad_qkv[:, width : width + HEAD_SIZE]
    grad_v = grad_qkv[:, width + HEAD_SIZE : width + 2 * HEAD_SIZE]
    gain_pair = [grad_qkv[:, width + 2 * HEAD_SIZE + i] for i in range(2)]
    section_out = jnp.stack([placings["out", 0], placings["out", 1]])
    input_grad = jnp.stack([placings["grad", 0], placings["grad", 1]])
    return (
        section_out[None],
        input_grad[None],
        gain_pair[0][None],
        grad_q[None],
        grad_k[None],
        grad_v[None],
        grad_o[None],
        gain_pair[1][None],
        gate_total[None, None],
        up_total[None, None],
        down_total[None, None],
    )


def solution(mesh):
    in_specs = (
        P(None, "dp", None),
        P(None, "dp", None),
        P("section", None, "dp", None),
        P("section", None, "dp", None),
        P("section", None),
        P("section", None, "shard"),
        P("section", None, "shard"),
        P("section", None, "shard"),
        P("section", None, "shard"),
        P("section", None),
        P("section", "dp", None, "shard"),
        P("section", "dp", None, "shard"),
        P("section", "dp", "shard", None),
        P(None, "dp", None),
    )
    out_specs = (
        P("section", None, "dp", "shard"),
        P("section", None, "dp", "shard"),
        P("section", "dp"),
        P("section", "dp", "shard"),
        P("section", "dp", "shard"),
        P("section", "dp", "shard"),
        P("section", "dp", "shard"),
        P("section", "dp"),
        P("section", "dp", None, "shard"),
        P("section", "dp", None, "shard"),
        P("section", "dp", "shard", None),
    )
    return jax.shard_map(local, mesh=mesh, in_specs=in_specs, out_specs=out_specs, check_vma=False)
```

```python
import functools

import jax
import jax.numpy as jnp
import numpy as np
from jax import lax
from jax.experimental import pallas as pl
from jax.experimental.pallas import tpu as pltpu
from jax.sharding import PartitionSpec as P

HEAD_SIZE = 128
epsilon = 1e-06
masked_value = -1e30
bf16 = jnp.bfloat16
f32 = jnp.float32


def wide(a):
    return a.astype(f32)


def dot_nn(a, b):
    return lax.dot_general(a, b, (((1,), (0,)), ((), ())), preferred_element_type=f32)


def dot_nt(a, b):
    return lax.dot_general(a, b, (((1,), (1,)), ((), ())), preferred_element_type=f32)


def dot_tn(a, b):
    return lax.dot_general(a, b, (((0,), (0,)), ((), ())), preferred_element_type=f32)


class Cube:
    def __init__(self):
        peers = lax.axis_size("dp")
        bits = [1 << i for i in range(peers.bit_length() - 1)]
        rest = bits[1:]
        self.core = ("dp", bits[0])
        self.x = ("dp", rest[0])
        self.y = ("dp", rest[len(rest) // 2])
        self.z = ("shard", 1)
        self.extra = [("dp", b) for b in rest if b not in (self.x[1], self.y[1])]
        inner = [0]
        for _, bit in self.extra:
            inner = inner + [m | bit for m in inner]
        self.inner = np.array(inner)
        x, y = self.x[1], self.y[1]
        self.corner = (x | y, 1)
        stages = [[(0, 0)], [(x, 0), (y, 0), (0, 1)], [(x | y, 0), (y, 1), (x, 1)], [self.corner]]
        self.stages = [(g, [(m | self.core[1], s) for m, s in g]) for g in stages]


def swap(value, direction):
    axis, bit = direction
    return lax.ppermute(value, axis, [(i, i ^ bit) for i in range(lax.axis_size(axis))])


def across(value, cube):
    mask, flip = cube.corner
    shards = lax.axis_size("shard")
    pairs = [
        (d * shards + s, (d ^ mask) * shards + (s ^ flip))
        for d in range(lax.axis_size("dp"))
        for s in range(shards)
    ]
    return lax.ppermute(value, ("dp", "shard"), pairs)


together = lax.optimization_barrier


def both(*thunks):
    def work(*groups):
        return [thunk[1](*group) for thunk, group in zip(thunks, groups)]

    return lambda: [thunk[0]() for thunk in thunks], work


def after(payload, thunks, step):
    if step >= len(thunks) or thunks[step] is None:
        return payload, lambda: ()
    inputs, work = thunks[step]
    payload, inputs = together((payload, inputs()))
    return payload, lambda: work(*inputs)


def gather_rows(cube, own, work, side=()):
    own, beside = after(own, side, 0)
    near = [swap(own, d) for d in (cube.x, cube.y, cube.z)]
    first = work(0, [own])
    near, first, _ = together((near, first, beside()))

    near, beside = after(near, side, 1)
    middle = [swap(block, d) for block, d in zip(near, (cube.y, cube.z, cube.x))]
    second = work(1, near)
    middle, second, _ = together((middle, second, beside()))

    middle, beside = after(middle, side, 2)
    corner = swap(middle[0], cube.z)
    third = work(2, middle)
    corner, third, _ = together((corner, third, beside()))
    return first, second, third, (lambda: [corner], lambda *blocks: work(3, list(blocks)))


def low_sum(*terms):
    return sum(wide(t) for t in terms).astype(bf16)


def reduce_start(cube, middle, corner, rest, side=()):
    (middle, rest), beside = after((middle, rest), side, 0)
    middle, inputs = together((middle, corner[0]()))
    arrived = [swap(t, d) for t, d in zip(middle, (cube.y, cube.z, cube.x))]
    return together((arrived, corner[1](*inputs), rest, beside()))[:3]


def reduce_finish(cube, arrived, corner, near, own, side=()):
    sent = [low_sum(*terms) for terms in [*([corner] if corner else []), *[[*t, a] for t, a in zip(near, arrived)]]]
    sent, beside = after(sent, side, 0)
    arrived = [swap(t, d) for t, d in zip(sent[-3:], (cube.x, cube.y, cube.z))]
    arrived += [across(t, cube) for t in sent[:-3]]
    arrived, own, _ = together((arrived, own, beside()))
    total = sum(wide(t) for t in [*own, *arrived])
    for direction in reversed(cube.extra):
        half = total.shape[0] // 2
        total = total[:half] + wide(swap(total[half:].astype(bf16), direction))
    return total


def norm_factor(values):
    return lax.rsqrt(jnp.mean(values * values, axis=1, keepdims=True) + epsilon)


def norm_back(values, factor, gain, grad):
    gain_grad = jnp.sum(grad * values * factor, axis=0, keepdims=True)
    scaled = grad * gain
    inner = jnp.mean(scaled * values, axis=1, keepdims=True)
    return factor * (scaled - values * factor * factor * inner), gain_grad


def stack_heads(rows):
    return jnp.concatenate(
        [rows[:, i : i + HEAD_SIZE] for i in range(0, rows.shape[1], HEAD_SIZE)], axis=0
    )


def spread_heads(stacked, rows):
    return jnp.concatenate(
        [stacked[i : i + rows] for i in range(0, stacked.shape[0], rows)], axis=1
    )


def head_probs(query, key, allowed):
    scores = jnp.where(allowed > 0.0, dot_nt(query, key) * HEAD_SIZE ** (-0.5), masked_value)
    exp_scores = jnp.exp(scores - jnp.max(scores, axis=1, keepdims=True))
    return exp_scores / jnp.sum(exp_scores, axis=1, keepdims=True)


def normed_rows(values, gain):
    return (values * norm_factor(values) * gain).astype(bf16)


def group_probs(qkv, allowed):
    width = qkv.shape[1] - 2 * HEAD_SIZE
    query = stack_heads(qkv[:, :width])
    key, value = qkv[:, width : width + HEAD_SIZE], qkv[:, width + HEAD_SIZE :]
    tiled = jnp.concatenate([allowed] * (width // HEAD_SIZE), axis=0)
    return query, key, value, head_probs(query, key, tiled)


def head_group(normed, allowed, weights, qkv, heads):
    *projections, w_out = weights
    at = 0
    for w in projections:
        part = dot_nn(normed, w()).astype(bf16)
        qkv[:, at : at + part.shape[1]] = part
        at += part.shape[1]
    _, _, value, probs = group_probs(qkv[...], allowed)
    heads[...] = spread_heads(dot_nn(probs.astype(bf16), value).astype(bf16), normed.shape[0])
    return dot_nt(heads[...], w_out())


VMEM = pl.BlockSpec(memory_space=pltpu.VMEM)
SMEM = pl.BlockSpec(memory_space=pltpu.SMEM)
ANY = pl.BlockSpec(memory_space=pl.ANY)
KERNEL_VMEM = 42 << 20
COST = 16
HELD = True


def held(shape, dtype):
    return pltpu.VMEM(shape, dtype)


def like(shape, dtype):
    return pltpu.HBM(shape, dtype)


def close(value):
    return pltpu.with_memory_space_constraint(value, pltpu.VMEM)


def distant(value):
    return pltpu.with_memory_space_constraint(value, pltpu.HBM)


def pinned(groups, axes=None):
    groups = [g if isinstance(g, (list, tuple)) else (g,) for g in groups]
    axes = axes or [0] * len(groups)
    values = [v for g in groups for v in g]
    shapes = [
        tuple(n * len(g) if i == axis else n for i, n in enumerate(g[0].shape)) for g, axis in zip(groups, axes)
    ]

    def body(*refs):
        ins, outs, sems = list(refs[: len(values)]), refs[len(values) : -1], refs[-1]
        copies, waits = Copies(sems), []
        for group, axis, out in zip(groups, axes, outs):
            for i, value in enumerate(group):
                size = value.shape[axis]
                place = [slice(None)] * axis + [pl.ds(i * size, size)]
                waits.append(copies.start(ins.pop(0), out.at[tuple(place)]))
        for copy in waits:
            copy.wait()

    return pl.pallas_call(
        body,
        out_shape=[held(shape, g[0].dtype) for g, shape in zip(groups, shapes)],
        in_specs=[ANY] * len(values),
        out_specs=[VMEM] * len(groups),
        scratch_shapes=[pltpu.SemaphoreType.DMA((len(values),))],
        compiler_params=pltpu.CompilerParams(vmem_limit_bytes=1 << 20),
    )(*map(distant, values))


def put_together(pieces, spans, shape):
    starts = jnp.stack([first for first, _, _ in spans]).astype(jnp.int32)

    def body(starts, *refs):
        ins, out, sems = refs[:-2], refs[-2], refs[-1]
        copies, waits = Copies(sems), []
        for i, (piece, (_, unit, column)) in enumerate(zip(ins, spans)):
            rows = pl.ds(pl.multiple_of(starts[i] * unit, unit), piece.shape[0])
            waits.append(copies.start(piece, out.at[rows, pl.ds(column, piece.shape[1])]))
        for copy in waits:
            copy.wait()

    return pl.pallas_call(
        body,
        out_shape=held(shape, pieces[0].dtype),
        in_specs=[SMEM] + [ANY] * len(pieces),
        out_specs=VMEM,
        scratch_shapes=[pltpu.SemaphoreType.DMA((len(pieces),))],
        compiler_params=pltpu.CompilerParams(vmem_limit_bytes=KERNEL_VMEM),
    )(starts, *map(distant, pieces))


class Copies:
    def __init__(self, sems):
        self.sems, self.count = sems, 0

    def start(self, source, target):
        copy = pltpu.make_async_copy(source, target, self.sems.at[self.count])
        self.count += 1
        copy.start()
        return copy

    def fetch(self, source, target):
        copy, waited = self.start(source, target), []

        def value():
            if not waited:
                copy.wait()
                waited.append(True)
            return target[...]

        return value


def on_device(body, outs, args, flops, scalars=(), kept=(), far=(), scratch=(), direct=False):
    moved = sum(a.size * a.dtype.itemsize for a in args)
    return pl.pallas_call(
        body,
        out_shape=outs,
        in_specs=[SMEM] * len(scalars) + [VMEM] * (len(args) + len(kept)) + [ANY] * len(far),
        out_specs=[SMEM if o.dtype == jnp.int32 else ANY if direct else VMEM for o in outs],
        scratch_shapes=scratch,
        compiler_params=pltpu.CompilerParams(vmem_limit_bytes=KERNEL_VMEM),
        cost_estimate=pl.CostEstimate(flops=COST * flops, bytes_accessed=moved, transcendentals=0),
    )(*scalars, *map(distant, args), *map(close, kept), *far)


def holders(*arrays):
    return [pltpu.VMEM(a.shape, a.dtype) for a in arrays] + [pltpu.SemaphoreType.DMA((len(arrays) + 1,))]


def geometry(lens, micro, side, rows, block):
    ends, total, best, start = [], 0, lens[micro, 0, 0], 0
    for i in range(lens.shape[2]):
        length = lens[micro, 0, i]
        if i:
            start = jnp.where(length > best, total, start)
            best = jnp.maximum(best, length)
        total = total + length
        ends.append(total)
    return ends, lax.rem(start + rows * side, block)


def positions(shape, axis, begin, block):
    place = lax.broadcasted_iota(jnp.int32, shape, axis) + begin
    return jnp.where(place >= block, place - block, place)


def selection(begin, rows, block):
    wanted = positions((rows, block), 0, begin, block)
    return (wanted == lax.broadcasted_iota(jnp.int32, (rows, block), 1)).astype(f32)


def sequence_mask(ends, begin, rows, block):
    row, col = [positions((rows, rows), axis, begin, block) for axis in (0, 1)]
    inside = sum(jnp.abs((row >= e).astype(jnp.int32) - (col >= e).astype(jnp.int32)) for e in ends)
    return ((inside == 0) & (col <= row)).astype(f32)


def gate_columns(pick, routes, gates):
    peers = lax.axis_size("dp")
    expert = lax.broadcasted_iota(jnp.int32, (128, routes.shape[1]), 0)
    table = jnp.zeros(expert.shape, f32)
    for k in range(routes.shape[0]):
        gate, route = gates[k : k + 1, :], routes[k : k + 1, :]
        high = wide(gate.astype(bf16))
        table += jnp.where(expert == route, high, 0.0) + jnp.where(expert == route + peers, gate - high, 0.0)
    return dot_nt(pick, table.astype(bf16)).astype(bf16)


def turned_body(lens, blocks, own, other, block_rows, sems):
    copy = Copies(sems).fetch(blocks.at[0], block_rows)
    block = block_rows.shape[0]
    here = jnp.where(lax.axis_index("section") == 0, 0.0, 1.0)
    shard = lax.axis_index("shard")
    for side, out in ((shard, own), (1 - shard, other)):
        _, begin = geometry(lens, 0, side, block // 2, block)
        out[...] = dot_nn((selection(begin, block // 2, block) * here).astype(bf16), copy()).astype(bf16)


def turned_block(lens, blocks):
    _, block, model = blocks.shape
    scratch = [pltpu.VMEM((block, model), bf16), pltpu.SemaphoreType.DMA((1,))]
    shapes = [like((block // 2, model), bf16)] * 2
    return on_device(
        turned_body, shapes, [], 2 * block * block * model, (lens,), far=[distant(blocks)], scratch=scratch
    )


def opening_body(lens, gain, tokens, *refs):
    wq, wk, wv, wo, inputs, part, sent, mask, qkv, heads, *scratch, sems = refs
    copies = Copies(sems)
    sources = [tokens.at[0], wq, wk, wv, wo]
    block_rows, *weights = [copies.fetch(a, b) for a, b in zip(sources, scratch)]
    block = tokens.shape[1]
    rows = block // 2
    shard = lax.axis_index("shard")
    first = jnp.where(lax.axis_index("section") == 0, 1.0, 0.0)
    sides = []
    for side in (shard, 1 - shard):
        ends, begin = geometry(lens, 0, side, rows, block)
        sides.append((selection(begin, rows, block) * first, sequence_mask(ends, begin, rows, block)))
    values = dot_nn(jnp.concatenate([pick for pick, _ in sides], axis=0).astype(bf16), block_rows())
    inputs[...] = values[:rows].astype(bf16)
    mask[...] = sides[0][1]
    normed = normed_rows(values, gain[...])
    *projections, w_out = weights
    projected = jnp.concatenate([dot_nn(normed, w()).astype(bf16) for w in projections], axis=1)
    for i, (_, allowed) in enumerate(sides):
        here = pl.ds(i * rows, rows)
        qkv[here, :] = projected[i * rows : (i + 1) * rows]
        _, _, value, probs = group_probs(qkv[here, :], allowed)
        heads[here, :] = spread_heads(dot_nn(probs.astype(bf16), value).astype(bf16), rows)
    result = dot_nt(heads[...], w_out())
    part[...] = values[:rows] + result[:rows]
    sent[...] = result[rows:].astype(bf16)


def opening(lens, tokens, gain, weights):
    _, block, model = tokens.shape
    rows = block // 2
    width, out = sum(w.shape[1] for w in weights[:3]), weights[3].shape[1]
    shapes = [
        like((rows, model), bf16), held((rows, model), f32), like((rows, model), bf16), like((rows, rows), f32)
    ]
    scratch = [pltpu.VMEM((block, n), bf16) for n in (width, out, model)] + holders(*weights)
    return on_device(
        opening_body, shapes, [gain], 4 * rows * model * (width + out), (lens,),
        far=[distant(t) for t in (tokens, *weights)], scratch=scratch,
    )


def settle_body(lens, routes0, gates0, routes1, gates1, tokens, grad, *refs):
    fresh, cot, mask, extra0, extra1, starts, token_rows, grad_rows, sems = refs
    copies = Copies(sems)
    for micro in range(2):
        _, starts[micro] = geometry(lens, micro, 0, tokens.shape[1] // 2, tokens.shape[1])
    token_rows = copies.fetch(tokens.at[1], token_rows)
    grad_rows = copies.fetch(grad.at[1], grad_rows)
    block = tokens.shape[1]
    rows = block // 2
    first = jnp.where(lax.axis_index("section") == 0, 1.0, 0.0)
    for micro, routes, gates, extra in ((0, routes0, gates0, extra0), (1, routes1, gates1, extra1)):
        ends, begin = geometry(lens, micro, lax.axis_index("shard"), rows, block)
        pick = selection(begin, rows, block)
        extra[...] = gate_columns(pick.astype(bf16), routes[...], gates[...])
    fresh[...] = dot_nn((pick * first).astype(bf16), token_rows()).astype(bf16)
    cot[...] = dot_nn((pick * (1.0 - first)).astype(bf16), grad_rows()).astype(bf16)
    mask[...] = sequence_mask(ends, begin, rows, block)


def settle(lens, tokens, grad, routes, gates):
    _, block, model = tokens.shape
    rows = block // 2
    shapes = [like((rows, model), bf16)] * 2 + [like((rows, rows), f32)] + [like((rows, 128), bf16)] * 2
    shapes.append(pltpu.SMEM((2,), jnp.int32))
    args = [routes[0], gates[0], routes[1], gates[1]]
    scratch = [pltpu.VMEM((block, model), bf16)] * 2 + [pltpu.SemaphoreType.DMA((2,))]
    return on_device(
        settle_body, shapes, args, 2 * block * block * model, (lens,), far=[distant(tokens), distant(grad)], scratch=scratch
    )


def joined_body(other, extra, gain, part, hidden, payload):
    total = part[...] + wide(other[...])
    hidden[...] = total
    model = total.shape[1]
    payload[:, :model] = normed_rows(total, gain[...])
    payload[:, model:] = extra[...]


def joined(part, other, gain, extra):
    rows, model = part.shape
    shapes = [like((rows, model), f32), like((rows, model + extra.shape[1]), bf16)]
    return on_device(joined_body, shapes, [other, extra, gain], 10 * rows * model, kept=[part])


def by_halves(refs):
    *own, packed, packed_out = refs
    widths = [w.shape[1] for w in own[:3]]
    firsts = [sum(widths[:i]) for i in range(3)]
    other = [lambda f=f, w=w: packed[:, f : f + w] for f, w in zip(firsts, widths)]
    return [lambda w=w: w[...] for w in own], [*other, lambda: packed_out[...]]


def attention_body(fresh, arriving, mask, extra, gain, gain_two, *refs):
    own, other = by_halves(refs[:6])
    inputs, hidden, payload, qkv0, qkv1, heads0, heads1 = refs[6:]
    rows = fresh[...] + arriving[...]
    inputs[...] = rows
    total = wide(rows)
    normed = normed_rows(total, gain[...])
    total = total + head_group(normed, mask[...], own, qkv0, heads0)
    total = total + head_group(normed, mask[...], other, qkv1, heads1)
    hidden[...] = total
    model = total.shape[1]
    payload[:, :model] = normed_rows(total, gain_two[...])
    payload[:, model:] = extra[...]


def attention_forward(fresh, arriving, mask, gain, gain_two, extra, weights, packed):
    rows, model = fresh.shape
    width, out = sum(w.shape[1] for w in weights[:3]), weights[3].shape[1]
    shapes = [
        like((rows, model), bf16), like((rows, model), f32), like((rows, model + extra.shape[1]), bf16),
        like((rows, width), bf16), like((rows, width), bf16), like((rows, out), bf16), like((rows, out), bf16),
    ]
    args = [fresh, arriving, mask, extra, gain, gain_two]
    outs = on_device(attention_body, shapes, args, 6 * rows * packed[0].size, kept=[*weights, *packed])
    inputs, hidden, payload, qkv0, qkv1, heads0, heads1 = outs
    return inputs, hidden, payload, [(qkv0, heads0), (qkv1, heads1)]


def attention_back_body(grad, grad_two, inputs, hidden, mask, q0, q1, gain, gain_two, *refs):
    own, other = by_halves(refs[:6])
    grad_input, grad_input_low, grad_low, normed, g0, g1, gain_grad, gain_two_grad = refs[6:]
    rows = inputs.shape[0]
    values = wide(inputs[...])
    normed[...] = normed_rows(values, gain[...])
    total = hidden[...]
    back, gain_two_grad[...] = norm_back(total, norm_factor(total), gain_two[...], grad_two[...])
    grad_hidden = wide(grad[...]) + back
    low = grad_hidden.astype(bf16)
    grad_low[...] = low
    grad_normed = jnp.zeros_like(grad_hidden)
    for qkv, weights, grad_qkv in ((q0, own, g0), (q1, other, g1)):
        query, key, value, probs = group_probs(qkv[...], mask[...])
        grad_heads = stack_heads(dot_nn(low, weights[3]()).astype(bf16))
        grad_probs = dot_nt(grad_heads, value)
        inner = jnp.sum(probs * grad_probs, axis=1, keepdims=True)
        grad_scores = (probs * (grad_probs - inner) * HEAD_SIZE ** (-0.5)).astype(bf16)
        grads = [
            spread_heads(dot_nn(grad_scores, key).astype(bf16), rows),
            dot_tn(grad_scores, query).astype(bf16),
            dot_tn(probs.astype(bf16), grad_heads).astype(bf16),
        ]
        at = 0
        for part, w in zip(grads, weights):
            grad_qkv[:, at : at + part.shape[1]] = part
            at += part.shape[1]
            grad_normed = grad_normed + dot_nt(part, w())
    back, gain_grad[...] = norm_back(values, norm_factor(values), gain[...], grad_normed)
    result = grad_hidden + back
    grad_input[...] = result
    grad_input_low[...] = result.astype(bf16)


def attention_backward(grad, grad_two, inputs, hidden, mask, gain, gain_two, projected, weights, packed):
    rows, model = inputs.shape
    width = projected[0].shape[1]
    shapes = [
        like((rows, model), f32), like((rows, model), bf16), like((rows, model), bf16),
        like((rows, model), bf16), like((rows, width), bf16), like((rows, width), bf16),
        like((1, model), f32), like((1, model), f32),
    ]
    args = [grad, grad_two, inputs, hidden, mask, *projected, gain, gain_two]
    return on_device(attention_back_body, shapes, args, 12 * rows * packed[0].size, kept=[*weights, *packed])


def place(copies, pieces, *targets):
    started, at = [], 0
    for piece in pieces:
        first, count = 0, piece.shape[0]
        for target in targets:
            source = piece.at[:, pl.ds(first, target.shape[1])]
            started.append(copies.start(source, target.at[pl.ds(at, count), :]))
            first += target.shape[1]
        at += count
    return started


def pair_gates(extra, width):
    me, peers = lax.axis_index("dp"), lax.axis_size("dp")
    lane = lax.broadcasted_iota(jnp.int32, extra.shape, 1)

    def gate(expert):
        return jnp.sum(jnp.where((lane == expert) | (lane == expert + peers), wide(extra), 0.0), axis=1, keepdims=True)

    column = lax.broadcasted_iota(jnp.int32, (extra.shape[0], width), 1)
    return jnp.where(column < width // 2, gate(me), gate(me ^ 1))


def expert_stage_body(count, w_gate, w_up, w_down, *refs):
    ins, (gate_out, up_out), outs = refs[:count], refs[count : count + 2], refs[count + 2 : 2 * count + 2]
    rows, extra, gate_held, up_held, part, sems = refs[2 * count + 2 :]
    copies, leaving = Copies(sems), []
    for copy in place(copies, ins, rows, extra):
        copy.wait()
    values = rows[...]
    gate = dot_nn(values, w_gate[...])
    up = dot_nn(values, w_up[...])
    gate_held[...] = gate.astype(bf16)
    leaving.append(copies.start(gate_held, gate_out))
    up_held[...] = up.astype(bf16)
    leaving.append(copies.start(up_held, up_out))
    act = gate / (1.0 + jnp.exp(-gate)) * up * pair_gates(extra[...], gate.shape[1])
    part[...] = dot_nn(act.astype(bf16), w_down[...]).astype(bf16)
    at = 0
    for out in outs:
        leaving.append(copies.start(part.at[pl.ds(at, out.shape[0]), :], out))
        at += out.shape[0]
    for copy in leaving:
        copy.wait()


def expert_stage(pieces, *weights):
    count = sum(p.shape[0] for p in pieces)
    model, units = weights[0].shape
    extra = pieces[0].shape[1] - model
    kind = held if HELD else like
    shapes = [like((count, units), bf16)] * 2 + [kind((p.shape[0], model), bf16) for p in pieces]
    scratch = [pltpu.VMEM((count, n), bf16) for n in (model, extra, units, units, model)]
    scratch.append(pltpu.SemaphoreType.DMA((3 * len(pieces) + 2,)))
    body = functools.partial(expert_stage_body, len(pieces))
    outs = on_device(
        body, shapes, [], 6 * count * weights[0].size, kept=weights, far=pieces, scratch=scratch, direct=True
    )
    return outs[2:], (pieces, *outs[:2])


def expert_back_body(count, w_gate, w_up, w_down, *refs):
    ins, payloads, (gate_in, up_in) = refs[:count], refs[count : 2 * count], refs[2 * count : 2 * count + 2]
    grad_outs, outs = refs[2 * count + 2 : 2 * count + 5], refs[2 * count + 5 : 3 * count + 5]
    grads, extra, gate_held, up_held, *held_back, part, sems = refs[3 * count + 5 :]
    copies, leaving, first = Copies(sems), [], w_gate.shape[0]
    arriving = place(copies, ins, grads)
    at = 0
    for payload in payloads:
        size = payload.shape[0]
        arriving.append(
            copies.start(payload.at[:, pl.ds(first, extra.shape[1])], extra.at[pl.ds(at, size), :])
        )
        at += size
    arriving += [copies.start(gate_in, gate_held), copies.start(up_in, up_held)]
    for copy in arriving:
        copy.wait()
    scale = pair_gates(extra[...], w_gate.shape[1])
    grad_act = scale * dot_nt(grads[...], w_down[...])
    gate, up = wide(gate_held[...]), wide(up_held[...])
    sig = 1.0 / (1.0 + jnp.exp(-gate))
    silu = gate * sig
    low_gate = (grad_act * up * sig * (1.0 + gate * (1.0 - sig))).astype(bf16)
    low_up = (grad_act * silu).astype(bf16)
    for value, held_value, out in zip((low_gate, low_up, (scale * silu * up).astype(bf16)), held_back, grad_outs):
        held_value[...] = value
        leaving.append(copies.start(held_value, out))
    part[...] = (dot_nt(low_gate, w_gate[...]) + dot_nt(low_up, w_up[...])).astype(bf16)
    at = 0
    for out in outs:
        leaving.append(copies.start(part.at[pl.ds(at, out.shape[0]), :], out))
        at += out.shape[0]
    for copy in leaving:
        copy.wait()


def expert_back_stage(pieces, saved, *weights):
    payloads, gate_out, up_out = saved
    count = sum(p.shape[0] for p in pieces)
    model, units = weights[0].shape
    extra = payloads[0].shape[1] - model
    kind = held if HELD else like
    shapes = [like((count, units), bf16)] * 3 + [kind((p.shape[0], model), bf16) for p in pieces]
    scratch = [pltpu.VMEM((count, n), bf16) for n in (model, extra, units, units, units, units, units, model)]
    scratch.append(pltpu.SemaphoreType.DMA((3 * len(pieces) + 5,)))
    body = functools.partial(expert_back_body, len(pieces))
    far = [*pieces, *payloads, gate_out, up_out]
    outs = on_device(
        body, shapes, [], 6 * count * weights[0].size, kept=weights, far=far, scratch=scratch, direct=True
    )
    return outs[3:], (payloads, pieces, *outs[:3])


def swept_products(swept, fixed, sums, swept_left, final):
    width = fixed[0][0].shape[1]
    step, steps = width // 2, 4
    rows = sum(t.shape[0] for t in swept)

    def body(*refs):
        refs = list(refs)
        left = jnp.concatenate([refs.pop(0)[...] for _ in swept], axis=0)
        rights = [jnp.concatenate([refs.pop(0)[...] for _ in group], axis=0) for group in fixed]
        totals = [refs.pop(0)[...] for _ in sums or ()] or [0.0] * len(fixed)
        others = []
        for total, right in zip(totals, rights):
            total = total + (dot_tn(left, right) if swept_left else dot_tn(right, left))
            if final:
                parts = (total[:, :step], total[:, step:]) if swept_left else (total[:step], total[step:])
                refs.pop(0)[...] = parts[0]
                others.append(parts[1].astype(bf16))
            else:
                refs.pop(0)[...] = total
        if final:
            refs.pop(0)[...] = jnp.concatenate(others, axis=1 if swept_left else 0)

    def spec(size):
        return pl.BlockSpec((step, size), lambda j: (j, 0)) if swept_left else pl.BlockSpec((size, step), lambda j: (0, j))

    def shape(size):
        return (step * steps, size) if swept_left else (size, step * steps)

    sizes = [(step if final else width, f32)] * len(fixed) + [(step * len(fixed), bf16)] * final
    shapes = [like(shape(size), dtype) for size, dtype in sizes]
    out_specs = [spec(size) for size, _ in sizes]
    in_specs = [pl.BlockSpec((t.shape[0], step), lambda j: (0, j)) for t in swept]
    in_specs += [pl.BlockSpec(t.shape, lambda j: (0, 0)) for group in fixed for t in group]
    in_specs += [spec(width) for _ in sums or ()]
    return pl.pallas_call(
        body,
        grid=(steps,),
        out_shape=shapes,
        in_specs=in_specs,
        out_specs=out_specs,
        compiler_params=pltpu.CompilerParams(vmem_limit_bytes=KERNEL_VMEM),
        cost_estimate=pl.CostEstimate(flops=COST * 2 * rows * width * step * steps * len(fixed), bytes_accessed=rows, transcendentals=0),
    )(*map(distant, [*swept, *[t for group in fixed for t in group], *(sums or ())]))


def expert_forward(rows, w_gate, w_up, w_down):
    gate_out = dot_nn(rows, w_gate)
    up_out = dot_nn(rows, w_up)
    act = (gate_out / (1.0 + jnp.exp(-gate_out)) * up_out).astype(bf16)
    part = dot_nn(act, w_down).astype(bf16)
    return part, (rows, gate_out.astype(bf16), up_out.astype(bf16))


def expert_backward(grad_rows, saved, w_gate, w_up, w_down):
    rows, gate_low, up_low = saved
    gate_out, up_out = wide(gate_low), wide(up_low)
    grad_act = dot_nt(grad_rows, w_down)
    sig = 1.0 / (1.0 + jnp.exp(-gate_out))
    silu = gate_out * sig
    grad_gate = (grad_act * up_out * sig * (1.0 + gate_out * (1.0 - sig))).astype(bf16)
    grad_up = (grad_act * silu).astype(bf16)
    act = (silu * up_out).astype(bf16)
    grad_in = (dot_nt(grad_gate, w_gate) + dot_nt(grad_up, w_up)).astype(bf16)
    return grad_in, (dot_tn(rows, grad_gate), dot_tn(rows, grad_up), dot_tn(act, grad_rows))


def halves(array):
    half = array.shape[0] // 2
    return array[:half], array[half:]


def owned_body(turns, groups, blocks, with_last, gains, *refs):
    refs = list(refs)
    lefts = [refs.pop(0) for _ in range(turns)]
    rights = [[refs.pop(0) for _ in range(turns + with_last)] for _ in range(groups)]
    last = [refs.pop(0) for _ in range(4 * with_last)]
    gains = [refs.pop(0)[...] for _ in range(gains)]
    outs, products, sems = refs[: 2 * len(blocks)], refs[-2], refs[-1]
    values = [t[...] for t in lefts]
    if with_last:
        grad, grad_two, hidden, gain = last
        total = hidden[...]
        back, _ = norm_back(total, norm_factor(total), gain[...], grad_two[...])
        values.append((wide(grad[...]) + back).astype(bf16))
    left = jnp.concatenate(values, axis=0)
    for g in range(groups):
        right = jnp.concatenate([t[...] for t in rights[g]], axis=0)
        products[g, :, : right.shape[1]] = dot_tn(left, right).astype(bf16)
        if gains:
            terms, at = [], right.shape[1]
            for gain in gains:
                high = gain.astype(bf16)
                terms += [high, (gain - wide(high)).astype(bf16)]
            rows = jnp.concatenate(terms + [jnp.zeros_like(terms[0])] * (-len(terms) % 16), axis=0)
            which = lax.broadcasted_iota(jnp.int32, (rows.shape[0], 128), 0)
            column = lax.broadcasted_iota(jnp.int32, (rows.shape[0], 128), 1)
            chosen = (column == (which // 2) % 2) & (which < len(terms))
            products[g, :, at : at + 128] = dot_tn(rows, jnp.where(chosen, 1.0, 0.0).astype(bf16)).astype(bf16)
    copies, leaving = Copies(sems), []
    me = lax.axis_index("dp")
    share = products.shape[1] // lax.axis_size("dp")
    for i, group in enumerate(blocks):
        for out, places in zip(outs[2 * i : 2 * i + 2], group):
            for j, (mask, side) in enumerate(places):
                rows = pl.ds(pl.multiple_of((me ^ mask) * share, share), share)
                leaving.append(copies.start(products.at[side, rows, :], out.at[pl.ds(j * share, share), :]))
    for copy in leaving:
        copy.wait()


def owned_products(cube, lefts, rights, last=(), gains=()):
    model, width = lefts[0].shape[1], rights[0][0].shape[1] + (128 if gains else 0)
    share = model // lax.axis_size("dp")
    stages = [[[(m ^ int(i), s) for m, s in side for i in cube.inner] for side in pair] for pair in cube.stages]
    own, near, middle, corner = stages
    blocks = [middle, [a + b + c for a, b, c in zip(own, near, corner)]]
    shapes = [like((len(places) * share, width), bf16) for pair in blocks for places in pair]
    scratch = [
        pltpu.VMEM((len(rights), model, width), bf16),
        pltpu.SemaphoreType.DMA((sum(len(places) for pair in blocks for places in pair),)),
    ]
    args = [*lefts, *[t for group in rights for t in group], *last, *gains]
    outs = pl.pallas_call(
        functools.partial(owned_body, len(lefts), len(rights), blocks, 1 if last else 0, len(gains)),
        out_shape=shapes,
        in_specs=[VMEM] * len(args),
        out_specs=[ANY] * len(shapes),
        scratch_shapes=scratch,
        compiler_params=pltpu.CompilerParams(vmem_limit_bytes=KERNEL_VMEM),
    )(*map(distant, args))
    return [(outs[2 * i], outs[2 * i + 1]) for i in range(len(blocks))]


class Blocks:
    def __init__(self, cube, weights):
        self.cube, self.weights = cube, weights

    def forward(self, payload, micro, side=()):
        saved = [None] * 4

        def work(stage, pieces):
            parts, saved[stage] = expert_stage(pieces, *self.weights)
            return parts

        return gather_rows(self.cube, payload, work, side), saved

    def backward(self, grad, micro, saved, side=()):
        keeps = [None] * 4

        def work(stage, pieces):
            parts, keeps[stage] = expert_back_stage(pieces, saved[stage], *self.weights)
            return parts

        return gather_rows(self.cube, grad, work, side), keeps

    def late_backward(self, pieces, saved):
        parts, keeps = [None] * 4, [None] * 4

        def run(*stages):
            def work(*gathered):
                for stage, rows in zip(stages, gathered):
                    parts[stage], keeps[stage] = expert_back_stage(rows, saved[stage], *self.weights)
                return [t for stage in stages for t in parts[stage]]

            return lambda: [pieces[stage] for stage in stages], work

        return run, parts, keeps

    def total_start(self, results, side=()):
        own, near, middle, corner = results
        arrived, corner, (own, near) = reduce_start(self.cube, middle, corner, (own, near), side)
        return arrived, corner, [[t] for t in near], own

    def total_finish(self, state, side=()):
        return reduce_finish(self.cube, *state, side)

    def total(self, results, side=()):
        return self.total_finish(self.total_start(results, side[:1]), side[1:])

    def weight_sums(self, slots, sums, final=False):
        def stages():
            return [stage for keeps in slots for stage in keeps]

        def hidden(*args):
            payloads, gates, ups = args
            sums[0] = swept_products(payloads, [gates, ups], sums[0], True, final)
            return sums[0]

        def down(*args):
            grads, acts = args
            sums[1] = swept_products(grads, [acts], sums[1], False, final)
            return sums[1]

        return [
            (lambda: [[t for s in stages() for t in s[0]], [s[2] for s in stages()], [s[3] for s in stages()]], hidden),
            (lambda: [[t for s in stages() for t in s[1]], [s[4] for s in stages()]], down),
        ]


def run_all(side):
    for thunk in side:
        if thunk is not None:
            thunk[1](*thunk[0]())


class Buckets:
    def __init__(self, cube, weights, routes, gates, capacity):
        self.cube, self.weights, self.capacity = cube, weights, capacity
        micros, self.rows, self.top = routes.shape
        self.experts = lax.axis_size("dp")
        self.tables = []
        for m in range(micros):
            flat = routes[m].reshape(-1)
            onehot = (flat[:, None] == jnp.arange(self.experts, dtype=jnp.int32)).astype(jnp.int32)
            earlier = jnp.cumsum(onehot, axis=0) - onehot
            target = flat * capacity + jnp.sum(earlier * onehot, axis=1)
            source = jnp.full((self.experts * capacity,), flat.shape[0], jnp.int32)
            source = source.at[target].set(jnp.arange(flat.shape[0], dtype=jnp.int32))
            self.tables.append((target, source, gates[m]))

    def table(self, micro):
        return jax.tree.map(lambda a, b: jnp.where(micro == 0, a, b), self.tables[0], self.tables[1])

    def exchange(self, rows):
        shape = (self.experts, self.capacity, rows.shape[1])
        moved = lax.all_to_all(rows.reshape(shape), "dp", split_axis=0, concat_axis=0, tiled=True)
        return moved.reshape(rows.shape)

    def whole(self, own):
        return jnp.concatenate([own, swap(own, self.cube.z)], axis=0)

    def forward(self, payload, micro, side=()):
        target, source, gates = self.table(micro)
        own = payload[:, : self.weights[0].shape[0]]
        padded = jnp.pad(self.whole(own), ((0, 1), (0, 0)))
        arrived = self.exchange(jnp.take(padded, source // self.top, axis=0))
        part, saved = expert_forward(arrived, *self.weights)
        picked = jnp.take(self.exchange(part), target, axis=0).reshape(self.rows, self.top, -1)
        run_all(side)
        return jnp.sum(gates[:, :, None] * picked, axis=1), saved

    def backward(self, grad, micro, saved, side=()):
        target, source, gates = self.table(micro)
        scaled = (gates[:, :, None] * wide(self.whole(grad))[:, None, :]).astype(bf16)
        padded = jnp.pad(scaled.reshape(self.rows * self.top, -1), ((0, 1), (0, 0)))
        arrived = self.exchange(jnp.take(padded, source, axis=0))
        grad_in, weights = expert_backward(arrived, saved, *self.weights)
        picked = jnp.take(self.exchange(grad_in), target, axis=0).reshape(self.rows, self.top, -1)
        run_all(side)
        return jnp.sum(picked, axis=1, dtype=f32), weights

    def total_start(self, results, side=()):
        run_all(side)
        return results

    def total_finish(self, results, side=()):
        own, other = halves(results.astype(bf16))
        run_all(side)
        return wide(own) + wide(swap(other, self.cube.z))

    def total(self, results, side=()):
        return self.total_finish(results, side)

    def weight_sums(self, slots, sums, final=False):
        def add(*slots):
            for weights in slots:
                for i, part in enumerate((list(weights[:2]), list(weights[2:]))):
                    sums[i] = part if sums[i] is None else [a + b for a, b in zip(sums[i], part)]

        return [None, (lambda: slots, add)]


def local(
    tokens, lengths, routes, gates, attn_gain, q_weight, key_projection, value_projection,
    o_weight, mlp_gain, expert_gate, expert_up, expert_down, cotangent,
):
    cube = Cube()
    section = lax.axis_index("section")
    shard = lax.axis_index("shard")
    me = lax.axis_index("dp")
    peers, shards = lax.axis_size("dp"), lax.axis_size("shard")
    _, block_rows, model = tokens.shape
    rows = block_rows // shards
    share = model // peers
    first = section == 0
    gain_one, gain_two = attn_gain[0][None], mlp_gain[0][None]
    weights = [q_weight[0], key_projection[0], value_projection[0], o_weight[0]]
    expert_w = (expert_gate[0, 0], expert_up[0, 0], expert_down[0, 0])
    capacity = 2 * block_rows * routes.shape[3] // peers
    whole_blocks = capacity >= block_rows

    def chosen(here, there):
        return jax.tree.map(lambda a, b: jnp.where(first, a, b), here, there)

    def begins(lens):
        lens = lens[:, 0]
        ends, longest = jnp.cumsum(lens, axis=1), jnp.argmax(lens, axis=1)
        return [ends[m, longest[m]] - lens[m, longest[m]] for m in range(2)]

    def turned(array, begin):
        doubled = jnp.concatenate([array, array], axis=0)
        return lax.dynamic_slice_in_dim(doubled, (begin + rows * shard) % block_rows, block_rows, 0)

    if not whole_blocks:
        early = begins(lengths)
        mixture = Buckets(
            cube,
            expert_w,
            jnp.stack([turned(routes[0, m], early[m]) for m in range(2)]),
            jnp.stack([turned(gates[0, m], early[m]) for m in range(2)]),
            capacity,
        )

    slices = [lax.dynamic_slice_in_dim(w, me * share, share, 0) for w in weights[:3]]
    qkv_slices = swap(jnp.concatenate(slices, axis=1), cube.z)
    half_share = share // 2
    mask = cube.x[1] | cube.y[1]
    far_places = [2 * (me ^ mask), 2 * (me ^ mask) + 1]
    plane_places = [2 * (me ^ m) for m in (0, cube.x[1], cube.y[1])]
    mate_bit = cube.core[1]

    def mate_places(places):
        return [p ^ (2 * mate_bit) for p in places]

    def parted(own):
        half = model // shards
        given = lax.dynamic_slice_in_dim(own, (1 - shard) * half, half, 1)
        return lax.dynamic_slice_in_dim(own, shard * half, half, 1), given.astype(bf16)

    def placed(parts, m, got=None):
        kept, given = parts
        got = (swap(given, cube.z) if got is None else got).astype(kept.dtype)
        low = jnp.where(shard == 0, kept, got)
        high = jnp.where(shard == 0, got, kept)
        return lax.dynamic_slice_in_dim(
            jnp.concatenate([low, high, low, high], axis=0), (block_rows - starts[m]) % block_rows, block_rows, 0
        )

    cot_own, cot_other = turned_block(lengths, cotangent)
    own_near = [swap(cot_own, d) for d in (cube.x, cube.y)] if whole_blocks else []
    opened = opening(lengths, tokens, gain_one, weights)
    settled = [tokens, cotangent, routes, gates]
    out_raw = weights[3]
    mates = [swap(expert_w[0], cube.core)] if whole_blocks else []
    opened, qkv_slices, own_near, cot_other, settled, mates, expert_w, out_raw = together(
        (opened, qkv_slices, own_near, cot_other, settled, mates, expert_w, out_raw)
    )
    out_slices = lax.dynamic_slice_in_dim(out_raw, me * share, share, 0)
    inputs, part, sent, mask0 = opened
    *settled, route_rows, gate_rows = settled
    settled += [[t[0, m].T for m in range(2)] for t in (route_rows, gate_rows)]
    other_near = [swap(cot_other, d) for d in (cube.x, cube.y)] if whole_blocks else []
    if whole_blocks:
        mates.append(swap(expert_w[1], cube.core))
    arrived, other_near, settled, mates, expert_w, out_slices = together(
        (swap(sent, cube.z), other_near, settle(lengths, *settled), mates, expert_w, out_slices)
    )
    fresh1, cot1, mask1, extra0, extra1, starts = settled
    hidden, payload = joined(part, arrived, gain_two, extra0)
    if whole_blocks:
        payload, expert_w, mates = together((payload, expert_w, mates))
        mates.append(swap(expert_w[2], cube.core))
        expert_w = pinned(list(zip(expert_w, mates)), (1, 1, 0))
        mixture = Blocks(cube, expert_w)
        plane = []

        def first_plane(qkv_slices, out_slices):
            near = [qkv_slices] + [swap(qkv_slices, d) for d in (cube.x, cube.y, ("dp", mask))]
            plane.extend([near, swap(out_slices, cube.z)])
            return plane

        side = [None, None, (lambda: [qkv_slices, out_slices], first_plane)]
        results, saved = mixture.forward(payload, 0, side)
        qkv_near, out_slices = plane
    else:
        results, saved = mixture.forward(payload, 0)
    first_mates = []

    def first_exchange(*near):
        first_mates.extend(swap(t, cube.core) for t in near)
        return first_mates

    mids = []

    def first_choice(*both_micros):
        mids.append(chosen(both_micros[2:], both_micros[:2]))
        mids.append(chosen(both_micros[:2], both_micros[2:]))
        return mids

    choice = (lambda: [mask0, extra0, mask1, extra1], first_choice)
    total = mixture.total(results, [both((lambda: qkv_near, first_exchange), choice) if whole_blocks else choice])
    result0 = (hidden + total).astype(bf16)
    if whole_blocks:
        result0, qkv_near, out_slices = together((result0, qkv_near, out_slices))
        arriving = lax.ppermute(result0, "section", [(0, 1)])
        out_near = [out_slices] + [swap(out_slices, d) for d in (cube.x, cube.y, ("dp", mask))]
        all_places = [*plane_places, far_places[0]]
        places = [*all_places, *mate_places(all_places)]

        def assembled(pieces):
            spans = [(p, half_share, 0) for p in places]
            return put_together(pieces, spans, (model, pieces[0].shape[1]))

        arriving, out_near, weights, qkv_packed = together(
            (arriving, out_near, pinned(weights), assembled([*qkv_near, *first_mates]))
        )
        packed = [qkv_packed, assembled([*out_near, *[swap(t, cube.core) for t in out_near]])]
    else:
        arriving = lax.ppermute(result0, "section", [(0, 1)])
        packed = [
            lax.all_gather(t, "dp", axis=0, tiled=True) for t in (qkv_slices, swap(out_slices, cube.z))
        ]

    (mask_mid, extra_mid), (mask_last, extra_last) = mids

    inputs1, hidden1, payload, groups1 = attention_forward(
        fresh1, arriving, mask_mid, gain_one, gain_two, extra_mid, weights, packed
    )
    micro_mid = 1 - section
    late = []

    def cot_far(x0, y1):
        late.extend([swap(x0, cube.y), swap(y1, cube.x)])
        return late

    side = []
    if whole_blocks:
        (x0, y0), (x1, y1) = own_near, other_near
        side = [None, None, (lambda: [x0, y1], cot_far)]
    results, saved1 = mixture.forward(payload, micro_mid, side)

    grad0 = cot_own
    if whole_blocks:
        pieces = [[cot_own], [x0, y0, cot_other], [late[0], y1, x1], [late[1]]]
        run, back_results, keeps0 = mixture.late_backward(pieces, saved1)
        total = mixture.total(results, [run(2), run(1, 0)])
        back_results[3] = run(3)
    else:
        back_results, keeps0 = mixture.backward(grad0, micro_mid, saved1)
        total = mixture.total(results)
    result1 = (hidden1 + total).astype(bf16)

    slot2 = []

    def last_attention(arriving):
        slot2.extend(
            attention_forward(inputs, arriving, mask_last, gain_one, gain_two, extra_last, weights, packed)
        )
        return slot2

    arrived = []

    def second_handoff(result):
        arrived.append(lax.ppermute(result, "section", [(0, 1)]))
        return arrived

    if whole_blocks:
        result1, back_results[:3] = together((result1, back_results[:3]))
    else:
        result1, back_results = together((result1, back_results))
    state = mixture.total_start(back_results, [(lambda: [result1], second_handoff)])
    grad_two = mixture.total_finish(state, [(lambda: arrived, last_attention)])
    inputs2, hidden2, payload, groups2 = slot2

    def attention_turn(grad, grad_two, state):
        inputs, hidden, mask, groups, _ = state
        outs = attention_backward(
            grad, grad_two, inputs, hidden, mask, gain_one, gain_two, [g[0] for g in groups], weights, packed
        )
        grad_input, low, grad_low, normed, g0, g1, attn_g, mlp_g = outs
        factors = (normed, grad_low, (g0, g1), [g[1] for g in groups])
        return grad_input, low, factors, (attn_g, mlp_g)

    state1 = [inputs1, hidden1, mask_mid, groups1, saved1]
    turn0, returned = [], []

    def first_turn(grad_two):
        turn0.extend(attention_turn(grad0, grad_two, state1))
        return turn0

    def first_return(low):
        returned.append(lax.ppermute(low, "section", [(1, 0)]))
        return returned

    side = [(lambda: [grad_two], first_turn), None, (lambda: [turn0[1]], first_return)]
    results2, saved2 = mixture.forward(payload, section, side)
    coming = returned[0]

    sums = [None, None]
    if whole_blocks:
        *results2, corner = results2
        coming, results2, inputs = together((coming, results2, corner[0]()))
        corner = corner[1](*inputs)
        results2 = [*results2, (lambda: [], lambda: [])]
    else:
        coming, results2, saved2 = together((coming, results2, saved2))
    grad1 = coming + cot1
    state2 = [inputs2, hidden2, mask_last, groups2, saved2]
    def run_both(*works):
        works = [w for w in works if w]
        return both(*works) if works else None

    placings = {}

    def placing(name, micro, own):
        def work(rows):
            placings[name, micro] = placed(parted(rows), micro)
            return placings[name, micro]

        return lambda: [own()], work

    place_first = placing("out", 0, lambda: chosen(result0, result1))
    back_results, keeps1 = mixture.backward(grad1, section, saved2, [None, None, place_first])
    corner_sums = []

    def corner_sum(t):
        corner_sums.append(across(t, cube))
        return corner_sums

    corner_work = (lambda: corner, corner_sum) if whole_blocks else None
    hidden_work, _ = mixture.weight_sums([keeps0], sums)
    _, down_work = mixture.weight_sums([keeps0, keeps1], sums)
    hidden_next, _ = mixture.weight_sums([keeps1], sums)
    grad_two = mixture.total(back_results, [run_both(hidden_work, corner_work), run_both(hidden_next)])
    grad_two, down_inputs = together((grad_two, down_work[0]())) if down_work else (grad_two, ())
    turn1 = attention_turn(grad1, grad_two, state2)
    if whole_blocks:
        low, results2[:3] = together((turn1[1], list(results2[:3])))
    else:
        low, results2 = together((turn1[1], results2))
    coming = lax.ppermute(low, "section", [(1, 0)])
    state = mixture.total_start(results2)
    if whole_blocks:
        state = (*state[:3], [*state[3], *corner_sums])
    grad2, state, _ = together((coming, state, down_work[1](*down_inputs) if down_work else ()))

    last_total = []

    def finish_last(*state):
        last_total.append(mixture.total_finish(state[0] if len(state) == 1 else state))
        return last_total

    side = [None, None, (lambda: [state] if not whole_blocks else list(state), finish_last)]
    back_results, keeps2 = mixture.backward(grad2, 1 - section, saved1, side)
    result2 = (hidden2 + last_total[0]).astype(bf16)
    placing_out = placing("out", 1, lambda: chosen(result1, result2))
    placing_grad = placing("grad", 0, lambda: chosen(turn1[0], turn0[0]))
    hidden_end, down_end = mixture.weight_sums([keeps2], sums, True)
    waiting = []

    def part_both(out, grad):
        waiting.extend([parted(out), parted(grad)])
        return waiting

    part_work = (lambda: [chosen(result1, result2), chosen(turn1[0], turn0[0])], part_both)
    grad_two = mixture.total(back_results, [part_work, run_both(hidden_end or down_end)])

    _, hidden, _, groups, _ = state1
    others = [t for t in sums[0] if t.dtype == bf16]
    grad_two, others, waiting = together((grad_two, others, waiting))
    others = [swap(t, cube.core) for t in others]
    received = [swap(given, cube.z) for _, given in waiting]
    heads_all = [[groups1[g][1], groups2[g][1], groups1[g][1]] for g in range(shards)]
    out_pairs = owned_products(cube, [turn0[2][1], turn1[2][1]], heads_all, (grad2, grad_two, hidden, gain_two))
    out_pairs, others, received = together((out_pairs, others, received))
    turn2 = []

    def last_turn(grad_two):
        turn2.extend(attention_turn(grad2, grad_two, state1))
        return turn2

    def exchange(*others):
        return [swap(t, cube.core) for t in others]

    def sums_start(pairs, side):
        middle, rest = pairs
        size = middle[0].shape[0] // 3

        def blocks(*terms):
            return [[t[i : i + size] for t in terms] for i in range(0, terms[0].shape[0], size)]

        middle = [low_sum(*terms) for terms in blocks(middle[0], swap(middle[1], cube.core))]
        other = (lambda: [rest[1]], lambda t: [swap(t, cube.core)])
        arrived, other, mine = reduce_start(cube, middle, other, rest[0], side)
        own, *near, corner = blocks(mine, *other)
        return arrived, corner, near, own

    out_state = sums_start(out_pairs, [(lambda: [grad_two], last_turn)])
    turns = (turn0, turn1, turn2)
    factors = [t[2] for t in turns]
    qkv_pairs = []

    def qkv_products(*_):
        rights = [[f[2][g] for f in factors] for g in range(shards)]
        gains = [g for t in turns for g in t[3]]
        qkv_pairs.extend(owned_products(cube, [f[0] for f in factors], rights, gains=gains))
        return qkv_pairs

    grad_o = reduce_finish(cube, *out_state, [(lambda: [], qkv_products)])
    qkv_pairs, grad_o = together((qkv_pairs, grad_o))

    expert_sums = list(sums[0][:2])

    def hidden_sums(*others):
        for other in others:
            expert_sums[:2] = [mine + wide(t) for mine, t in zip(expert_sums, jnp.split(other, 2, axis=1))]
        return expert_sums

    def down_sums(*others):
        for other in others:
            expert_sums[2] = expert_sums[2] + wide(swap(other, cube.core))
        return expert_sums[2]

    def waited(*got):
        placings["out", 1], placings["grad", 0] = placed(waiting[0], 1, got[0]), placed(waiting[1], 0, got[1])
        return placings["out", 1], placings["grad", 0]

    last_rows = placing("grad", 1, lambda: chosen(turn2[0], turn1[0]))
    last_end = down_end if whole_blocks else None
    qkv_state = sums_start(qkv_pairs, [run_both(last_rows, last_end)])
    expert_sums.append(sums[1][0])
    last_side = run_both((lambda: sums[1][1:], down_sums), (lambda: others, hidden_sums), (lambda: received, waited))
    grad_qkv = reduce_finish(cube, *qkv_state, [last_side])
    gate_total, up_total, down_total = expert_sums
    width = q_weight.shape[2]
    grad_q = grad_qkv[:, :width]
    grad_k = grad_qkv[:, width : width + HEAD_SIZE]
    grad_v = grad_qkv[:, width + HEAD_SIZE : width + 2 * HEAD_SIZE]
    gain_pair = [grad_qkv[:, width + 2 * HEAD_SIZE + i] for i in range(2)]
    section_out = jnp.stack([placings["out", 0], placings["out", 1]])
    input_grad = jnp.stack([placings["grad", 0], placings["grad", 1]])
    return (
        section_out[None],
        input_grad[None],
        gain_pair[0][None],
        grad_q[None],
        grad_k[None],
        grad_v[None],
        grad_o[None],
        gain_pair[1][None],
        gate_total[None, None],
        up_total[None, None],
        down_total[None, None],
    )


def solution(mesh):
    in_specs = (
        P(None, "dp", None),
        P(None, "dp", None),
        P("section", None, "dp", None),
        P("section", None, "dp", None),
        P("section", None),
        P("section", None, "shard"),
        P("section", None, "shard"),
        P("section", None, "shard"),
        P("section", None, "shard"),
        P("section", None),
        P("section", "dp", None, "shard"),
        P("section", "dp", None, "shard"),
        P("section", "dp", "shard", None),
        P(None, "dp", None),
    )
    out_specs = (
        P("section", None, "dp", "shard"),
        P("section", None, "dp", "shard"),
        P("section", "dp"),
        P("section", "dp", "shard"),
        P("section", "dp", "shard"),
        P("section", "dp", "shard"),
        P("section", "dp", "shard"),
        P("section", "dp"),
        P("section", "dp", None, "shard"),
        P("section", "dp", None, "shard"),
        P("section", "dp", "shard", None),
    )
    return jax.shard_map(local, mesh=mesh, in_specs=in_specs, out_specs=out_specs, check_vma=False)
```
